32 devices in a mesh: section: 2 (over core), dp: 16 (over z, y, x).
Axes of the slice: x: 2, y: 2, z: 4, core: 2. Of those that a mesh axis runs over, the one named last changes fastest.
Arguments:
- x_in: bfloat16 [4096, 1024], P('dp'), may hold values from -6 to 6
- cotangent: bfloat16 [4096, 1024], P('dp'), may hold values from -6 to 6
- doc_lengths: int32 [32, 8], P('dp'), may hold values from 1 to 64, 128 in all within a row
- w_qkv: float32 [2, 1024, 3072], P('section', 'dp'), may hold values from -0.1875 to 0.1875
- w_out: float32 [2, 1024, 1024], P('section', 'dp'), may hold values from -0.5 to 0.5
- w_up: float32 [2, 1024, 4096], P('section', 'dp'), may hold values from -0.1875 to 0.1875
- w_down: float32 [2, 4096, 1024], P('section', 'dp'), may hold values from -0.09375 to 0.09375
- vectors: float32 [2, 11264], P('section', 'dp'), may hold values from -1 to 3.5, as said below
- m_qkv: float32 [2, 1024, 3072], P('section', 'dp'), may hold values from -0.00012207031 to 0.00012207031
- m_out: float32 [2, 1024, 1024], P('section', 'dp'), may hold values from -0.00012207031 to 0.00012207031
- m_up: float32 [2, 1024, 4096], P('section', 'dp'), may hold values from -0.00012207031 to 0.00012207031
- m_down: float32 [2, 4096, 1024], P('section', 'dp'), may hold values from -0.00012207031 to 0.00012207031
- m_vectors: float32 [2, 11264], P('section', 'dp'), may hold values from -0.00048828125 to 0.00048828125
- v_qkv: float32 [2, 1024, 3072], P('section', 'dp'), may hold values from 1.0441334e-09 to 1.6714075e-08
- v_out: float32 [2, 1024, 1024], P('section', 'dp'), may hold values from 1.0441334e-09 to 1.6714075e-08
- v_up: float32 [2, 1024, 4096], P('section', 'dp'), may hold values from 1.0441334e-09 to 1.6714075e-08
- v_down: float32 [2, 4096, 1024], P('section', 'dp'), may hold values from 1.0441334e-09 to 1.6714075e-08
- v_vectors: float32 [2, 11264], P('section', 'dp'), may hold values from 1.6674374e-08 to 2.6599596e-07
Outputs:
- hidden_out: bfloat16 [2, 4096, 1024], P('section', 'dp')
- input_grads: bfloat16 [2, 4096, 1024], P('section', 'dp')
- new_qkv: float32 [2, 1024, 3072], P('section', 'dp')
- new_out: float32 [2, 1024, 1024], P('section', 'dp')
- new_up: float32 [2, 1024, 4096], P('section', 'dp')
- new_down: float32 [2, 4096, 1024], P('section', 'dp')
- new_vectors: float32 [2, 11264], P('section', 'dp')
- first_qkv: float32 [2, 1024, 3072], P('section', 'dp')
- first_out: float32 [2, 1024, 1024], P('section', 'dp')
- first_up: float32 [2, 1024, 4096], P('section', 'dp')
- first_down: float32 [2, 4096, 1024], P('section', 'dp')
- first_vectors: float32 [2, 11264], P('section', 'dp')
- second_qkv: float32 [2, 1024, 3072], P('section', 'dp')
- second_out: float32 [2, 1024, 1024], P('section', 'dp')
- second_up: float32 [2, 1024, 4096], P('section', 'dp')
- second_down: float32 [2, 4096, 1024], P('section', 'dp')
- second_vectors: float32 [2, 11264], P('section', 'dp')
- grad_norm: float32 [], replicated
The draws below stay inside these ranges and needn't reach their ends.
Inputs may be any that keep to these rules, and one draw needn't show every extreme that they name: `doc_lengths`: each row gives, in order, the lengths of the 8 documents of one packed sequence; they sum to 128, and the longest has exactly 64 tokens. `vectors`: per block, in order: query, key and value biases, output bias, up bias, down bias, the norm's gain, the norm's bias.
All inputs are finite; a program needn't handle non-finite values.
Results may differ from the reference program's by a relative error of at most 0.018.
The reference program's roundings to bfloat16 on the way count: a program that leaves them out, or rounds other values in their place, can miss the bound.
Values may be sent and summed in bfloat16 or wider, within the bound.
No kernel may reach another device: no remote copies, remote signals or barrier semaphores. Data moves between devices by JAX's collectives and lax.ppermute only.
A program may use at most 512 MiB of HBM per device.

```python
import math
import jax
import jax.numpy as jnp
import numpy as np
from jax import lax

D = 1024
FF = 4096
HEADS = 16
HEAD_DIM = 64
ROT = 16
SEQ = 128
DOCS = 8
STEP = 10
NV = 11264
NSEQ = 32
TOKENS = 4096


def draw_vectors(key, part):
    key = jax.random.fold_in(key, 11)
    noise_key, gain_key = jax.random.split(key)
    values = 0.2 * jnp.clip(jax.random.normal(noise_key, (2, 7 * D + FF), jnp.float32), -5.0, 5.0)
    fraction = jnp.arange(D, dtype=jnp.float32) / D
    section_level = 1.0 + 0.4 * jnp.arange(2, dtype=jnp.float32)
    rising = 0.5 * 3.0 ** fraction
    jitter = jax.random.uniform(gain_key, (2, D), jnp.float32, 0.85, 1.15)
    gains = section_level[:, None] * rising[None, :] * jitter
    gain_start = 5 * D + FF
    return values.at[:, gain_start:gain_start + D].set(gains)


def shard_levels(stream_key, dims, shards, low, top_value):
    level = 1.0
    for dim, shards_of in shards:
        steps = jax.random.uniform(jax.random.fold_in(jax.random.fold_in(stream_key, 6), dim), (shards_of,), jnp.float32, low / len(shards), top_value / len(shards))
        level = level * jnp.repeat(jnp.exp(steps), dims[dim] // shards_of).reshape((-1,) + (1,) * (len(dims) - 1 - dim))
    return level


def profile(count, total, bound, lean):
    weights = [(1 << 20) // math.isqrt(grade ** lean) + 1 for grade in range(2, count + 1)]
    spare, holding = total - bound - (count - 1), [1] * (count - 1)
    while spare > 0:
        free = [i for i in range(count - 1) if holding[i] < bound]
        pool, left = sum([weights[i] for i in free]), spare
        for i in free:
            more = min(bound - holding[i], max(1, left * weights[i] // pool), spare)
            holding[i] = holding[i] + more
            spare = spare - more
    return np.array([bound] + holding)


def ragged(key, amount, total, bound, lean):
    if amount == 2:
        one = jax.random.randint(key, (), max(1, total - bound), min(bound, total - 1) + 1)
        return jnp.stack([one, total - one])
    sizes = jnp.asarray(profile(amount, total, bound, lean), jnp.int32)
    pairs = (amount - 1) // 2
    source_of, taker = sizes[1:1 + 2 * pairs:2], sizes[2:2 + 2 * pairs:2]
    room = jnp.minimum(source_of - 1, bound - taker)
    moved = jax.random.randint(jax.random.fold_in(key, 1), (pairs,), 0, 1 << 20) % (room + 1)
    sizes = sizes.at[1:1 + 2 * pairs:2].set(source_of - moved).at[2:2 + 2 * pairs:2].set(taker + moved)
    return sizes[jax.random.permutation(jax.random.fold_in(key, 2), amount)]


def centred(own_key, shape, deviation, bound, cuts=(), held_as=jnp.bfloat16):
    drawn = deviation * jax.random.normal(own_key, shape, jnp.float32)
    if cuts:
        drawn = drawn * shard_levels(own_key, shape, cuts, -0.22, 0.18)
    return jnp.clip(drawn, -bound, bound).astype(held_as)


def setup_inputs(seed: int = 0) -> dict:
    arg_keys = jax.random.split(jax.random.key(seed), 19)
    x_in = centred(arg_keys[0], (TOKENS, D), 1.0, 6.0, ((0, 16),))
    cotangent = centred(arg_keys[1], (TOKENS, D), 1.0, 6.0, ((0, 16),))
    doc_lengths = jax.vmap(lambda own: ragged(own, DOCS, SEQ, SEQ // 2, 2))(jax.random.split(arg_keys[2], NSEQ)).reshape((NSEQ, DOCS)).astype(jnp.int32)
    w_qkv = centred(arg_keys[3], (2, D, 3 * D), D ** -0.5, 0.1875, ((0, 2), (1, 16)), jnp.float32)
    w_out = centred(arg_keys[4], (2, D, D), (D // 8) ** -0.5, 0.5, ((0, 2), (1, 16)), jnp.float32)
    w_up = centred(arg_keys[5], (2, D, FF), D ** -0.5, 0.1875, ((0, 2), (1, 16)), jnp.float32)
    w_down = centred(arg_keys[6], (2, FF, D), FF ** -0.5, 0.09375, ((0, 2), (1, 16)), jnp.float32)
    vectors = draw_vectors(jax.random.fold_in(arg_keys[18], 71), 0)
    m_qkv = centred(arg_keys[8], (2, D, 3 * D), (0.111 / (2 * (4 * D * D + 2 * D * FF + 7 * D + FF)) ** 0.5), 0.00012207031, ((0, 2), (1, 16)), jnp.float32)
    m_out = centred(arg_keys[9], (2, D, D), (0.111 / (2 * (4 * D * D + 2 * D * FF + 7 * D + FF)) ** 0.5), 0.00012207031, ((0, 2), (1, 16)), jnp.float32)
    m_up = centred(arg_keys[10], (2, D, FF), (0.111 / (2 * (4 * D * D + 2 * D * FF + 7 * D + FF)) ** 0.5), 0.00012207031, ((0, 2), (1, 16)), jnp.float32)
    m_down = centred(arg_keys[11], (2, FF, D), (0.111 / (2 * (4 * D * D + 2 * D * FF + 7 * D + FF)) ** 0.5), 0.00012207031, ((0, 2), (1, 16)), jnp.float32)
    m_vectors = centred(arg_keys[12], (2, NV), (0.444 / (2 * (4 * D * D + 2 * D * FF + 7 * D + FF)) ** 0.5), 0.00048828125, ((0, 2), (1, 16)), jnp.float32)
    v_qkv = jnp.clip(jnp.exp(math.log(1.6714075457002764e-08) - 2.773064 * jax.random.uniform(arg_keys[13], (2, D, 3 * D), jnp.float32) ** shard_levels(arg_keys[13], (2, D, 3 * D), ((0, 2), (1, 16)), -0.2, 0.2)), 1.0441334463706653e-09, 1.6714075457002764e-08)
    v_out = jnp.clip(jnp.exp(math.log(1.6714075457002764e-08) - 2.773064 * jax.random.uniform(arg_keys[14], (2, D, D), jnp.float32) ** shard_levels(arg_keys[14], (2, D, D), ((0, 2), (1, 16)), -0.2, 0.2)), 1.0441334463706653e-09, 1.6714075457002764e-08)
    v_up = jnp.clip(jnp.exp(math.log(1.6714075457002764e-08) - 2.773064 * jax.random.uniform(arg_keys[15], (2, D, FF), jnp.float32) ** shard_levels(arg_keys[15], (2, D, FF), ((0, 2), (1, 16)), -0.2, 0.2)), 1.0441334463706653e-09, 1.6714075457002764e-08)
    v_down = jnp.clip(jnp.exp(math.log(1.6714075457002764e-08) - 2.773064 * jax.random.uniform(arg_keys[16], (2, FF, D), jnp.float32) ** shard_levels(arg_keys[16], (2, FF, D), ((0, 2), (1, 16)), -0.2, 0.2)), 1.0441334463706653e-09, 1.6714075457002764e-08)
    v_vectors = jnp.clip(jnp.exp(math.log(2.659959648099175e-07) - 2.769608 * jax.random.uniform(arg_keys[17], (2, NV), jnp.float32) ** shard_levels(arg_keys[17], (2, NV), ((0, 2), (1, 16)), -0.2, 0.2)), 1.6674373881642168e-08, 2.659959648099175e-07)
    return {"x_in": x_in, "cotangent": cotangent, "doc_lengths": doc_lengths, "w_qkv": w_qkv, "w_out": w_out, "w_up": w_up, "w_down": w_down, "vectors": vectors, "m_qkv": m_qkv, "m_out": m_out, "m_up": m_up, "m_down": m_down, "m_vectors": m_vectors, "v_qkv": v_qkv, "v_out": v_out, "v_up": v_up, "v_down": v_down, "v_vectors": v_vectors}


@jax.custom_vjp
def low(v):
    return lax.optimization_barrier(v.astype(jnp.bfloat16)).astype(jnp.float32)

@jax.custom_vjp
def low_back(v):
    return v

def low_keep(v):
    return (low(v), None)

def low_pass(kept, grad):
    return (grad,)

def back_keep(v):
    return (v, None)

def back_low(kept, grad):
    return (low(grad),)
low.defvjp(low_keep, low_pass)
low_back.defvjp(back_keep, back_low)
HIGHEST_MODE = lax.Precision.HIGHEST
NORM_EPS = 1e-05
BETA_ONE = 0.9
BETA_TWO = 0.95
LEARN_RATE = 0.05
VECTOR_RATE = 0.3
WEIGHT_DECAY = 0.01
CLIP_LEVEL = 1.0
ADAM_EPS = 1e-08

def doc_layout(lengths, row_count):
    lengths = lengths.astype(jnp.int32)
    ends = jnp.cumsum(lengths).astype(jnp.int32)
    starts = (ends - lengths).astype(jnp.int32)
    places = jnp.arange(row_count, dtype=jnp.int32)
    segment = lax.optimization_barrier(jnp.sum((places[:, None] >= ends[None, :]).astype(jnp.int32), axis=1)).astype(jnp.int32)
    onehot = segment[:, None] == jnp.arange(lengths.shape[0], dtype=jnp.int32)[None, :]
    begins = lax.optimization_barrier(jnp.sum(jnp.where(onehot, starts[None, :], 0), axis=1)).astype(jnp.int32)
    return (segment, (places - begins).astype(jnp.int32))

def rotary_tables(position):
    half = ROT // 2
    inverse = 10000.0 ** (-(jnp.arange(half, dtype=jnp.float32) * 2.0) / ROT)
    angles = position.astype(jnp.float32)[:, None] * inverse[None, :]
    angles = jnp.concatenate([angles, angles], axis=1)
    return (jnp.cos(angles), jnp.sin(angles))

def rotate_heads(part, cosine, sine):
    half = ROT // 2
    head = part[..., :ROT]
    turned = jnp.concatenate([-head[..., half:], head[..., :half]], axis=-1)
    head = head * cosine[:, None, :] + turned * sine[:, None, :]
    return jnp.concatenate([head, part[..., ROT:]], axis=-1)

def split_vectors(vec):
    widths = [3 * D, D, FF, D, D, D]
    pieces = []
    offset = 0
    for size_now in widths:
        pieces.append(vec[offset:offset + size_now])
        offset += size_now
    return pieces

def sequence_block(rows, lengths, params):
    w_qkv, w_out, w_up, w_down, vec = params
    b_qkv, b_out, b_up, b_down, gain, ln_bias = split_vectors(vec)
    row_count = rows.shape[0]
    row_mean = lax.optimization_barrier(jnp.mean(rows, axis=-1, keepdims=True))
    centered = rows - row_mean
    variance = lax.optimization_barrier(jnp.mean(centered * centered, axis=-1, keepdims=True))
    normed = centered * lax.rsqrt(variance + NORM_EPS)
    normed_low = low(normed * gain + ln_bias)
    qkv = low_back(jnp.dot(normed_low, w_qkv, precision=HIGHEST_MODE) + b_qkv)
    parts = qkv.reshape(row_count, 3, HEADS, HEAD_DIM)
    segment, position = doc_layout(lengths, row_count)
    cosine, sine = rotary_tables(position)
    query = low(rotate_heads(parts[:, 0], cosine, sine))
    keys = low(rotate_heads(parts[:, 1], cosine, sine))
    values = low(parts[:, 2])
    scale_factor = HEAD_DIM ** (-0.5)
    scores = low_back(jnp.einsum('qhd,khd->hqk', query, keys, precision=HIGHEST_MODE) * scale_factor)
    places = jnp.arange(row_count, dtype=jnp.int32)
    allowed = (segment[:, None] == segment[None, :]) & (places[None, :] <= places[:, None])
    masked = jnp.where(allowed[None], scores, -1e+30)
    top_score = lax.optimization_barrier(jnp.max(masked, axis=-1, keepdims=True))
    expo = jnp.exp(masked - top_score)
    denom = lax.optimization_barrier(jnp.sum(expo, axis=-1, keepdims=True))
    probs = low(expo / denom)
    mixed = jnp.einsum('hqk,khd->qhd', probs, values, precision=HIGHEST_MODE).reshape(row_count, D)
    mixed = low_back(low(mixed))
    hidden = low_back(jnp.dot(normed_low, w_up, precision=HIGHEST_MODE) + b_up)
    active = low(jax.nn.gelu(hidden, approximate=False))
    branch = jnp.dot(mixed, w_out, precision=HIGHEST_MODE) + b_out + jnp.dot(active, w_down, precision=HIGHEST_MODE) + b_down
    branch = low_back(branch)
    return rows + branch

def block_apply(seqs, lengths, params):
    params = tuple((low(p) for p in params))
    seq_count, seq_len, width = seqs.shape
    group = math.gcd(seq_count, max(1, 4096 // seq_len))
    grouped = seqs.reshape(seq_count // group, group, seq_len, width)
    grouped_lengths = lengths.reshape(seq_count // group, group, lengths.shape[1])

    def group_block(pair):
        return jax.vmap(lambda a, b: sequence_block(a, b, params))(pair[0], pair[1])
    result = lax.map(jax.checkpoint(group_block), (grouped, grouped_lengths))
    return result.reshape(seqs.shape)

def adam_update(weight, grad, first, second, factor, rate):
    clipped = grad * factor
    first_new = BETA_ONE * first + (1.0 - BETA_ONE) * clipped
    second_new = BETA_TWO * second + (1.0 - BETA_TWO) * clipped * clipped
    first_hat = first_new / (1.0 - BETA_ONE ** STEP)
    second_hat = second_new / (1.0 - BETA_TWO ** STEP)
    weight_new = weight - rate * (first_hat / (jnp.sqrt(second_hat) + ADAM_EPS) + WEIGHT_DECAY * weight)
    return (weight_new, first_new, second_new)

def reference(x_in, cotangent, doc_lengths, w_qkv, w_out, w_up, w_down, vectors, m_qkv, m_out, m_up, m_down, m_vectors, v_qkv, v_out, v_up, v_down, v_vectors):
    seq_count = x_in.shape[0] // SEQ
    masters = (w_qkv, w_out, w_up, w_down, vectors)
    first_block = tuple((w[0] for w in masters))
    second_block = tuple((w[1] for w in masters))
    seqs = x_in.astype(jnp.float32).reshape(seq_count, SEQ, D)
    out_first, back_first = jax.vjp(lambda a, p: block_apply(a, doc_lengths, p), seqs, first_block)
    sent = out_first.astype(jnp.bfloat16)
    out_second, back_second = jax.vjp(lambda a, p: block_apply(a, doc_lengths, p), sent.astype(jnp.float32), second_block)
    incoming = cotangent.astype(jnp.float32).reshape(seq_count, SEQ, D)
    grad_mid, grads_second = back_second(incoming)
    grad_mid_low = grad_mid.astype(jnp.bfloat16)
    grad_start, grads_first = back_first(grad_mid_low.astype(jnp.float32))
    hidden_out = jnp.stack([sent, out_second.astype(jnp.bfloat16)]).reshape(2, x_in.shape[0], D)
    input_grads = jnp.stack([grad_start.astype(jnp.bfloat16), grad_mid_low]).reshape(2, x_in.shape[0], D)
    grads = tuple((jnp.stack([a, b]) for a, b in zip(grads_first, grads_second)))
    squares = jnp.float32(0.0)
    for grad in grads:
        squares = squares + jnp.sum(grad * grad)
    grad_norm = jnp.sqrt(squares)
    factor = jnp.minimum(1.0, CLIP_LEVEL / (grad_norm + 1e-06))
    firsts = (m_qkv, m_out, m_up, m_down, m_vectors)
    seconds = (v_qkv, v_out, v_up, v_down, v_vectors)
    rates = (LEARN_RATE, LEARN_RATE, LEARN_RATE, LEARN_RATE, VECTOR_RATE)
    updated = [adam_update(w, g, m, v, factor, r) for w, g, m, v, r in zip(masters, grads, firsts, seconds, rates)]
    return (hidden_out, input_grads, updated[0][0], updated[1][0], updated[2][0], updated[3][0], updated[4][0], updated[0][1], updated[1][1], updated[2][1], updated[3][1], updated[4][1], updated[0][2], updated[1][2], updated[2][2], updated[3][2], updated[4][2], grad_norm)
```

```python
import jax
import jax.numpy as jnp
from jax import lax
from jax.sharding import PartitionSpec as P

D = 1024
FF = 4096
HEADS = 16
HEAD_DIM = 64
ROT = 16
STEP = 10


NORM_EPS = 1e-05
BETA_ONE = 0.9
BETA_TWO = 0.95
LEARN_RATE = 0.05
VECTOR_RATE = 0.3
WEIGHT_DECAY = 0.01
CLIP_LEVEL = 1.0
ADAM_EPS = 1e-08


def doc_layout(lengths, row_count):
    ends = jnp.cumsum(lengths)
    starts = ends - lengths
    places = jnp.arange(row_count, dtype=jnp.int32)
    segment = jnp.sum((places[:, None] >= ends[None, :]).astype(jnp.int32), axis=1)
    onehot = segment[:, None] == jnp.arange(lengths.shape[0], dtype=jnp.int32)[None, :]
    begins = jnp.sum(jnp.where(onehot, starts[None, :], 0), axis=1)
    return (segment, places - begins)


def rotary_tables(position):
    half = ROT // 2
    inverse = 10000.0 ** (-(jnp.arange(half, dtype=jnp.float32) * 2.0) / ROT)
    angles = position.astype(jnp.float32)[:, None] * inverse[None, :]
    angles = jnp.concatenate([angles, angles], axis=1)
    return (jnp.cos(angles), jnp.sin(angles))


def rotate_heads(part, cosine, sine):
    half = ROT // 2
    head = part[..., :ROT]
    turned = jnp.concatenate([-head[..., half:], head[..., :half]], axis=-1)
    head = head * cosine[:, None, :] + turned * sine[:, None, :]
    return jnp.concatenate([head, part[..., ROT:]], axis=-1)


def contract_rows(left, right):
    return lax.dot_general(
        left, right, (((0,), (0,)), ((), ())), preferred_element_type=jnp.float32
    )


def contract_cols(left, right):
    return lax.dot_general(
        left, right, (((1,), (1,)), ((), ())), preferred_element_type=jnp.float32
    )


def adam_update(weight, grad, first, second, factor, rate):
    clipped = grad * factor
    first_new = BETA_ONE * first + (1.0 - BETA_ONE) * clipped
    second_new = BETA_TWO * second + (1.0 - BETA_TWO) * clipped * clipped
    first_hat = first_new / (1.0 - BETA_ONE**STEP)
    second_hat = second_new / (1.0 - BETA_TWO**STEP)
    weight_new = weight - rate * (
        first_hat / (jnp.sqrt(second_hat) + ADAM_EPS) + WEIGHT_DECAY * weight
    )
    return (weight_new, first_new, second_new)

PLANES = 4
AXES = ("section", "dp")


class Place:
    def __init__(self):
        self.count = lax.axis_size("dp")
        self.ring = self.count // PLANES
        self.bits = self.ring.bit_length() - 1
        self.core = lax.axis_index("section")
        index = lax.axis_index("dp")
        self.plane = index // self.ring
        self.spot = index % self.ring

    def move(self, block, where):
        route = []
        for core in range(2):
            for plane in range(PLANES):
                for spot in range(self.ring):
                    c, z, t = where(core, plane, spot)
                    route.append(
                        (core * self.count + plane * self.ring + spot, c * self.count + z * self.ring + t)
                    )
        return lax.ppermute(block, AXES, route)

    def sibling(self, block):
        return self.move(block, lambda c, z, t: (1 - c, z, t))

    def to_plane(self, block, distance):
        return self.move(block, lambda c, z, t: (c, (z + distance) % PLANES, t))

    def ring_bit(self, core, step):
        return step if core == 0 else self.bits - 1 - step

    def across(self, block, step):
        return self.move(block, lambda c, z, t: (c, z, t ^ (1 << self.ring_bit(c, step))))

    def ring_place(self, spot, core):
        low = jnp.bitwise_xor(spot, self.spot)
        turned = sum(((low >> b) & 1) << (self.bits - 1 - b) for b in range(self.bits))
        return jnp.where(core == 0, low, turned)


def take(block, index, axis=0):
    return lax.dynamic_index_in_dim(block, index, axis, keepdims=False)


def gather_planes(place, block):
    parts = [block]
    for distance in range(1, PLANES):
        parts.append(place.to_plane(block, -distance))
    return parts


def ring_gather(place, block):
    held = block[None]
    for step in range(place.bits):
        held = jnp.concatenate([held, place.across(held, step)])
    return held


def ring_reduce(place, held):
    for step in reversed(range(place.bits)):
        half = held.shape[0] // 2
        came = place.across(held[half:].astype(jnp.bfloat16), step)
        held = held[:half] + came.astype(jnp.float32)
    return held[0]


def all_sum(place, block):
    for step in range(2):
        block = block + place.move(block, lambda c, z, t: (c, z ^ (1 << step), t))
    for step in range(place.bits):
        block = block + place.across(block, step)
    return block + place.sibling(block)


def split_vec(vec):
    widths = [3 * D, D, FF, D, D, D]
    pieces = []
    offset = 0
    for size_now in widths:
        pieces.append(vec[offset : offset + size_now])
        offset += size_now
    return pieces


def layer_norm(rows):
    row_mean = jnp.mean(rows, axis=-1, keepdims=True)
    centered = rows - row_mean
    variance = jnp.mean(centered * centered, axis=-1, keepdims=True)
    inverse_std = lax.rsqrt(variance + NORM_EPS)
    return centered * inverse_std, inverse_std


def forward(rows_low, lengths, weights, biases):
    w_qkv, w_out, w_up, w_down = weights
    b_qkv, b_up, gain, ln_bias = biases
    seqs, row_count, width = rows_low.shape
    heads = HEADS // PLANES
    normed, _ = layer_norm(rows_low.astype(jnp.float32))
    y_low = (normed * gain + ln_bias).astype(jnp.bfloat16).reshape(seqs * row_count, width)
    qkv = jnp.dot(y_low, w_qkv, preferred_element_type=jnp.float32) + b_qkv
    parts = qkv.reshape(seqs, row_count, 3, heads, HEAD_DIM)
    segment, position = jax.vmap(lambda one: doc_layout(one, row_count))(lengths)
    cosine, sine = jax.vmap(rotary_tables)(position)
    turn = jax.vmap(rotate_heads)
    query = turn(parts[:, :, 0], cosine, sine).astype(jnp.bfloat16)
    keys = turn(parts[:, :, 1], cosine, sine).astype(jnp.bfloat16)
    values = parts[:, :, 2].astype(jnp.bfloat16)
    scores = jnp.einsum("sqhd,skhd->shqk", query, keys, preferred_element_type=jnp.float32)
    scores = scores * HEAD_DIM ** (-0.5)
    places = jnp.arange(row_count, dtype=jnp.int32)
    allowed = (segment[:, :, None] == segment[:, None, :]) & (places[None, :] <= places[:, None])
    masked = jnp.where(allowed[:, None], scores, -1e30)
    top_score = jnp.max(masked, axis=-1, keepdims=True)
    expo = jnp.exp(masked - top_score)
    probs = expo / jnp.sum(expo, axis=-1, keepdims=True)
    probs_low = probs.astype(jnp.bfloat16)
    mixed = jnp.einsum("shqk,skhd->sqhd", probs_low, values, preferred_element_type=jnp.float32)
    mixed_low = mixed.reshape(seqs * row_count, heads * HEAD_DIM).astype(jnp.bfloat16)
    hidden = jnp.dot(y_low, w_up, preferred_element_type=jnp.float32) + b_up
    active_low = jax.nn.gelu(hidden, approximate=False).astype(jnp.bfloat16)
    branch = jnp.dot(mixed_low, w_out, preferred_element_type=jnp.float32)
    branch = branch + jnp.dot(active_low, w_down, preferred_element_type=jnp.float32)
    kept = (y_low, cosine, sine, query, keys, values, probs, mixed_low, hidden, active_low)
    return branch.astype(jnp.bfloat16).reshape(seqs, row_count, width), kept


def rotate_back(part, cosine, sine):
    half = ROT // 2
    head = part[..., :ROT]
    turned = jnp.concatenate([head[..., half:], -head[..., :half]], axis=-1)
    head = head * cosine[:, :, None, :] + turned * sine[:, :, None, :]
    return jnp.concatenate([head, part[..., ROT:]], axis=-1)


def backward(kept, weights, grad_low):
    w_qkv, w_out, w_up, w_down = weights
    y_low, cosine, sine, query, keys, values, probs, mixed_low, hidden, active_low = kept
    seqs, row_count, width = grad_low.shape
    heads = HEADS // PLANES
    out_low = grad_low.reshape(seqs * row_count, width)
    grad_wout = contract_rows(mixed_low, out_low)
    grad_wdown = contract_rows(active_low, out_low)
    mixed_grad = contract_cols(out_low, w_out).astype(jnp.bfloat16)
    active_grad = contract_cols(out_low, w_down)
    _, gelu_back = jax.vjp(lambda h: jax.nn.gelu(h, approximate=False), hidden)
    hidden_grad = gelu_back(active_grad)[0].astype(jnp.bfloat16)
    grad_wup = contract_rows(y_low, hidden_grad)
    grad_bup = jnp.sum(hidden_grad.astype(jnp.float32), axis=0)
    heads_grad = mixed_grad.reshape(seqs, row_count, heads, HEAD_DIM)
    probs_grad = jnp.einsum("sqhd,skhd->shqk", heads_grad, values, preferred_element_type=jnp.float32)
    probs_low = probs.astype(jnp.bfloat16)
    values_grad = jnp.einsum("shqk,sqhd->skhd", probs_low, heads_grad, preferred_element_type=jnp.float32)
    score_grad = probs * (probs_grad - jnp.sum(probs * probs_grad, axis=-1, keepdims=True))
    score_low = score_grad.astype(jnp.bfloat16)
    scale_factor = HEAD_DIM ** (-0.5)
    query_grad = jnp.einsum("shqk,skhd->sqhd", score_low, keys, preferred_element_type=jnp.float32)
    keys_grad = jnp.einsum("shqk,sqhd->skhd", score_low, query, preferred_element_type=jnp.float32)
    query_raw = rotate_back(query_grad * scale_factor, cosine, sine)
    keys_raw = rotate_back(keys_grad * scale_factor, cosine, sine)
    qkv_grad = jnp.stack([query_raw, keys_raw, values_grad], axis=2)
    qkv_grad = qkv_grad.reshape(seqs * row_count, 3 * heads * HEAD_DIM).astype(jnp.bfloat16)
    grad_wqkv = contract_rows(y_low, qkv_grad)
    grad_bqkv = jnp.sum(qkv_grad.astype(jnp.float32), axis=0)
    y_grad = contract_cols(qkv_grad, w_qkv) + contract_cols(hidden_grad, w_up)
    y_grad = y_grad.astype(jnp.bfloat16).reshape(seqs, row_count, width)
    return y_grad, (grad_wqkv, grad_wout, grad_wup, grad_wdown, grad_bqkv, grad_bup)


def to_owners(place, parts):
    total = parts[0].astype(jnp.float32)
    for distance in range(1, PLANES):
        total = total + place.to_plane(parts[distance], distance).astype(jnp.float32)
    return total


def shards(
    x_in,
    cotangent,
    doc_lengths,
    w_qkv,
    w_out,
    w_up,
    w_down,
    vectors,
    m_qkv,
    m_out,
    m_up,
    m_down,
    m_vectors,
    v_qkv,
    v_out,
    v_up,
    v_down,
    v_vectors,
):
    place = Place()
    core, plane = place.core, place.plane
    low = jnp.bfloat16
    masters = (w_qkv, w_out, w_up, w_down, vectors)
    local_rows, width = x_in.shape
    seq_rows = local_rows // doc_lengths.shape[0]
    own_seqs = doc_lengths.shape[0] // 2
    own_rows = own_seqs * seq_rows
    in_rows = w_qkv.shape[1]
    ff_rows = w_down.shape[1]
    group_d, group_f = D // PLANES, FF // PLANES
    qu_width = 3 * group_d + group_f

    x_own = take(x_in.reshape(2, own_rows, width), core)
    cot_own = take(cotangent.reshape(2, own_rows, width), core)
    len_own = take(doc_lengths.reshape(2, own_seqs, -1), core)

    qkv_low = w_qkv[0].astype(low).reshape(2, in_rows // 2, 3, PLANES, group_d)
    qkv_low = qkv_low.transpose(0, 3, 1, 2, 4).reshape(2, PLANES, in_rows // 2, 3 * group_d)
    up_low = w_up[0].astype(low).reshape(2, in_rows // 2, PLANES, group_f).transpose(0, 2, 1, 3)
    qu_low = jnp.concatenate([qkv_low, up_low], axis=3)
    od_low = jnp.concatenate(
        [
            w_out[0].astype(low).reshape(2, in_rows // 2, width),
            w_down[0].astype(low).reshape(2, ff_rows // 2, width),
        ],
        axis=1,
    )
    vec_low = vectors[0].astype(low)

    def both_blocks(halves):
        kept, came = take(halves, core), place.sibling(take(halves, 1 - core))
        return [jnp.where(core == b, kept, came) for b in range(2)]

    qu_half = both_blocks(qu_low)
    od_half = both_blocks(od_low)
    vec_came = place.sibling(vec_low)
    vec_both = jnp.stack([jnp.where(core == b, vec_low, vec_came) for b in range(2)])

    vec_all = jnp.stack(gather_planes(place, vec_both))
    vec_all = ring_gather(place, vec_all)
    vec_all = jnp.stack([take(vec_all, place.ring_place(t, core)) for t in range(place.ring)])
    vec_all = jnp.stack([take(vec_all, (z - plane) % PLANES, 1) for z in range(PLANES)])

    def block_weights(block):
        od_mine = ring_gather(place, od_half[block])
        od_other = place.sibling(od_mine)
        qu_own = qu_half[block]
        planes = [take(qu_own, plane)]
        for distance in range(1, PLANES):
            planes.append(place.to_plane(take(qu_own, (plane + distance) % PLANES), distance))
        qu_mine = ring_gather(place, jnp.stack(planes))
        qu_other = place.sibling(qu_mine)
        od_cores = [jnp.where(core == h, od_mine, od_other) for h in range(2)]
        qu_cores = [jnp.where(core == h, qu_mine, qu_other) for h in range(2)]
        od_parts, qu_parts = [], []
        for spot in range(place.ring):
            for h in range(2):
                od_parts.append(take(od_cores[h], place.ring_place(spot, h)))
        for z in range(PLANES):
            for spot in range(place.ring):
                for h in range(2):
                    piece = take(qu_cores[h], place.ring_place(spot, h))
                    qu_parts.append(take(piece, (plane - z) % PLANES))
        od_all = jnp.stack(od_parts)
        full_out = od_all[:, : in_rows // 2].reshape(group_d, width)
        full_down = od_all[:, in_rows // 2 :].reshape(group_f, width)
        qu_all = jnp.concatenate(qu_parts)
        return qu_all[:, : 3 * group_d], full_out, qu_all[:, 3 * group_d :], full_down

    def block_vectors(block):
        vec = vec_all[:, :, block].reshape(-1).astype(jnp.float32)
        b_qkv, b_out, b_up, b_down, gain, ln_bias = split_vec(vec)
        b_qkv = take(b_qkv.reshape(3, PLANES, group_d), plane, 1).reshape(-1)
        b_up = take(b_up.reshape(PLANES, group_f), plane)
        return (b_qkv, b_up, gain, ln_bias), b_out + b_down, gain

    x_group = gather_planes(place, x_own)
    len_group = jnp.concatenate(gather_planes(place, len_own))
    grad_group = gather_planes(place, cot_own)

    def as_seqs(parts):
        return jnp.concatenate(parts).reshape(PLANES * own_seqs, seq_rows, width)

    def as_slots(block):
        return block.reshape(PLANES, own_rows, width)

    weights = [block_weights(0), block_weights(1)]
    vecs = [block_vectors(0), block_vectors(1)]

    branch, kept_first = forward(as_seqs(x_group), len_group, weights[0], vecs[0][0])
    branch = to_owners(place, as_slots(branch))
    hidden_first = (x_own.astype(jnp.float32) + branch + vecs[0][1]).astype(low)
    hidden_group = gather_planes(place, hidden_first)
    branch, kept_second = forward(as_seqs(hidden_group), len_group, weights[1], vecs[1][0])
    branch = to_owners(place, as_slots(branch))
    hidden_second = (hidden_first.astype(jnp.float32) + branch + vecs[1][1]).astype(low)

    def rows_backward(rows_low, grad_low, y_parts, gain):
        y_grad = to_owners(place, as_slots(y_parts))
        normed, inverse_std = layer_norm(rows_low.astype(jnp.float32))
        grad_gain = jnp.sum(y_grad * normed, axis=0)
        grad_lnbias = jnp.sum(y_grad, axis=0)
        scaled = y_grad * gain
        inner_mean = jnp.mean(scaled, axis=-1, keepdims=True)
        inner_cross = jnp.mean(scaled * normed, axis=-1, keepdims=True)
        out_grad = grad_low.astype(jnp.float32)
        rows_grad = out_grad + inverse_std * (scaled - inner_mean - normed * inner_cross)
        return rows_grad.astype(low), (jnp.sum(out_grad, axis=0), grad_gain, grad_lnbias)

    y_parts, grads_second = backward(kept_second, weights[1], as_seqs(grad_group))
    mid_grad, vec_grads_second = rows_backward(hidden_first, cot_own, y_parts, vecs[1][2])
    mid_group = gather_planes(place, mid_grad)
    y_parts, grads_first = backward(kept_first, weights[0], as_seqs(mid_group))
    start_grad, vec_grads_first = rows_backward(x_own, mid_grad, y_parts, vecs[0][2])

    def reduce_pieces(halves):
        came = place.sibling(take(halves, 1 - core).astype(low))
        held = take(halves, core) + came.astype(jnp.float32)
        held = jnp.stack([take(held, jnp.bitwise_xor(place.spot, turn)) for turn in slot_spots])
        return ring_reduce(place, held)

    slot_spots = [
        jnp.where(
            core == 0, j, sum(((j >> b) & 1) << (place.bits - 1 - b) for b in range(place.bits))
        )
        for j in range(place.ring)
    ]

    def block_shares(grads):
        grad_wqkv, grad_wout, grad_wup, grad_wdown, _, _ = grads
        od = jnp.concatenate(
            [
                grad_wout.reshape(place.ring, 2, in_rows // 2, width),
                grad_wdown.reshape(place.ring, 2, ff_rows // 2, width),
            ],
            axis=2,
        ).swapaxes(0, 1)
        od = reduce_pieces(od)
        qu = jnp.concatenate([grad_wqkv, grad_wup], axis=1)
        qu = qu.reshape(PLANES, place.ring, 2, in_rows // 2, qu_width).transpose(2, 1, 0, 3, 4)
        qu = reduce_pieces(qu)
        squares = jnp.sum(od * od) + jnp.sum(qu * qu)
        qu_low = qu.astype(low)
        planes = [take(qu_low, plane)]
        for distance in range(1, PLANES):
            planes.append(place.to_plane(take(qu_low, (plane + distance) % PLANES), distance))
        planes = jnp.stack(planes)
        planes = jnp.stack([take(planes, (plane - z) % PLANES) for z in range(PLANES)])
        return od.astype(low), planes, squares

    def vector_grads(grads, row_grads):
        bias_grad, grad_gain, grad_lnbias = row_grads
        grad_bqkv = jnp.zeros((3, PLANES, group_d), jnp.float32)
        grad_bqkv = lax.dynamic_update_index_in_dim(grad_bqkv, grads[4].reshape(3, group_d), plane, 1)
        grad_bup = lax.dynamic_update_index_in_dim(
            jnp.zeros((PLANES, group_f), jnp.float32), grads[5], plane, 0
        )
        return jnp.concatenate(
            [grad_bqkv.reshape(-1), bias_grad, grad_bup.reshape(-1), bias_grad, grad_gain, grad_lnbias]
        )

    vec_grad = jnp.stack(
        [vector_grads(grads_first, vec_grads_first), vector_grads(grads_second, vec_grads_second)]
    )
    vec_grad = all_sum(place, vec_grad)
    vec_share = take(vec_grad, core).reshape(place.count, -1)
    vec_share = take(vec_share, lax.axis_index("dp"))

    od_first, qu_first, sq_first = block_shares(grads_first)
    od_second, qu_second, sq_second = block_shares(grads_second)
    squares = all_sum(place, jnp.broadcast_to(sq_first + sq_second, (8, 128)))[0, 0]
    grad_norm = jnp.sqrt(squares + jnp.sum(vec_grad * vec_grad))
    factor = jnp.minimum(1.0, CLIP_LEVEL / (grad_norm + 1e-06))

    def own_block(first, second):
        came = place.sibling(jnp.where(core == 0, second, first))
        mine = jnp.where(core == 0, first, second)
        return [jnp.where(core == h, mine, came) for h in range(2)]

    od = jnp.stack(own_block(od_first, od_second))
    qu = jnp.stack(own_block(qu_first, qu_second))
    share_out = od[:, : in_rows // 2].reshape(1, in_rows, width)
    share_down = od[:, in_rows // 2 :].reshape(1, ff_rows, width)
    share_qkv = qu[..., : 3 * group_d].reshape(2, PLANES, in_rows // 2, 3, group_d)
    share_qkv = share_qkv.transpose(0, 2, 3, 1, 4).reshape(1, in_rows, 3 * D)
    share_up = qu[..., 3 * group_d :].transpose(0, 2, 1, 3).reshape(1, in_rows, FF)
    shares = (share_qkv, share_out, share_up, share_down, vec_share[None])
    firsts = (m_qkv, m_out, m_up, m_down, m_vectors)
    seconds = (v_qkv, v_out, v_up, v_down, v_vectors)
    rates = (LEARN_RATE, LEARN_RATE, LEARN_RATE, LEARN_RATE, VECTOR_RATE)
    updated = [
        adam_update(w, g.astype(jnp.float32), m, v, factor, r)
        for w, g, m, v, r in zip(masters, shares, firsts, seconds, rates)
    ]

    def own_rows_of_block(first, second):
        came = place.sibling(jnp.where(core == 0, second, first))
        mine = jnp.where(core == 0, first, second)
        both = [jnp.where(core == h, mine, came) for h in range(2)]
        return jnp.concatenate(both)[None]

    hidden_out = own_rows_of_block(hidden_first, hidden_second)
    input_grads = own_rows_of_block(start_grad, mid_grad)
    return (
        hidden_out,
        input_grads,
        updated[0][0],
        updated[1][0],
        updated[2][0],
        updated[3][0],
        updated[4][0],
        updated[0][1],
        updated[1][1],
        updated[2][1],
        updated[3][1],
        updated[4][1],
        updated[0][2],
        updated[1][2],
        updated[2][2],
        updated[3][2],
        updated[4][2],
        grad_norm,
    )


def solution(mesh):
    return jax.shard_map(
        shards,
        mesh=mesh,
        in_specs=(
            P("dp", None),
            P("dp", None),
            P("dp", None),
            P("section", "dp", None),
            P("section", "dp", None),
            P("section", "dp", None),
            P("section", "dp", None),
            P("section", "dp"),
            P("section", "dp", None),
            P("section", "dp", None),
            P("section", "dp", None),
            P("section", "dp", None),
            P("section", "dp"),
            P("section", "dp", None),
            P("section", "dp", None),
            P("section", "dp", None),
            P("section", "dp", None),
            P("section", "dp"),
        ),
        out_specs=(
            P("section", "dp", None),
            P("section", "dp", None),
            P("section", "dp", None),
            P("section", "dp", None),
            P("section", "dp", None),
            P("section", "dp", None),
            P("section", "dp"),
            P("section", "dp", None),
            P("section", "dp", None),
            P("section", "dp", None),
            P("section", "dp", None),
            P("section", "dp"),
            P("section", "dp", None),
            P("section", "dp", None),
            P("section", "dp", None),
            P("section", "dp", None),
            P("section", "dp"),
            P(),
        ),
        check_vma=False,
    )
```

```python
import functools

import jax
import jax.numpy as jnp
from jax import lax
from jax.experimental import pallas as pl
from jax.experimental.pallas import tpu as pltpu
from jax.sharding import PartitionSpec as P

D = 1024
FF = 4096
HEADS = 16
HEAD_DIM = 64
ROT = 16
STEP = 10


NORM_EPS = 1e-05
BETA_ONE = 0.9
BETA_TWO = 0.95
LEARN_RATE = 0.05
VECTOR_RATE = 0.3
WEIGHT_DECAY = 0.01
CLIP_LEVEL = 1.0
ADAM_EPS = 1e-08

AXES = ("section", "dp")
GROUP = 4
SPREAD = 1
LOW = jnp.bfloat16
F32 = jnp.float32
SIDE = D // GROUP
UNITS = FF // GROUP
MIXED = 3 * SIDE + UNITS
PART = MIXED // 2
WIRE = PART + 128
VMEM = 48 * 1024 * 1024


class Ring:
    def __init__(self, count):
        self.count = count
        self.low = count // (GROUP * SPREAD)
        self.size = SPREAD * self.low
        self.bits = self.size.bit_length() - 1

    def index(self, g, t):
        return ((t // self.low) * GROUP + g) * self.low + t % self.low

    def group_of(self, dp):
        return (dp // self.low) % GROUP

    def spot_of(self, dp):
        return (dp // (GROUP * self.low)) * self.low + dp % self.low

    def order(self, core):
        steps = list(range(self.bits))
        if SPREAD > 1 or core == 1:
            steps.reverse()
        return steps

    def turn(self, slot, core):
        return sum(((slot >> s) & 1) << b for s, b in enumerate(self.order(core)))

    def slot(self, difference, core):
        return sum(((difference >> b) & 1) << s for s, b in enumerate(self.order(core)))


class Place:
    def __init__(self):
        self.ring = Ring(lax.axis_size("dp"))
        self.core = lax.axis_index("section")
        dp = lax.axis_index("dp")
        self.group = self.ring.group_of(dp)
        self.spot = self.ring.spot_of(dp)

    def info(self):
        return jnp.stack([self.core, self.group, self.spot]).astype(jnp.int32)

    def move(self, block, where):
        ring = self.ring
        route = []
        for core in range(2):
            for g in range(GROUP):
                for t in range(ring.size):
                    c, h, u = where(core, g, t)
                    route.append((core * ring.count + ring.index(g, t), c * ring.count + ring.index(h, u)))
        return lax.ppermute(block, AXES, route)

    def sibling(self, block):
        return self.move(block, lambda c, g, t: (1 - c, g, t))

    def member(self, block, distance):
        return self.move(block, lambda c, g, t: (c, g ^ distance, t))

    def across(self, block, step):
        return self.move(block, lambda c, g, t: (c, g, t ^ (1 << self.ring.order(c)[step])))


def take(block, index, axis=0):
    return lax.dynamic_index_in_dim(block, index, axis, keepdims=False)


def dot(left, right):
    return jnp.dot(left, right, preferred_element_type=F32)


def dot_cols(left, right):
    return lax.dot_general(left, right, (((1,), (1,)), ((), ())), preferred_element_type=F32)


def dot_rows(left, right):
    return lax.dot_general(left, right, (((0,), (0,)), ((), ())), preferred_element_type=F32)


def full_spec(shape):
    return pl.BlockSpec(shape, lambda *_: (0,) * len(shape))


def any_spec():
    return pl.BlockSpec(memory_space=pl.ANY)


def smem_spec():
    return pl.BlockSpec(memory_space=pltpu.SMEM)


def shaped(shape, dtype):
    return jax.ShapeDtypeStruct(shape, dtype)


def kernel_params():
    return pltpu.CompilerParams(vmem_limit_bytes=VMEM)


def up_pieces():
    run = UNITS // SPREAD
    cuts = sorted({0, PART - 3 * SIDE, UNITS} | {run * i for i in range(SPREAD)})
    pieces = []
    for begin, end in zip(cuts[:-1], cuts[1:]):
        column = 3 * SIDE + begin
        pieces.append((begin, column // PART, column % PART, end - begin))
    return pieces


def up_column(g, local):
    run = UNITS // SPREAD
    return (local // run * GROUP + g) * run + local % run


def qkv_column(kind, run, g):
    width = SIDE // SPREAD
    return ((kind * SPREAD + run) * GROUP + g) * width


def pack_kernel(info, w_qkv, w_out, w_up, w_down, vec, keep_qu, send_qu, keep_od, send_od):
    rows = w_qkv.shape[1]
    ff_rows = w_down.shape[1]
    width = SIDE // SPREAD
    core = info[0]

    def write(halves):
        for g in range(GROUP):
            for kind in range(3):
                for run in range(SPREAD):
                    at = (kind * SPREAD + run) * width
                    column = qkv_column(kind, run, g)
                    halves[0][0][g, :, at : at + width] = w_qkv[0, :, column : column + width].astype(LOW)
            for local, half, at, length in up_pieces():
                column = up_column(g, local)
                halves[half][0][g, :, at : at + length] = w_up[0, :, column : column + length].astype(LOW)
            for half in range(2):
                halves[half][0][g, :, PART:WIRE] = vec[...]
        for half in range(2):
            columns = slice(half * (D // 2), (half + 1) * (D // 2))
            halves[half][1][0:ff_rows] = w_down[0, :, columns].astype(LOW)
            halves[half][1][ff_rows : ff_rows + rows] = w_out[0, :, columns].astype(LOW)

    @pl.when(core == 0)
    def _():
        write([(keep_qu, keep_od), (send_qu, send_od)])

    @pl.when(core == 1)
    def _():
        write([(send_qu, send_od), (keep_qu, keep_od)])


def pack(info, w_qkv, w_out, w_up, w_down, vec):
    rows, ff_rows = w_qkv.shape[1], w_down.shape[1]
    qu = shaped((GROUP, rows, WIRE), LOW)
    od = shaped((ff_rows + rows, D // 2), LOW)
    return pl.pallas_call(
        pack_kernel,
        out_shape=(qu, qu, od, od),
        in_specs=[smem_spec()] + [full_spec(a.shape) for a in (w_qkv, w_out, w_up, w_down, vec)],
        out_specs=tuple(full_spec(a.shape) for a in (qu, qu, od, od)),
        compiler_params=kernel_params(),
        name="pack_weights",
    )(info, w_qkv, w_out, w_up, w_down, vec)


def weight_copies(ring, info, parts, wqu, wout, wdown, sems):
    core, group, spot = info[0], info[1], info[2]
    qu_copies, od_copies = [], []
    for which in range(2):
        qu, od = parts[2 * which], parts[2 * which + 1]
        half = core if which == 0 else 1 - core
        rows = qu.shape[2]
        ff_rows = od.shape[1] - rows
        qu_at = pl.multiple_of(half * PART, 128)
        od_at = pl.multiple_of(half * (D // 2), 128)
        for slot in range(ring.size):
            straight, turned = ring.turn(slot, 0), ring.turn(slot, 1)
            there = spot ^ (straight + half * (turned - straight))
            od_copies.append(
                pltpu.make_async_copy(
                    od.at[slot, pl.ds(0, ff_rows)],
                    wdown.at[pl.ds(pl.multiple_of(there * ff_rows, ff_rows), ff_rows), pl.ds(od_at, D // 2)],
                    sems.at[0],
                )
            )
            od_copies.append(
                pltpu.make_async_copy(
                    od.at[slot, pl.ds(ff_rows, rows)],
                    wout.at[pl.ds(pl.multiple_of(there * rows, rows), rows), pl.ds(od_at, D // 2)],
                    sems.at[0],
                )
            )
            for r in range(GROUP):
                row = ring.index(group ^ r, there) * rows
                qu_copies.append(
                    pltpu.make_async_copy(
                        qu.at[slot, r, :, pl.ds(0, PART)],
                        wqu.at[pl.ds(pl.multiple_of(row, rows), rows), pl.ds(qu_at, PART)],
                        sems.at[1],
                    )
                )
    return qu_copies, od_copies


def head_masks(dtype):
    lane = lax.broadcasted_iota(jnp.int32, (1, SIDE), 1) // HEAD_DIM
    return [(lane == h).astype(dtype) for h in range(SIDE // HEAD_DIM)]


def by_head(parts):
    lane = lax.broadcasted_iota(jnp.int32, (1, SIDE), 1) // HEAD_DIM
    total = parts[-1]
    for h in range(len(parts) - 2, -1, -1):
        total = jnp.where(lane == h, parts[h], total)
    return total


def turning(cosine, sine, back):
    lane = lax.broadcasted_iota(jnp.int32, sine.shape, 1) % HEAD_DIM
    first = jnp.where(lane < ROT // 2, sine, 0.0)
    second = jnp.where(lane < ROT // 2, 0.0, sine)
    if back:
        second = -second
    else:
        first = -first
    wide = SIDE // cosine.shape[1]
    return [jnp.concatenate([a] * wide, axis=1) for a in (cosine, first, second)]


def turn(part, tables):
    cosine, first, second = tables
    ahead = pltpu.roll(part, SIDE - ROT // 2, 1)
    behind = pltpu.roll(part, ROT // 2, 1)
    return part * cosine + ahead * first + behind * second


def normalise(rows):
    centered = rows - jnp.mean(rows, axis=-1, keepdims=True)
    variance = jnp.mean(centered * centered, axis=-1, keepdims=True)
    return centered * lax.rsqrt(variance + NORM_EPS)


def forward_part(x_refs, tables, vecs, wqu, wout, wdown, kept, z_refs, waits):
    cosine, sine, mask = tables
    b_qkv, b_up, gain, ln_bias = vecs
    y, qkv, probs, mixed, active, slope = kept
    rows = z_refs[0].shape[0]
    for r in range(GROUP):
        normed = normalise(x_refs[r][0:rows, :].astype(F32))
        y[r * rows : (r + 1) * rows, :] = (normed * gain[...] + ln_bias[...]).astype(LOW)
    waits[0]()
    forth = turning(cosine[...], sine[...], False)
    for kind in range(3):
        columns = slice(kind * SIDE, (kind + 1) * SIDE)
        part = dot(y[...], wqu[:, columns]) + b_qkv[:, columns]
        if kind < 2:
            part = turn(part, forth)
        qkv[:, columns] = part.astype(LOW)
    masks = head_masks(LOW)
    heads = len(masks)
    for r in range(GROUP):
        here = slice(r * rows, (r + 1) * rows)
        query, keys, values = [qkv[here, k * SIDE : (k + 1) * SIDE] for k in range(3)]
        stacked = jnp.concatenate([query * m for m in masks], axis=0)
        scores = dot_cols(stacked, keys) * HEAD_DIM ** (-0.5)
        scores = scores.reshape(heads, rows, rows) + mask[here, :][None]
        expo = jnp.exp(scores - jnp.max(scores, axis=-1, keepdims=True))
        prob = expo / jnp.sum(expo, axis=-1, keepdims=True)
        prob = prob.reshape(heads * rows, rows)
        probs[r * heads * rows : (r + 1) * heads * rows, :] = prob
        full = dot(prob.astype(LOW), values)
        mixed[here, :] = by_head([full[h * rows : (h + 1) * rows] for h in range(heads)]).astype(LOW)
    tile = 256
    for at in range(0, UNITS, tile):
        hidden = dot(y[...], wqu[:, 3 * SIDE + at : 3 * SIDE + at + tile]) + b_up[:, at : at + tile]
        share = 0.5 * (1.0 + lax.erf(hidden * (0.5**0.5)))
        density = jnp.exp(-0.5 * hidden * hidden) * (0.5 / jnp.pi) ** 0.5
        active[:, at : at + tile] = (hidden * share).astype(LOW)
        slope[:, at : at + tile] = share + hidden * density
    waits[1]()
    for at in range(0, D, tile):
        branch = dot(mixed[...], wout[:, at : at + tile]) + dot(active[...], wdown[:, at : at + tile])
        for r in range(GROUP):
            z_refs[r][:, at : at + tile] = branch[r * rows : (r + 1) * rows].astype(LOW)


def backward_part(grad, tables, wqu, wout, wdown, kept, dqu, dy_refs, db):
    cosine, sine, _ = tables
    y, qkv, probs, mixed, active, slope = kept
    rows = dy_refs[0].shape[0]
    tile = 256
    dmixed = dot_cols(grad[...], wout[...]).astype(LOW)
    for at in range(0, UNITS, tile):
        dactive = dot_cols(grad[...], wdown[at : at + tile, :])
        dhidden = (dactive * slope[:, at : at + tile]).astype(LOW)
        dqu[:, 3 * SIDE + at : 3 * SIDE + at + tile] = dhidden
    masks = head_masks(LOW)
    heads = len(masks)
    back = turning(cosine[...], sine[...], True)
    for r in range(GROUP):
        here = slice(r * rows, (r + 1) * rows)
        query, keys, values = [qkv[here, k * SIDE : (k + 1) * SIDE] for k in range(3)]
        dstack = jnp.concatenate([dmixed[here] * m for m in masks], axis=0)
        dprob = dot_cols(dstack, values)
        prob = probs[r * heads * rows : (r + 1) * heads * rows, :]
        dvalues = dot_rows(prob.astype(LOW), dstack)
        dscore = (prob * (dprob - jnp.sum(prob * dprob, axis=-1, keepdims=True))).astype(LOW)
        full = dot(dscore, keys)
        dquery = by_head([full[h * rows : (h + 1) * rows] for h in range(heads)])
        dkeys = dot_rows(dscore, jnp.concatenate([query * m for m in masks], axis=0))
        scale = HEAD_DIM ** (-0.5)
        slot_tables = [a[here] for a in back]
        dqu[here, 0:SIDE] = turn(dquery * scale, slot_tables).astype(LOW)
        dqu[here, SIDE : 2 * SIDE] = turn(dkeys * scale, slot_tables).astype(LOW)
        dqu[here, 2 * SIDE : 3 * SIDE] = dvalues.astype(LOW)
    for at in range(0, MIXED, tile):
        db[:, at : at + tile] = jnp.sum(dqu[:, at : at + tile].astype(F32), axis=0, keepdims=True)
    for at in range(0, D, tile):
        dy = dot_cols(dqu[...], wqu[at : at + tile, :])
        for r in range(GROUP):
            dy_refs[r][:, at : at + tile] = dy[r * rows : (r + 1) * rows].astype(LOW)


def kept_shapes(tokens, rows):
    return [
        ((tokens, D), LOW),
        ((tokens, 3 * SIDE), LOW),
        ((tokens * (SIDE // HEAD_DIM), rows), F32),
        ((tokens, SIDE), LOW),
        ((tokens, UNITS), LOW),
        ((tokens, UNITS), F32),
    ]


def weight_scratch():
    return [
        pltpu.VMEM((D, MIXED), LOW),
        pltpu.VMEM((SIDE, D), LOW),
        pltpu.VMEM((UNITS, D), LOW),
        pltpu.SemaphoreType.DMA((2,)),
    ]


def start_weights(ring, info, parts, scratch):
    qu_copies, od_copies = weight_copies(ring, info, parts, *scratch)
    for copy in qu_copies + od_copies:
        copy.start()

    def waiter(copies):
        def wait():
            for copy in copies:
                copy.wait()

        return wait

    return waiter(qu_copies), waiter(od_copies)


def cost(flops, moved):
    return pl.CostEstimate(flops=flops, bytes_accessed=moved, transcendentals=0)


def forward_kernel(ring, info, *refs):
    parts, refs = refs[:4], refs[4:]
    x_refs, refs = refs[:4], refs[4:]
    tables, refs = refs[:3], refs[3:]
    vecs, refs = refs[:4], refs[4:]
    z_refs, refs = refs[:4], refs[4:]
    kept, scratch = refs[:6], refs[6:]
    waits = start_weights(ring, info, parts, scratch)
    forward_part(x_refs, tables, vecs, *scratch[:3], kept, z_refs, waits)


def forward(ring, info, parts, xs, tables, vecs, rows):
    tokens = GROUP * rows
    outs = [shaped((rows, D), LOW)] * GROUP + [shaped(*a) for a in kept_shapes(tokens, rows)]
    return pl.pallas_call(
        functools.partial(forward_kernel, ring),
        out_shape=tuple(outs),
        in_specs=[smem_spec()] + [any_spec()] * 4 + [full_spec(a.shape) for a in (*xs, *tables, *vecs)],
        out_specs=tuple(full_spec(a.shape) for a in outs),
        scratch_shapes=weight_scratch(),
        compiler_params=kernel_params(),
        cost_estimate=cost(2 * tokens * D * (D + 2 * FF // GROUP), 16 * 1024 * 1024),
        name="forward_shard",
    )(info, *parts, *xs, *tables, *vecs)


def middle_kernel(ring, info, *refs):
    parts, refs = refs[:4], refs[4:]
    x_refs, refs = refs[:4], refs[4:]
    g_refs, refs = refs[:4], refs[4:]
    tables, refs = refs[:3], refs[3:]
    vecs, refs = refs[:4], refs[4:]
    z_refs, refs = refs[:4], refs[4:]
    dy_refs, refs = refs[:4], refs[4:]
    (y, mixed, active, dqu, db), refs = refs[:5], refs[5:]
    (qkv, probs, slope, grad), scratch = refs[:4], refs[4:]
    kept = (y, qkv, probs, mixed, active, slope)
    waits = start_weights(ring, info, parts, scratch)
    rows = z_refs[0].shape[0]
    for r in range(GROUP):
        grad[r * rows : (r + 1) * rows, :] = g_refs[r][...]
    forward_part(x_refs, tables, vecs, *scratch[:3], kept, z_refs, waits)
    backward_part(grad, tables, *scratch[:3], kept, dqu, dy_refs, db)


def middle(ring, info, parts, xs, gs, tables, vecs, rows):
    tokens = GROUP * rows
    shapes = kept_shapes(tokens, rows)
    outs = [shaped((rows, D), LOW)] * (2 * GROUP)
    outs += [shaped(*shapes[i]) for i in (0, 3, 4)]
    outs += [shaped((tokens, MIXED), LOW), shaped((1, MIXED), F32)]
    return pl.pallas_call(
        functools.partial(middle_kernel, ring),
        out_shape=tuple(outs),
        in_specs=[smem_spec()] + [any_spec()] * 4 + [full_spec(a.shape) for a in (*xs, *gs, *tables, *vecs)],
        out_specs=tuple(full_spec(a.shape) for a in outs),
        scratch_shapes=[pltpu.VMEM(*shapes[i]) for i in (1, 2, 5)]
        + [pltpu.VMEM((tokens, D), LOW)]
        + weight_scratch(),
        compiler_params=kernel_params(),
        cost_estimate=cost(4 * tokens * D * (D + 2 * FF // GROUP), 16 * 1024 * 1024),
        name="forward_backward_shard",
    )(info, *parts, *xs, *gs, *tables, *vecs)


def backward_kernel(ring, info, *refs):
    parts, refs = refs[:4], refs[4:]
    g_refs, refs = refs[:4], refs[4:]
    tables, refs = refs[:3], refs[3:]
    (qkv, probs, slope), refs = refs[:3], refs[3:]
    dy_refs, refs = refs[:4], refs[4:]
    (dqu, db), refs = refs[:2], refs[2:]
    grad, scratch = refs[0], refs[1:]
    kept = (None, qkv, probs, None, None, slope)
    waits = start_weights(ring, info, parts, scratch)
    rows = dy_refs[0].shape[0]
    for r in range(GROUP):
        grad[r * rows : (r + 1) * rows, :] = g_refs[r][...]
    waits[0]()
    waits[1]()
    backward_part(grad, tables, *scratch[:3], kept, dqu, dy_refs, db)


def backward(ring, info, parts, gs, tables, kept, rows):
    tokens = GROUP * rows
    outs = [shaped((rows, D), LOW)] * GROUP + [shaped((tokens, MIXED), LOW), shaped((1, MIXED), F32)]
    used = [kept[1], kept[2], kept[5]]
    return pl.pallas_call(
        functools.partial(backward_kernel, ring),
        out_shape=tuple(outs),
        in_specs=[smem_spec()] + [any_spec()] * 4 + [full_spec(a.shape) for a in (*gs, *tables, *used)],
        out_specs=tuple(full_spec(a.shape) for a in outs),
        scratch_shapes=[pltpu.VMEM((tokens, D), LOW)] + weight_scratch(),
        compiler_params=kernel_params(),
        cost_estimate=cost(2 * tokens * D * (D + 2 * FF // GROUP), 16 * 1024 * 1024),
        name="backward_shard",
    )(info, *parts, *gs, *tables, *used)


def od_kernel(ring, info, mixed, active, g0, g1, g2, g3, out, grad):
    spot = info[2]
    rows = g0.shape[0]
    for r, ref in enumerate((g0, g1, g2, g3)):
        grad[r * rows : (r + 1) * rows, :] = ref[...]
    out_rows = SIDE // ring.size
    ff_rows = UNITS // ring.size
    for half in range(2):
        columns = slice(half * (D // 2), (half + 1) * (D // 2))
        block = dot_rows(mixed[...], grad[:, columns]).astype(LOW)
        for there in range(ring.size):
            slot = ring.slot(spot ^ there, half)
            out[half, slot, ff_rows : ff_rows + out_rows, :] = block[there * out_rows : (there + 1) * out_rows]
            piece = dot_rows(active[:, there * ff_rows : (there + 1) * ff_rows], grad[:, columns])
            out[half, slot, 0:ff_rows, :] = piece.astype(LOW)


def od_grads(ring, info, mixed, active, gs):
    tokens = mixed.shape[0]
    out = shaped((2, ring.size, (SIDE + UNITS) // ring.size, D // 2), LOW)
    return pl.pallas_call(
        functools.partial(od_kernel, ring),
        out_shape=out,
        in_specs=[smem_spec()] + [full_spec(a.shape) for a in (mixed, active, *gs)],
        out_specs=full_spec(out.shape),
        scratch_shapes=[pltpu.VMEM((tokens, D), LOW)],
        compiler_params=kernel_params(),
        cost_estimate=cost(2 * tokens * D * (SIDE + UNITS), 5 * 1024 * 1024),
        name="out_down_grads",
    )(info, mixed, active, *gs)


def qu_kernel(ring, info, y, dqu, out):
    group, spot = info[1], info[2]
    rows = D // ring.count
    tile = 256
    for half in range(2):
        columns = slice(half * PART, (half + 1) * PART)
        for at in range(0, D, tile):
            block = dot_rows(y[:, at : at + tile], dqu[:, columns]).astype(LOW)
            for offset in range(0, tile, rows):
                dp = (at + offset) // rows
                slot = ring.slot(spot ^ ring.spot_of(dp), half)
                out[half, slot, group ^ ring.group_of(dp), :, :] = block[offset : offset + rows]


def qu_grads(ring, info, y, dqu):
    tokens = y.shape[0]
    out = shaped((2, ring.size, GROUP, D // ring.count, PART), LOW)
    return pl.pallas_call(
        functools.partial(qu_kernel, ring),
        out_shape=out,
        in_specs=[smem_spec()] + [full_spec(a.shape) for a in (y, dqu)],
        out_specs=full_spec(out.shape),
        compiler_params=kernel_params(),
        cost_estimate=cost(2 * tokens * D * MIXED, 7 * 1024 * 1024),
        name="qkv_up_grads",
    )(info, y, dqu)


def adam_update(weight, grad, first, second, factor, rate):
    clipped = grad * factor
    first_new = BETA_ONE * first + (1.0 - BETA_ONE) * clipped
    second_new = BETA_TWO * second + (1.0 - BETA_TWO) * clipped * clipped
    first_hat = first_new / (1.0 - BETA_ONE**STEP)
    second_hat = second_new / (1.0 - BETA_TWO**STEP)
    weight_new = weight - rate * (
        first_hat / (jnp.sqrt(second_hat) + ADAM_EPS) + WEIGHT_DECAY * weight
    )
    return (weight_new, first_new, second_new)


def adam_kernel(info, factor_ref, qu0, qu1, down0, out0, down1, out1, *refs):
    group = info[1]
    factor = factor_ref[0]
    olds, news = refs[:12], refs[12:]
    qus = (qu0, qu1)

    def update(which, columns, grad):
        weight, first, second = [olds[3 * which + i][0, :, columns] for i in range(3)]
        fresh = adam_update(weight, grad.astype(F32), first, second, factor, LEARN_RATE)
        for i in range(3):
            news[3 * which + i][0, :, columns] = fresh[i]

    width = SIDE // SPREAD
    for g in range(GROUP):
        for kind in range(3):
            for run in range(SPREAD):
                at = (kind * SPREAD + run) * width
                column = qkv_column(kind, run, g)
                update(0, slice(column, column + width), qu0[group ^ g, :, at : at + width])
        for local, half, at, length in up_pieces():
            column = up_column(g, local)
            update(2, slice(column, column + length), qus[half][group ^ g, :, at : at + length])
    for half, (down, out) in enumerate(((down0, out0), (down1, out1))):
        columns = slice(half * (D // 2), (half + 1) * (D // 2))
        update(1, columns, out[...])
        update(3, columns, down[...])


def adam(info, factor, qus, ods, olds):
    rows = olds[0].shape[1]
    ff_rows = olds[9].shape[1]
    steps = max(1, rows // 16)
    few, many = rows // steps, ff_rows // steps

    def master(a):
        return pl.BlockSpec((1, a.shape[1] // steps, a.shape[2]), lambda i: (0, i, 0))

    qu_spec = pl.BlockSpec((GROUP, few, PART), lambda i: (0, i, 0))
    down_spec = pl.BlockSpec((many, D // 2), lambda i: (i, 0))
    out_spec = pl.BlockSpec((few, D // 2), lambda i: (ff_rows // few + i, 0))
    return pl.pallas_call(
        adam_kernel,
        grid=(steps,),
        out_shape=tuple(shaped(a.shape, F32) for a in olds),
        in_specs=[smem_spec(), smem_spec(), qu_spec, qu_spec]
        + [down_spec, out_spec] * 2
        + [master(a) for a in olds],
        out_specs=tuple(master(a) for a in olds),
        compiler_params=kernel_params(),
        name="adamw",
    )(info, factor, qus[0], qus[1], ods[0], ods[0], ods[1], ods[1], *olds)


def doc_tables(lengths, rows):
    seqs = lengths.shape[0]
    ends = jnp.cumsum(lengths, axis=1)
    places = jnp.arange(rows, dtype=jnp.int32)
    past = places[None, :, None] >= ends[:, None, :]
    begins = jnp.sum(jnp.where(past, lengths[:, None, :], 0), axis=2)
    position = (places[None, :] - begins).reshape(seqs * rows, 1)
    half = ROT // 2
    inverse = 10000.0 ** (-(jnp.arange(half, dtype=F32) * 2.0) / ROT)
    lanes = jnp.concatenate([inverse, inverse, jnp.zeros(HEAD_DIM - ROT, F32)])
    angles = position.astype(F32) * jnp.concatenate([lanes, lanes])[None, :]
    allowed = (places[None, None, :] <= places[None, :, None]) & (places[None, None, :] >= begins[:, :, None])
    mask = jnp.where(allowed, 0.0, -1e30).reshape(seqs * rows, rows).astype(F32)
    return jnp.cos(angles), jnp.sin(angles), mask


def shards(
    x_in,
    cotangent,
    doc_lengths,
    w_qkv,
    w_out,
    w_up,
    w_down,
    vectors,
    m_qkv,
    m_out,
    m_up,
    m_down,
    m_vectors,
    v_qkv,
    v_out,
    v_up,
    v_down,
    v_vectors,
):
    place = Place()
    ring, core, group, spot = place.ring, place.core, place.group, place.spot
    info = place.info()
    local_rows, width = x_in.shape
    seqs, docs = doc_lengths.shape
    rows = local_rows // seqs
    in_rows = w_qkv.shape[1]
    shard = vectors.shape[1]
    members = range(1, GROUP)

    vec_block = jnp.pad(vectors[0].astype(LOW), (0, in_rows * 128 - shard)).reshape(in_rows, 128)
    keep_qu, send_qu, keep_od, send_od = pack(info, w_qkv, w_out, w_up, w_down, vec_block)
    came_qu = place.sibling(send_qu)
    came_od = place.sibling(send_od)

    def block_weights(block):
        mine = core == block
        qu = jnp.where(mine, keep_qu, came_qu)
        slots = [take(qu, group)] + [place.member(take(qu, group ^ r), r) for r in members]
        qu = jnp.stack(slots)[None]
        od = jnp.where(mine, keep_od, came_od)[None]
        for step in range(ring.bits):
            od = jnp.concatenate([od, place.across(od, step)])
        for step in range(ring.bits):
            qu = jnp.concatenate([qu, place.across(qu, step)])
        return (qu, od, place.sibling(qu), place.sibling(od))

    def block_vectors(parts):
        pieces = parts[0][:, :, 0 : -(-shard // 128), PART:].reshape(ring.size * GROUP, -1)[:, :shard]
        dp = jnp.arange(ring.count, dtype=jnp.int32)
        difference = ring.spot_of(dp) ^ spot
        slot = jnp.where(core == 0, ring.slot(difference, 0), ring.slot(difference, 1))
        vec = jnp.take(pieces, slot * GROUP + (ring.group_of(dp) ^ group), axis=0, mode="clip")
        vec = vec.reshape(-1).astype(F32)
        b_qkv, b_out, b_up, b_down, gain, ln_bias = jnp.split(
            vec, [3 * D, 4 * D, 4 * D + FF, 5 * D + FF, 6 * D + FF]
        )
        b_qkv = take(b_qkv.reshape(3 * SPREAD, GROUP, -1), group, 1).reshape(1, -1)
        b_up = take(b_up.reshape(SPREAD, GROUP, -1), group, 1).reshape(1, -1)
        return (b_qkv, b_up, gain[None], ln_bias[None]), (b_out + b_down)[None], gain[None]

    x_own = take(x_in.reshape(2, rows, width), core)
    cot_own = take(cotangent.reshape(2, rows, width), core)
    len_own = take(doc_lengths, core)
    len_rows = jnp.zeros((16, width), LOW).at[0, :docs].set(len_own.astype(LOW))
    x_sent = jnp.concatenate([x_own, len_rows])
    x_group = [x_sent] + [place.member(x_sent, r) for r in members]
    lengths = jnp.stack([a[rows, :docs] for a in x_group]).astype(jnp.int32)
    tables = doc_tables(lengths, rows)

    parts_first = block_weights(0)
    vecs_first, bias_first, gain_first = block_vectors(parts_first)
    parts_second = block_weights(1)
    vecs_second, bias_second, gain_second = block_vectors(parts_second)
    cot_group = [cot_own] + [place.member(cot_own, r) for r in members]

    def to_owner(slots):
        total = slots[0].astype(F32)
        for r in members:
            total = total + place.member(slots[r], r).astype(F32)
        return total

    first = forward(ring, info, parts_first, x_group, tables, vecs_first, rows)
    kept_first = first[GROUP:]
    hidden_first = (x_own.astype(F32) + to_owner(first[:GROUP]) + bias_first).astype(LOW)
    hidden_group = [hidden_first] + [place.member(hidden_first, r) for r in members]
    second = middle(ring, info, parts_second, hidden_group, cot_group, tables, vecs_second, rows)
    y_second, mixed_second, active_second, dqu_second, db_second = second[2 * GROUP :]

    def rows_backward(rows_low, grad_low, dy_slots, gain):
        dy = to_owner(dy_slots)
        rows_now = rows_low.astype(F32)
        centered = rows_now - jnp.mean(rows_now, axis=-1, keepdims=True)
        variance = jnp.mean(centered * centered, axis=-1, keepdims=True)
        inverse_std = lax.rsqrt(variance + NORM_EPS)
        normed = centered * inverse_std
        scaled = dy * gain
        inner_mean = jnp.mean(scaled, axis=-1, keepdims=True)
        inner_cross = jnp.mean(scaled * normed, axis=-1, keepdims=True)
        out_grad = grad_low.astype(F32)
        dx = out_grad + inverse_std * (scaled - inner_mean - normed * inner_cross)
        return dx.astype(LOW), (
            jnp.sum(out_grad, axis=0),
            jnp.sum(dy * normed, axis=0),
            jnp.sum(dy, axis=0),
        )

    mid_grad, row_sums_second = rows_backward(hidden_first, cot_own, second[GROUP : 2 * GROUP], gain_second)
    mid_group = [mid_grad] + [place.member(mid_grad, r) for r in members]
    hidden_second = (hidden_first.astype(F32) + to_owner(second[:GROUP]) + bias_second).astype(LOW)

    def reduce_ring(halves):
        came = place.sibling(take(halves, 1 - core))
        held = take(halves, core).astype(F32) + came.astype(F32)
        for step in reversed(range(ring.bits)):
            half = held.shape[0] // 2
            came = place.across(held[half:].astype(LOW), step)
            held = held[:half] + came.astype(F32)
        return held[0]

    od_second = reduce_ring(od_grads(ring, info, mixed_second, active_second, cot_group))
    qu_second = reduce_ring(qu_grads(ring, info, y_second, dqu_second))
    od_first = reduce_ring(od_grads(ring, info, kept_first[3], kept_first[4], mid_group))
    back = backward(ring, info, parts_first, mid_group, tables, kept_first, rows)
    dqu_first, db_first = back[GROUP:]
    qu_first = reduce_ring(qu_grads(ring, info, kept_first[0], dqu_first))
    start_grad, row_sums_first = rows_backward(x_own, mid_grad, back[:GROUP], gain_first)

    def all_sum(block):
        for step in range(2):
            block = block + place.member(block, 1 << step)
        for step in range(ring.bits):
            block = block + place.across(block, step)
        return block + place.sibling(block)

    def vector_grads(db, row_sums):
        bias_grad, grad_gain, grad_lnbias = row_sums
        member = (jnp.arange(GROUP, dtype=jnp.int32) == group)[None, :, None]
        grad_bqkv = db[0, : 3 * SIDE].reshape(3 * SPREAD, 1, -1)
        grad_bqkv = jnp.where(member, grad_bqkv, 0.0).reshape(-1)
        grad_bup = jnp.where(member, db[0, 3 * SIDE :].reshape(SPREAD, 1, -1), 0.0).reshape(-1)
        return jnp.concatenate([grad_bqkv, bias_grad, grad_bup, bias_grad, grad_gain, grad_lnbias])

    vec_grad = jnp.stack([vector_grads(db_first, row_sums_first), vector_grads(db_second, row_sums_second)])
    vec_grad = all_sum(vec_grad)
    vec_share = take(take(vec_grad, core).reshape(ring.count, shard), lax.axis_index("dp"))[None]

    squares = sum(jnp.sum(a * a) for a in (od_first, qu_first, od_second, qu_second))
    squares = all_sum(jnp.broadcast_to(squares, (8, 128)))[0, 0]
    grad_norm = jnp.sqrt(squares + jnp.sum(vec_grad * vec_grad))
    factor = jnp.minimum(1.0, CLIP_LEVEL / (grad_norm + 1e-06))

    def to_members(qu):
        qu = qu.astype(LOW)
        return jnp.stack([qu[0]] + [place.member(qu[r], r) for r in members])

    def own_block(one, two):
        came = place.sibling(jnp.where(core == 0, two, one))
        mine = jnp.where(core == 0, one, two)
        return [jnp.where(core == h, mine, came) for h in range(2)]

    ods = own_block(od_first.astype(LOW), od_second.astype(LOW))
    qus = own_block(to_members(qu_first), to_members(qu_second))
    olds = (w_qkv, m_qkv, v_qkv, w_out, m_out, v_out, w_up, m_up, v_up, w_down, m_down, v_down)
    news = adam(info, factor[None], qus, ods, olds)
    new_vec = adam_update(vectors, vec_share, m_vectors, v_vectors, factor, VECTOR_RATE)

    def rows_of_block(one, two):
        return jnp.concatenate(own_block(one, two))[None]

    hidden_out = rows_of_block(hidden_first, hidden_second)
    input_grads = rows_of_block(start_grad, mid_grad)
    return (
        hidden_out,
        input_grads,
        *(news[3 * i] for i in range(4)),
        new_vec[0],
        *(news[3 * i + 1] for i in range(4)),
        new_vec[1],
        *(news[3 * i + 2] for i in range(4)),
        new_vec[2],
        grad_norm,
    )


def solution(mesh):
    return jax.shard_map(
        shards,
        mesh=mesh,
        in_specs=(
            P("dp", None),
            P("dp", None),
            P("dp", None),
            P("section", "dp", None),
            P("section", "dp", None),
            P("section", "dp", None),
            P("section", "dp", None),
            P("section", "dp"),
            P("section", "dp", None),
            P("section", "dp", None),
            P("section", "dp", None),
            P("section", "dp", None),
            P("section", "dp"),
            P("section", "dp", None),
            P("section", "dp", None),
            P("section", "dp", None),
            P("section", "dp", None),
            P("section", "dp"),
        ),
        out_specs=(
            P("section", "dp", None),
            P("section", "dp", None),
            P("section", "dp", None),
            P("section", "dp", None),
            P("section", "dp", None),
            P("section", "dp", None),
            P("section", "dp"),
            P("section", "dp", None),
            P("section", "dp", None),
            P("section", "dp", None),
            P("section", "dp", None),
            P("section", "dp"),
            P("section", "dp", None),
            P("section", "dp", None),
            P("section", "dp", None),
            P("section", "dp", None),
            P("section", "dp"),
            P(),
        ),
        check_vma=False,
    )
```

```python
import functools

import jax
import jax.numpy as jnp
from jax import lax
from jax.experimental import pallas as pl
from jax.experimental.pallas import tpu as pltpu
from jax.sharding import PartitionSpec as P

D = 1024
FF = 4096
HEADS = 16
HEAD_DIM = 64
ROT = 16
STEP = 10


NORM_EPS = 1e-05
BETA_ONE = 0.9
BETA_TWO = 0.95
LEARN_RATE = 0.05
VECTOR_RATE = 0.3
WEIGHT_DECAY = 0.01
CLIP_LEVEL = 1.0
ADAM_EPS = 1e-08

AXES = ("section", "dp")
GROUP = 4
SPREAD = 2
LOW = jnp.bfloat16
F32 = jnp.float32
SIDE = D // GROUP
UNITS = FF // GROUP
MIXED = 3 * SIDE + UNITS
PART = MIXED // 2
WIRE = PART + 128
VMEM = 48 * 1024 * 1024


class Ring:
    def __init__(self, count):
        self.count = count
        self.low = count // (GROUP * SPREAD)
        self.size = SPREAD * self.low
        self.bits = self.size.bit_length() - 1

    def index(self, g, t):
        return ((t // self.low) * GROUP + g) * self.low + t % self.low

    def group_of(self, dp):
        return (dp // self.low) % GROUP

    def spot_of(self, dp):
        return (dp // (GROUP * self.low)) * self.low + dp % self.low

    def order(self, core):
        steps = list(range(self.bits))
        if SPREAD > 1 or core == 1:
            steps.reverse()
        return steps

    def turn(self, slot, core):
        return sum(((slot >> s) & 1) << b for s, b in enumerate(self.order(core)))

    def slot(self, difference, core):
        return sum(((difference >> b) & 1) << s for s, b in enumerate(self.order(core)))


class Place:
    def __init__(self):
        self.ring = Ring(lax.axis_size("dp"))
        self.core = lax.axis_index("section")
        dp = lax.axis_index("dp")
        self.group = self.ring.group_of(dp)
        self.spot = self.ring.spot_of(dp)

    def info(self):
        return jnp.stack([self.core, self.group, self.spot]).astype(jnp.int32)

    def move(self, block, where):
        ring = self.ring
        route = []
        for core in range(2):
            for g in range(GROUP):
                for t in range(ring.size):
                    c, h, u = where(core, g, t)
                    route.append((core * ring.count + ring.index(g, t), c * ring.count + ring.index(h, u)))
        return lax.ppermute(block, AXES, route)

    def sibling(self, block):
        return self.move(block, lambda c, g, t: (1 - c, g, t))

    def member(self, block, distance):
        return self.move(block, lambda c, g, t: (c, g ^ distance, t))

    def across(self, block, step):
        return self.move(block, lambda c, g, t: (c, g, t ^ (1 << self.ring.order(c)[step])))


def take(block, index, axis=0):
    return lax.dynamic_index_in_dim(block, index, axis, keepdims=False)


def after(block, *waited):
    return lax.optimization_barrier((block, waited))[0]


def dot(left, right):
    return jnp.dot(left, right, preferred_element_type=F32)


def dot_cols(left, right):
    return lax.dot_general(left, right, (((1,), (1,)), ((), ())), preferred_element_type=F32)


def dot_rows(left, right):
    return lax.dot_general(left, right, (((0,), (0,)), ((), ())), preferred_element_type=F32)


def full_spec(shape):
    return pl.BlockSpec(shape, lambda *_: (0,) * len(shape))


def any_spec():
    return pl.BlockSpec(memory_space=pl.ANY)


def smem_spec():
    return pl.BlockSpec(memory_space=pltpu.SMEM)


def shaped(shape, dtype):
    return jax.ShapeDtypeStruct(shape, dtype)


def kernel_params():
    return pltpu.CompilerParams(vmem_limit_bytes=VMEM)


def up_pieces():
    run = UNITS // SPREAD
    cuts = sorted({0, PART - 3 * SIDE, UNITS} | {run * i for i in range(SPREAD)})
    pieces = []
    for begin, end in zip(cuts[:-1], cuts[1:]):
        column = 3 * SIDE + begin
        pieces.append((begin, column // PART, column % PART, end - begin))
    return pieces


def up_column(g, local):
    run = UNITS // SPREAD
    return (local // run * GROUP + g) * run + local % run


def qkv_column(kind, run, g):
    width = SIDE // SPREAD
    return ((kind * SPREAD + run) * GROUP + g) * width


def pack_kernel(info, w_qkv, w_out, w_up, w_down, vec, keep_qu, send_qu, keep_od, send_od):
    rows = w_qkv.shape[1]
    ff_rows = w_down.shape[1]
    width = SIDE // SPREAD
    core = info[0]

    def write(halves):
        for g in range(GROUP):
            for kind in range(3):
                for run in range(SPREAD):
                    at = (kind * SPREAD + run) * width
                    column = qkv_column(kind, run, g)
                    halves[0][0][g, :, at : at + width] = w_qkv[0, :, column : column + width].astype(LOW)
            for local, half, at, length in up_pieces():
                column = up_column(g, local)
                halves[half][0][g, :, at : at + length] = w_up[0, :, column : column + length].astype(LOW)
            for half in range(2):
                halves[half][0][g, :, PART:WIRE] = vec[...]
        for half in range(2):
            columns = slice(half * (D // 2), (half + 1) * (D // 2))
            halves[half][1][0:ff_rows] = w_down[0, :, columns].astype(LOW)
            halves[half][1][ff_rows : ff_rows + rows] = w_out[0, :, columns].astype(LOW)

    @pl.when(core == 0)
    def _():
        write([(keep_qu, keep_od), (send_qu, send_od)])

    @pl.when(core == 1)
    def _():
        write([(send_qu, send_od), (keep_qu, keep_od)])


def pack(info, w_qkv, w_out, w_up, w_down, vec):
    rows, ff_rows = w_qkv.shape[1], w_down.shape[1]
    qu = shaped((GROUP, rows, WIRE), LOW)
    od = shaped((ff_rows + rows, D // 2), LOW)
    return pl.pallas_call(
        pack_kernel,
        out_shape=(qu, qu, od, od),
        in_specs=[smem_spec()] + [full_spec(a.shape) for a in (w_qkv, w_out, w_up, w_down, vec)],
        out_specs=tuple(full_spec(a.shape) for a in (qu, qu, od, od)),
        compiler_params=kernel_params(),
        name="pack_weights",
    )(info, w_qkv, w_out, w_up, w_down, vec)


def weight_copies(ring, info, parts, wqu, wout, wdown, sems):
    core, group, spot = info[0], info[1], info[2]
    qu_copies, od_copies = [], []
    for which in range(2):
        qu, od = parts[2 * which], parts[2 * which + 1]
        half = core if which == 0 else 1 - core
        rows = qu.shape[2]
        ff_rows = od.shape[1] - rows
        qu_at = pl.multiple_of(half * PART, 128)
        od_at = pl.multiple_of(half * (D // 2), 128)
        for slot in range(ring.size):
            straight, turned = ring.turn(slot, 0), ring.turn(slot, 1)
            there = spot ^ (straight + half * (turned - straight))
            od_copies.append(
                pltpu.make_async_copy(
                    od.at[slot, pl.ds(0, ff_rows)],
                    wdown.at[pl.ds(pl.multiple_of(there * ff_rows, ff_rows), ff_rows), pl.ds(od_at, D // 2)],
                    sems.at[0],
                )
            )
            od_copies.append(
                pltpu.make_async_copy(
                    od.at[slot, pl.ds(ff_rows, rows)],
                    wout.at[pl.ds(pl.multiple_of(there * rows, rows), rows), pl.ds(od_at, D // 2)],
                    sems.at[0],
                )
            )
            for r in range(GROUP):
                row = ring.index(group ^ r, there) * rows
                qu_copies.append(
                    pltpu.make_async_copy(
                        qu.at[slot, r, :, pl.ds(0, PART)],
                        wqu.at[pl.ds(pl.multiple_of(row, rows), rows), pl.ds(qu_at, PART)],
                        sems.at[1],
                    )
                )
    return qu_copies, od_copies


def head_masks(dtype):
    lane = lax.broadcasted_iota(jnp.int32, (1, SIDE), 1) // HEAD_DIM
    return [(lane == h).astype(dtype) for h in range(SIDE // HEAD_DIM)]


def by_head(parts):
    lane = lax.broadcasted_iota(jnp.int32, (1, SIDE), 1) // HEAD_DIM
    total = parts[-1]
    for h in range(len(parts) - 2, -1, -1):
        total = jnp.where(lane == h, parts[h], total)
    return total


def turning(cosine, sine, back):
    lane = lax.broadcasted_iota(jnp.int32, sine.shape, 1) % HEAD_DIM
    first = jnp.where(lane < ROT // 2, sine, 0.0)
    second = jnp.where(lane < ROT // 2, 0.0, sine)
    if back:
        second = -second
    else:
        first = -first
    wide = SIDE // cosine.shape[1]
    return [jnp.concatenate([a] * wide, axis=1) for a in (cosine, first, second)]


def turn(part, tables):
    cosine, first, second = tables
    ahead = pltpu.roll(part, SIDE - ROT // 2, 1)
    behind = pltpu.roll(part, ROT // 2, 1)
    return part * cosine + ahead * first + behind * second


def normalise(rows):
    centered = rows - jnp.mean(rows, axis=-1, keepdims=True)
    variance = jnp.mean(centered * centered, axis=-1, keepdims=True)
    return centered * lax.rsqrt(variance + NORM_EPS)


def forward_part(x_refs, tables, vecs, wqu, wout, wdown, kept, z_refs, waits, normed_ref=None):
    cosine, sine, mask = tables
    b_qkv, b_up, gain, ln_bias = vecs
    y, qkv, probs, mixed, active, slope = kept
    rows = z_refs[0].shape[0]
    for r in range(GROUP):
        normed = normalise(x_refs[r][0:rows, :].astype(F32))
        if normed_ref is not None:
            normed_ref[r * rows : (r + 1) * rows, :] = normed
        y[r * rows : (r + 1) * rows, :] = (normed * gain[...] + ln_bias[...]).astype(LOW)
    waits[0]()
    forth = turning(cosine[...], sine[...], False)
    for kind in range(3):
        columns = slice(kind * SIDE, (kind + 1) * SIDE)
        part = dot(y[...], wqu[:, columns]) + b_qkv[:, columns]
        if kind < 2:
            part = turn(part, forth)
        qkv[:, columns] = part.astype(LOW)
    masks = head_masks(LOW)
    heads = len(masks)
    for r in range(GROUP):
        here = slice(r * rows, (r + 1) * rows)
        query, keys, values = [qkv[here, k * SIDE : (k + 1) * SIDE] for k in range(3)]
        stacked = jnp.concatenate([query * m for m in masks], axis=0)
        scores = dot_cols(stacked, keys) * HEAD_DIM ** (-0.5)
        scores = scores.reshape(heads, rows, rows) + mask[here, :][None]
        expo = jnp.exp(scores - jnp.max(scores, axis=-1, keepdims=True))
        prob = expo / jnp.sum(expo, axis=-1, keepdims=True)
        prob = prob.reshape(heads * rows, rows)
        probs[r * heads * rows : (r + 1) * heads * rows, :] = prob
        full = dot(prob.astype(LOW), values)
        mixed[here, :] = by_head([full[h * rows : (h + 1) * rows] for h in range(heads)]).astype(LOW)
    tile = 256
    for at in range(0, UNITS, tile):
        hidden = dot(y[...], wqu[:, 3 * SIDE + at : 3 * SIDE + at + tile]) + b_up[:, at : at + tile]
        share = 0.5 * (1.0 + lax.erf(hidden * (0.5**0.5)))
        density = jnp.exp(-0.5 * hidden * hidden) * (0.5 / jnp.pi) ** 0.5
        active[:, at : at + tile] = (hidden * share).astype(LOW)
        slope[:, at : at + tile] = share + hidden * density
    waits[1]()
    for at in range(0, D, tile):
        branch = dot(mixed[...], wout[:, at : at + tile]) + dot(active[...], wdown[:, at : at + tile])
        for r in range(GROUP):
            z_refs[r][:, at : at + tile] = branch[r * rows : (r + 1) * rows].astype(LOW)


def backward_part(grad, normed, tables, wqu, wout, wdown, kept, dqu, dy_refs, sums):
    cosine, sine, _ = tables
    y, qkv, probs, mixed, active, slope = kept
    rows = grad.shape[0] // GROUP
    tile = 256
    dmixed = dot_cols(grad[...], wout[...]).astype(LOW)
    for at in range(0, UNITS, tile):
        dactive = dot_cols(grad[...], wdown[at : at + tile, :])
        dhidden = (dactive * slope[:, at : at + tile]).astype(LOW)
        dqu[:, 3 * SIDE + at : 3 * SIDE + at + tile] = dhidden
    masks = head_masks(LOW)
    heads = len(masks)
    back = turning(cosine[...], sine[...], True)
    for r in range(GROUP):
        here = slice(r * rows, (r + 1) * rows)
        query, keys, values = [qkv[here, k * SIDE : (k + 1) * SIDE] for k in range(3)]
        dstack = jnp.concatenate([dmixed[here] * m for m in masks], axis=0)
        dprob = dot_cols(dstack, values)
        prob = probs[r * heads * rows : (r + 1) * heads * rows, :]
        dvalues = dot_rows(prob.astype(LOW), dstack)
        dscore = (prob * (dprob - jnp.sum(prob * dprob, axis=-1, keepdims=True))).astype(LOW)
        full = dot(dscore, keys)
        dquery = by_head([full[h * rows : (h + 1) * rows] for h in range(heads)])
        dkeys = dot_rows(dscore, jnp.concatenate([query * m for m in masks], axis=0))
        scale = HEAD_DIM ** (-0.5)
        slot_tables = [a[here] for a in back]
        dqu[here, 0:SIDE] = turn(dquery * scale, slot_tables).astype(LOW)
        dqu[here, SIDE : 2 * SIDE] = turn(dkeys * scale, slot_tables).astype(LOW)
        dqu[here, 2 * SIDE : 3 * SIDE] = dvalues.astype(LOW)
    for at in range(0, MIXED, tile):
        sums[:, at : at + tile] = jnp.sum(dqu[:, at : at + tile].astype(F32), axis=0, keepdims=True)
    for at in range(0, D, tile):
        dy = dot_cols(dqu[...], wqu[at : at + tile, :])
        for r in range(GROUP):
            dy_refs[r][0:rows, at : at + tile] = dy[r * rows : (r + 1) * rows].astype(LOW)
        own = grad[0:rows, at : at + tile].astype(F32)
        for i, terms in enumerate((own, dy * normed[:, at : at + tile], dy)):
            begin = MIXED + i * D + at
            sums[:, begin : begin + tile] = jnp.sum(terms, axis=0, keepdims=True)


def kept_shapes(tokens, rows):
    return [
        ((tokens, D), LOW),
        ((tokens, 3 * SIDE), LOW),
        ((tokens * (SIDE // HEAD_DIM), rows), F32),
        ((tokens, SIDE), LOW),
        ((tokens, UNITS), LOW),
        ((tokens, UNITS), F32),
    ]


def weight_scratch():
    return [
        pltpu.VMEM((D, MIXED), LOW),
        pltpu.VMEM((SIDE, D), LOW),
        pltpu.VMEM((UNITS, D), LOW),
        pltpu.SemaphoreType.DMA((2,)),
    ]


def start_weights(ring, info, parts, scratch):
    qu_copies, od_copies = weight_copies(ring, info, parts, *scratch)
    for copy in qu_copies + od_copies:
        copy.start()

    def waiter(copies):
        def wait():
            for copy in copies:
                copy.wait()

        return wait

    return waiter(qu_copies), waiter(od_copies)


def cost(flops, moved):
    return pl.CostEstimate(flops=2 * flops, bytes_accessed=2 * moved, transcendentals=0)


def forward_kernel(ring, info, *refs):
    parts, refs = refs[:4], refs[4:]
    x_refs, refs = refs[:4], refs[4:]
    tables, refs = refs[:3], refs[3:]
    vecs, refs = refs[:4], refs[4:]
    z_refs, refs = refs[:4], refs[4:]
    kept, scratch = refs[:6], refs[6:]
    waits = start_weights(ring, info, parts, scratch)
    forward_part(x_refs, tables, vecs, *scratch[:3], kept, z_refs, waits)


def forward(ring, info, parts, xs, tables, vecs, rows):
    tokens = GROUP * rows
    outs = [shaped((rows, D), LOW)] * GROUP + [shaped(*a) for a in kept_shapes(tokens, rows)]
    return pl.pallas_call(
        functools.partial(forward_kernel, ring),
        out_shape=tuple(outs),
        in_specs=[smem_spec()] + [any_spec()] * 4 + [full_spec(a.shape) for a in (*xs, *tables, *vecs)],
        out_specs=tuple(full_spec(a.shape) for a in outs),
        scratch_shapes=weight_scratch(),
        compiler_params=kernel_params(),
        cost_estimate=cost(2 * tokens * D * (D + 2 * FF // GROUP), 16 * 1024 * 1024),
        name="forward_shard",
    )(info, *parts, *xs, *tables, *vecs)


def middle_kernel(ring, info, *refs):
    parts, refs = refs[:4], refs[4:]
    x_refs, refs = refs[:4], refs[4:]
    g_refs, refs = refs[:4], refs[4:]
    tables, refs = refs[:3], refs[3:]
    vecs, refs = refs[:4], refs[4:]
    z_refs, refs = refs[:4], refs[4:]
    dy_refs, refs = refs[:4], refs[4:]
    (y, mixed, active, dqu, db), refs = refs[:5], refs[5:]
    (qkv, probs, slope, grad, normed), scratch = refs[:5], refs[5:]
    kept = (y, qkv, probs, mixed, active, slope)
    waits = start_weights(ring, info, parts, scratch)
    rows = z_refs[0].shape[0]
    for r in range(GROUP):
        grad[r * rows : (r + 1) * rows, :] = g_refs[r][...]
    forward_part(x_refs, tables, vecs, *scratch[:3], kept, z_refs, waits, normed)
    backward_part(grad, normed, tables, *scratch[:3], kept, dqu, dy_refs, db)


def middle(ring, info, parts, xs, gs, tables, vecs, rows):
    tokens = GROUP * rows
    shapes = kept_shapes(tokens, rows)
    outs = [shaped((rows, D), LOW)] * (2 * GROUP)
    outs += [shaped(*shapes[i]) for i in (0, 3, 4)]
    outs += [shaped((tokens, MIXED), LOW), shaped((1, MIXED + 3 * D), F32)]
    return pl.pallas_call(
        functools.partial(middle_kernel, ring),
        out_shape=tuple(outs),
        in_specs=[smem_spec()] + [any_spec()] * 4 + [full_spec(a.shape) for a in (*xs, *gs, *tables, *vecs)],
        out_specs=tuple(full_spec(a.shape) for a in outs),
        scratch_shapes=[pltpu.VMEM(*shapes[i]) for i in (1, 2, 5)]
        + [pltpu.VMEM((tokens, D), LOW), pltpu.VMEM((tokens, D), F32)]
        + weight_scratch(),
        compiler_params=kernel_params(),
        cost_estimate=cost(4 * tokens * D * (D + 2 * FF // GROUP), 16 * 1024 * 1024),
        name="forward_backward_shard",
    )(info, *parts, *xs, *gs, *tables, *vecs)


def backward_kernel(ring, info, *refs):
    parts, refs = refs[:4], refs[4:]
    x_refs, refs = refs[:4], refs[4:]
    g_refs, refs = refs[:4], refs[4:]
    z_refs, refs = refs[:4], refs[4:]
    tables, refs = refs[:3], refs[3:]
    (qkv, probs, slope), refs = refs[:3], refs[3:]
    sent_refs, refs = refs[:4], refs[4:]
    (dqu, sums), refs = refs[:2], refs[2:]
    (grad, normed), scratch = refs[:2], refs[2:]
    kept = (None, qkv, probs, None, None, slope)
    waits = start_weights(ring, info, parts, scratch)
    rows = g_refs[0].shape[0]
    for r in range(GROUP):
        grad[r * rows : (r + 1) * rows, :] = g_refs[r][...]
        normed[r * rows : (r + 1) * rows, :] = normalise(x_refs[r][0:rows, :].astype(F32))
        sent_refs[r][rows : 2 * rows, :] = z_refs[r][...]
    waits[0]()
    waits[1]()
    backward_part(grad, normed, tables, *scratch[:3], kept, dqu, sent_refs, sums)


def backward(ring, info, parts, xs, gs, zs, tables, kept, rows):
    tokens = GROUP * rows
    outs = [shaped((2 * rows, D), LOW)] * GROUP
    outs += [shaped((tokens, MIXED), LOW), shaped((1, MIXED + 3 * D), F32)]
    used = [kept[1], kept[2], kept[5]]
    blocks = (*xs, *gs, *zs, *tables, *used)
    return pl.pallas_call(
        functools.partial(backward_kernel, ring),
        out_shape=tuple(outs),
        in_specs=[smem_spec()] + [any_spec()] * 4 + [full_spec(a.shape) for a in blocks],
        out_specs=tuple(full_spec(a.shape) for a in outs),
        scratch_shapes=[pltpu.VMEM((tokens, D), LOW), pltpu.VMEM((tokens, D), F32)] + weight_scratch(),
        compiler_params=kernel_params(),
        cost_estimate=cost(2 * tokens * D * (D + 2 * FF // GROUP), 16 * 1024 * 1024),
        name="backward_shard",
    )(info, *parts, *blocks)


def od_kernel(ring, info, mixed, active, g0, g1, g2, g3, out, grad):
    spot = info[2]
    rows = g0.shape[0]
    for r, ref in enumerate((g0, g1, g2, g3)):
        grad[r * rows : (r + 1) * rows, :] = ref[...]
    out_rows = SIDE // ring.size
    ff_rows = UNITS // ring.size
    for half in range(2):
        columns = slice(half * (D // 2), (half + 1) * (D // 2))
        block = dot_rows(mixed[...], grad[:, columns]).astype(LOW)
        for there in range(ring.size):
            slot = ring.slot(spot ^ there, half)
            out[half, slot, ff_rows : ff_rows + out_rows, :] = block[there * out_rows : (there + 1) * out_rows]
            piece = dot_rows(active[:, there * ff_rows : (there + 1) * ff_rows], grad[:, columns])
            out[half, slot, 0:ff_rows, :] = piece.astype(LOW)


def od_grads(ring, info, mixed, active, gs):
    tokens = mixed.shape[0]
    out = shaped((2, ring.size, (SIDE + UNITS) // ring.size, D // 2), LOW)
    return pl.pallas_call(
        functools.partial(od_kernel, ring),
        out_shape=out,
        in_specs=[smem_spec()] + [full_spec(a.shape) for a in (mixed, active, *gs)],
        out_specs=full_spec(out.shape),
        scratch_shapes=[pltpu.VMEM((tokens, D), LOW)],
        compiler_params=kernel_params(),
        cost_estimate=cost(2 * tokens * D * (SIDE + UNITS), 5 * 1024 * 1024),
        name="out_down_grads",
    )(info, mixed, active, *gs)


def qu_kernel(ring, info, y, dqu, out):
    group, spot = info[1], info[2]
    rows = D // ring.count
    tile = 256
    for half in range(2):
        columns = slice(half * PART, (half + 1) * PART)
        for at in range(0, D, tile):
            block = dot_rows(y[:, at : at + tile], dqu[:, columns]).astype(LOW)
            for offset in range(0, tile, rows):
                dp = (at + offset) // rows
                slot = ring.slot(spot ^ ring.spot_of(dp), half)
                out[half, slot, group ^ ring.group_of(dp), :, :] = block[offset : offset + rows]


def qu_grads(ring, info, y, dqu):
    tokens = y.shape[0]
    out = shaped((2, ring.size, GROUP, D // ring.count, PART), LOW)
    return pl.pallas_call(
        functools.partial(qu_kernel, ring),
        out_shape=out,
        in_specs=[smem_spec()] + [full_spec(a.shape) for a in (y, dqu)],
        out_specs=full_spec(out.shape),
        compiler_params=kernel_params(),
        cost_estimate=cost(2 * tokens * D * MIXED, 7 * 1024 * 1024),
        name="qkv_up_grads",
    )(info, y, dqu)


def adam_update(weight, grad, first, second, factor, rate):
    clipped = grad * factor
    first_new = BETA_ONE * first + (1.0 - BETA_ONE) * clipped
    second_new = BETA_TWO * second + (1.0 - BETA_TWO) * clipped * clipped
    first_hat = first_new / (1.0 - BETA_ONE**STEP)
    second_hat = second_new / (1.0 - BETA_TWO**STEP)
    weight_new = weight - rate * (
        first_hat / (jnp.sqrt(second_hat) + ADAM_EPS) + WEIGHT_DECAY * weight
    )
    return (weight_new, first_new, second_new)


def adam_kernel(info, factor_ref, qu0, qu1, down0, out0, down1, out1, *refs):
    group = info[1]
    factor = factor_ref[0]
    olds, news = refs[:12], refs[12:]
    qus = (qu0, qu1)

    def update(which, columns, grad):
        weight, first, second = [olds[3 * which + i][0, :, columns] for i in range(3)]
        fresh = adam_update(weight, grad.astype(F32), first, second, factor, LEARN_RATE)
        for i in range(3):
            news[3 * which + i][0, :, columns] = fresh[i]

    width = SIDE // SPREAD
    for g in range(GROUP):
        for kind in range(3):
            for run in range(SPREAD):
                at = (kind * SPREAD + run) * width
                column = qkv_column(kind, run, g)
                update(0, slice(column, column + width), qu0[group ^ g, :, at : at + width])
        for local, half, at, length in up_pieces():
            column = up_column(g, local)
            update(2, slice(column, column + length), qus[half][group ^ g, :, at : at + length])
    for half, (down, out) in enumerate(((down0, out0), (down1, out1))):
        columns = slice(half * (D // 2), (half + 1) * (D // 2))
        update(1, columns, out[...])
        update(3, columns, down[...])


def adam(info, factor, qus, ods, olds):
    rows = olds[0].shape[1]
    ff_rows = olds[9].shape[1]
    steps = max(1, rows // 16)
    few, many = rows // steps, ff_rows // steps

    def master(a):
        return pl.BlockSpec((1, a.shape[1] // steps, a.shape[2]), lambda i: (0, i, 0))

    qu_spec = pl.BlockSpec((GROUP, few, PART), lambda i: (0, i, 0))
    down_spec = pl.BlockSpec((many, D // 2), lambda i: (i, 0))
    out_spec = pl.BlockSpec((few, D // 2), lambda i: (ff_rows // few + i, 0))
    return pl.pallas_call(
        adam_kernel,
        grid=(steps,),
        out_shape=tuple(shaped(a.shape, F32) for a in olds),
        in_specs=[smem_spec(), smem_spec(), qu_spec, qu_spec]
        + [down_spec, out_spec] * 2
        + [master(a) for a in olds],
        out_specs=tuple(master(a) for a in olds),
        compiler_params=kernel_params(),
        name="adamw",
    )(info, factor, qus[0], qus[1], ods[0], ods[0], ods[1], ods[1], *olds)


def doc_tables(lengths, rows):
    seqs = lengths.shape[0]
    ends = jnp.cumsum(lengths, axis=1)
    places = jnp.arange(rows, dtype=jnp.int32)
    past = places[None, :, None] >= ends[:, None, :]
    begins = jnp.sum(jnp.where(past, lengths[:, None, :], 0), axis=2)
    position = (places[None, :] - begins).reshape(seqs * rows, 1)
    half = ROT // 2
    inverse = 10000.0 ** (-(jnp.arange(half, dtype=F32) * 2.0) / ROT)
    lanes = jnp.concatenate([inverse, inverse, jnp.zeros(HEAD_DIM - ROT, F32)])
    angles = position.astype(F32) * jnp.concatenate([lanes, lanes])[None, :]
    allowed = (places[None, None, :] <= places[None, :, None]) & (places[None, None, :] >= begins[:, :, None])
    mask = jnp.where(allowed, 0.0, -1e30).reshape(seqs * rows, rows).astype(F32)
    return jnp.cos(angles), jnp.sin(angles), mask


def shards(
    x_in,
    cotangent,
    doc_lengths,
    w_qkv,
    w_out,
    w_up,
    w_down,
    vectors,
    m_qkv,
    m_out,
    m_up,
    m_down,
    m_vectors,
    v_qkv,
    v_out,
    v_up,
    v_down,
    v_vectors,
):
    place = Place()
    ring, core, group, spot = place.ring, place.core, place.group, place.spot
    info = place.info()
    local_rows, width = x_in.shape
    seqs, docs = doc_lengths.shape
    rows = local_rows // seqs
    in_rows = w_qkv.shape[1]
    shard = vectors.shape[1]
    members = range(1, GROUP)

    vec_block = jnp.pad(vectors[0].astype(LOW), (0, in_rows * 128 - shard)).reshape(in_rows, 128)
    keep_qu, send_qu, keep_od, send_od = pack(info, w_qkv, w_out, w_up, w_down, vec_block)
    came_qu = place.sibling(send_qu)
    came_od = place.sibling(send_od)

    def member_columns(block, *waited):
        qu = jnp.where(core == block, keep_qu, came_qu)
        sent = [after(take(qu, group ^ r), *waited) for r in members]
        return jnp.stack([take(qu, group)] + [place.member(a, r) for a, r in zip(sent, members)])

    def ring_step(held, step, *waited):
        came = place.across(after(held, *waited), step)
        return jnp.concatenate([held, came])

    def joined(held, came, *waited):
        return jnp.concatenate([held, after(came, *waited)])

    def block_vectors(parts):
        pieces = parts[0][:, :, 0 : -(-shard // 128), PART:].reshape(ring.size * GROUP, -1)[:, :shard]
        dp = jnp.arange(ring.count, dtype=jnp.int32)
        difference = ring.spot_of(dp) ^ spot
        slot = jnp.where(core == 0, ring.slot(difference, 0), ring.slot(difference, 1))
        vec = jnp.take(pieces, slot * GROUP + (ring.group_of(dp) ^ group), axis=0, mode="clip")
        vec = vec.reshape(-1).astype(F32)
        b_qkv, b_out, b_up, b_down, gain, ln_bias = jnp.split(
            vec, [3 * D, 4 * D, 4 * D + FF, 5 * D + FF, 6 * D + FF]
        )
        b_qkv = take(b_qkv.reshape(3 * SPREAD, GROUP, -1), group, 1).reshape(1, -1)
        b_up = take(b_up.reshape(SPREAD, GROUP, -1), group, 1).reshape(1, -1)
        return (b_qkv, b_up, gain[None], ln_bias[None]), (b_out + b_down)[None], gain[None]

    x_own = take(x_in.reshape(2, rows, width), core)
    cot_own = take(cotangent.reshape(2, rows, width), core)
    len_own = take(doc_lengths, core)
    len_rows = jnp.zeros((16, width), LOW).at[0, :docs].set(len_own.astype(LOW))
    x_sent = jnp.concatenate([x_own, len_rows])

    qu = member_columns(0)[None]
    od = jnp.where(core == 0, keep_od, came_od)[None]
    x_late = after(x_sent, qu)
    x_group = [x_sent] + [place.member(x_late, r) for r in members]
    qu_late = member_columns(1, *x_group[1:])[None]
    cot_late = after(cot_own, qu_late)
    cot_group = [cot_own] + [place.member(cot_late, r) for r in members]
    od_late = jnp.where(core == 1, keep_od, came_od)[None]
    od = ring_step(od, 0)
    qu = ring_step(qu, 0)
    od_late = ring_step(od_late, 0, qu)
    qu_came = place.across(after(qu_late, qu), 0)
    for step in range(1, ring.bits):
        od = ring_step(od, step)
        qu = ring_step(qu, step)
    parts_first = (qu, od, place.sibling(after(qu, *x_group, *cot_group)), place.sibling(od))
    lengths = jnp.stack([a[rows, :docs] for a in x_group]).astype(jnp.int32)
    tables = doc_tables(lengths, rows)
    vecs_first, bias_first, gain_first = block_vectors(parts_first)
    x_group[0] = after(x_group[0], od_late)
    first = forward(ring, info, parts_first, x_group, tables, vecs_first, rows)
    qu_late = qu_half = joined(qu_late, qu_came, first[0])
    od_came = place.across(od_late, 1)
    qu_came = place.across(qu_late, 1)

    def to_owner(slots, *waited):
        total = slots[0].astype(F32)
        for r in members:
            total = total + after(place.member(slots[r], r), *waited).astype(F32)
        return total

    kept_first = first[GROUP:]
    hidden_first = (x_own.astype(F32) + to_owner(first[:GROUP], qu_half) + bias_first).astype(LOW)
    hidden_group = [hidden_first] + [place.member(hidden_first, r) for r in members]
    od_late = joined(od_late, od_came, *hidden_group)
    qu_late = joined(qu_late, qu_came, *hidden_group)
    for step in range(2, ring.bits):
        od_late = ring_step(od_late, step)
        qu_late = ring_step(qu_late, step)
    parts_second = (qu_late, od_late, place.sibling(qu_late), place.sibling(od_late))
    vecs_second, bias_second, gain_second = block_vectors(parts_second)
    second = middle(ring, info, parts_second, hidden_group, cot_group, tables, vecs_second, rows)
    y_second, mixed_second, active_second, dqu_second, sums_second = second[2 * GROUP :]

    def rows_backward(rows_low, grad_low, dy, gain):
        rows_now = rows_low.astype(F32)
        centered = rows_now - jnp.mean(rows_now, axis=-1, keepdims=True)
        variance = jnp.mean(centered * centered, axis=-1, keepdims=True)
        inverse_std = lax.rsqrt(variance + NORM_EPS)
        normed = centered * inverse_std
        scaled = dy * gain
        inner_mean = jnp.mean(scaled, axis=-1, keepdims=True)
        inner_cross = jnp.mean(scaled * normed, axis=-1, keepdims=True)
        return (grad_low.astype(F32) + inverse_std * (scaled - inner_mean - normed * inner_cross)).astype(LOW)

    od_second = od_grads(ring, info, mixed_second, active_second, cot_group)
    qu_second = qu_grads(ring, info, y_second, dqu_second)
    dy_second = to_owner(second[GROUP : 2 * GROUP])
    mid_grad = rows_backward(hidden_first, cot_own, dy_second, gain_second)
    mid_group = [mid_grad] + [place.member(mid_grad, r) for r in members]

    def sibling_sum(halves):
        came = place.sibling(take(halves, 1 - core))
        return take(halves, core).astype(F32) + came.astype(F32)

    def ring_sum(held, steps):
        for step in steps:
            half = held.shape[0] // 2
            came = place.across(held[half:].astype(LOW), step)
            held = held[:half] + came.astype(F32)
        return held

    steps = list(reversed(range(ring.bits)))

    def to_members(qu):
        qu = qu.astype(LOW)
        return jnp.stack([qu[0]] + [place.member(qu[r], r) for r in members])

    od_second = sibling_sum(od_second)
    qu_second = sibling_sum(qu_second)
    mid_late = mid_group
    od_second = ring_sum(od_second, steps[:1])
    qu_second = ring_sum(qu_second, steps[:1])

    od_first = od_grads(ring, info, kept_first[3], kept_first[4], mid_late)
    od_pair = sibling_sum(od_first)
    mid_late = [after(a, od_first) for a in mid_group]
    back = backward(ring, info, parts_first, x_group, mid_late, second[:GROUP], tables, kept_first, rows)
    dqu_first, sums_first = back[GROUP:]
    dqu_first = after(dqu_first, od_pair, od_second, qu_second)
    qu_pair = sibling_sum(qu_grads(ring, info, kept_first[0], dqu_first))
    qu_half = ring_sum(qu_pair, steps[:1])
    qu_first = ring_sum(qu_half, steps[1:])[0]
    od_first = ring_sum(od_pair, steps)[0]
    od_second = ring_sum(od_second, steps[1:])[0]
    qu_second = ring_sum(qu_second, steps[1:])[0]

    last = to_owner([after(a, qu_half) for a in back[:GROUP]])
    start_grad = rows_backward(x_own, mid_grad, last[:rows], gain_first)
    hidden_second = (hidden_first.astype(F32) + last[rows:] + bias_second).astype(LOW)

    def all_sum(block):
        for step in range(2):
            block = block + place.member(block, 1 << step)
        for step in range(ring.bits):
            block = block + place.across(block, step)
        return block + place.sibling(block)

    def vector_grads(sums):
        member = (jnp.arange(GROUP, dtype=jnp.int32) == group)[None, :, None]
        grad_bqkv = jnp.where(member, sums[0, : 3 * SIDE].reshape(3 * SPREAD, 1, -1), 0.0)
        grad_bup = jnp.where(member, sums[0, 3 * SIDE : MIXED].reshape(SPREAD, 1, -1), 0.0)
        bias_grad = sums[0, MIXED : MIXED + D]
        return jnp.concatenate(
            [grad_bqkv.reshape(-1), bias_grad, grad_bup.reshape(-1), bias_grad, sums[0, MIXED + D :]]
        )

    vec_grad = jnp.stack([vector_grads(after(a, qu_half)) for a in (sums_first, sums_second)])
    vec_grad = all_sum(vec_grad)
    vec_share = take(take(vec_grad, core).reshape(ring.count, shard), lax.axis_index("dp"))[None]

    squares = sum(jnp.sum(a * a) for a in (od_first, qu_first, od_second, qu_second))
    squares = all_sum(jnp.broadcast_to(squares, (8, 128)))[0, 0]
    grad_norm = jnp.sqrt(squares + jnp.sum(vec_grad * vec_grad))
    factor = jnp.minimum(1.0, CLIP_LEVEL / (grad_norm + 1e-06))

    def own_block(one, two):
        came = place.sibling(jnp.where(core == 0, two, one))
        mine = jnp.where(core == 0, one, two)
        return [jnp.where(core == h, mine, came) for h in range(2)]

    ods = own_block(od_first.astype(LOW), od_second.astype(LOW))
    qus = own_block(to_members(qu_first), to_members(qu_second))
    olds = (w_qkv, m_qkv, v_qkv, w_out, m_out, v_out, w_up, m_up, v_up, w_down, m_down, v_down)
    news = adam(info, factor[None], qus, ods, olds)
    new_vec = adam_update(vectors, vec_share, m_vectors, v_vectors, factor, VECTOR_RATE)

    outputs = own_block(jnp.stack([hidden_first, start_grad]), jnp.stack([hidden_second, mid_grad]))
    outputs = jnp.concatenate(outputs, axis=1)
    hidden_out, input_grads = outputs[:1], outputs[1:]
    return (
        hidden_out,
        input_grads,
        *(news[3 * i] for i in range(4)),
        new_vec[0],
        *(news[3 * i + 1] for i in range(4)),
        new_vec[1],
        *(news[3 * i + 2] for i in range(4)),
        new_vec[2],
        grad_norm,
    )


def solution(mesh):
    return jax.shard_map(
        shards,
        mesh=mesh,
        in_specs=(
            P("dp", None),
            P("dp", None),
            P("dp", None),
            P("section", "dp", None),
            P("section", "dp", None),
            P("section", "dp", None),
            P("section", "dp", None),
            P("section", "dp"),
            P("section", "dp", None),
            P("section", "dp", None),
            P("section", "dp", None),
            P("section", "dp", None),
            P("section", "dp"),
            P("section", "dp", None),
            P("section", "dp", None),
            P("section", "dp", None),
            P("section", "dp", None),
            P("section", "dp"),
        ),
        out_specs=(
            P("section", "dp", None),
            P("section", "dp", None),
            P("section", "dp", None),
            P("section", "dp", None),
            P("section", "dp", None),
            P("section", "dp", None),
            P("section", "dp"),
            P("section", "dp", None),
            P("section", "dp", None),
            P("section", "dp", None),
            P("section", "dp", None),
            P("section", "dp"),
            P("section", "dp", None),
            P("section", "dp", None),
            P("section", "dp", None),
            P("section", "dp", None),
            P("section", "dp"),
            P(),
        ),
        check_vma=False,
    )
```

```python
import functools

import jax
import jax.numpy as jnp
from jax import lax
from jax.experimental import pallas as pl
from jax.experimental.pallas import tpu as pltpu
from jax.sharding import PartitionSpec as P

D = 1024
FF = 4096
HEADS = 16
HEAD_DIM = 64
ROT = 16
STEP = 10


NORM_EPS = 1e-05
BETA_ONE = 0.9
BETA_TWO = 0.95
LEARN_RATE = 0.05
VECTOR_RATE = 0.3
WEIGHT_DECAY = 0.01
CLIP_LEVEL = 1.0
ADAM_EPS = 1e-08

AXES = ("section", "dp")
GROUP = 4
SPREAD = 1
LOW = jnp.bfloat16
F32 = jnp.float32
SIDE = D // GROUP
UNITS = FF // GROUP
MIXED = 3 * SIDE + UNITS
PART = MIXED // 2
WIRE = PART + 128


class Ring:
    def __init__(self, count):
        self.count = count
        self.low = count // (GROUP * SPREAD)
        self.size = SPREAD * self.low
        self.bits = self.size.bit_length() - 1

    def index(self, g, t):
        return ((t // self.low) * GROUP + g) * self.low + t % self.low

    def group_of(self, dp):
        return (dp // self.low) % GROUP

    def spot_of(self, dp):
        return (dp // (GROUP * self.low)) * self.low + dp % self.low

    def order(self, core):
        steps = list(range(self.bits))
        if SPREAD > 1 or core == 1:
            steps.reverse()
        return steps

    def turn(self, slot, core):
        return sum(((slot >> s) & 1) << b for s, b in enumerate(self.order(core)))

    def slot(self, difference, core):
        return sum(((difference >> b) & 1) << s for s, b in enumerate(self.order(core)))


class Place:
    def __init__(self):
        self.ring = Ring(lax.axis_size("dp"))
        self.core = lax.axis_index("section")
        dp = lax.axis_index("dp")
        self.group = self.ring.group_of(dp)
        self.spot = self.ring.spot_of(dp)

    def info(self):
        return jnp.stack([self.core, self.group, self.spot]).astype(jnp.int32)

    def move(self, block, where):
        ring = self.ring
        route = []
        for core in range(2):
            for g in range(GROUP):
                for t in range(ring.size):
                    c, h, u = where(core, g, t)
                    route.append((core * ring.count + ring.index(g, t), c * ring.count + ring.index(h, u)))
        return lax.ppermute(block, AXES, route)

    def sibling(self, block):
        return self.move(block, lambda c, g, t: (1 - c, g, t))

    def member(self, block, distance):
        return self.move(block, lambda c, g, t: (c, g ^ distance, t))

    def toward(self, block, step):
        return self.move(block, lambda c, g, t: (c, g ^ (2, 1)[(step + c) % 2], t))

    def across(self, block, step):
        return self.move(block, lambda c, g, t: (c, g, t ^ (1 << self.ring.order(c)[step])))


def take(block, index, axis=0):
    return lax.dynamic_index_in_dim(block, index, axis, keepdims=False)


def after(block, *waited):
    return lax.optimization_barrier((block, waited))[0]


def dot(left, right):
    return jnp.dot(left, right, preferred_element_type=F32)


def dot_cols(left, right):
    return lax.dot_general(left, right, (((1,), (1,)), ((), ())), preferred_element_type=F32)


def dot_rows(left, right):
    return lax.dot_general(left, right, (((0,), (0,)), ((), ())), preferred_element_type=F32)


def full_spec(shape):
    return pl.BlockSpec(shape, lambda *_: (0,) * len(shape))


def any_spec():
    return pl.BlockSpec(memory_space=pl.ANY)


def smem_spec():
    return pl.BlockSpec(memory_space=pltpu.SMEM)


def shaped(shape, dtype):
    return jax.ShapeDtypeStruct(shape, dtype)


def kernel_params(mebibytes):
    return pltpu.CompilerParams(vmem_limit_bytes=mebibytes * 1024 * 1024)


def up_pieces():
    run = UNITS // SPREAD
    cuts = sorted({0, PART - 3 * SIDE, UNITS} | {run * i for i in range(SPREAD)})
    pieces = []
    for begin, end in zip(cuts[:-1], cuts[1:]):
        column = 3 * SIDE + begin
        pieces.append((begin, column // PART, column % PART, end - begin))
    return pieces


def up_column(g, local):
    run = UNITS // SPREAD
    return (local // run * GROUP + g) * run + local % run


def qkv_column(kind, run, g):
    width = SIDE // SPREAD
    return ((kind * SPREAD + run) * GROUP + g) * width


def pack_kernel(info, qkv_hbm, out_hbm, up_hbm, down_hbm, vec, keep_qu, send_qu, keep_od, send_od, *scratch):
    w_qkv, w_out, w_up, w_down, sems = scratch
    pairs = ((qkv_hbm, w_qkv), (up_hbm, w_up), (down_hbm, w_down), (out_hbm, w_out))
    copies = [pltpu.make_async_copy(far.at[0], near, sems.at[i]) for i, (far, near) in enumerate(pairs)]
    for copy in copies:
        copy.start()
    rows = w_qkv.shape[0]
    ff_rows = w_down.shape[0]
    width = SIDE // SPREAD
    core = info[0]

    def write_qu(halves):
        for g in range(GROUP):
            for kind in range(3):
                for run in range(SPREAD):
                    at = (kind * SPREAD + run) * width
                    column = qkv_column(kind, run, g)
                    halves[0][g, :, at : at + width] = w_qkv[:, column : column + width].astype(LOW)
            for local, half, at, length in up_pieces():
                column = up_column(g, local)
                halves[half][g, :, at : at + length] = w_up[:, column : column + length].astype(LOW)
            for half in range(2):
                halves[half][g, :, PART:WIRE] = vec[...]

    def write_od(halves):
        for half in range(2):
            columns = slice(half * (D // 2), (half + 1) * (D // 2))
            halves[half][0:ff_rows] = w_down[:, columns].astype(LOW)
            halves[half][ff_rows : ff_rows + rows] = w_out[:, columns].astype(LOW)

    for first, last, write, kept, sent in ((0, 2, write_qu, keep_qu, send_qu), (2, 4, write_od, keep_od, send_od)):
        for copy in copies[first:last]:
            copy.wait()
        pl.when(core == 0)(functools.partial(write, (kept, sent)))
        pl.when(core == 1)(functools.partial(write, (sent, kept)))


def pack(info, w_qkv, w_out, w_up, w_down, vec):
    rows, ff_rows = w_qkv.shape[1], w_down.shape[1]
    qu = shaped((GROUP, rows, WIRE), LOW)
    od = shaped((ff_rows + rows, D // 2), LOW)
    return pl.pallas_call(
        pack_kernel,
        out_shape=(qu, qu, od, od),
        in_specs=[smem_spec()] + [any_spec()] * 4 + [full_spec(vec.shape)],
        out_specs=tuple(full_spec(a.shape) for a in (qu, qu, od, od)),
        scratch_shapes=[pltpu.VMEM(a.shape[1:], F32) for a in (w_qkv, w_out, w_up, w_down)]
        + [pltpu.SemaphoreType.DMA((4,))],
        compiler_params=kernel_params(24),
        name="pack_weights",
    )(info, w_qkv, w_out, w_up, w_down, vec)


def weight_copies(ring, info, parts, wqu, wout, wdown, sems):
    core, group, spot = info[0], info[1], info[2]
    qu_copies, od_copies = [], []
    count = len(parts) // 4
    for which in range(2):
        half = core if which == 0 else 1 - core
        qu_at = pl.multiple_of(half * PART, 128)
        od_at = pl.multiple_of(half * (D // 2), 128)
        slot = 0
        for piece in range(count):
            qu, od = parts[2 * count * which + piece], parts[2 * count * which + count + piece]
            rows = qu.shape[2]
            ff_rows = od.shape[1] - rows
            for i in range(qu.shape[0]):
                straight, turned = ring.turn(slot, 0), ring.turn(slot, 1)
                there = spot ^ (straight + half * (turned - straight))
                slot += 1
                ff_row = pl.multiple_of(there * ff_rows, ff_rows)
                out_row = pl.multiple_of(there * rows, rows)
                far = wdown.at[pl.ds(ff_row, ff_rows), pl.ds(od_at, D // 2)]
                od_copies.append(pltpu.make_async_copy(od.at[i, pl.ds(0, ff_rows)], far, sems.at[0]))
                far = wout.at[pl.ds(out_row, rows), pl.ds(od_at, D // 2)]
                od_copies.append(pltpu.make_async_copy(od.at[i, pl.ds(ff_rows, rows)], far, sems.at[0]))
                for r in range(GROUP):
                    row = pl.multiple_of(ring.index(group ^ r, there) * rows, rows)
                    far = wqu.at[pl.ds(row, rows), pl.ds(qu_at, PART)]
                    qu_copies.append(pltpu.make_async_copy(qu.at[i, r, :, pl.ds(0, PART)], far, sems.at[1]))
    return qu_copies, od_copies


def head_masks(dtype):
    lane = lax.broadcasted_iota(jnp.int32, (1, SIDE), 1) // HEAD_DIM
    return [(lane == h).astype(dtype) for h in range(SIDE // HEAD_DIM)]


def by_head(parts):
    lane = lax.broadcasted_iota(jnp.int32, (1, SIDE), 1) // HEAD_DIM
    total = parts[-1]
    for h in range(len(parts) - 2, -1, -1):
        total = jnp.where(lane == h, parts[h], total)
    return total


def turning(cosine, sine, back):
    lane = lax.broadcasted_iota(jnp.int32, sine.shape, 1) % HEAD_DIM
    first = jnp.where(lane < ROT // 2, sine, 0.0)
    second = jnp.where(lane < ROT // 2, 0.0, sine)
    if back:
        second = -second
    else:
        first = -first
    wide = SIDE // cosine.shape[1]
    return [jnp.concatenate([a] * wide, axis=1) for a in (cosine, first, second)]


def turn(part, tables):
    cosine, first, second = tables
    ahead = pltpu.roll(part, SIDE - ROT // 2, 1)
    behind = pltpu.roll(part, ROT // 2, 1)
    return part * cosine + ahead * first + behind * second


def normalise(rows):
    centered = rows - jnp.mean(rows, axis=-1, keepdims=True)
    variance = jnp.mean(centered * centered, axis=-1, keepdims=True)
    return centered * lax.rsqrt(variance + NORM_EPS)


def forward_part(x_refs, tables, vecs, wqu, wout, wdown, kept, z_refs, waits, normed_ref=None):
    cosine, sine, mask = tables
    b_qkv, b_up, gain, ln_bias = vecs
    y, qkv, probs, mixed, active, slope = kept
    rows = z_refs[0].shape[0]
    for r in range(GROUP):
        normed = normalise(x_refs[r][0:rows, :].astype(F32))
        if normed_ref is not None:
            normed_ref[r * rows : (r + 1) * rows, :] = normed
        y[r * rows : (r + 1) * rows, :] = (normed * gain[...] + ln_bias[...]).astype(LOW)
    waits[0]()
    forth = turning(cosine[...], sine[...], False)
    for kind in range(3):
        columns = slice(kind * SIDE, (kind + 1) * SIDE)
        part = dot(y[...], wqu[:, columns]) + b_qkv[:, columns]
        if kind < 2:
            part = turn(part, forth)
        qkv[:, columns] = part.astype(LOW)
    masks = head_masks(LOW)
    heads = len(masks)
    for r in range(GROUP):
        here = slice(r * rows, (r + 1) * rows)
        query, keys, values = [qkv[here, k * SIDE : (k + 1) * SIDE] for k in range(3)]
        stacked = jnp.concatenate([query * m for m in masks], axis=0)
        scores = dot_cols(stacked, keys) * HEAD_DIM ** (-0.5)
        scores = scores.reshape(heads, rows, rows) + mask[here, :][None]
        expo = jnp.exp(scores - jnp.max(scores, axis=-1, keepdims=True))
        prob = expo / jnp.sum(expo, axis=-1, keepdims=True)
        prob = prob.reshape(heads * rows, rows)
        probs[r * heads * rows : (r + 1) * heads * rows, :] = prob
        full = dot(prob.astype(LOW), values)
        mixed[here, :] = by_head([full[h * rows : (h + 1) * rows] for h in range(heads)]).astype(LOW)
    tile = 256
    for at in range(0, UNITS, tile):
        hidden = dot(y[...], wqu[:, 3 * SIDE + at : 3 * SIDE + at + tile]) + b_up[:, at : at + tile]
        share = 0.5 * (1.0 + lax.erf(hidden * (0.5**0.5)))
        density = jnp.exp(-0.5 * hidden * hidden) * (0.5 / jnp.pi) ** 0.5
        active[:, at : at + tile] = (hidden * share).astype(LOW)
        slope[:, at : at + tile] = share + hidden * density
    waits[1]()
    for at in range(0, D, tile):
        branch = dot(mixed[...], wout[:, at : at + tile]) + dot(active[...], wdown[:, at : at + tile])
        for r in range(GROUP):
            z_refs[r][:, at : at + tile] = branch[r * rows : (r + 1) * rows].astype(LOW)


def backward_part(grad, normed, tables, wqu, wout, wdown, kept, dqu, dy_refs, sums):
    cosine, sine, _ = tables
    y, qkv, probs, mixed, active, slope = kept
    rows = grad.shape[0] // GROUP
    tile = 256
    dmixed = dot_cols(grad[...], wout[...]).astype(LOW)
    for at in range(0, UNITS, tile):
        dactive = dot_cols(grad[...], wdown[at : at + tile, :])
        dhidden = (dactive * slope[:, at : at + tile]).astype(LOW)
        dqu[:, 3 * SIDE + at : 3 * SIDE + at + tile] = dhidden
    masks = head_masks(LOW)
    heads = len(masks)
    back = turning(cosine[...], sine[...], True)
    for r in range(GROUP):
        here = slice(r * rows, (r + 1) * rows)
        query, keys, values = [qkv[here, k * SIDE : (k + 1) * SIDE] for k in range(3)]
        dstack = jnp.concatenate([dmixed[here] * m for m in masks], axis=0)
        dprob = dot_cols(dstack, values)
        prob = probs[r * heads * rows : (r + 1) * heads * rows, :]
        dvalues = dot_rows(prob.astype(LOW), dstack)
        dscore = (prob * (dprob - jnp.sum(prob * dprob, axis=-1, keepdims=True))).astype(LOW)
        full = dot(dscore, keys)
        dquery = by_head([full[h * rows : (h + 1) * rows] for h in range(heads)])
        dkeys = dot_rows(dscore, jnp.concatenate([query * m for m in masks], axis=0))
        scale = HEAD_DIM ** (-0.5)
        slot_tables = [a[here] for a in back]
        dqu[here, 0:SIDE] = turn(dquery * scale, slot_tables).astype(LOW)
        dqu[here, SIDE : 2 * SIDE] = turn(dkeys * scale, slot_tables).astype(LOW)
        dqu[here, 2 * SIDE : 3 * SIDE] = dvalues.astype(LOW)
    for at in range(0, MIXED, tile):
        sums[:, at : at + tile] = jnp.sum(dqu[:, at : at + tile].astype(F32), axis=0, keepdims=True)
    for at in range(0, D, tile):
        dy = dot_cols(dqu[...], wqu[at : at + tile, :])
        for r in range(GROUP):
            dy_refs[r][:, at : at + tile] = dy[r * rows : (r + 1) * rows].astype(LOW)
        own = grad[0:rows, at : at + tile].astype(F32)
        for i, terms in enumerate((own, dy * normed[:, at : at + tile], dy)):
            begin = MIXED + i * D + at
            sums[:, begin : begin + tile] = jnp.sum(terms, axis=0, keepdims=True)


def kept_shapes(tokens, rows):
    return [
        ((tokens, D), LOW),
        ((tokens, 3 * SIDE), LOW),
        ((tokens * (SIDE // HEAD_DIM), rows), F32),
        ((tokens, SIDE), LOW),
        ((tokens, UNITS), LOW),
        ((tokens, UNITS), F32),
    ]


def weight_scratch():
    return [
        pltpu.VMEM((D, MIXED), LOW),
        pltpu.VMEM((SIDE, D), LOW),
        pltpu.VMEM((UNITS, D), LOW),
        pltpu.SemaphoreType.DMA((2,)),
    ]


def start_weights(ring, info, parts, scratch):
    qu_copies, od_copies = weight_copies(ring, info, parts, *scratch)
    for copy in qu_copies + od_copies:
        copy.start()

    def waiter(copies):
        def wait():
            for copy in copies:
                copy.wait()

        return wait

    return waiter(qu_copies), waiter(od_copies)


def cost(flops, moved):
    return pl.CostEstimate(flops=2 * flops, bytes_accessed=2 * moved, transcendentals=0)


def slots_of(*refs):
    return [ref.at[i] for ref in refs for i in range(2)]


def forward_kernel(ring, count, info, *refs):
    parts, refs = refs[:count], refs[count:]
    x_refs, refs = slots_of(*refs[:2]), refs[2:]
    tables, refs = refs[:3], refs[3:]
    vecs, refs = refs[:4], refs[4:]
    z_refs, refs = slots_of(*refs[:2]), refs[2:]
    kept, scratch = refs[:6], refs[6:]
    waits = start_weights(ring, info, parts, scratch)
    forward_part(x_refs, tables, vecs, *scratch[:3], kept, z_refs, waits)


def forward(ring, info, parts, xs, tables, vecs, rows):
    tokens = GROUP * rows
    outs = [shaped((2, rows, D), LOW)] * 2 + [shaped(*a) for a in kept_shapes(tokens, rows)]
    blocks = (*xs, *tables, *vecs)
    return pl.pallas_call(
        functools.partial(forward_kernel, ring, len(parts)),
        out_shape=tuple(outs),
        in_specs=[smem_spec()] + [any_spec()] * len(parts) + [full_spec(a.shape) for a in blocks],
        out_specs=tuple(full_spec(a.shape) for a in outs),
        scratch_shapes=weight_scratch(),
        compiler_params=kernel_params(32),
        cost_estimate=cost(2 * tokens * D * (D + 2 * FF // GROUP), 16 * 1024 * 1024),
        name="forward_shard",
    )(info, *parts, *blocks)


def middle_kernel(ring, count, info, *refs):
    parts, refs = refs[:count], refs[count:]
    x_refs, refs = slots_of(*refs[:2]), refs[2:]
    g_refs, refs = slots_of(*refs[:2]), refs[2:]
    tables, refs = refs[:3], refs[3:]
    vecs, refs = refs[:4], refs[4:]
    z_refs, refs = slots_of(*refs[:2]), refs[2:]
    dy_refs, refs = slots_of(*refs[:2]), refs[2:]
    (y, mixed, active, dqu, sums), refs = refs[:5], refs[5:]
    (qkv, probs, slope, grad, normed), scratch = refs[:5], refs[5:]
    kept = (y, qkv, probs, mixed, active, slope)
    waits = start_weights(ring, info, parts, scratch)
    rows = z_refs[0].shape[0]
    for r in range(GROUP):
        grad[r * rows : (r + 1) * rows, :] = g_refs[r][...]
    forward_part(x_refs, tables, vecs, *scratch[:3], kept, z_refs, waits, normed)
    backward_part(grad, normed, tables, *scratch[:3], kept, dqu, dy_refs, sums)


def middle(ring, info, parts, xs, gs, tables, vecs, rows):
    tokens = GROUP * rows
    shapes = kept_shapes(tokens, rows)
    outs = [shaped((2, rows, D), LOW)] * 4
    outs += [shaped(*shapes[i]) for i in (0, 3, 4)]
    outs += [shaped((tokens, MIXED), LOW), shaped((1, MIXED + 3 * D), F32)]
    blocks = (*xs, *gs, *tables, *vecs)
    return pl.pallas_call(
        functools.partial(middle_kernel, ring, len(parts)),
        out_shape=tuple(outs),
        in_specs=[smem_spec()] + [any_spec()] * len(parts) + [full_spec(a.shape) for a in blocks],
        out_specs=tuple(full_spec(a.shape) for a in outs),
        scratch_shapes=[pltpu.VMEM(*shapes[i]) for i in (1, 2, 5)]
        + [pltpu.VMEM((tokens, D), LOW), pltpu.VMEM((tokens, D), F32)]
        + weight_scratch(),
        compiler_params=kernel_params(40),
        cost_estimate=cost(4 * tokens * D * (D + 2 * FF // GROUP), 16 * 1024 * 1024),
        name="forward_backward_shard",
    )(info, *parts, *blocks)


def backward_kernel(ring, count, info, *refs):
    parts, refs = refs[:count], refs[count:]
    x_refs, refs = slots_of(*refs[:2]), refs[2:]
    g_refs, refs = slots_of(*refs[:2]), refs[2:]
    tables, refs = refs[:3], refs[3:]
    (qkv, probs, slope), refs = refs[:3], refs[3:]
    dy_refs, refs = slots_of(*refs[:2]), refs[2:]
    (dqu, sums), refs = refs[:2], refs[2:]
    (grad, normed), scratch = refs[:2], refs[2:]
    kept = (None, qkv, probs, None, None, slope)
    waits = start_weights(ring, info, parts, scratch)
    rows = g_refs[0].shape[0]
    for r in range(GROUP):
        grad[r * rows : (r + 1) * rows, :] = g_refs[r][...]
        normed[r * rows : (r + 1) * rows, :] = normalise(x_refs[r][0:rows, :].astype(F32))
    waits[0]()
    waits[1]()
    backward_part(grad, normed, tables, *scratch[:3], kept, dqu, dy_refs, sums)


def backward(ring, info, parts, xs, gs, tables, kept, rows):
    tokens = GROUP * rows
    outs = [shaped((2, rows, D), LOW)] * 2
    outs += [shaped((tokens, MIXED), LOW), shaped((1, MIXED + 3 * D), F32)]
    blocks = (*xs, *gs, *tables, kept[1], kept[2], kept[5])
    return pl.pallas_call(
        functools.partial(backward_kernel, ring, len(parts)),
        out_shape=tuple(outs),
        in_specs=[smem_spec()] + [any_spec()] * len(parts) + [full_spec(a.shape) for a in blocks],
        out_specs=tuple(full_spec(a.shape) for a in outs),
        scratch_shapes=[pltpu.VMEM((tokens, D), LOW), pltpu.VMEM((tokens, D), F32)] + weight_scratch(),
        compiler_params=kernel_params(32),
        cost_estimate=cost(2 * tokens * D * (D + 2 * FF // GROUP), 16 * 1024 * 1024),
        name="backward_shard",
    )(info, *parts, *blocks)


def slot_in(ring, difference, half):
    straight, turned = ring.slot(difference, 0), ring.slot(difference, 1)
    return straight + half * (turned - straight)


def od_kernel(ring, info, mixed, active, g01, g23, keep, send, grad):
    core, spot = info[0], info[2]
    rows = g01.shape[1]
    for r, ref in enumerate(slots_of(g01, g23)):
        grad[r * rows : (r + 1) * rows, :] = ref[...]
    out_rows = SIDE // ring.size
    ff_rows = UNITS // ring.size
    for out, half in ((send, 1 - core), (keep, core)):
        columns = pl.ds(pl.multiple_of(half * (D // 2), D // 2), D // 2)
        part = grad[:, columns]
        block = dot_rows(mixed[...], part).astype(LOW)
        for there in range(ring.size):
            slot = slot_in(ring, spot ^ there, half)
            out[slot, ff_rows : ff_rows + out_rows, :] = block[there * out_rows : (there + 1) * out_rows]
            piece = dot_rows(active[:, there * ff_rows : (there + 1) * ff_rows], part)
            out[slot, 0:ff_rows, :] = piece.astype(LOW)


def od_grads(ring, info, mixed, active, gs):
    tokens = mixed.shape[0]
    out = shaped((ring.size, (SIDE + UNITS) // ring.size, D // 2), LOW)
    return pl.pallas_call(
        functools.partial(od_kernel, ring),
        out_shape=(out, out),
        in_specs=[smem_spec()] + [full_spec(a.shape) for a in (mixed, active, *gs)],
        out_specs=(full_spec(out.shape),) * 2,
        scratch_shapes=[pltpu.VMEM((tokens, D), LOW)],
        compiler_params=kernel_params(24),
        cost_estimate=cost(2 * tokens * D * (SIDE + UNITS), 5 * 1024 * 1024),
        name="out_down_grads",
    )(info, mixed, active, *gs)


def qu_kernel(ring, info, y, dqu, keep, send):
    core, group, spot = info[0], info[1], info[2]
    rows = D // ring.count
    tile = 256
    for out, half in ((send, 1 - core), (keep, core)):
        columns = pl.ds(pl.multiple_of(half * PART, 128), PART)
        for at in range(0, D, tile):
            block = dot_rows(y[:, at : at + tile], dqu[:, columns]).astype(LOW)
            for offset in range(0, tile, rows):
                dp = (at + offset) // rows
                slot = slot_in(ring, spot ^ ring.spot_of(dp), half)
                out[slot, group ^ ring.group_of(dp), :, :] = block[offset : offset + rows]


def qu_grads(ring, info, y, dqu):
    tokens = y.shape[0]
    out = shaped((ring.size, GROUP, D // ring.count, PART), LOW)
    return pl.pallas_call(
        functools.partial(qu_kernel, ring),
        out_shape=(out, out),
        in_specs=[smem_spec()] + [full_spec(a.shape) for a in (y, dqu)],
        out_specs=(full_spec(out.shape),) * 2,
        compiler_params=kernel_params(24),
        cost_estimate=cost(2 * tokens * D * MIXED, 7 * 1024 * 1024),
        name="qkv_up_grads",
    )(info, y, dqu)


def adam_update(weight, grad, first, second, factor, rate):
    clipped = grad * factor
    first_new = BETA_ONE * first + (1.0 - BETA_ONE) * clipped
    second_new = BETA_TWO * second + (1.0 - BETA_TWO) * clipped * clipped
    first_hat = first_new / (1.0 - BETA_ONE**STEP)
    second_hat = second_new / (1.0 - BETA_TWO**STEP)
    weight_new = weight - rate * (
        first_hat / (jnp.sqrt(second_hat) + ADAM_EPS) + WEIGHT_DECAY * weight
    )
    return (weight_new, first_new, second_new)


def adam_kernel(info, factor_ref, qu0, qu1, down0, out0, down1, out1, *refs):
    group = info[1]
    factor = factor_ref[0]
    olds, news = refs[:12], refs[12:]
    qus = (qu0, qu1)

    def update(which, columns, grad):
        weight, first, second = [olds[3 * which + i][0, :, columns] for i in range(3)]
        fresh = adam_update(weight, grad.astype(F32), first, second, factor, LEARN_RATE)
        for i in range(3):
            news[3 * which + i][0, :, columns] = fresh[i]

    width = SIDE // SPREAD
    for g in range(GROUP):
        for kind in range(3):
            for run in range(SPREAD):
                at = (kind * SPREAD + run) * width
                column = qkv_column(kind, run, g)
                update(0, slice(column, column + width), qu0[group ^ g, :, at : at + width])
        for local, half, at, length in up_pieces():
            column = up_column(g, local)
            update(2, slice(column, column + length), qus[half][group ^ g, :, at : at + length])
    for half, (down, out) in enumerate(((down0, out0), (down1, out1))):
        columns = slice(half * (D // 2), (half + 1) * (D // 2))
        update(1, columns, out[...])
        update(3, columns, down[...])


def adam(info, factor, qus, ods, olds):
    rows = olds[0].shape[1]
    ff_rows = olds[9].shape[1]
    steps = max(1, rows // 16)
    few, many = rows // steps, ff_rows // steps

    def master(a):
        return pl.BlockSpec((1, a.shape[1] // steps, a.shape[2]), lambda i: (0, i, 0))

    qu_spec = pl.BlockSpec((GROUP, few, PART), lambda i: (0, i, 0))
    down_spec = pl.BlockSpec((many, D // 2), lambda i: (i, 0))
    out_spec = pl.BlockSpec((few, D // 2), lambda i: (ff_rows // few + i, 0))
    return pl.pallas_call(
        adam_kernel,
        grid=(steps,),
        out_shape=tuple(shaped(a.shape, F32) for a in olds),
        in_specs=[smem_spec(), smem_spec(), qu_spec, qu_spec]
        + [down_spec, out_spec] * 2
        + [master(a) for a in olds],
        out_specs=tuple(master(a) for a in olds),
        compiler_params=kernel_params(32),
        name="adamw",
    )(info, factor, qus[0], qus[1], ods[0], ods[0], ods[1], ods[1], *olds)


def doc_tables(lengths, rows):
    seqs = lengths.shape[0]
    ends = jnp.cumsum(lengths, axis=1)
    places = jnp.arange(rows, dtype=jnp.int32)
    past = places[None, :, None] >= ends[:, None, :]
    begins = jnp.sum(jnp.where(past, lengths[:, None, :], 0), axis=2)
    position = (places[None, :] - begins).reshape(seqs * rows, 1)
    half = ROT // 2
    inverse = 10000.0 ** (-(jnp.arange(half, dtype=F32) * 2.0) / ROT)
    lanes = jnp.concatenate([inverse, inverse, jnp.zeros(HEAD_DIM - ROT, F32)])
    angles = position.astype(F32) * jnp.concatenate([lanes, lanes])[None, :]
    allowed = (places[None, None, :] <= places[None, :, None]) & (places[None, None, :] >= begins[:, :, None])
    mask = jnp.where(allowed, 0.0, -1e30).reshape(seqs * rows, rows).astype(F32)
    return jnp.cos(angles), jnp.sin(angles), mask


def shards(
    x_in,
    cotangent,
    doc_lengths,
    w_qkv,
    w_out,
    w_up,
    w_down,
    vectors,
    m_qkv,
    m_out,
    m_up,
    m_down,
    m_vectors,
    v_qkv,
    v_out,
    v_up,
    v_down,
    v_vectors,
):
    place = Place()
    ring, core, group, spot = place.ring, place.core, place.group, place.spot
    info = place.info()
    local_rows, width = x_in.shape
    seqs, docs = doc_lengths.shape
    rows = local_rows // seqs
    in_rows = w_qkv.shape[1]
    shard = vectors.shape[1]
    members = range(1, GROUP)

    vec_block = jnp.pad(vectors[0].astype(LOW), (0, in_rows * 128 - shard)).reshape(in_rows, 128)
    keep_qu, send_qu, keep_od, send_od = pack(info, w_qkv, w_out, w_up, w_down, vec_block)
    came_qu = place.sibling(send_qu)
    came_od = place.sibling(send_od)

    def member_columns(block, *waited):
        qu = jnp.where(core == block, keep_qu, came_qu)
        sent = [after(take(qu, group ^ r), *waited) for r in members]
        return [take(qu, group)] + [place.member(a, r) for a, r in zip(sent, members)]

    def gather(block, first=(), second=()):
        pair = jnp.stack([block, place.toward(after(block, *first), 0)])
        return [pair, place.toward(after(pair, *second), 1)]

    def reduce(keep, came):
        second = (keep[1].astype(F32) + came[1].astype(F32)).astype(LOW)
        return keep[0].astype(F32) + came[0].astype(F32) + place.toward(second, 0).astype(F32)

    def block_vectors(parts):
        pieces = jnp.concatenate([a[:, :, 0 : -(-shard // 128), PART:] for a in parts])
        pieces = pieces.reshape(ring.size * GROUP, -1)[:, :shard]
        dp = jnp.arange(ring.count, dtype=jnp.int32)
        difference = ring.spot_of(dp) ^ spot
        slot = jnp.where(core == 0, ring.slot(difference, 0), ring.slot(difference, 1))
        vec = jnp.take(pieces, slot * GROUP + (ring.group_of(dp) ^ group), axis=0, mode="clip")
        vec = vec.reshape(-1).astype(F32)
        b_qkv, b_out, b_up, b_down, gain, ln_bias = jnp.split(
            vec, [3 * D, 4 * D, 4 * D + FF, 5 * D + FF, 6 * D + FF]
        )
        b_qkv = take(b_qkv.reshape(3 * SPREAD, GROUP, -1), group, 1).reshape(1, -1)
        b_up = take(b_up.reshape(SPREAD, GROUP, -1), group, 1).reshape(1, -1)
        return (b_qkv, b_up, gain[None], ln_bias[None]), (b_out + b_down)[None], gain[None]

    x_own = take(x_in.reshape(2, rows, width), core)
    cot_own = take(cotangent.reshape(2, rows, width), core)
    len_own = take(doc_lengths, core)
    len_rows = jnp.zeros((16, width), LOW).at[0, :docs].set(len_own.astype(LOW))
    x_sent = jnp.concatenate([x_own, len_rows])

    qu_came = member_columns(0)
    qu_next = member_columns(1, *qu_came)
    qu_own = jnp.stack(qu_came)[None]
    od_own = jnp.where(core == 0, keep_od, came_od)[None]
    x_pair, x_rest = gather(x_sent, qu_came)
    od = [jnp.concatenate([od_own, place.across(od_own, 0)])]
    qu = [jnp.concatenate([qu_own, place.across(qu_own, 0)])]
    for step in range(1, ring.bits):
        od.append(place.across(after(jnp.concatenate(od), x_pair), step))
        qu.append(place.across(jnp.concatenate(qu), step))
    qu_sibling = [place.sibling(a) for a in qu[:-1]] + [place.sibling(after(qu[-1], x_rest))]
    parts_first = (*qu, *od, *qu_sibling, *(place.sibling(a) for a in od))
    lengths = jnp.concatenate([x_pair, x_rest])[:, rows, :docs].astype(jnp.int32)
    tables = doc_tables(lengths, rows)
    vecs_first, bias_first, gain_first = block_vectors(qu)

    cot_pair = jnp.stack([cot_own, place.toward(after(cot_own, x_rest), 0)])
    cot_rest = place.toward(cot_pair, 1)
    cot_group = [cot_pair, cot_rest]
    od_own = jnp.where(core == 1, keep_od, came_od)[None]
    od_came = place.across(after(od_own, *qu), 0)
    x_group = [after(x_pair, *qu_next[1:], cot_pair), x_rest]
    first = forward(ring, info, parts_first, x_group, tables, vecs_first, rows)
    qu_own = jnp.stack(qu_next)[None]
    kept_first = first[2:]
    qu_late = [jnp.concatenate([qu_own, after(place.across(qu_own, 0), first[0])])]
    od_late = [jnp.concatenate([od_own, after(od_came, first[0])])]
    came = after(place.toward(first[1], 1), qu_late[0], od_late[0], cot_rest)
    hidden_first = (x_own.astype(F32) + reduce(first[0], came) + bias_first).astype(LOW)
    late_sibling = [place.sibling(qu_late[0]), place.sibling(od_late[0])]
    hidden_pair, hidden_rest = gather(hidden_first, late_sibling)
    for step in range(1, ring.bits):
        od_late.append(after(place.across(jnp.concatenate(od_late), step), hidden_pair))
        qu_late.append(after(place.across(jnp.concatenate(qu_late), step), hidden_pair))
    qu_sibling = [late_sibling[0]] + [place.sibling(a) for a in qu_late[1:]]
    od_sibling = [late_sibling[1]] + [place.sibling(a) for a in od_late[1:]]
    parts_second = (*qu_late, *od_late, *qu_sibling, *od_sibling)
    vecs_second, bias_second, gain_second = block_vectors(qu_late)
    hidden_group = [hidden_pair, hidden_rest]
    second = middle(ring, info, parts_second, hidden_group, cot_group, tables, vecs_second, rows)
    y_second, mixed_second, active_second, dqu_second, sums_second = second[4:]

    def rows_backward(rows_low, grad_low, dy, gain):
        rows_now = rows_low.astype(F32)
        centered = rows_now - jnp.mean(rows_now, axis=-1, keepdims=True)
        variance = jnp.mean(centered * centered, axis=-1, keepdims=True)
        inverse_std = lax.rsqrt(variance + NORM_EPS)
        normed = centered * inverse_std
        scaled = dy * gain
        inner_mean = jnp.mean(scaled, axis=-1, keepdims=True)
        inner_cross = jnp.mean(scaled * normed, axis=-1, keepdims=True)
        return (grad_low.astype(F32) + inverse_std * (scaled - inner_mean - normed * inner_cross)).astype(LOW)

    def halved(held, came):
        half = held.shape[0] // 2
        kept = held[:half].astype(F32) + came[:half].astype(F32)
        return kept, (held[half:].astype(F32) + came[half:].astype(F32)).astype(LOW)

    def sibling_sum(grads):
        keep, send = grads
        return halved(keep, place.sibling(send))

    def ring_sum(held, steps):
        kept, sent = held
        for step in steps:
            came = place.across(sent, step)
            if kept.shape[0] == 1:
                return kept[0] + came[0].astype(F32)
            kept, sent = halved(kept, came)
        return kept, sent

    steps = list(reversed(range(ring.bits)))

    def to_members(qu):
        qu = qu.astype(LOW)
        return [qu[0]] + [place.member(qu[r], r) for r in members]

    came = place.toward(second[3], 1)
    od_second = od_grads(ring, info, after(mixed_second, came), active_second, cot_group)
    qu_second = qu_grads(ring, info, y_second, dqu_second)
    dy_second = reduce(second[2], came)
    mid_grad = rows_backward(hidden_first, cot_own, dy_second, gain_second)
    mid_pair, mid_rest = gather(mid_grad)
    od_second = ring_sum(sibling_sum(od_second), steps[:-1])
    qu_second = ring_sum(sibling_sum(qu_second), steps[:-1])

    mid_group = [after(mid_pair, od_second, qu_second), mid_rest]
    od_first = od_grads(ring, info, kept_first[3], kept_first[4], mid_group)
    od_pair = sibling_sum(od_first)
    mid_late = [after(a, od_first) for a in mid_group]
    back = backward(ring, info, parts_first, x_group, mid_late, tables, kept_first, rows)
    dqu_first, sums_first = back[2:]
    z_came = after(place.toward(after(second[1], mid_rest), 1), dqu_first)
    od_second = ring_sum(od_second, steps[-1:])
    qu_second = ring_sum(qu_second, steps[-1:])
    qu_sent = to_members(qu_second)
    dqu_first = after(dqu_first, *od_pair, od_second)
    qu_keep, qu_send = qu_grads(ring, info, kept_first[0], dqu_first)
    branch = reduce(second[0], z_came)
    hidden_second = (hidden_first.astype(F32) + branch + bias_second).astype(LOW)

    def vector_grads(sums):
        member = (jnp.arange(GROUP, dtype=jnp.int32) == group)[None, :, None]
        grad_bqkv = jnp.where(member, sums[0, : 3 * SIDE].reshape(3 * SPREAD, 1, -1), 0.0)
        grad_bup = jnp.where(member, sums[0, 3 * SIDE : MIXED].reshape(SPREAD, 1, -1), 0.0)
        bias_grad = sums[0, MIXED : MIXED + D]
        return jnp.concatenate(
            [grad_bqkv.reshape(-1), bias_grad, grad_bup.reshape(-1), bias_grad, sums[0, MIXED + D :]]
        )

    def all_sum(block, first, last):
        hops = [place.sibling]
        hops += [functools.partial(place.across, step=step) for step in range(ring.bits)]
        hops += [functools.partial(place.member, distance=1), functools.partial(place.member, distance=2)]
        for hop in hops[first:last]:
            block = block + hop(block)
        return block

    vec_grad = jnp.stack([vector_grads(sums_first), vector_grads(sums_second)])
    vec_grad = all_sum(vec_grad, 0, 1)
    kept, sent = halved(qu_keep, after(place.sibling(qu_send), vec_grad))
    vec_grad = all_sum(after(vec_grad, kept), 1, 1 + ring.bits)
    kept, sent = ring_sum((kept, sent), steps[:-1])
    sent = after(sent, vec_grad, *qu_sent[1:])
    qu_first = ring_sum((kept, sent), steps[-1:])
    vec_grad = all_sum(after(vec_grad, sent), 1 + ring.bits, None)
    vec_share = take(take(vec_grad, core).reshape(ring.count, shard), lax.axis_index("dp"))[None]
    od_first = ring_sum(od_pair, steps)

    last = reduce(back[0], after(place.toward(back[1], 1), sent))
    start_grad = rows_backward(x_own, mid_grad, last, gain_first)

    squares = sum(jnp.sum(a * a) for a in (od_first, qu_first, od_second, qu_second))
    qu_mine = to_members(qu_first)
    squares = all_sum(jnp.broadcast_to(squares, (8, 128)), 0, 2)
    squares = all_sum(after(squares, *qu_mine[1:]), 2, None)[0, 0]
    grad_norm = jnp.sqrt(squares + jnp.sum(vec_grad * vec_grad))
    factor = jnp.minimum(1.0, CLIP_LEVEL / (grad_norm + 1e-06))

    def own_block(one, two):
        came = place.sibling(jnp.where(core == 0, two, one))
        mine = jnp.where(core == 0, one, two)
        return [jnp.where(core == h, mine, came) for h in range(2)]

    ods = own_block(after(od_first.astype(LOW), sent), od_second.astype(LOW))
    qus = own_block(jnp.stack(qu_mine), jnp.stack(qu_sent))
    olds = (w_qkv, m_qkv, v_qkv, w_out, m_out, v_out, w_up, m_up, v_up, w_down, m_down, v_down)
    news = adam(info, factor[None], qus, ods, olds)
    new_vec = adam_update(vectors, vec_share, m_vectors, v_vectors, factor, VECTOR_RATE)

    outputs = own_block(jnp.stack([hidden_first, start_grad]), jnp.stack([hidden_second, mid_grad]))
    outputs = jnp.concatenate(outputs, axis=1)
    hidden_out, input_grads = outputs[:1], outputs[1:]
    return (
        hidden_out,
        input_grads,
        *(news[3 * i] for i in range(4)),
        new_vec[0],
        *(news[3 * i + 1] for i in range(4)),
        new_vec[1],
        *(news[3 * i + 2] for i in range(4)),
        new_vec[2],
        grad_norm,
    )


def solution(mesh):
    return jax.shard_map(
        shards,
        mesh=mesh,
        in_specs=(
            P("dp", None),
            P("dp", None),
            P("dp", None),
            P("section", "dp", None),
            P("section", "dp", None),
            P("section", "dp", None),
            P("section", "dp", None),
            P("section", "dp"),
            P("section", "dp", None),
            P("section", "dp", None),
            P("section", "dp", None),
            P("section", "dp", None),
            P("section", "dp"),
            P("section", "dp", None),
            P("section", "dp", None),
            P("section", "dp", None),
            P("section", "dp", None),
            P("section", "dp"),
        ),
        out_specs=(
            P("section", "dp", None),
            P("section", "dp", None),
            P("section", "dp", None),
            P("section", "dp", None),
            P("section", "dp", None),
            P("section", "dp", None),
            P("section", "dp"),
            P("section", "dp", None),
            P("section", "dp", None),
            P("section", "dp", None),
            P("section", "dp", None),
            P("section", "dp"),
            P("section", "dp", None),
            P("section", "dp", None),
            P("section", "dp", None),
            P("section", "dp", None),
            P("section", "dp"),
            P(),
        ),
        check_vma=False,
    )
```

```python
import functools

import jax
import jax.numpy as jnp
from jax import lax
from jax.experimental import pallas as pl
from jax.experimental.pallas import tpu as pltpu
from jax.sharding import PartitionSpec as P

D = 1024
FF = 4096
HEADS = 16
HEAD_DIM = 64
ROT = 16
STEP = 10


NORM_EPS = 1e-05
BETA_ONE = 0.9
BETA_TWO = 0.95
LEARN_RATE = 0.05
VECTOR_RATE = 0.3
WEIGHT_DECAY = 0.01
CLIP_LEVEL = 1.0
ADAM_EPS = 1e-08

AXES = ("section", "dp")
GROUP = 4
SPREAD = 1
LOW = jnp.bfloat16
F32 = jnp.float32
SIDE = D // GROUP
UNITS = FF // GROUP
MIXED = 3 * SIDE + UNITS
PART = MIXED // 2
WIRE = PART + 128


class Ring:
    def __init__(self, count):
        self.count = count
        self.low = count // (GROUP * SPREAD)
        self.size = SPREAD * self.low
        self.bits = self.size.bit_length() - 1

    def index(self, g, t):
        return ((t // self.low) * GROUP + g) * self.low + t % self.low

    def group_of(self, dp):
        return (dp // self.low) % GROUP

    def spot_of(self, dp):
        return (dp // (GROUP * self.low)) * self.low + dp % self.low

    def order(self, core):
        steps = list(range(self.bits))
        if SPREAD > 1 or core == 1:
            steps.reverse()
        return steps

    def turn(self, slot, core):
        return sum(((slot >> s) & 1) << b for s, b in enumerate(self.order(core)))

    def slot(self, difference, core):
        return sum(((difference >> b) & 1) << s for s, b in enumerate(self.order(core)))


class Place:
    def __init__(self):
        self.ring = Ring(lax.axis_size("dp"))
        self.core = lax.axis_index("section")
        dp = lax.axis_index("dp")
        self.group = self.ring.group_of(dp)
        self.spot = self.ring.spot_of(dp)

    def info(self):
        return jnp.stack([self.core, self.group, self.spot]).astype(jnp.int32)

    def move(self, block, where):
        ring = self.ring
        route = []
        for core in range(2):
            for g in range(GROUP):
                for t in range(ring.size):
                    c, h, u = where(core, g, t)
                    route.append((core * ring.count + ring.index(g, t), c * ring.count + ring.index(h, u)))
        return lax.ppermute(block, AXES, route)

    def sibling(self, block):
        return self.move(block, lambda c, g, t: (1 - c, g, t))

    def member(self, block, distance):
        return self.move(block, lambda c, g, t: (c, g ^ distance, t))

    def across(self, block, step):
        return self.move(block, lambda c, g, t: (c, g, t ^ (1 << self.ring.order(c)[step])))


def take(block, index, axis=0):
    return lax.dynamic_index_in_dim(block, index, axis, keepdims=False)


def after(block, *waited):
    return lax.optimization_barrier((block, waited))[0]


def dot(left, right):
    return jnp.dot(left, right, preferred_element_type=F32)


def dot_cols(left, right):
    return lax.dot_general(left, right, (((1,), (1,)), ((), ())), preferred_element_type=F32)


def dot_rows(left, right):
    return lax.dot_general(left, right, (((0,), (0,)), ((), ())), preferred_element_type=F32)


def full_spec(shape):
    return pl.BlockSpec(shape, lambda *_: (0,) * len(shape))


def far_spec():
    return pl.BlockSpec(memory_space=pltpu.HBM)


def smem_spec():
    return pl.BlockSpec(memory_space=pltpu.SMEM)


def shaped(shape, dtype):
    return jax.ShapeDtypeStruct(shape, dtype)


def kernel_params(mebibytes):
    return pltpu.CompilerParams(vmem_limit_bytes=mebibytes * 1024 * 1024)


def up_pieces():
    run = UNITS // SPREAD
    cuts = sorted({0, PART - 3 * SIDE, UNITS} | {run * i for i in range(SPREAD)})
    pieces = []
    for begin, end in zip(cuts[:-1], cuts[1:]):
        column = 3 * SIDE + begin
        pieces.append((begin, column // PART, column % PART, end - begin))
    return pieces


def up_column(g, local):
    run = UNITS // SPREAD
    return (local // run * GROUP + g) * run + local % run


def qkv_column(kind, run, g):
    width = SIDE // SPREAD
    return ((kind * SPREAD + run) * GROUP + g) * width


def pack_kernel(info, qkv_hbm, out_hbm, up_hbm, down_hbm, vec, keep_qu, send_qu, keep_od, send_od, *scratch):
    w_qkv, w_out, w_up, w_down, sems = scratch
    pairs = ((qkv_hbm, w_qkv), (up_hbm, w_up), (down_hbm, w_down), (out_hbm, w_out))
    copies = [pltpu.make_async_copy(far.at[0], near, sems.at[i]) for i, (far, near) in enumerate(pairs)]
    for copy in copies:
        copy.start()
    rows = w_qkv.shape[0]
    ff_rows = w_down.shape[0]
    width = SIDE // SPREAD
    core = info[0]

    def write_qu(halves):
        for g in range(GROUP):
            for kind in range(3):
                for run in range(SPREAD):
                    at = (kind * SPREAD + run) * width
                    column = qkv_column(kind, run, g)
                    halves[0][g, :, at : at + width] = w_qkv[:, column : column + width].astype(LOW)
            for local, half, at, length in up_pieces():
                column = up_column(g, local)
                halves[half][g, :, at : at + length] = w_up[:, column : column + length].astype(LOW)
            for half in range(2):
                halves[half][g, :, PART:WIRE] = vec[...]

    def write_od(halves):
        for half in range(2):
            columns = slice(half * (D // 2), (half + 1) * (D // 2))
            halves[half][0:ff_rows] = w_down[:, columns].astype(LOW)
            halves[half][ff_rows : ff_rows + rows] = w_out[:, columns].astype(LOW)

    for first, last, write, kept, sent in ((0, 2, write_qu, keep_qu, send_qu), (2, 4, write_od, keep_od, send_od)):
        for copy in copies[first:last]:
            copy.wait()
        pl.when(core == 0)(functools.partial(write, (kept, sent)))
        pl.when(core == 1)(functools.partial(write, (sent, kept)))


def pack(info, w_qkv, w_out, w_up, w_down, vec):
    rows, ff_rows = w_qkv.shape[1], w_down.shape[1]
    qu = shaped((GROUP, rows, WIRE), LOW)
    od = shaped((ff_rows + rows, D // 2), LOW)
    return pl.pallas_call(
        pack_kernel,
        out_shape=(qu, qu, od, od),
        in_specs=[smem_spec()] + [far_spec()] * 4 + [full_spec(vec.shape)],
        out_specs=tuple(full_spec(a.shape) for a in (qu, qu, od, od)),
        scratch_shapes=[pltpu.VMEM(a.shape[1:], F32) for a in (w_qkv, w_out, w_up, w_down)]
        + [pltpu.SemaphoreType.DMA((4,))],
        compiler_params=kernel_params(24),
        name="pack_weights",
    )(info, w_qkv, w_out, w_up, w_down, vec)


def weight_copies(ring, info, parts, wqu, wout, wdown, sems):
    core, group, spot = info[0], info[1], info[2]
    qu_copies, od_copies = [], []
    count = len(parts) // 4
    for which in range(2):
        half = core if which == 0 else 1 - core
        qu_at = pl.multiple_of(half * PART, 128)
        od_at = pl.multiple_of(half * (D // 2), 128)
        slot = 0
        for piece in range(count):
            qu, od = parts[2 * count * which + piece], parts[2 * count * which + count + piece]
            rows = qu.shape[2]
            ff_rows = od.shape[1] - rows
            for i in range(qu.shape[0]):
                straight, turned = ring.turn(slot, 0), ring.turn(slot, 1)
                there = spot ^ (straight + half * (turned - straight))
                slot += 1
                ff_row = pl.multiple_of(there * ff_rows, ff_rows)
                out_row = pl.multiple_of(there * rows, rows)
                far = wdown.at[pl.ds(ff_row, ff_rows), pl.ds(od_at, D // 2)]
                od_copies.append(pltpu.make_async_copy(od.at[i, pl.ds(0, ff_rows)], far, sems.at[0]))
                far = wout.at[pl.ds(out_row, rows), pl.ds(od_at, D // 2)]
                od_copies.append(pltpu.make_async_copy(od.at[i, pl.ds(ff_rows, rows)], far, sems.at[0]))
                for r in range(GROUP):
                    row = pl.multiple_of(ring.index(group ^ r, there) * rows, rows)
                    far = wqu.at[pl.ds(row, rows), pl.ds(qu_at, PART)]
                    qu_copies.append(pltpu.make_async_copy(qu.at[i, r, :, pl.ds(0, PART)], far, sems.at[1]))
    return qu_copies, od_copies


def head_masks(dtype):
    lane = lax.broadcasted_iota(jnp.int32, (1, SIDE), 1) // HEAD_DIM
    return [(lane == h).astype(dtype) for h in range(SIDE // HEAD_DIM)]


def by_head(parts):
    lane = lax.broadcasted_iota(jnp.int32, (1, SIDE), 1) // HEAD_DIM
    total = parts[-1]
    for h in range(len(parts) - 2, -1, -1):
        total = jnp.where(lane == h, parts[h], total)
    return total


def turning(cosine, sine, back):
    lane = lax.broadcasted_iota(jnp.int32, sine.shape, 1) % HEAD_DIM
    first = jnp.where(lane < ROT // 2, sine, 0.0)
    second = jnp.where(lane < ROT // 2, 0.0, sine)
    if back:
        second = -second
    else:
        first = -first
    wide = SIDE // cosine.shape[1]
    return [jnp.concatenate([a] * wide, axis=1) for a in (cosine, first, second)]


def turn(part, tables):
    cosine, first, second = tables
    ahead = pltpu.roll(part, SIDE - ROT // 2, 1)
    behind = pltpu.roll(part, ROT // 2, 1)
    return part * cosine + ahead * first + behind * second


def normalise(rows):
    centered = rows - jnp.mean(rows, axis=-1, keepdims=True)
    variance = jnp.mean(centered * centered, axis=-1, keepdims=True)
    return centered * lax.rsqrt(variance + NORM_EPS)


def no_wait():
    pass


def forward_part(x_refs, tables, vecs, wqu, wout, wdown, kept, z_refs, waits, done, normed_ref=None):
    cosine, sine, mask = tables
    b_qkv, b_up, gain, ln_bias = vecs
    y, qkv, probs, mixed, active, slope = kept
    rows = z_refs[0].shape[0]
    for r in range(GROUP):
        normed = normalise(x_refs[r][0:rows, :].astype(F32))
        if normed_ref is not None:
            normed_ref[r * rows : (r + 1) * rows, :] = normed
        y[r * rows : (r + 1) * rows, :] = (normed * gain[...] + ln_bias[...]).astype(LOW)
    done(0)
    waits[0]()
    waits[2]()
    forth = turning(cosine[...], sine[...], False)
    for kind in range(3):
        columns = slice(kind * SIDE, (kind + 1) * SIDE)
        part = dot(y[...], wqu[:, columns]) + b_qkv[:, columns]
        if kind < 2:
            part = turn(part, forth)
        qkv[:, columns] = part.astype(LOW)
    done(1)
    masks = head_masks(LOW)
    heads = len(masks)
    for r in range(GROUP):
        here = slice(r * rows, (r + 1) * rows)
        query, keys, values = [qkv[here, k * SIDE : (k + 1) * SIDE] for k in range(3)]
        stacked = jnp.concatenate([query * m for m in masks], axis=0)
        scores = dot_cols(stacked, keys) * HEAD_DIM ** (-0.5)
        scores = scores.reshape(heads, rows, rows) + mask[here, :][None]
        expo = jnp.exp(scores - jnp.max(scores, axis=-1, keepdims=True))
        prob = expo / jnp.sum(expo, axis=-1, keepdims=True)
        prob = prob.reshape(heads * rows, rows)
        probs[r * heads * rows : (r + 1) * heads * rows, :] = prob
        full = dot(prob.astype(LOW), values)
        mixed[here, :] = by_head([full[h * rows : (h + 1) * rows] for h in range(heads)]).astype(LOW)
    done(2)
    done(3)
    tile = 256
    for at in range(0, UNITS, tile):
        hidden = dot(y[...], wqu[:, 3 * SIDE + at : 3 * SIDE + at + tile]) + b_up[:, at : at + tile]
        share = 0.5 * (1.0 + lax.erf(hidden * (0.5**0.5)))
        density = jnp.exp(-0.5 * hidden * hidden) * (0.5 / jnp.pi) ** 0.5
        active[:, at : at + tile] = (hidden * share).astype(LOW)
        slope[:, at : at + tile] = share + hidden * density
    done(4)
    done(5)
    waits[1]()
    for at in range(0, D, tile):
        branch = dot(mixed[...], wout[:, at : at + tile]) + dot(active[...], wdown[:, at : at + tile])
        for r in range(GROUP):
            z_refs[r][:, at : at + tile] = branch[r * rows : (r + 1) * rows].astype(LOW)


def backward_part(grad, normed, tables, wqu, wout, wdown, kept, dqu, dy_refs, sums, waits, done):
    cosine, sine, _ = tables
    y, qkv, probs, mixed, active, slope = kept
    rows = grad.shape[0] // GROUP
    tile = 256
    waits[0]()
    dmixed = dot_cols(grad[...], wout[...]).astype(LOW)
    for at in range(0, UNITS, tile):
        dactive = dot_cols(grad[...], wdown[at : at + tile, :])
        dhidden = (dactive * slope[:, at : at + tile]).astype(LOW)
        dqu[:, 3 * SIDE + at : 3 * SIDE + at + tile] = dhidden
    waits[1]()
    masks = head_masks(LOW)
    heads = len(masks)
    back = turning(cosine[...], sine[...], True)
    for r in range(GROUP):
        here = slice(r * rows, (r + 1) * rows)
        query, keys, values = [qkv[here, k * SIDE : (k + 1) * SIDE] for k in range(3)]
        dstack = jnp.concatenate([dmixed[here] * m for m in masks], axis=0)
        dprob = dot_cols(dstack, values)
        prob = probs[r * heads * rows : (r + 1) * heads * rows, :]
        dvalues = dot_rows(prob.astype(LOW), dstack)
        dscore = (prob * (dprob - jnp.sum(prob * dprob, axis=-1, keepdims=True))).astype(LOW)
        full = dot(dscore, keys)
        dquery = by_head([full[h * rows : (h + 1) * rows] for h in range(heads)])
        dkeys = dot_rows(dscore, jnp.concatenate([query * m for m in masks], axis=0))
        scale = HEAD_DIM ** (-0.5)
        slot_tables = [a[here] for a in back]
        dqu[here, 0:SIDE] = turn(dquery * scale, slot_tables).astype(LOW)
        dqu[here, SIDE : 2 * SIDE] = turn(dkeys * scale, slot_tables).astype(LOW)
        dqu[here, 2 * SIDE : 3 * SIDE] = dvalues.astype(LOW)
    done()
    for at in range(0, MIXED, tile):
        sums[:, at : at + tile] = jnp.sum(dqu[:, at : at + tile].astype(F32), axis=0, keepdims=True)
    waits[2]()
    for at in range(0, D, tile):
        dy = dot_cols(dqu[...], wqu[at : at + tile, :])
        for r in range(GROUP):
            dy_refs[r][:, at : at + tile] = dy[r * rows : (r + 1) * rows].astype(LOW)
        own = grad[0:rows, at : at + tile].astype(F32)
        for i, terms in enumerate((own, dy * normed[:, at : at + tile], dy)):
            begin = MIXED + i * D + at
            sums[:, begin : begin + tile] = jnp.sum(terms, axis=0, keepdims=True)


def kept_shapes(tokens, rows):
    return [
        ((tokens, D), LOW),
        ((tokens, 3 * SIDE), LOW),
        ((tokens * (SIDE // HEAD_DIM), rows), F32),
        ((tokens, SIDE), LOW),
        ((tokens, UNITS), LOW),
        ((tokens, UNITS), F32),
    ]


def weight_scratch():
    return [
        pltpu.VMEM((D, MIXED), LOW),
        pltpu.VMEM((SIDE, D), LOW),
        pltpu.VMEM((UNITS, D), LOW),
        pltpu.SemaphoreType.DMA((2,)),
    ]


def waiter(copies):
    def wait():
        for copy in copies:
            copy.wait()

    return wait


def started(pairs, sem):
    copies = [pltpu.make_async_copy(source, target, sem) for source, target in pairs]
    for copy in copies:
        copy.start()
    return waiter(copies)


def table_scratch(tokens, rows):
    return [pltpu.VMEM((tokens, 128), F32), pltpu.VMEM((tokens, 128), F32), pltpu.VMEM((tokens, rows), F32)]


def cost(flops, moved):
    return pl.CostEstimate(flops=2 * flops, bytes_accessed=2 * moved, transcendentals=0)


def leaving(pairs, sems):
    copies = [pltpu.make_async_copy(near, far, sems.at[i]) for i, (near, far) in enumerate(pairs)]

    def go(i):
        copies[i].start()

    return go, waiter(copies)


def forward_kernel(ring, count, info, *refs):
    parts, refs = refs[:count], refs[count:]
    x_refs, refs = refs[:4], refs[4:]
    far_tables, refs = refs[:3], refs[3:]
    vecs, refs = refs[:4], refs[4:]
    z_refs, refs = refs[:4], refs[4:]
    far_kept, refs = refs[:6], refs[6:]
    kept, refs = refs[:6], refs[6:]
    tables, refs = refs[:3], refs[3:]
    (in_sems, out_sems), scratch = refs[:2], refs[2:]
    qu_copies, od_copies = weight_copies(ring, info, parts, *scratch)
    for copy in qu_copies:
        copy.start()
    tables_in = started(zip(far_tables, tables), in_sems.at[0])
    for copy in od_copies:
        copy.start()
    go, out = leaving(list(zip(kept, far_kept)), out_sems)
    waits = (waiter(qu_copies), waiter(od_copies), tables_in)
    forward_part(x_refs, tables, vecs, *scratch[:3], kept, z_refs, waits, go)
    out()


def forward(ring, info, parts, xs, tables, vecs, rows):
    tokens = GROUP * rows
    shapes = kept_shapes(tokens, rows)
    outs = [shaped((rows, D), LOW)] * GROUP + [shaped(*a) for a in shapes]
    return pl.pallas_call(
        functools.partial(forward_kernel, ring, len(parts)),
        out_shape=tuple(outs),
        in_specs=[smem_spec()]
        + [far_spec()] * len(parts)
        + [full_spec(a.shape) for a in xs]
        + [far_spec()] * 3
        + [full_spec(a.shape) for a in vecs],
        out_specs=tuple([full_spec((rows, D))] * GROUP + [far_spec()] * 6),
        scratch_shapes=[pltpu.VMEM(*a) for a in shapes]
        + table_scratch(tokens, rows)
        + [pltpu.SemaphoreType.DMA((1,)), pltpu.SemaphoreType.DMA((6,))]
        + weight_scratch(),
        compiler_params=kernel_params(32),
        cost_estimate=cost(2 * tokens * D * (D + 2 * FF // GROUP), 16 * 1024 * 1024),
        name="forward_shard",
    )(info, *parts, *xs, *tables, *vecs)


def grad_rows(refs, grad):
    rows = refs[0].shape[0]
    return [(ref, grad.at[pl.ds(r * rows, rows)]) for r, ref in enumerate(refs)]


def middle_kernel(ring, count, info, *refs):
    parts, refs = refs[:count], refs[count:]
    x_refs, refs = refs[:4], refs[4:]
    g_refs, refs = refs[:4], refs[4:]
    far_tables, refs = refs[:3], refs[3:]
    vecs, refs = refs[:4], refs[4:]
    z_refs, refs = refs[:4], refs[4:]
    dy_refs, refs = refs[:4], refs[4:]
    (far_y, far_mixed, far_active, far_dqu, sums), refs = refs[:5], refs[5:]
    kept, refs = refs[:6], refs[6:]
    tables, refs = refs[:3], refs[3:]
    (grad, normed, dqu, in_sems, out_sems), scratch = refs[:5], refs[5:]
    qu_copies, od_copies = weight_copies(ring, info, parts, *scratch)
    for copy in qu_copies:
        copy.start()
    tables_in = started(zip(far_tables, tables), in_sems.at[0])
    for copy in od_copies:
        copy.start()
    grad_in = started(grad_rows(g_refs, grad), in_sems.at[1])
    pairs = [(kept[0], far_y), (kept[3], far_mixed), (kept[4], far_active), (dqu, far_dqu)]
    go, out = leaving(pairs, out_sems)

    def done(i):
        if i in (0, 3, 4):
            go((0, 3, 4).index(i))

    waits = (waiter(qu_copies), waiter(od_copies), tables_in)
    forward_part(x_refs, tables, vecs, *scratch[:3], kept, z_refs, waits, done, normed)
    waits = (grad_in, no_wait, no_wait)
    done = functools.partial(go, 3)
    backward_part(grad, normed, tables, *scratch[:3], kept, dqu, dy_refs, sums, waits, done)
    out()


def middle(ring, info, parts, xs, gs, tables, vecs, rows):
    tokens = GROUP * rows
    shapes = kept_shapes(tokens, rows)
    outs = [shaped((rows, D), LOW)] * (2 * GROUP)
    outs += [shaped(*shapes[i]) for i in (0, 3, 4)]
    outs += [shaped((tokens, MIXED), LOW), shaped((1, MIXED + 3 * D), F32)]
    return pl.pallas_call(
        functools.partial(middle_kernel, ring, len(parts)),
        out_shape=tuple(outs),
        in_specs=[smem_spec()]
        + [far_spec()] * len(parts)
        + [full_spec(a.shape) for a in xs]
        + [far_spec()] * (GROUP + 3)
        + [full_spec(a.shape) for a in vecs],
        out_specs=tuple(
            [full_spec((rows, D))] * (2 * GROUP) + [far_spec()] * 4 + [full_spec((1, MIXED + 3 * D))]
        ),
        scratch_shapes=[pltpu.VMEM(*a) for a in shapes]
        + table_scratch(tokens, rows)
        + [pltpu.VMEM((tokens, D), LOW), pltpu.VMEM((tokens, D), F32), pltpu.VMEM((tokens, MIXED), LOW)]
        + [pltpu.SemaphoreType.DMA((2,)), pltpu.SemaphoreType.DMA((4,))]
        + weight_scratch(),
        compiler_params=kernel_params(36),
        cost_estimate=cost(4 * tokens * D * (D + 2 * FF // GROUP), 16 * 1024 * 1024),
        name="forward_backward_shard",
    )(info, *parts, *xs, *gs, *tables, *vecs)


def backward_kernel(ring, count, info, *refs):
    parts, refs = refs[:count], refs[count:]
    x_refs, refs = refs[:4], refs[4:]
    g_refs, refs = refs[:4], refs[4:]
    far_tables, refs = refs[:3], refs[3:]
    (far_y, far_qkv, far_probs, far_slope), refs = refs[:4], refs[4:]
    dy_refs, refs = refs[:4], refs[4:]
    (keep, send), refs = refs[:2], refs[2:]
    (y, qkv, probs, slope), refs = refs[:4], refs[4:]
    tables, refs = refs[:3], refs[3:]
    (grad, normed, dqu, sums, in_sems), scratch = refs[:5], refs[5:]
    kept = (None, qkv, probs, None, None, slope)
    qu_copies, od_copies = weight_copies(ring, info, parts, *scratch)
    grad_in = started(grad_rows(g_refs, grad), in_sems.at[0])
    for copy in od_copies:
        copy.start()
    slope_in = started([(far_slope, slope)], in_sems.at[1])
    heads_in = started([(far_qkv, qkv), (far_probs, probs), *zip(far_tables, tables)], in_sems.at[2])
    for copy in qu_copies:
        copy.start()
    y_in = started([(far_y, y)], in_sems.at[3])
    rows = g_refs[0].shape[0]
    for r in range(GROUP):
        normed[r * rows : (r + 1) * rows, :] = normalise(x_refs[r][0:rows, :].astype(F32))
    od_in, qu_in = waiter(od_copies), waiter(qu_copies)

    def units_in():
        grad_in()
        od_in()
        slope_in()

    waits = (units_in, heads_in, qu_in)
    backward_part(grad, normed, tables, *scratch[:3], kept, dqu, dy_refs, sums, waits, no_wait)
    y_in()
    qu_part(ring, info, y, dqu, sums, keep, send)


def backward(ring, info, parts, xs, gs, tables, kept, rows):
    tokens = GROUP * rows
    shapes = kept_shapes(tokens, rows)
    used = [0, 1, 2, 5]
    out = qu_shape(ring)
    return pl.pallas_call(
        functools.partial(backward_kernel, ring, len(parts)),
        out_shape=(*[shaped((rows, D), LOW)] * GROUP, out, out),
        in_specs=[smem_spec()]
        + [far_spec()] * len(parts)
        + [full_spec(a.shape) for a in xs]
        + [far_spec()] * (GROUP + 3 + len(used)),
        out_specs=(*[full_spec((rows, D))] * GROUP, full_spec(out.shape), full_spec(out.shape)),
        scratch_shapes=[pltpu.VMEM(*shapes[i]) for i in used]
        + table_scratch(tokens, rows)
        + [pltpu.VMEM((tokens, D), LOW), pltpu.VMEM((tokens, D), F32), pltpu.VMEM((tokens, MIXED), LOW)]
        + [pltpu.VMEM((1, MIXED + 3 * D), F32), pltpu.SemaphoreType.DMA((4,))]
        + weight_scratch(),
        compiler_params=kernel_params(36),
        cost_estimate=cost(4 * tokens * D * (D + 2 * FF // GROUP), 16 * 1024 * 1024),
        name="backward_shard",
    )(info, *parts, *xs, *gs, *tables, *[kept[i] for i in used])


def slot_in(ring, difference, half):
    straight, turned = ring.slot(difference, 0), ring.slot(difference, 1)
    return straight + half * (turned - straight)


def od_kernel(ring, info, far_mixed, far_active, g0, g1, g2, g3, keep, send, mixed, active, grad, sems):
    core, spot = info[0], info[2]
    pairs = [*grad_rows((g0, g1, g2, g3), grad), (far_mixed, mixed)]
    grad_in = started(pairs, sems.at[0])
    active_in = started([(far_active, active)], sems.at[1])
    grad_in()
    out_rows = SIDE // ring.size
    ff_rows = UNITS // ring.size
    for i, (out, half) in enumerate(((send, 1 - core), (keep, core))):
        columns = pl.ds(pl.multiple_of(half * (D // 2), D // 2), D // 2)
        part = grad[:, columns]
        block = dot_rows(mixed[...], part).astype(LOW)
        if i == 0:
            active_in()
        for there in range(ring.size):
            row = slot_in(ring, spot ^ there, half) * (ff_rows + out_rows)
            piece = dot_rows(active[:, there * ff_rows : (there + 1) * ff_rows], part)
            out[pl.ds(pl.multiple_of(row, out_rows), ff_rows), :] = piece.astype(LOW)
            row = pl.multiple_of(row + ff_rows, out_rows)
            out[pl.ds(row, out_rows), :] = block[there * out_rows : (there + 1) * out_rows]


def od_grads(ring, info, mixed, active, gs):
    tokens = mixed.shape[0]
    out = shaped((SIDE + UNITS, D // 2), LOW)
    return pl.pallas_call(
        functools.partial(od_kernel, ring),
        out_shape=(out, out),
        in_specs=[smem_spec()] + [far_spec()] * (2 + GROUP),
        out_specs=(full_spec(out.shape),) * 2,
        scratch_shapes=[
            pltpu.VMEM(mixed.shape, LOW),
            pltpu.VMEM(active.shape, LOW),
            pltpu.VMEM((tokens, D), LOW),
            pltpu.SemaphoreType.DMA((2,)),
        ],
        compiler_params=kernel_params(24),
        cost_estimate=cost(40 * tokens * D * (SIDE + UNITS), 5 * 1024 * 1024),
        name="out_down_grads",
    )(info, mixed, active, *gs)


def qu_shape(ring):
    return shaped((D + 16, PART), LOW)


def vector_rows(group, sums):
    row = lax.broadcasted_iota(jnp.int32, (16, PART), 0)
    tails = [sums[:, MIXED + i * D + PART : MIXED + (i + 1) * D] for i in range(3)]
    tails.append(jnp.zeros((1, PART - 3 * (D - PART)), F32))
    places = [(group, sums[:, 0:PART]), (GROUP + group, sums[:, PART:MIXED])]
    places += [(2 * GROUP + i, sums[:, MIXED + i * D : MIXED + i * D + PART]) for i in range(3)]
    places.append((2 * GROUP + 3, jnp.concatenate(tails, axis=1)))
    return sum(jnp.where(row == at, values, 0.0) for at, values in places)


def vectors_of(total):
    width = SIDE // SPREAD
    b_qkv = total[:GROUP, : 3 * SIDE].reshape(GROUP, 3 * SPREAD, width).swapaxes(0, 1).reshape(-1)
    b_up = jnp.concatenate([total[:GROUP, 3 * SIDE :], total[GROUP : 2 * GROUP]], axis=1)
    b_up = b_up.reshape(GROUP, SPREAD, UNITS // SPREAD).swapaxes(0, 1).reshape(-1)
    tails = total[2 * GROUP + 3, : 3 * (D - PART)].reshape(3, D - PART)
    bias, gain, ln_bias = jnp.concatenate([total[2 * GROUP : 2 * GROUP + 3], tails], axis=1)
    return jnp.concatenate([b_qkv, bias, b_up, bias, gain, ln_bias])


def qu_part(ring, info, y, dqu, sums, keep, send):
    core, group, spot = info[0], info[1], info[2]
    rows = D // ring.count
    tile = 256
    extra = vector_rows(group, sums).astype(LOW)
    for out, half in ((send, 1 - core), (keep, core)):
        columns = pl.ds(pl.multiple_of(half * PART, 128), PART)
        out[D : D + 16, :] = extra
        for at in range(0, D, tile):
            block = dot_rows(y[:, at : at + tile], dqu[:, columns]).astype(LOW)
            for offset in range(0, tile, rows):
                dp = (at + offset) // rows
                slot = slot_in(ring, spot ^ ring.spot_of(dp), half)
                row = (slot * GROUP + (group ^ ring.group_of(dp))) * rows
                out[pl.ds(pl.multiple_of(row, rows), rows), :] = block[offset : offset + rows]


def qu_kernel(ring, info, far_y, far_dqu, sums, keep, send, y, dqu, sems):
    started([(far_y, y), (far_dqu, dqu)], sems.at[0])()
    qu_part(ring, info, y, dqu, sums, keep, send)


def qu_grads(ring, info, y, dqu, sums):
    tokens = y.shape[0]
    out = qu_shape(ring)
    return pl.pallas_call(
        functools.partial(qu_kernel, ring),
        out_shape=(out, out),
        in_specs=[smem_spec(), far_spec(), far_spec(), full_spec(sums.shape)],
        out_specs=(full_spec(out.shape),) * 2,
        scratch_shapes=[
            pltpu.VMEM(y.shape, LOW),
            pltpu.VMEM(dqu.shape, LOW),
            pltpu.SemaphoreType.DMA((1,)),
        ],
        compiler_params=kernel_params(24),
        cost_estimate=cost(2 * tokens * D * MIXED, 7 * 1024 * 1024),
        name="qkv_up_grads",
    )(info, y, dqu, sums)


def fold_kernel(extra, held, came, kept, sent):
    half = (held.shape[0] - extra) // 2
    full = 2 * half
    kept[0:half, :] = held[0:half, :].astype(F32) + came[0:half, :].astype(F32)
    sent[0:half, :] = (held[half:full, :].astype(F32) + came[half:full, :].astype(F32)).astype(LOW)
    if extra:
        sides = held[full : full + extra, :].astype(LOW).astype(F32) + came[full : full + extra, :].astype(F32)
        kept[half : half + extra, :] = sides
        sent[half : half + extra, :] = sides.astype(LOW)


def fold(held, came, extra):
    half = (held.shape[0] - extra) // 2 + extra
    outs = (shaped((half, held.shape[1]), F32), shaped((half, held.shape[1]), LOW))
    return pl.pallas_call(
        functools.partial(fold_kernel, extra),
        out_shape=outs,
        in_specs=[full_spec(held.shape), full_spec(came.shape)],
        out_specs=tuple(full_spec(a.shape) for a in outs),
        compiler_params=kernel_params(16),
        cost_estimate=cost(0, 1024 * 1024),
        name="fold_gradients",
    )(held, came)


def close_kernel(extra, held, came, *outs):
    pieces, squares = outs[:-1], outs[-1]
    rows = pieces[0].shape[0] - extra
    lanes = jnp.zeros((8, 128), F32)
    if extra:
        full = rows * len(pieces)
        sides = held[full : full + extra, :].astype(LOW).astype(F32) + came[full : full + extra, :].astype(F32)
    for i, piece in enumerate(pieces):
        here = slice(i * rows, (i + 1) * rows)
        total = held[here, :].astype(F32) + came[here, :].astype(F32)
        piece[0:rows, :] = total.astype(LOW)
        if extra:
            piece[rows : rows + extra, :] = sides.astype(LOW)
        square = jnp.sum((total * total).reshape(rows // 8, 8, total.shape[1]), axis=0)
        for at in range(0, total.shape[1], 128):
            lanes = lanes + square[:, at : at + 128]
    squares[...] = lanes


def close(held, came, extra, count):
    rows = (held.shape[0] - extra) // count + extra
    outs = [shaped((rows, held.shape[1]), LOW)] * count + [shaped((8, 128), F32)]
    return pl.pallas_call(
        functools.partial(close_kernel, extra),
        out_shape=tuple(outs),
        in_specs=[full_spec(held.shape), full_spec(came.shape)],
        out_specs=tuple(full_spec(a.shape) for a in outs),
        compiler_params=kernel_params(16),
        cost_estimate=cost(0, 1024 * 1024),
        name="close_gradients",
    )(held, came)


def adam_update(weight, grad, first, second, factor, rate):
    clipped = grad * factor
    first_new = BETA_ONE * first + (1.0 - BETA_ONE) * clipped
    second_new = BETA_TWO * second + (1.0 - BETA_TWO) * clipped * clipped
    first_hat = first_new / (1.0 - BETA_ONE**STEP)
    second_hat = second_new / (1.0 - BETA_TWO**STEP)
    weight_new = weight - rate * (
        first_hat / (jnp.sqrt(second_hat) + ADAM_EPS) + WEIGHT_DECAY * weight
    )
    return (weight_new, first_new, second_new)


def adam_kernel(info, factor_ref, *refs):
    core, group = info[0], info[1]
    factor = factor_ref[0]
    qus, refs = (refs[:4], refs[4:8]), refs[8:]
    ods, refs = (refs[:2], refs[2:4]), refs[4:]
    (qu_came, down_came, out_came), refs = refs[:3], refs[3:]
    olds, news = refs[:12], refs[12:]
    width = SIDE // SPREAD

    def update(which, columns, grad):
        weight, first, second = [olds[3 * which + i][0, :, columns] for i in range(3)]
        fresh = adam_update(weight, grad.astype(F32), first, second, factor, LEARN_RATE)
        for i in range(3):
            news[3 * which + i][0, :, columns] = fresh[i]

    def update_qu(half, member, piece):
        if half == 0:
            for kind in range(3):
                for run in range(SPREAD):
                    at = (kind * SPREAD + run) * width
                    column = qkv_column(kind, run, member)
                    update(0, slice(column, column + width), piece(at, width))
        for local, where, at, length in up_pieces():
            if where == half:
                column = up_column(member, local)
                update(2, slice(column, column + length), piece(at, length))

    def both_halves(here):
        for half in range(2):
            columns = slice(half * (D // 2), (half + 1) * (D // 2))
            down, out = ods[here] if half == here else (down_came, out_came)
            update(1, columns, out[...])
            update(3, columns, down[...])

            for member in range(GROUP):
                if half == here:
                    for g in range(GROUP):

                        @pl.when(group == g)
                        def _(ref=qus[here][member ^ g]):
                            update_qu(half, member, lambda at, length: ref[:, at : at + length])
                else:
                    update_qu(half, member, lambda at, length: qu_came[group ^ member, :, at : at + length])

    for here in range(2):
        pl.when(core == here)(functools.partial(both_halves, here))


def adam(info, factor, qus, ods, qu_came, od_came, olds):
    rows = olds[0].shape[1]
    ff_rows = olds[9].shape[1]
    steps = max(1, rows // 16)
    few, many = rows // steps, ff_rows // steps

    def master(a):
        return pl.BlockSpec((1, a.shape[1] // steps, a.shape[2]), lambda i: (0, i, 0))

    piece_spec = pl.BlockSpec((few, PART), lambda i: (i, 0))
    came_spec = pl.BlockSpec((GROUP, few, PART), lambda i: (0, i, 0))
    down_spec = pl.BlockSpec((many, D // 2), lambda i: (i, 0))
    out_spec = pl.BlockSpec((few, D // 2), lambda i: (ff_rows // few + i, 0))
    return pl.pallas_call(
        adam_kernel,
        grid=(steps,),
        out_shape=tuple(shaped(a.shape, F32) for a in olds),
        in_specs=[smem_spec(), smem_spec()]
        + [piece_spec] * 8
        + [down_spec, out_spec] * 2
        + [came_spec, down_spec, out_spec]
        + [master(a) for a in olds],
        out_specs=tuple(master(a) for a in olds),
        compiler_params=kernel_params(32),
        name="adamw",
    )(info, factor, *qus[0], *qus[1], ods[0], ods[0], ods[1], ods[1], qu_came, od_came, od_came, *olds)


def doc_tables(lengths, rows):
    seqs = lengths.shape[0]
    ends = jnp.cumsum(lengths, axis=1)
    places = jnp.arange(rows, dtype=jnp.int32)
    past = places[None, :, None] >= ends[:, None, :]
    begins = jnp.sum(jnp.where(past, lengths[:, None, :], 0), axis=2)
    position = (places[None, :] - begins).reshape(seqs * rows, 1)
    half = ROT // 2
    inverse = 10000.0 ** (-(jnp.arange(half, dtype=F32) * 2.0) / ROT)
    lanes = jnp.concatenate([inverse, inverse, jnp.zeros(HEAD_DIM - ROT, F32)])
    angles = position.astype(F32) * jnp.concatenate([lanes, lanes])[None, :]
    allowed = (places[None, None, :] <= places[None, :, None]) & (places[None, None, :] >= begins[:, :, None])
    mask = jnp.where(allowed, 0.0, -1e30).reshape(seqs * rows, rows).astype(F32)
    return jnp.cos(angles), jnp.sin(angles), mask


def shards(
    x_in,
    cotangent,
    doc_lengths,
    w_qkv,
    w_out,
    w_up,
    w_down,
    vectors,
    m_qkv,
    m_out,
    m_up,
    m_down,
    m_vectors,
    v_qkv,
    v_out,
    v_up,
    v_down,
    v_vectors,
):
    place = Place()
    ring, core, group, spot = place.ring, place.core, place.group, place.spot
    info = place.info()
    local_rows, width = x_in.shape
    seqs, docs = doc_lengths.shape
    rows = local_rows // seqs
    in_rows = w_qkv.shape[1]
    shard = vectors.shape[1]
    members = range(1, GROUP)

    vec_block = jnp.pad(vectors[0].astype(LOW), (0, in_rows * 128 - shard)).reshape(in_rows, 128)
    keep_qu, send_qu, keep_od, send_od = pack(info, w_qkv, w_out, w_up, w_down, vec_block)
    came_qu = place.sibling(send_qu)
    came_od = place.sibling(send_od)

    def member_columns(block, *waited):
        qu = jnp.where(core == block, keep_qu, came_qu)
        sent = [after(take(qu, group ^ r), *waited) for r in members]
        return [take(qu, group)] + [place.member(a, r) for a, r in zip(sent, members)]

    def gather(block, *waited):
        late = after(block, *waited)
        return [block] + [place.member(late, r) for r in members]

    def to_owners(slots):
        return [slots[0]] + [place.member(slots[r], r) for r in members]

    def total_of(slots):
        return sum(a.astype(F32) for a in slots)

    def block_vectors(parts):
        pieces = jnp.concatenate([a[:, :, 0 : -(-shard // 128), PART:] for a in parts])
        pieces = pieces.reshape(ring.size * GROUP, -1)[:, :shard]
        dp = jnp.arange(ring.count, dtype=jnp.int32)
        difference = ring.spot_of(dp) ^ spot
        slot = jnp.where(core == 0, ring.slot(difference, 0), ring.slot(difference, 1))
        vec = jnp.take(pieces, slot * GROUP + (ring.group_of(dp) ^ group), axis=0, mode="clip")
        vec = vec.reshape(-1).astype(F32)
        b_qkv, b_out, b_up, b_down, gain, ln_bias = jnp.split(
            vec, [3 * D, 4 * D, 4 * D + FF, 5 * D + FF, 6 * D + FF]
        )
        b_qkv = take(b_qkv.reshape(3 * SPREAD, GROUP, -1), group, 1).reshape(1, -1)
        b_up = take(b_up.reshape(SPREAD, GROUP, -1), group, 1).reshape(1, -1)
        return (b_qkv, b_up, gain[None], ln_bias[None]), (b_out + b_down)[None], gain[None]

    x_own = take(x_in.reshape(2, rows, width), core)
    cot_own = take(cotangent.reshape(2, rows, width), core)
    len_own = take(doc_lengths, core)
    len_rows = jnp.zeros((16, width), LOW).at[0, :docs].set(len_own.astype(LOW))
    x_sent = jnp.concatenate([x_own, len_rows])

    qu_came = member_columns(0)
    qu_own = jnp.stack(qu_came)[None]
    x_group = gather(x_sent, qu_came[1])
    qu_next = member_columns(1, *x_group[1:])
    cot_group = gather(cot_own, *qu_next[1:])
    od_own = jnp.where(core == 0, keep_od, came_od)[None]
    od = [jnp.concatenate([od_own, place.across(od_own, 0)])]
    qu = [jnp.concatenate([qu_own, place.across(qu_own, 0)])]
    for step in range(1, ring.bits):
        od.append(place.across(jnp.concatenate(od), step))
        qu.append(place.across(jnp.concatenate(qu), step))
    qu_sibling = [place.sibling(a) for a in qu]
    parts_first = (*qu, *od, *qu_sibling, *(place.sibling(a) for a in od))
    lengths = jnp.stack([a[rows, :docs] for a in x_group]).astype(jnp.int32)
    tables = doc_tables(lengths, rows)
    vecs_first, bias_first, gain_first = block_vectors(qu)

    od_own = jnp.where(core == 1, keep_od, came_od)[None]
    xs_first = [after(x_group[0], *qu_next[1:])] + x_group[1:]
    first = forward(ring, info, parts_first, xs_first, tables, vecs_first, rows)
    qu_own = after(jnp.stack(qu_next)[None], first[0], *cot_group[1:])
    od_own = after(od_own, first[0], *cot_group[1:])
    kept_first = first[GROUP:]
    qu_late = [jnp.concatenate([qu_own, place.across(qu_own, 0)])]
    od_late = [jnp.concatenate([od_own, place.across(od_own, 0)])]
    came = to_owners(first[:GROUP])
    came[1] = after(came[1], qu_late[0], od_late[0])
    hidden_first = (x_own.astype(F32) + total_of(came) + bias_first).astype(LOW)
    late_sibling = [place.sibling(qu_late[0]), place.sibling(od_late[0])]
    hidden_group = gather(hidden_first, *late_sibling)
    for step in range(1, ring.bits):
        od_late.append(after(place.across(jnp.concatenate(od_late), step), hidden_group[1]))
        qu_late.append(after(place.across(jnp.concatenate(qu_late), step), hidden_group[1]))
    qu_sibling = [late_sibling[0]] + [place.sibling(a) for a in qu_late[1:]]
    od_sibling = [late_sibling[1]] + [place.sibling(a) for a in od_late[1:]]
    parts_second = (*qu_late, *od_late, *qu_sibling, *od_sibling)
    vecs_second, bias_second, gain_second = block_vectors(qu_late)
    second = middle(ring, info, parts_second, hidden_group, cot_group, tables, vecs_second, rows)
    y_second, mixed_second, active_second, dqu_second, sums_second = second[2 * GROUP :]

    def rows_backward(rows_low, grad_low, dy, gain):
        rows_now = rows_low.astype(F32)
        centered = rows_now - jnp.mean(rows_now, axis=-1, keepdims=True)
        variance = jnp.mean(centered * centered, axis=-1, keepdims=True)
        inverse_std = lax.rsqrt(variance + NORM_EPS)
        normed = centered * inverse_std
        scaled = dy * gain
        inner_mean = jnp.mean(scaled, axis=-1, keepdims=True)
        inner_cross = jnp.mean(scaled * normed, axis=-1, keepdims=True)
        return (grad_low.astype(F32) + inverse_std * (scaled - inner_mean - normed * inner_cross)).astype(LOW)

    extra = 16

    def ring_fold(kept, sent, steps, extra, *waited):
        for step in steps:
            kept, sent = fold(kept, after(place.across(sent, step), *waited), extra)
        return kept, sent

    def to_members(pieces):
        came = [place.member(pieces[r], r) for r in members]
        sides = [a[in_rows:].astype(F32) for a in (pieces[0], *came)]
        return [pieces[0], *came], (sides[0] + sides[1]) + (sides[2] + sides[3])

    steps = list(reversed(range(ring.bits)))

    dy_second = to_owners(second[GROUP : 2 * GROUP])
    qu_second = qu_grads(ring, info, y_second, dqu_second, sums_second)
    od_second = od_grads(ring, info, mixed_second, active_second, cot_group)
    mid_grad = rows_backward(hidden_first, cot_own, total_of(dy_second), gain_second)
    mid_group = gather(mid_grad)
    od_second = fold(od_second[0], place.sibling(od_second[1]), 0)
    qu_second = fold(qu_second[0], place.sibling(qu_second[1]), extra)

    od_first = od_grads(ring, info, kept_first[3], kept_first[4], mid_group)
    mid_late = [after(mid_group[0], *od_first, *od_second, *qu_second)] + mid_group[1:]
    back = backward(ring, info, parts_first, x_group, mid_late, tables, kept_first, rows)
    qu_keep, qu_send = back[GROUP:]
    z_came = to_owners([second[0]] + [after(a, mid_group[3]) for a in second[1:GROUP]])
    od_second = ring_fold(*od_second, steps[:-1], 0, qu_send)
    qu_second = ring_fold(*qu_second, steps[:-1], extra, qu_send)
    qu_send = after(qu_send, *od_second, *qu_second)
    *od_second, od_squares_second = close(od_second[0], place.across(od_second[1], 0), 0, 1)
    *qu_second, qu_squares_second = close(qu_second[0], place.across(qu_second[1], 0), extra, GROUP)
    held = fold(qu_keep, place.sibling(qu_send), extra)
    od_first = fold(od_first[0], place.sibling(od_first[1]), 0)
    qu_slots_second, vec_second = to_members(qu_second)
    kept, sent = ring_fold(*held, steps[:-1], extra)
    came = place.across(after(sent, *qu_slots_second[1:]), 0)
    *qu_first, qu_squares_first = close(kept, came, extra, GROUP)
    kept, sent = ring_fold(*od_first, steps[:-1], 0)
    *od_first, od_squares_first = close(kept, place.across(sent, 0), 0, 1)
    hidden_second = (hidden_first.astype(F32) + total_of(z_came) + bias_second).astype(LOW)
    start_came = to_owners(back[:GROUP])
    start_came[1] = after(start_came[1], *qu_first)
    start_grad = rows_backward(x_own, mid_grad, total_of(start_came), gain_first)

    def all_sum(block, first, last):
        hops = [place.sibling]
        hops += [functools.partial(place.across, step=step) for step in range(ring.bits)]
        hops += [functools.partial(place.member, distance=1), functools.partial(place.member, distance=2)]
        for hop in hops[first:last]:
            block = block + hop(block)
        return block

    squares = od_squares_first + qu_squares_first + od_squares_second + qu_squares_second
    qu_slots_first, vec_first = to_members(qu_first)
    squares = all_sum(squares, 0, 2)
    squares = all_sum(after(squares, *qu_slots_first[1:]), 2, None)
    squares = jnp.sum(squares)
    for vec in (vec_first, vec_second):
        bias, tail = vec[2 * GROUP], vec[2 * GROUP + 3, : D - PART]
        squares = squares + jnp.sum(vec * vec) + jnp.sum(bias * bias) + jnp.sum(tail * tail)
    grad_norm = jnp.sqrt(squares)
    factor = jnp.minimum(1.0, CLIP_LEVEL / (grad_norm + 1e-06))

    def own_block(one, two):
        came = place.sibling(jnp.where(core == 0, two, one))
        mine = jnp.where(core == 0, one, two)
        return [jnp.where(core == h, mine, came) for h in range(2)]

    od_first, od_second = after(od_first[0], *qu_first), od_second[0]
    od_came = place.sibling(jnp.where(core == 0, od_second, od_first))
    qu_sent = jnp.stack([jnp.where(core == 0, b, a)[:in_rows] for a, b in zip(qu_slots_first, qu_slots_second)])
    qu_came = place.sibling(qu_sent)
    vec = after(jnp.where(core == 0, vec_first, vec_second), qu_sent)
    vec_share = take(vectors_of(vec).reshape(ring.count, shard), lax.axis_index("dp"))[None]
    olds = (w_qkv, m_qkv, v_qkv, w_out, m_out, v_out, w_up, m_up, v_up, w_down, m_down, v_down)
    qus = (qu_slots_first, qu_slots_second)
    news = adam(info, factor[None], qus, (od_first, od_second), qu_came, od_came, olds)
    new_vec = adam_update(vectors, vec_share, m_vectors, v_vectors, factor, VECTOR_RATE)

    outputs = own_block(jnp.stack([hidden_first, start_grad]), jnp.stack([hidden_second, mid_grad]))
    outputs = jnp.concatenate(outputs, axis=1)
    hidden_out, input_grads = outputs[:1], outputs[1:]
    return (
        hidden_out,
        input_grads,
        *(news[3 * i] for i in range(4)),
        new_vec[0],
        *(news[3 * i + 1] for i in range(4)),
        new_vec[1],
        *(news[3 * i + 2] for i in range(4)),
        new_vec[2],
        grad_norm,
    )


def solution(mesh):
    return jax.shard_map(
        shards,
        mesh=mesh,
        in_specs=(
            P("dp", None),
            P("dp", None),
            P("dp", None),
            P("section", "dp", None),
            P("section", "dp", None),
            P("section", "dp", None),
            P("section", "dp", None),
            P("section", "dp"),
            P("section", "dp", None),
            P("section", "dp", None),
            P("section", "dp", None),
            P("section", "dp", None),
            P("section", "dp"),
            P("section", "dp", None),
            P("section", "dp", None),
            P("section", "dp", None),
            P("section", "dp", None),
            P("section", "dp"),
        ),
        out_specs=(
            P("section", "dp", None),
            P("section", "dp", None),
            P("section", "dp", None),
            P("section", "dp", None),
            P("section", "dp", None),
            P("section", "dp", None),
            P("section", "dp"),
            P("section", "dp", None),
            P("section", "dp", None),
            P("section", "dp", None),
            P("section", "dp", None),
            P("section", "dp"),
            P("section", "dp", None),
            P("section", "dp", None),
            P("section", "dp", None),
            P("section", "dp", None),
            P("section", "dp"),
            P(),
        ),
        check_vma=False,
    )
```

```python
import functools

import jax
import jax.numpy as jnp
from jax import lax
from jax.experimental import pallas as pl
from jax.experimental.pallas import tpu as pltpu
from jax.sharding import PartitionSpec as P

D = 1024
FF = 4096
HEADS = 16
HEAD_DIM = 64
ROT = 16
STEP = 10


NORM_EPS = 1e-05
BETA_ONE = 0.9
BETA_TWO = 0.95
LEARN_RATE = 0.05
VECTOR_RATE = 0.3
WEIGHT_DECAY = 0.01
CLIP_LEVEL = 1.0
ADAM_EPS = 1e-08

AXES = ("section", "dp")
GROUP = 4
SPREAD = 1
LOW = jnp.bfloat16
F32 = jnp.float32
SIDE = D // GROUP
UNITS = FF // GROUP
MIXED = 3 * SIDE + UNITS
PART = MIXED // 2
WIRE = PART + 128


class Ring:
    def __init__(self, count):
        self.count = count
        self.low = count // (GROUP * SPREAD)
        self.size = SPREAD * self.low
        self.bits = self.size.bit_length() - 1

    def index(self, g, t):
        return ((t // self.low) * GROUP + g) * self.low + t % self.low

    def group_of(self, dp):
        return (dp // self.low) % GROUP

    def spot_of(self, dp):
        return (dp // (GROUP * self.low)) * self.low + dp % self.low

    def order(self, core):
        steps = list(range(self.bits))
        if SPREAD > 1 or core == 1:
            steps.reverse()
        return steps

    def turn(self, slot, core):
        return sum(((slot >> s) & 1) << b for s, b in enumerate(self.order(core)))

    def slot(self, difference, core):
        return sum(((difference >> b) & 1) << s for s, b in enumerate(self.order(core)))


class Place:
    def __init__(self):
        self.ring = Ring(lax.axis_size("dp"))
        self.core = lax.axis_index("section")
        dp = lax.axis_index("dp")
        self.group = self.ring.group_of(dp)
        self.spot = self.ring.spot_of(dp)

    def info(self):
        return jnp.stack([self.core, self.group, self.spot]).astype(jnp.int32)

    def move(self, block, where):
        ring = self.ring
        route = []
        for core in range(2):
            for g in range(GROUP):
                for t in range(ring.size):
                    c, h, u = where(core, g, t)
                    route.append((core * ring.count + ring.index(g, t), c * ring.count + ring.index(h, u)))
        return lax.ppermute(block, AXES, route)

    def groups(self):
        ring = self.ring
        return [[ring.index(g, t) for g in range(GROUP)] for t in range(ring.size)]

    def group_gather(self, block):
        return lax.all_gather(block, "dp", axis=0, axis_index_groups=self.groups(), tiled=False)

    def group_sum(self, blocks):
        return lax.psum_scatter(
            blocks, "dp", scatter_dimension=0, axis_index_groups=self.groups(), tiled=False
        )

    def sibling(self, block):
        return self.move(block, lambda c, g, t: (1 - c, g, t))

    def member(self, block, distance):
        return self.move(block, lambda c, g, t: (c, g ^ distance, t))

    def across(self, block, step):
        return self.move(block, lambda c, g, t: (c, g, t ^ (1 << self.ring.order(c)[step])))


def take(block, index, axis=0):
    return lax.dynamic_index_in_dim(block, index, axis, keepdims=False)


def after(block, *waited):
    return lax.optimization_barrier((block, waited))[0]


def dot(left, right):
    return jnp.dot(left, right, preferred_element_type=F32)


def dot_cols(left, right):
    return lax.dot_general(left, right, (((1,), (1,)), ((), ())), preferred_element_type=F32)


def dot_rows(left, right):
    return lax.dot_general(left, right, (((0,), (0,)), ((), ())), preferred_element_type=F32)


def full_spec(shape):
    return pl.BlockSpec(shape, lambda *_: (0,) * len(shape))


def far_spec():
    return pl.BlockSpec(memory_space=pltpu.HBM)


def far(block):
    return pltpu.with_memory_space_constraint(block, pltpu.HBM)


def any_spec():
    return pl.BlockSpec(memory_space=pl.ANY)


def smem_spec():
    return pl.BlockSpec(memory_space=pltpu.SMEM)


def shaped(shape, dtype):
    return jax.ShapeDtypeStruct(shape, dtype)


def kernel_params(mebibytes):
    return pltpu.CompilerParams(vmem_limit_bytes=mebibytes * 1024 * 1024)


def up_pieces():
    run = UNITS // SPREAD
    cuts = sorted({0, PART - 3 * SIDE, UNITS} | {run * i for i in range(SPREAD)})
    pieces = []
    for begin, end in zip(cuts[:-1], cuts[1:]):
        column = 3 * SIDE + begin
        pieces.append((begin, column // PART, column % PART, end - begin))
    return pieces


def up_column(g, local):
    run = UNITS // SPREAD
    return (local // run * GROUP + g) * run + local % run


def qkv_column(kind, run, g):
    width = SIDE // SPREAD
    return ((kind * SPREAD + run) * GROUP + g) * width


def pack_kernel(info, qkv_hbm, out_hbm, up_hbm, down_hbm, vec, keep_qu, send_qu, keep_od, send_od, *scratch):
    w_qkv, w_out, w_up, w_down, sems = scratch
    pairs = ((qkv_hbm, w_qkv), (up_hbm, w_up), (down_hbm, w_down), (out_hbm, w_out))
    copies = [pltpu.make_async_copy(far.at[0], near, sems.at[i]) for i, (far, near) in enumerate(pairs)]
    for copy in copies:
        copy.start()
    rows = w_qkv.shape[0]
    ff_rows = w_down.shape[0]
    width = SIDE // SPREAD
    core = info[0]

    def write_qu(halves):
        for g in range(GROUP):
            for kind in range(3):
                for run in range(SPREAD):
                    at = (kind * SPREAD + run) * width
                    column = qkv_column(kind, run, g)
                    halves[0][g, :, at : at + width] = w_qkv[:, column : column + width].astype(LOW)
            for local, half, at, length in up_pieces():
                column = up_column(g, local)
                halves[half][g, :, at : at + length] = w_up[:, column : column + length].astype(LOW)
            for half in range(2):
                halves[half][g, :, PART:WIRE] = vec[...]

    def write_od(halves):
        for half in range(2):
            columns = slice(half * (D // 2), (half + 1) * (D // 2))
            halves[half][0:ff_rows] = w_down[:, columns].astype(LOW)
            halves[half][ff_rows : ff_rows + rows] = w_out[:, columns].astype(LOW)

    for first, last, write, kept, sent in ((0, 2, write_qu, keep_qu, send_qu), (2, 4, write_od, keep_od, send_od)):
        for copy in copies[first:last]:
            copy.wait()
        pl.when(core == 0)(functools.partial(write, (kept, sent)))
        pl.when(core == 1)(functools.partial(write, (sent, kept)))


def pack(info, w_qkv, w_out, w_up, w_down, vec):
    rows, ff_rows = w_qkv.shape[1], w_down.shape[1]
    qu = shaped((GROUP, rows, WIRE), LOW)
    od = shaped((ff_rows + rows, D // 2), LOW)
    return pl.pallas_call(
        pack_kernel,
        out_shape=(qu, qu, od, od),
        in_specs=[smem_spec()] + [far_spec()] * 4 + [full_spec(vec.shape)],
        out_specs=tuple(full_spec(a.shape) for a in (qu, qu, od, od)),
        scratch_shapes=[pltpu.VMEM(a.shape[1:], F32) for a in (w_qkv, w_out, w_up, w_down)]
        + [pltpu.SemaphoreType.DMA((4,))],
        compiler_params=kernel_params(24),
        name="pack_weights",
    )(info, far(w_qkv), far(w_out), far(w_up), far(w_down), vec)


def weight_copies(ring, info, parts, wqu, wout, wdown, sems):
    core, group, spot = info[0], info[1], info[2]
    qu_copies, od_copies = [], []
    count = len(parts) // 4
    for which in range(2):
        half = core if which == 0 else 1 - core
        qu_at = pl.multiple_of(half * PART, 128)
        od_at = pl.multiple_of(half * (D // 2), 128)
        slot = 0
        for piece in range(count):
            qu, od = parts[2 * count * which + piece], parts[2 * count * which + count + piece]
            rows = qu.shape[2]
            ff_rows = od.shape[1] - rows
            for i in range(qu.shape[0]):
                straight, turned = ring.turn(slot, 0), ring.turn(slot, 1)
                there = spot ^ (straight + half * (turned - straight))
                slot += 1
                ff_row = pl.multiple_of(there * ff_rows, ff_rows)
                out_row = pl.multiple_of(there * rows, rows)
                far = wdown.at[pl.ds(ff_row, ff_rows), pl.ds(od_at, D // 2)]
                od_copies.append(pltpu.make_async_copy(od.at[i, pl.ds(0, ff_rows)], far, sems.at[0]))
                far = wout.at[pl.ds(out_row, rows), pl.ds(od_at, D // 2)]
                od_copies.append(pltpu.make_async_copy(od.at[i, pl.ds(ff_rows, rows)], far, sems.at[0]))
                for r in range(GROUP):
                    row = pl.multiple_of(ring.index(group ^ r, there) * rows, rows)
                    far = wqu.at[pl.ds(row, rows), pl.ds(qu_at, PART)]
                    qu_copies.append(pltpu.make_async_copy(qu.at[i, r, :, pl.ds(0, PART)], far, sems.at[1]))
    return qu_copies, od_copies


def head_masks(dtype):
    lane = lax.broadcasted_iota(jnp.int32, (1, SIDE), 1) // HEAD_DIM
    return [(lane == h).astype(dtype) for h in range(SIDE // HEAD_DIM)]


def by_head(parts):
    lane = lax.broadcasted_iota(jnp.int32, (1, SIDE), 1) // HEAD_DIM
    total = parts[-1]
    for h in range(len(parts) - 2, -1, -1):
        total = jnp.where(lane == h, parts[h], total)
    return total


def turning(cosine, sine, back):
    lane = lax.broadcasted_iota(jnp.int32, sine.shape, 1) % HEAD_DIM
    first = jnp.where(lane < ROT // 2, sine, 0.0)
    second = jnp.where(lane < ROT // 2, 0.0, sine)
    if back:
        second = -second
    else:
        first = -first
    wide = SIDE // cosine.shape[1]
    return [jnp.concatenate([a] * wide, axis=1) for a in (cosine, first, second)]


def turn(part, tables):
    cosine, first, second = tables
    ahead = pltpu.roll(part, SIDE - ROT // 2, 1)
    behind = pltpu.roll(part, ROT // 2, 1)
    return part * cosine + ahead * first + behind * second


def normalise(rows):
    centered = rows - jnp.mean(rows, axis=-1, keepdims=True)
    variance = jnp.mean(centered * centered, axis=-1, keepdims=True)
    return centered * lax.rsqrt(variance + NORM_EPS)


def no_wait():
    pass


def forward_part(x_refs, tables, vecs, wqu, wout, wdown, kept, z_refs, waits, done, normed_ref=None):
    cosine, sine, mask = tables
    b_qkv, b_up, gain, ln_bias = vecs
    y, qkv, probs, mixed, active, slope = kept
    rows = z_refs[0].shape[0]
    for r in range(GROUP):
        normed = normalise(x_refs[r][0:rows, :].astype(F32))
        if normed_ref is not None:
            normed_ref[r * rows : (r + 1) * rows, :] = normed
        y[r * rows : (r + 1) * rows, :] = (normed * gain[...] + ln_bias[...]).astype(LOW)
    done(0)
    waits[0]()
    waits[2]()
    forth = turning(cosine[...], sine[...], False)
    for kind in range(3):
        columns = slice(kind * SIDE, (kind + 1) * SIDE)
        part = dot(y[...], wqu[:, columns]) + b_qkv[:, columns]
        if kind < 2:
            part = turn(part, forth)
        qkv[:, columns] = part.astype(LOW)
    done(1)
    masks = head_masks(LOW)
    heads = len(masks)
    for r in range(GROUP):
        here = slice(r * rows, (r + 1) * rows)
        query, keys, values = [qkv[here, k * SIDE : (k + 1) * SIDE] for k in range(3)]
        stacked = jnp.concatenate([query * m for m in masks], axis=0)
        scores = dot_cols(stacked, keys) * HEAD_DIM ** (-0.5)
        scores = scores.reshape(heads, rows, rows) + mask[here, :][None]
        expo = jnp.exp(scores - jnp.max(scores, axis=-1, keepdims=True))
        prob = expo / jnp.sum(expo, axis=-1, keepdims=True)
        prob = prob.reshape(heads * rows, rows)
        probs[r * heads * rows : (r + 1) * heads * rows, :] = prob
        full = dot(prob.astype(LOW), values)
        mixed[here, :] = by_head([full[h * rows : (h + 1) * rows] for h in range(heads)]).astype(LOW)
    done(2)
    done(3)
    tile = 256
    for at in range(0, UNITS, tile):
        hidden = dot(y[...], wqu[:, 3 * SIDE + at : 3 * SIDE + at + tile]) + b_up[:, at : at + tile]
        share = 0.5 * (1.0 + lax.erf(hidden * (0.5**0.5)))
        density = jnp.exp(-0.5 * hidden * hidden) * (0.5 / jnp.pi) ** 0.5
        active[:, at : at + tile] = (hidden * share).astype(LOW)
        slope[:, at : at + tile] = share + hidden * density
    done(4)
    done(5)
    waits[1]()
    for at in range(0, D, tile):
        branch = dot(mixed[...], wout[:, at : at + tile]) + dot(active[...], wdown[:, at : at + tile])
        for r in range(GROUP):
            z_refs[r][:, at : at + tile] = branch[r * rows : (r + 1) * rows].astype(LOW)


def backward_part(grad, normed, tables, wqu, wout, wdown, kept, dqu, dy_refs, sums, waits, done):
    cosine, sine, _ = tables
    y, qkv, probs, mixed, active, slope = kept
    rows = grad.shape[0] // GROUP
    tile = 256
    waits[0]()
    dmixed = dot_cols(grad[...], wout[...]).astype(LOW)
    for at in range(0, UNITS, tile):
        dactive = dot_cols(grad[...], wdown[at : at + tile, :])
        dhidden = (dactive * slope[:, at : at + tile]).astype(LOW)
        dqu[:, 3 * SIDE + at : 3 * SIDE + at + tile] = dhidden
    waits[1]()
    masks = head_masks(LOW)
    heads = len(masks)
    back = turning(cosine[...], sine[...], True)
    for r in range(GROUP):
        here = slice(r * rows, (r + 1) * rows)
        query, keys, values = [qkv[here, k * SIDE : (k + 1) * SIDE] for k in range(3)]
        dstack = jnp.concatenate([dmixed[here] * m for m in masks], axis=0)
        dprob = dot_cols(dstack, values)
        prob = probs[r * heads * rows : (r + 1) * heads * rows, :]
        dvalues = dot_rows(prob.astype(LOW), dstack)
        dscore = (prob * (dprob - jnp.sum(prob * dprob, axis=-1, keepdims=True))).astype(LOW)
        full = dot(dscore, keys)
        dquery = by_head([full[h * rows : (h + 1) * rows] for h in range(heads)])
        dkeys = dot_rows(dscore, jnp.concatenate([query * m for m in masks], axis=0))
        scale = HEAD_DIM ** (-0.5)
        slot_tables = [a[here] for a in back]
        dqu[here, 0:SIDE] = turn(dquery * scale, slot_tables).astype(LOW)
        dqu[here, SIDE : 2 * SIDE] = turn(dkeys * scale, slot_tables).astype(LOW)
        dqu[here, 2 * SIDE : 3 * SIDE] = dvalues.astype(LOW)
    done()
    for at in range(0, MIXED, tile):
        sums[:, at : at + tile] = jnp.sum(dqu[:, at : at + tile].astype(F32), axis=0, keepdims=True)
    waits[2]()
    for at in range(0, D, tile):
        dy = dot_cols(dqu[...], wqu[at : at + tile, :])
        for r in range(GROUP):
            dy_refs[r][:, at : at + tile] = dy[r * rows : (r + 1) * rows].astype(LOW)
        own = grad[0:rows, at : at + tile].astype(F32)
        for i, terms in enumerate((own, dy * normed[:, at : at + tile], dy)):
            begin = MIXED + i * D + at
            sums[:, begin : begin + tile] = jnp.sum(terms, axis=0, keepdims=True)


def kept_shapes(tokens, rows):
    return [
        ((tokens, D), LOW),
        ((tokens, 3 * SIDE), LOW),
        ((tokens * (SIDE // HEAD_DIM), rows), F32),
        ((tokens, SIDE), LOW),
        ((tokens, UNITS), LOW),
        ((tokens, UNITS), F32),
    ]


def weight_scratch():
    return [
        pltpu.VMEM((D, MIXED), LOW),
        pltpu.VMEM((SIDE, D), LOW),
        pltpu.VMEM((UNITS, D), LOW),
        pltpu.SemaphoreType.DMA((2,)),
    ]


def waiter(copies):
    def wait():
        for copy in copies:
            copy.wait()

    return wait


def started(pairs, sem):
    copies = [pltpu.make_async_copy(source, target, sem) for source, target in pairs]
    for copy in copies:
        copy.start()
    return waiter(copies)


def table_scratch(tokens, rows):
    return [pltpu.VMEM((tokens, 128), F32), pltpu.VMEM((tokens, 128), F32), pltpu.VMEM((tokens, rows), F32)]


def cost(flops, moved):
    return pl.CostEstimate(flops=2 * flops, bytes_accessed=2 * moved, transcendentals=0)


def leaving(pairs, sems):
    copies = [pltpu.make_async_copy(near, far, sems.at[i]) for i, (near, far) in enumerate(pairs)]

    def go(i):
        copies[i].start()

    return go, waiter(copies)


def forward_kernel(ring, count, info, *refs):
    parts, refs = refs[:count], refs[count:]
    x_refs, refs = refs[:4], refs[4:]
    tables, refs = refs[:3], refs[3:]
    vecs, refs = refs[:4], refs[4:]
    z_refs, refs = refs[:4], refs[4:]
    far_kept, far_weights, far_tables, refs = refs[:7], refs[7:10], refs[10:13], refs[13:]
    kept, refs = refs[:7], refs[7:]
    out_sems, scratch = refs[0], refs[1:]
    weights = scratch[:3]
    qu_copies, od_copies = weight_copies(ring, info, parts, *scratch)
    for copy in qu_copies + od_copies:
        copy.start()
    pairs = [*zip(kept, far_kept), *zip(weights, far_weights), *zip(tables, far_tables)]
    go, out = leaving(pairs, out_sems)
    for i in range(10, 13):
        go(i)

    def qu_in():
        waiter(qu_copies)()
        go(7)

    def od_in():
        waiter(od_copies)()
        go(8)
        go(9)

    def done(i):
        go(i)
        if i == 0:
            go(6)

    forward_part(x_refs, tables, vecs, *weights, kept[:6], z_refs, (qu_in, od_in, no_wait), done, kept[6])
    out()


def forward(ring, info, parts, xs, tables, vecs, rows):
    tokens = GROUP * rows
    shapes = kept_shapes(tokens, rows) + [((tokens, D), F32)]
    away = [*shapes, ((D, MIXED), LOW), ((SIDE, D), LOW), ((UNITS, D), LOW)] + [(a.shape, F32) for a in tables]
    blocks = (*xs, *tables, *vecs)
    return pl.pallas_call(
        functools.partial(forward_kernel, ring, len(parts)),
        out_shape=(*[shaped((rows, D), LOW)] * GROUP, *[pltpu.HBM(*a) for a in away]),
        in_specs=[smem_spec()] + [any_spec()] * len(parts) + [full_spec(a.shape) for a in blocks],
        out_specs=tuple([full_spec((rows, D))] * GROUP + [far_spec()] * len(away)),
        scratch_shapes=[pltpu.VMEM(*a) for a in shapes]
        + [pltpu.SemaphoreType.DMA((len(away),))]
        + weight_scratch(),
        compiler_params=kernel_params(28),
        cost_estimate=cost(2 * tokens * D * (D + 2 * FF // GROUP), 16 * 1024 * 1024),
        name="forward_shard",
    )(info, *parts, *blocks)


def middle_kernel(ring, count, info, *refs):
    group = info[1]
    parts, refs = refs[:count], refs[count:]
    x_refs, refs = refs[:4], refs[4:]
    far_grads, refs = refs[0], refs[1:]
    far_tables, refs = refs[:3], refs[3:]
    vecs, refs = refs[:4], refs[4:]
    dy_refs, refs = refs[:4], refs[4:]
    sums, away, far_z, refs = refs[0], refs[1:6], refs[6], refs[7:]
    kept, refs = refs[:6], refs[6:]
    z_refs, tables, refs = refs[:4], refs[4:7], refs[7:]
    (grad, normed, dqu, in_sems, out_sems), scratch = refs[:5], refs[5:]
    rows = z_refs[0].shape[0]
    qu_copies, od_copies = weight_copies(ring, info, parts, *scratch)
    for copy in qu_copies:
        copy.start()
    tables_in = started(zip(far_tables, tables), in_sems.at[0])
    for copy in od_copies:
        copy.start()
    pairs = [(far_grads.at[group ^ r], grad.at[pl.ds(r * rows, rows)]) for r in range(GROUP)]
    grad_in = started(pairs, in_sems.at[1])
    pairs = list(zip([kept[0], kept[3], kept[4], dqu, grad], away))
    pairs += [(z_refs[r], far_z.at[group ^ r]) for r in range(GROUP)]
    go, out = leaving(pairs, out_sems)

    def done(i):
        if i in (0, 3, 4):
            go((0, 3, 4).index(i))

    waits = (waiter(qu_copies), waiter(od_copies), tables_in)
    forward_part(x_refs, tables, vecs, *scratch[:3], kept, z_refs, waits, done, normed)
    grad_in()
    for i in range(4, 9):
        go(i)
    waits = (no_wait, no_wait, no_wait)
    done = functools.partial(go, 3)
    backward_part(grad, normed, tables, *scratch[:3], kept, dqu, dy_refs, sums, waits, done)
    out()


def middle(ring, info, parts, xs, grads, tables, vecs, rows):
    tokens = GROUP * rows
    shapes = kept_shapes(tokens, rows)
    away = [shapes[0], shapes[3], shapes[4], ((tokens, MIXED), LOW), ((tokens, D), LOW), ((GROUP, rows, D), LOW)]
    sums = shaped((1, MIXED + 3 * D), F32)
    return pl.pallas_call(
        functools.partial(middle_kernel, ring, len(parts)),
        out_shape=(*[shaped((rows, D), LOW)] * GROUP, sums, *[pltpu.HBM(*a) for a in away]),
        in_specs=[smem_spec()]
        + [any_spec()] * len(parts)
        + [full_spec(a.shape) for a in xs]
        + [far_spec()] * 4
        + [full_spec(a.shape) for a in vecs],
        out_specs=tuple([full_spec((rows, D))] * GROUP + [full_spec(sums.shape)] + [far_spec()] * len(away)),
        scratch_shapes=[pltpu.VMEM(*a) for a in shapes]
        + [pltpu.VMEM((rows, D), LOW)] * GROUP
        + table_scratch(tokens, rows)
        + [pltpu.VMEM((tokens, D), LOW), pltpu.VMEM((tokens, D), F32), pltpu.VMEM((tokens, MIXED), LOW)]
        + [pltpu.SemaphoreType.DMA((2,)), pltpu.SemaphoreType.DMA((9,))]
        + weight_scratch(),
        compiler_params=kernel_params(32),
        cost_estimate=cost(4 * tokens * D * (D + 2 * FF // GROUP), 16 * 1024 * 1024),
        name="forward_backward_shard",
    )(info, *parts, *xs, far(grads), *[far(a) for a in tables], *vecs)


def backward_kernel(ring, info, *refs):
    group = info[1]
    g_refs, refs = refs[:4], refs[4:]
    far_kept, far_weights, far_tables, refs = refs[:7], refs[7:10], refs[10:13], refs[13:]
    dy_refs, refs = [refs[0].at[group ^ r] for r in range(GROUP)], refs[1:]
    (od_keep, od_send, keep, send), refs = refs[:4], refs[4:]
    kept, refs = refs[:7], refs[7:]
    weights, tables, refs = refs[:3], refs[3:6], refs[6:]
    grad, dqu, sums, in_sems = refs
    y, qkv, probs, mixed, active, slope, normed = kept
    wqu, wout, wdown = weights
    far_y, far_qkv, far_probs, far_mixed, far_active, far_slope, far_normed = far_kept
    mixed_in = started([(far_mixed, mixed)], in_sems.at[0])
    active_in = started([(far_active, active)], in_sems.at[1])
    units_in = started([*zip(far_weights[1:], weights[1:]), (far_slope, slope)], in_sems.at[2])
    heads_in = started([(far_qkv, qkv), (far_probs, probs), *zip(far_tables, tables)], in_sems.at[3])
    dy_in = started([(far_weights[0], wqu), (far_normed, normed)], in_sems.at[4])
    y_in = started([(far_y, y)], in_sems.at[5])
    rows = g_refs[0].shape[0]
    for r in range(GROUP):
        grad[r * rows : (r + 1) * rows, :] = g_refs[r][...]
    mixed_in()
    od_part(ring, info, mixed, active, grad, od_keep, od_send, active_in)
    waits = (units_in, heads_in, dy_in)
    backward_part(grad, normed, tables, *weights, kept[:6], dqu, dy_refs, sums, waits, no_wait)
    y_in()
    qu_part(ring, info, y, dqu, sums, keep, send)


def backward(ring, info, gs, held, rows):
    tokens = GROUP * rows
    qu, od = qu_shape(ring), od_shape()
    outs = [shaped((GROUP, rows, D), LOW), od, od, qu, qu]
    return pl.pallas_call(
        functools.partial(backward_kernel, ring),
        out_shape=tuple(outs),
        in_specs=[smem_spec()] + [full_spec(a.shape) for a in gs] + [far_spec()] * len(held),
        out_specs=tuple(full_spec(a.shape) for a in outs),
        scratch_shapes=[pltpu.VMEM(a.shape, a.dtype) for a in held]
        + [pltpu.VMEM((tokens, D), LOW), pltpu.VMEM((tokens, MIXED), LOW)]
        + [pltpu.VMEM((1, MIXED + 3 * D), F32), pltpu.SemaphoreType.DMA((6,))],
        compiler_params=kernel_params(36),
        cost_estimate=cost(4 * tokens * D * (D + 2 * FF // GROUP), 16 * 1024 * 1024),
        name="backward_shard",
    )(info, *gs, *[far(a) for a in held])


def slot_in(ring, difference, half):
    straight, turned = ring.slot(difference, 0), ring.slot(difference, 1)
    return straight + half * (turned - straight)


def od_shape():
    return shaped((SIDE + UNITS, D // 2), LOW)


def od_part(ring, info, mixed, active, grad, keep, send, active_in):
    core, spot = info[0], info[2]
    out_rows = SIDE // ring.size
    ff_rows = UNITS // ring.size
    for i, (out, half) in enumerate(((send, 1 - core), (keep, core))):
        columns = pl.ds(pl.multiple_of(half * (D // 2), D // 2), D // 2)
        part = grad[:, columns]
        block = dot_rows(mixed[...], part).astype(LOW)
        if i == 0:
            active_in()
        for there in range(ring.size):
            row = slot_in(ring, spot ^ there, half) * (ff_rows + out_rows)
            piece = dot_rows(active[:, there * ff_rows : (there + 1) * ff_rows], part)
            out[pl.ds(pl.multiple_of(row, out_rows), ff_rows), :] = piece.astype(LOW)
            row = pl.multiple_of(row + ff_rows, out_rows)
            out[pl.ds(row, out_rows), :] = block[there * out_rows : (there + 1) * out_rows]


def od_kernel(ring, info, far_mixed, far_active, far_grad, keep, send, mixed, active, grad, sems):
    grad_in = started([(far_grad, grad), (far_mixed, mixed)], sems.at[0])
    active_in = started([(far_active, active)], sems.at[1])
    grad_in()
    od_part(ring, info, mixed, active, grad, keep, send, active_in)


def od_grads(ring, info, mixed, active, grad):
    tokens = mixed.shape[0]
    blocks = (mixed, active, grad)
    return pl.pallas_call(
        functools.partial(od_kernel, ring),
        out_shape=(od_shape(),) * 2,
        in_specs=[smem_spec()] + [far_spec()] * 3,
        out_specs=(full_spec(od_shape().shape),) * 2,
        scratch_shapes=[pltpu.VMEM(a.shape, LOW) for a in blocks] + [pltpu.SemaphoreType.DMA((2,))],
        compiler_params=kernel_params(16),
        cost_estimate=cost(40 * tokens * D * (SIDE + UNITS), 5 * 1024 * 1024),
        name="out_down_grads",
    )(info, *[far(a) for a in blocks])


def qu_shape(ring):
    return shaped((D + 16, PART), LOW)


def vector_rows(group, sums):
    row = lax.broadcasted_iota(jnp.int32, (16, PART), 0)
    tails = [sums[:, MIXED + i * D + PART : MIXED + (i + 1) * D] for i in range(3)]
    tails.append(jnp.zeros((1, PART - 3 * (D - PART)), F32))
    places = [(group, sums[:, 0:PART]), (GROUP + group, sums[:, PART:MIXED])]
    places += [(2 * GROUP + i, sums[:, MIXED + i * D : MIXED + i * D + PART]) for i in range(3)]
    places.append((2 * GROUP + 3, jnp.concatenate(tails, axis=1)))
    return sum(jnp.where(row == at, values, 0.0) for at, values in places)


def vectors_of(total):
    width = SIDE // SPREAD
    b_qkv = total[:GROUP, : 3 * SIDE].reshape(GROUP, 3 * SPREAD, width).swapaxes(0, 1).reshape(-1)
    b_up = jnp.concatenate([total[:GROUP, 3 * SIDE :], total[GROUP : 2 * GROUP]], axis=1)
    b_up = b_up.reshape(GROUP, SPREAD, UNITS // SPREAD).swapaxes(0, 1).reshape(-1)
    tails = total[2 * GROUP + 3, : 3 * (D - PART)].reshape(3, D - PART)
    bias, gain, ln_bias = jnp.concatenate([total[2 * GROUP : 2 * GROUP + 3], tails], axis=1)
    return jnp.concatenate([b_qkv, bias, b_up, bias, gain, ln_bias])


def qu_part(ring, info, y, dqu, sums, keep, send):
    core, group, spot = info[0], info[1], info[2]
    rows = D // ring.count
    tile = 256
    extra = vector_rows(group, sums).astype(LOW)
    for out, half in ((send, 1 - core), (keep, core)):
        columns = pl.ds(pl.multiple_of(half * PART, 128), PART)
        out[D : D + 16, :] = extra
        for at in range(0, D, tile):
            block = dot_rows(y[:, at : at + tile], dqu[:, columns]).astype(LOW)
            for offset in range(0, tile, rows):
                dp = (at + offset) // rows
                slot = slot_in(ring, spot ^ ring.spot_of(dp), half)
                row = (slot * GROUP + (group ^ ring.group_of(dp))) * rows
                out[pl.ds(pl.multiple_of(row, rows), rows), :] = block[offset : offset + rows]


def qu_kernel(ring, info, far_y, far_dqu, sums, keep, send, y, dqu, sems):
    started([(far_y, y), (far_dqu, dqu)], sems.at[0])()
    qu_part(ring, info, y, dqu, sums, keep, send)


def qu_grads(ring, info, y, dqu, sums):
    tokens = y.shape[0]
    out = qu_shape(ring)
    return pl.pallas_call(
        functools.partial(qu_kernel, ring),
        out_shape=(out, out),
        in_specs=[smem_spec(), far_spec(), far_spec(), full_spec(sums.shape)],
        out_specs=(full_spec(out.shape),) * 2,
        scratch_shapes=[
            pltpu.VMEM(y.shape, LOW),
            pltpu.VMEM(dqu.shape, LOW),
            pltpu.SemaphoreType.DMA((1,)),
        ],
        compiler_params=kernel_params(20),
        cost_estimate=cost(2 * tokens * D * MIXED, 7 * 1024 * 1024),
        name="qkv_up_grads",
    )(info, far(y), far(dqu), sums)


def fold_kernel(extra, held, came, kept, sent):
    half = (held.shape[0] - extra) // 2
    full = 2 * half
    kept[0:half, :] = held[0:half, :].astype(F32) + came[0:half, :].astype(F32)
    sent[0:half, :] = (held[half:full, :].astype(F32) + came[half:full, :].astype(F32)).astype(LOW)
    if extra:
        sides = held[full : full + extra, :].astype(LOW).astype(F32) + came[full : full + extra, :].astype(F32)
        kept[half : half + extra, :] = sides
        sent[half : half + extra, :] = sides.astype(LOW)


def fold(held, came, extra):
    half = (held.shape[0] - extra) // 2 + extra
    outs = (shaped((half, held.shape[1]), F32), shaped((half, held.shape[1]), LOW))
    return pl.pallas_call(
        functools.partial(fold_kernel, extra),
        out_shape=outs,
        in_specs=[full_spec(held.shape), full_spec(came.shape)],
        out_specs=tuple(full_spec(a.shape) for a in outs),
        compiler_params=kernel_params(16),
        cost_estimate=cost(0, 1024 * 1024),
        name="fold_gradients",
    )(held, came)


def close_kernel(extra, held, came, *outs):
    pieces, squares = outs[:-1], outs[-1]
    rows = pieces[0].shape[0] - extra
    lanes = jnp.zeros((8, 128), F32)
    if extra:
        full = rows * len(pieces)
        sides = held[full : full + extra, :].astype(LOW).astype(F32) + came[full : full + extra, :].astype(F32)
    for i, piece in enumerate(pieces):
        here = slice(i * rows, (i + 1) * rows)
        total = held[here, :].astype(F32) + came[here, :].astype(F32)
        piece[0:rows, :] = total.astype(LOW)
        if extra:
            piece[rows : rows + extra, :] = sides.astype(LOW)
        square = jnp.sum((total * total).reshape(rows // 8, 8, total.shape[1]), axis=0)
        for at in range(0, total.shape[1], 128):
            lanes = lanes + square[:, at : at + 128]
    squares[...] = lanes


def close(held, came, extra, count):
    rows = (held.shape[0] - extra) // count + extra
    outs = [shaped((rows, held.shape[1]), LOW)] * count + [shaped((8, 128), F32)]
    return pl.pallas_call(
        functools.partial(close_kernel, extra),
        out_shape=tuple(outs),
        in_specs=[full_spec(held.shape), full_spec(came.shape)],
        out_specs=tuple(full_spec(a.shape) for a in outs),
        compiler_params=kernel_params(16),
        cost_estimate=cost(0, 1024 * 1024),
        name="close_gradients",
    )(held, came)


def join_kernel(info, *refs):
    core = info[0]
    firsts, seconds, (sent, vec_first, vec_second) = refs[:4], refs[4:8], refs[8:]
    rows = sent.shape[1]
    for vec, pieces in ((vec_first, firsts), (vec_second, seconds)):
        sides = [a[rows : rows + 16, :].astype(F32) for a in pieces]
        vec[...] = (sides[0] + sides[1]) + (sides[2] + sides[3])

    def write(pieces):
        for r in range(GROUP):
            sent[r] = pieces[r][0:rows, :]

    pl.when(core == 0)(functools.partial(write, seconds))
    pl.when(core == 1)(functools.partial(write, firsts))


def join(info, firsts, seconds, rows):
    sent = shaped((GROUP, rows, PART), LOW)
    vec = shaped((16, PART), F32)
    return pl.pallas_call(
        join_kernel,
        out_shape=(sent, vec, vec),
        in_specs=[smem_spec()] + [full_spec(a.shape) for a in (*firsts, *seconds)],
        out_specs=tuple(full_spec(a.shape) for a in (sent, vec, vec)),
        compiler_params=kernel_params(16),
        cost_estimate=cost(0, 1024 * 1024),
        name="join_members",
    )(info, *firsts, *seconds)


def adam_update(weight, grad, first, second, factor, rate):
    clipped = grad * factor
    first_new = BETA_ONE * first + (1.0 - BETA_ONE) * clipped
    second_new = BETA_TWO * second + (1.0 - BETA_TWO) * clipped * clipped
    first_hat = first_new / (1.0 - BETA_ONE**STEP)
    second_hat = second_new / (1.0 - BETA_TWO**STEP)
    weight_new = weight - rate * (
        first_hat / (jnp.sqrt(second_hat) + ADAM_EPS) + WEIGHT_DECAY * weight
    )
    return (weight_new, first_new, second_new)


def adam_kernel(info, factor_ref, *refs):
    core, group = info[0], info[1]
    factor = factor_ref[0]
    qus, refs = (refs[:4], refs[4:8]), refs[8:]
    ods, refs = (refs[:2], refs[2:4]), refs[4:]
    (qu_came, down_came, out_came), refs = refs[:3], refs[3:]
    olds, news = refs[:12], refs[12:]
    width = SIDE // SPREAD

    def update(which, columns, grad):
        weight, first, second = [olds[3 * which + i][0, :, columns] for i in range(3)]
        fresh = adam_update(weight, grad.astype(F32), first, second, factor, LEARN_RATE)
        for i in range(3):
            news[3 * which + i][0, :, columns] = fresh[i]

    def update_qu(half, member, piece):
        if half == 0:
            for kind in range(3):
                for run in range(SPREAD):
                    at = (kind * SPREAD + run) * width
                    column = qkv_column(kind, run, member)
                    update(0, slice(column, column + width), piece(at, width))
        for local, where, at, length in up_pieces():
            if where == half:
                column = up_column(member, local)
                update(2, slice(column, column + length), piece(at, length))

    def both_halves(here):
        for half in range(2):
            columns = slice(half * (D // 2), (half + 1) * (D // 2))
            down, out = ods[here] if half == here else (down_came, out_came)
            update(1, columns, out[...])
            update(3, columns, down[...])

            for member in range(GROUP):
                if half == here:
                    for g in range(GROUP):

                        @pl.when(group == g)
                        def _(ref=qus[here][member ^ g]):
                            update_qu(half, member, lambda at, length: ref[:, at : at + length])
                else:
                    update_qu(half, member, lambda at, length: qu_came[group ^ member, :, at : at + length])

    for here in range(2):
        pl.when(core == here)(functools.partial(both_halves, here))


def adam(info, factor, qus, ods, qu_came, od_came, olds):
    rows = olds[0].shape[1]
    ff_rows = olds[9].shape[1]
    steps = max(1, rows // 16)
    few, many = rows // steps, ff_rows // steps

    def master(a):
        return pl.BlockSpec((1, a.shape[1] // steps, a.shape[2]), lambda i: (0, i, 0))

    piece_spec = pl.BlockSpec((few, PART), lambda i: (i, 0))
    came_spec = pl.BlockSpec((GROUP, few, PART), lambda i: (0, i, 0))
    down_spec = pl.BlockSpec((many, D // 2), lambda i: (i, 0))
    out_spec = pl.BlockSpec((few, D // 2), lambda i: (ff_rows // few + i, 0))
    return pl.pallas_call(
        adam_kernel,
        grid=(steps,),
        out_shape=tuple(shaped(a.shape, F32) for a in olds),
        in_specs=[smem_spec(), smem_spec()]
        + [piece_spec] * 8
        + [down_spec, out_spec] * 2
        + [came_spec, down_spec, out_spec]
        + [master(a) for a in olds],
        out_specs=tuple(master(a) for a in olds),
        compiler_params=kernel_params(32),
        name="adamw",
    )(info, factor, *qus[0], *qus[1], ods[0], ods[0], ods[1], ods[1], qu_came, od_came, od_came, *[far(a) for a in olds])


def doc_tables(lengths, rows):
    seqs = lengths.shape[0]
    ends = jnp.cumsum(lengths, axis=1)
    places = jnp.arange(rows, dtype=jnp.int32)
    past = places[None, :, None] >= ends[:, None, :]
    begins = jnp.sum(jnp.where(past, lengths[:, None, :], 0), axis=2)
    position = (places[None, :] - begins).reshape(seqs * rows, 1)
    half = ROT // 2
    inverse = 10000.0 ** (-(jnp.arange(half, dtype=F32) * 2.0) / ROT)
    lanes = jnp.concatenate([inverse, inverse, jnp.zeros(HEAD_DIM - ROT, F32)])
    angles = position.astype(F32) * jnp.concatenate([lanes, lanes])[None, :]
    allowed = (places[None, None, :] <= places[None, :, None]) & (places[None, None, :] >= begins[:, :, None])
    mask = jnp.where(allowed, 0.0, -1e30).reshape(seqs * rows, rows).astype(F32)
    return jnp.cos(angles), jnp.sin(angles), mask


def shards(
    x_in,
    cotangent,
    doc_lengths,
    w_qkv,
    w_out,
    w_up,
    w_down,
    vectors,
    m_qkv,
    m_out,
    m_up,
    m_down,
    m_vectors,
    v_qkv,
    v_out,
    v_up,
    v_down,
    v_vectors,
):
    place = Place()
    ring, core, group, spot = place.ring, place.core, place.group, place.spot
    info = place.info()
    local_rows, width = x_in.shape
    seqs, docs = doc_lengths.shape
    rows = local_rows // seqs
    in_rows = w_qkv.shape[1]
    shard = vectors.shape[1]
    members = range(1, GROUP)

    vec_block = jnp.pad(vectors[0].astype(LOW), (0, in_rows * 128 - shard)).reshape(in_rows, 128)
    keep_qu, send_qu, keep_od, send_od = pack(info, w_qkv, w_out, w_up, w_down, vec_block)
    came_qu = place.sibling(send_qu)
    came_od = place.sibling(send_od)

    def member_columns(block, *waited):
        qu = jnp.where(core == block, keep_qu, came_qu)
        sent = [after(take(qu, group ^ r), *waited) for r in members]
        return [take(qu, group)] + [place.member(a, r) for a, r in zip(sent, members)]

    def gather(block, *waited):
        late = after(block, *waited)
        return [block] + [place.member(late, r) for r in members]

    def to_owners(slots):
        return [slots[0]] + [place.member(slots[r], r) for r in members]

    def total_of(slots):
        return sum(a.astype(F32) for a in slots)

    def block_vectors(parts):
        pieces = jnp.concatenate([a[:, :, 0 : -(-shard // 128), PART:] for a in parts])
        pieces = pieces.reshape(ring.size * GROUP, -1)[:, :shard]
        dp = jnp.arange(ring.count, dtype=jnp.int32)
        difference = ring.spot_of(dp) ^ spot
        slot = jnp.where(core == 0, ring.slot(difference, 0), ring.slot(difference, 1))
        vec = jnp.take(pieces, slot * GROUP + (ring.group_of(dp) ^ group), axis=0, mode="clip")
        vec = vec.reshape(-1).astype(F32)
        b_qkv, b_out, b_up, b_down, gain, ln_bias = jnp.split(
            vec, [3 * D, 4 * D, 4 * D + FF, 5 * D + FF, 6 * D + FF]
        )
        b_qkv = take(b_qkv.reshape(3 * SPREAD, GROUP, -1), group, 1).reshape(1, -1)
        b_up = take(b_up.reshape(SPREAD, GROUP, -1), group, 1).reshape(1, -1)
        return (b_qkv, b_up, gain[None], ln_bias[None]), (b_out + b_down)[None], gain[None]

    x_own = take(x_in.reshape(2, rows, width), core)
    cot_own = take(cotangent.reshape(2, rows, width), core)
    len_own = take(doc_lengths, core)
    len_rows = jnp.zeros((16, width), LOW).at[0, :docs].set(len_own.astype(LOW))
    x_sent = jnp.concatenate([x_own, len_rows])
    cot_all = place.group_gather(cot_own)

    qu_came = member_columns(0)
    qu_own = jnp.stack(qu_came)[None]
    x_group = gather(x_sent, qu_came[1])
    qu_next = member_columns(1, *x_group[2:])
    od_own = jnp.where(core == 0, keep_od, came_od)[None]
    od = [jnp.concatenate([od_own, place.across(od_own, 0)])]
    qu = [jnp.concatenate([qu_own, after(place.across(qu_own, 0), x_group[1])])]
    for step in range(1, ring.bits):
        od.append(place.across(jnp.concatenate(od), step))
        qu.append(place.across(jnp.concatenate(qu), step))
    qu_sibling = [place.sibling(a) for a in qu[:-1]] + [place.sibling(after(qu[-1], *x_group[2:]))]
    parts_first = (*qu, *od, *qu_sibling, *(place.sibling(a) for a in od))
    lengths = jnp.stack([a[rows, :docs] for a in x_group]).astype(jnp.int32)
    tables = doc_tables(lengths, rows)
    vecs_first, bias_first, gain_first = block_vectors(qu)

    od_own = after(jnp.where(core == 1, keep_od, came_od)[None], qu[-1])
    od_late = [jnp.concatenate([od_own, place.across(od_own, 0)])]
    x_group[0] = after(x_group[0], od_late[0])
    first = forward(ring, info, parts_first, x_group, tables, vecs_first, rows)
    came = to_owners(first[:GROUP])
    qu_own = jnp.stack([qu_next[0]] + [after(a, first[0]) for a in qu_next[1:]])[None]
    qu_own = after(qu_own, *came[1:])
    qu_late = [jnp.concatenate([qu_own, place.across(qu_own, 0)])]
    for step in range(1, ring.bits):
        od_late.append(after(place.across(jnp.concatenate(od_late), step), first[0]))
        qu_late.append(place.across(jnp.concatenate(qu_late), step))
    qu_sibling, od_sibling = [[place.sibling(a) for a in late] for late in (qu_late, od_late)]
    kept_first, tables = first[GROUP:], first[-3:]
    hidden_first = (x_own.astype(F32) + total_of(came) + bias_first).astype(LOW)
    hidden_group = gather(hidden_first)
    parts_second = (*qu_late, *od_late, *qu_sibling, *od_sibling)
    vecs_second, bias_second, gain_second = block_vectors(qu_late)
    second = middle(ring, info, parts_second, hidden_group, cot_all, tables, vecs_second, rows)
    sums_second, y_second, mixed_second, active_second, dqu_second, grad_second, z_second = second[GROUP:]

    def rows_backward(rows_low, grad_low, dy, gain):
        rows_now = rows_low.astype(F32)
        centered = rows_now - jnp.mean(rows_now, axis=-1, keepdims=True)
        variance = jnp.mean(centered * centered, axis=-1, keepdims=True)
        inverse_std = lax.rsqrt(variance + NORM_EPS)
        normed = centered * inverse_std
        scaled = dy * gain
        inner_mean = jnp.mean(scaled, axis=-1, keepdims=True)
        inner_cross = jnp.mean(scaled * normed, axis=-1, keepdims=True)
        return (grad_low.astype(F32) + inverse_std * (scaled - inner_mean - normed * inner_cross)).astype(LOW)

    extra = 16

    def ring_fold(kept, sent, steps, extra, *waited):
        for step in steps:
            kept, sent = fold(kept, after(place.across(sent, step), *waited), extra)
        return kept, sent

    def to_members(pieces):
        return [pieces[0]] + [place.member(pieces[r], r) for r in members]

    steps = list(reversed(range(ring.bits)))

    dy_second = to_owners(second[:GROUP])
    od_second = od_grads(ring, info, mixed_second, active_second, grad_second)
    qu_second = qu_grads(ring, info, y_second, dqu_second, after(sums_second, dy_second[1]))
    mid_grad = rows_backward(hidden_first, cot_own, total_of(dy_second), gain_second)
    mid_group = gather(mid_grad)
    od_second = fold(od_second[0], place.sibling(od_second[1]), 0)
    qu_second = fold(qu_second[0], place.sibling(qu_second[1]), extra)

    mid_late = [after(mid_group[0], *od_second, *qu_second)] + mid_group[1:]
    back = backward(ring, info, mid_late, kept_first, rows)
    dy_first, od_keep, od_send, qu_keep, qu_send = back
    z_total = place.group_sum(after(z_second, *mid_group[1:]))
    dy_total = place.group_sum(dy_first)
    od_second = ring_fold(*od_second, steps[:-1], 0, qu_send)
    qu_second = ring_fold(*qu_second, steps[:-1], extra, qu_send)
    qu_send = after(qu_send, *od_second, *qu_second)
    *od_second, od_squares_second = close(od_second[0], place.across(od_second[1], 0), 0, 1)
    *qu_second, qu_squares_second = close(qu_second[0], place.across(qu_second[1], 0), extra, GROUP)
    held = fold(qu_keep, place.sibling(qu_send), extra)
    od_first = fold(od_keep, place.sibling(od_send), 0)
    qu_slots_second = to_members(qu_second)
    kept, sent = ring_fold(*held, steps[:-1], extra)
    came = place.across(after(sent, *qu_slots_second[1:]), 0)
    *qu_first, qu_squares_first = close(kept, came, extra, GROUP)
    kept, sent = ring_fold(*od_first, steps[:-1], 0)
    *od_first, od_squares_first = close(kept, place.across(sent, 0), 0, 1)
    qu_slots_first = to_members(qu_first)
    qu_sent, vec_first, vec_second = join(info, qu_slots_first, qu_slots_second, in_rows)
    dy_total = after(dy_total, qu_sent).astype(F32)
    start_grad = rows_backward(x_own, mid_grad, dy_total, gain_first)
    z_total = after(z_total, qu_sent).astype(F32)
    hidden_second = (hidden_first.astype(F32) + z_total + bias_second).astype(LOW)

    def all_sum(block, first, last):
        hops = [place.sibling]
        hops += [functools.partial(place.across, step=step) for step in range(ring.bits)]
        hops += [functools.partial(place.member, distance=1), functools.partial(place.member, distance=2)]
        for hop in hops[first:last]:
            block = block + hop(block)
        return block

    squares = od_squares_first + qu_squares_first + od_squares_second + qu_squares_second
    squares = all_sum(squares, 0, 2)
    squares = all_sum(after(squares, *qu_slots_first[1:]), 2, None)
    squares = jnp.sum(squares)
    for vec in (vec_first, vec_second):
        bias, tail = vec[2 * GROUP], vec[2 * GROUP + 3, : D - PART]
        squares = squares + jnp.sum(vec * vec) + jnp.sum(bias * bias) + jnp.sum(tail * tail)
    grad_norm = jnp.sqrt(squares)
    factor = jnp.minimum(1.0, CLIP_LEVEL / (grad_norm + 1e-06))

    def own_block(one, two):
        came = place.sibling(jnp.where(core == 0, two, one))
        mine = jnp.where(core == 0, one, two)
        return [jnp.where(core == h, mine, came) for h in range(2)]

    od_first, od_second = after(od_first[0], *qu_first), od_second[0]
    od_came = place.sibling(jnp.where(core == 0, od_second, od_first))
    qu_came = place.sibling(qu_sent)
    vec = after(jnp.where(core == 0, vec_first, vec_second), qu_sent)
    vec_share = take(vectors_of(vec).reshape(ring.count, shard), lax.axis_index("dp"))[None]
    olds = (w_qkv, m_qkv, v_qkv, w_out, m_out, v_out, w_up, m_up, v_up, w_down, m_down, v_down)
    qus = (qu_slots_first, qu_slots_second)
    news = adam(info, factor[None], qus, (od_first, od_second), qu_came, od_came, olds)
    new_vec = adam_update(vectors, vec_share, m_vectors, v_vectors, factor, VECTOR_RATE)

    outputs = own_block(jnp.stack([hidden_first, start_grad]), jnp.stack([hidden_second, mid_grad]))
    outputs = jnp.concatenate(outputs, axis=1)
    hidden_out, input_grads = outputs[:1], outputs[1:]
    return (
        hidden_out,
        input_grads,
        *(news[3 * i] for i in range(4)),
        new_vec[0],
        *(news[3 * i + 1] for i in range(4)),
        new_vec[1],
        *(news[3 * i + 2] for i in range(4)),
        new_vec[2],
        grad_norm,
    )


def solution(mesh):
    return jax.shard_map(
        shards,
        mesh=mesh,
        in_specs=(
            P("dp", None),
            P("dp", None),
            P("dp", None),
            P("section", "dp", None),
            P("section", "dp", None),
            P("section", "dp", None),
            P("section", "dp", None),
            P("section", "dp"),
            P("section", "dp", None),
            P("section", "dp", None),
            P("section", "dp", None),
            P("section", "dp", None),
            P("section", "dp"),
            P("section", "dp", None),
            P("section", "dp", None),
            P("section", "dp", None),
            P("section", "dp", None),
            P("section", "dp"),
        ),
        out_specs=(
            P("section", "dp", None),
            P("section", "dp", None),
            P("section", "dp", None),
            P("section", "dp", None),
            P("section", "dp", None),
            P("section", "dp", None),
            P("section", "dp"),
            P("section", "dp", None),
            P("section", "dp", None),
            P("section", "dp", None),
            P("section", "dp", None),
            P("section", "dp"),
            P("section", "dp", None),
            P("section", "dp", None),
            P("section", "dp", None),
            P("section", "dp", None),
            P("section", "dp"),
            P(),
        ),
        check_vma=False,
    )
```

```python
import functools

import jax
import jax.numpy as jnp
from jax import lax
from jax.experimental import pallas as pl
from jax.experimental.pallas import tpu as pltpu
from jax.sharding import PartitionSpec as P

D = 1024
FF = 4096
HEADS = 16
HEAD_DIM = 64
ROT = 16
STEP = 10


NORM_EPS = 1e-05
BETA_ONE = 0.9
BETA_TWO = 0.95
LEARN_RATE = 0.05
VECTOR_RATE = 0.3
WEIGHT_DECAY = 0.01
CLIP_LEVEL = 1.0
ADAM_EPS = 1e-08

AXES = ("section", "dp")
GROUP = 4
SPREAD = 1
LOW = jnp.bfloat16
F32 = jnp.float32
SIDE = D // GROUP
UNITS = FF // GROUP
MIXED = 3 * SIDE + UNITS
PART = MIXED // 2
WIRE = PART + 128


class Ring:
    def __init__(self, count):
        self.count = count
        self.low = count // (GROUP * SPREAD)
        self.size = SPREAD * self.low
        self.bits = self.size.bit_length() - 1

    def index(self, g, t):
        return ((t // self.low) * GROUP + g) * self.low + t % self.low

    def group_of(self, dp):
        return (dp // self.low) % GROUP

    def spot_of(self, dp):
        return (dp // (GROUP * self.low)) * self.low + dp % self.low

    def order(self, core):
        steps = list(range(self.bits))
        if SPREAD > 1 or core == 1:
            steps.reverse()
        return steps

    def turn(self, slot, core):
        return sum(((slot >> s) & 1) << b for s, b in enumerate(self.order(core)))

    def slot(self, difference, core):
        return sum(((difference >> b) & 1) << s for s, b in enumerate(self.order(core)))


class Place:
    def __init__(self):
        self.ring = Ring(lax.axis_size("dp"))
        self.core = lax.axis_index("section")
        dp = lax.axis_index("dp")
        self.group = self.ring.group_of(dp)
        self.spot = self.ring.spot_of(dp)

    def info(self):
        return jnp.stack([self.core, self.group, self.spot]).astype(jnp.int32)

    def move(self, block, where):
        ring = self.ring
        route = []
        for core in range(2):
            for g in range(GROUP):
                for t in range(ring.size):
                    c, h, u = where(core, g, t)
                    route.append((core * ring.count + ring.index(g, t), c * ring.count + ring.index(h, u)))
        return lax.ppermute(block, AXES, route)

    def sibling(self, block):
        return self.move(block, lambda c, g, t: (1 - c, g, t))

    def member(self, block, distance):
        return self.move(block, lambda c, g, t: (c, g ^ distance, t))

    def across(self, block, step):
        return self.move(block, lambda c, g, t: (c, g, t ^ (1 << self.ring.order(c)[step])))


def take(block, index, axis=0):
    return lax.dynamic_index_in_dim(block, index, axis, keepdims=False)


def after(block, *waited):
    return lax.optimization_barrier((block, waited))[0]


def dot(left, right):
    return jnp.dot(left, right, preferred_element_type=F32)


def dot_cols(left, right):
    return lax.dot_general(left, right, (((1,), (1,)), ((), ())), preferred_element_type=F32)


def dot_rows(left, right):
    return lax.dot_general(left, right, (((0,), (0,)), ((), ())), preferred_element_type=F32)


def full_spec(shape):
    return pl.BlockSpec(shape, lambda *_: (0,) * len(shape))


def far_spec():
    return pl.BlockSpec(memory_space=pltpu.HBM)


def far(block):
    return pltpu.with_memory_space_constraint(block, pltpu.HBM)


def any_spec():
    return pl.BlockSpec(memory_space=pl.ANY)


def smem_spec():
    return pl.BlockSpec(memory_space=pltpu.SMEM)


def shaped(shape, dtype):
    return jax.ShapeDtypeStruct(shape, dtype)


def kernel_params(mebibytes):
    return pltpu.CompilerParams(vmem_limit_bytes=mebibytes * 1024 * 1024)


def up_pieces():
    run = UNITS // SPREAD
    cuts = sorted({0, PART - 3 * SIDE, UNITS} | {run * i for i in range(SPREAD)})
    pieces = []
    for begin, end in zip(cuts[:-1], cuts[1:]):
        column = 3 * SIDE + begin
        pieces.append((begin, column // PART, column % PART, end - begin))
    return pieces


def up_column(g, local):
    run = UNITS // SPREAD
    return (local // run * GROUP + g) * run + local % run


def qkv_column(kind, run, g):
    width = SIDE // SPREAD
    return ((kind * SPREAD + run) * GROUP + g) * width


def pack_kernel(info, qkv_hbm, out_hbm, up_hbm, down_hbm, vec, keep_qu, send_qu, keep_od, send_od, *scratch):
    w_qkv, w_out, w_up, w_down, sems = scratch
    pairs = ((qkv_hbm, w_qkv), (up_hbm, w_up), (down_hbm, w_down), (out_hbm, w_out))
    copies = [pltpu.make_async_copy(far.at[0], near, sems.at[i]) for i, (far, near) in enumerate(pairs)]
    for copy in copies:
        copy.start()
    rows = w_qkv.shape[0]
    ff_rows = w_down.shape[0]
    width = SIDE // SPREAD
    core = info[0]

    def write_qu(halves):
        for g in range(GROUP):
            for kind in range(3):
                for run in range(SPREAD):
                    at = (kind * SPREAD + run) * width
                    column = qkv_column(kind, run, g)
                    halves[0][g, :, at : at + width] = w_qkv[:, column : column + width].astype(LOW)
            for local, half, at, length in up_pieces():
                column = up_column(g, local)
                halves[half][g, :, at : at + length] = w_up[:, column : column + length].astype(LOW)
            for half in range(2):
                halves[half][g, :, PART:WIRE] = vec[...]

    def write_od(halves):
        for half in range(2):
            columns = slice(half * (D // 2), (half + 1) * (D // 2))
            halves[half][0:ff_rows] = w_down[:, columns].astype(LOW)
            halves[half][ff_rows : ff_rows + rows] = w_out[:, columns].astype(LOW)

    for first, last, write, kept, sent in ((0, 2, write_qu, keep_qu, send_qu), (2, 4, write_od, keep_od, send_od)):
        for copy in copies[first:last]:
            copy.wait()
        pl.when(core == 0)(functools.partial(write, (kept, sent)))
        pl.when(core == 1)(functools.partial(write, (sent, kept)))


def pack(info, w_qkv, w_out, w_up, w_down, vec):
    rows, ff_rows = w_qkv.shape[1], w_down.shape[1]
    qu = shaped((GROUP, rows, WIRE), LOW)
    od = shaped((ff_rows + rows, D // 2), LOW)
    return pl.pallas_call(
        pack_kernel,
        out_shape=(qu, qu, od, od),
        in_specs=[smem_spec()] + [far_spec()] * 4 + [full_spec(vec.shape)],
        out_specs=tuple(full_spec(a.shape) for a in (qu, qu, od, od)),
        scratch_shapes=[pltpu.VMEM(a.shape[1:], F32) for a in (w_qkv, w_out, w_up, w_down)]
        + [pltpu.SemaphoreType.DMA((4,))],
        compiler_params=kernel_params(24),
        name="pack_weights",
    )(info, far(w_qkv), far(w_out), far(w_up), far(w_down), vec)


def stack_kernel(*refs):
    for i, ref in enumerate(refs[:-1]):
        refs[-1][0, i] = ref[...]


def stack_members(pieces):
    out = shaped((1, len(pieces), *pieces[0].shape), LOW)
    return pl.pallas_call(
        stack_kernel,
        out_shape=out,
        in_specs=[full_spec(a.shape) for a in pieces],
        out_specs=full_spec(out.shape),
        compiler_params=kernel_params(16),
        cost_estimate=cost(50 * 10**9, 1024 * 1024),
        name="stack_members",
    )(*pieces)


def weight_copies(ring, info, parts, wqu, wout, wdown, sems):
    core, group, spot = info[0], info[1], info[2]
    qu_copies, od_copies = [], []
    count = len(parts) // 4
    for which in range(2):
        half = core if which == 0 else 1 - core
        qu_at = pl.multiple_of(half * PART, 128)
        od_at = pl.multiple_of(half * (D // 2), 128)
        slot = 0
        for piece in range(count):
            qu, od = parts[2 * count * which + piece], parts[2 * count * which + count + piece]
            rows = qu.shape[2]
            ff_rows = od.shape[1] - rows
            for i in range(qu.shape[0]):
                straight, turned = ring.turn(slot, 0), ring.turn(slot, 1)
                there = spot ^ (straight + half * (turned - straight))
                slot += 1
                ff_row = pl.multiple_of(there * ff_rows, ff_rows)
                out_row = pl.multiple_of(there * rows, rows)
                far = wdown.at[pl.ds(ff_row, ff_rows), pl.ds(od_at, D // 2)]
                od_copies.append(pltpu.make_async_copy(od.at[i, pl.ds(0, ff_rows)], far, sems.at[0]))
                far = wout.at[pl.ds(out_row, rows), pl.ds(od_at, D // 2)]
                od_copies.append(pltpu.make_async_copy(od.at[i, pl.ds(ff_rows, rows)], far, sems.at[0]))
                for r in range(GROUP):
                    row = pl.multiple_of(ring.index(group ^ r, there) * rows, rows)
                    far = wqu.at[pl.ds(row, rows), pl.ds(qu_at, PART)]
                    qu_copies.append(pltpu.make_async_copy(qu.at[i, r, :, pl.ds(0, PART)], far, sems.at[1]))
    return qu_copies, od_copies


def head_masks(dtype):
    lane = lax.broadcasted_iota(jnp.int32, (1, SIDE), 1) // HEAD_DIM
    return [(lane == h).astype(dtype) for h in range(SIDE // HEAD_DIM)]


def by_head(parts):
    lane = lax.broadcasted_iota(jnp.int32, (1, SIDE), 1) // HEAD_DIM
    total = parts[-1]
    for h in range(len(parts) - 2, -1, -1):
        total = jnp.where(lane == h, parts[h], total)
    return total


def turning(cosine, sine, back):
    lane = lax.broadcasted_iota(jnp.int32, sine.shape, 1) % HEAD_DIM
    first = jnp.where(lane < ROT // 2, sine, 0.0)
    second = jnp.where(lane < ROT // 2, 0.0, sine)
    if back:
        second = -second
    else:
        first = -first
    wide = SIDE // cosine.shape[1]
    return [jnp.concatenate([a] * wide, axis=1) for a in (cosine, first, second)]


def turn(part, tables):
    cosine, first, second = tables
    ahead = pltpu.roll(part, SIDE - ROT // 2, 1)
    behind = pltpu.roll(part, ROT // 2, 1)
    return part * cosine + ahead * first + behind * second


def normalise(rows):
    centered = rows - jnp.mean(rows, axis=-1, keepdims=True)
    variance = jnp.mean(centered * centered, axis=-1, keepdims=True)
    return centered * lax.rsqrt(variance + NORM_EPS)


def no_wait():
    pass


def forward_part(x_refs, tables, vecs, wqu, wout, wdown, kept, z_refs, waits, done, normed_ref=None):
    cosine, sine, mask = tables
    b_qkv, b_up, gain, ln_bias = vecs
    y, qkv, probs, mixed, active, slope = kept
    rows = z_refs[0].shape[0]
    for r in range(GROUP):
        normed = normalise(x_refs[r][0:rows, :].astype(F32))
        if normed_ref is not None:
            normed_ref[r * rows : (r + 1) * rows, :] = normed
        y[r * rows : (r + 1) * rows, :] = (normed * gain[...] + ln_bias[...]).astype(LOW)
    done(0)
    waits[0]()
    waits[2]()
    forth = turning(cosine[...], sine[...], False)
    for kind in range(3):
        columns = slice(kind * SIDE, (kind + 1) * SIDE)
        part = dot(y[...], wqu[:, columns]) + b_qkv[:, columns]
        if kind < 2:
            part = turn(part, forth)
        qkv[:, columns] = part.astype(LOW)
    done(1)
    masks = head_masks(LOW)
    heads = len(masks)
    for r in range(GROUP):
        here = slice(r * rows, (r + 1) * rows)
        query, keys, values = [qkv[here, k * SIDE : (k + 1) * SIDE] for k in range(3)]
        stacked = jnp.concatenate([query * m for m in masks], axis=0)
        scores = dot_cols(stacked, keys) * HEAD_DIM ** (-0.5)
        scores = scores.reshape(heads, rows, rows) + mask[here, :][None]
        expo = jnp.exp(scores - jnp.max(scores, axis=-1, keepdims=True))
        prob = expo / jnp.sum(expo, axis=-1, keepdims=True)
        prob = prob.reshape(heads * rows, rows)
        probs[r * heads * rows : (r + 1) * heads * rows, :] = prob
        full = dot(prob.astype(LOW), values)
        mixed[here, :] = by_head([full[h * rows : (h + 1) * rows] for h in range(heads)]).astype(LOW)
    done(2)
    done(3)
    tile = 256
    for at in range(0, UNITS, tile):
        hidden = dot(y[...], wqu[:, 3 * SIDE + at : 3 * SIDE + at + tile]) + b_up[:, at : at + tile]
        share = 0.5 * (1.0 + lax.erf(hidden * (0.5**0.5)))
        density = jnp.exp(-0.5 * hidden * hidden) * (0.5 / jnp.pi) ** 0.5
        active[:, at : at + tile] = (hidden * share).astype(LOW)
        slope[:, at : at + tile] = share + hidden * density
    done(4)
    done(5)
    waits[1]()
    for at in range(0, D, tile):
        branch = dot(mixed[...], wout[:, at : at + tile]) + dot(active[...], wdown[:, at : at + tile])
        for r in range(GROUP):
            z_refs[r][:, at : at + tile] = branch[r * rows : (r + 1) * rows].astype(LOW)


def backward_part(grad, normed, tables, wqu, wout, wdown, kept, dqu, dy_refs, sums, waits, done):
    cosine, sine, _ = tables
    y, qkv, probs, mixed, active, slope = kept
    rows = grad.shape[0] // GROUP
    tile = 256
    waits[0]()
    dmixed = dot_cols(grad[...], wout[...]).astype(LOW)
    for at in range(0, UNITS, tile):
        dactive = dot_cols(grad[...], wdown[at : at + tile, :])
        dhidden = (dactive * slope[:, at : at + tile]).astype(LOW)
        dqu[:, 3 * SIDE + at : 3 * SIDE + at + tile] = dhidden
    waits[1]()
    masks = head_masks(LOW)
    heads = len(masks)
    back = turning(cosine[...], sine[...], True)
    for r in range(GROUP):
        here = slice(r * rows, (r + 1) * rows)
        query, keys, values = [qkv[here, k * SIDE : (k + 1) * SIDE] for k in range(3)]
        dstack = jnp.concatenate([dmixed[here] * m for m in masks], axis=0)
        dprob = dot_cols(dstack, values)
        prob = probs[r * heads * rows : (r + 1) * heads * rows, :]
        dvalues = dot_rows(prob.astype(LOW), dstack)
        dscore = (prob * (dprob - jnp.sum(prob * dprob, axis=-1, keepdims=True))).astype(LOW)
        full = dot(dscore, keys)
        dquery = by_head([full[h * rows : (h + 1) * rows] for h in range(heads)])
        dkeys = dot_rows(dscore, jnp.concatenate([query * m for m in masks], axis=0))
        scale = HEAD_DIM ** (-0.5)
        slot_tables = [a[here] for a in back]
        dqu[here, 0:SIDE] = turn(dquery * scale, slot_tables).astype(LOW)
        dqu[here, SIDE : 2 * SIDE] = turn(dkeys * scale, slot_tables).astype(LOW)
        dqu[here, 2 * SIDE : 3 * SIDE] = dvalues.astype(LOW)
    done()
    for at in range(0, MIXED, tile):
        sums[:, at : at + tile] = jnp.sum(dqu[:, at : at + tile].astype(F32), axis=0, keepdims=True)
    waits[2]()
    for at in range(0, D, tile):
        dy = dot_cols(dqu[...], wqu[at : at + tile, :])
        for r in range(GROUP):
            dy_refs[r][:, at : at + tile] = dy[r * rows : (r + 1) * rows].astype(LOW)
        own = grad[0:rows, at : at + tile].astype(F32)
        for i, terms in enumerate((own, dy * normed[:, at : at + tile], dy)):
            begin = MIXED + i * D + at
            sums[:, begin : begin + tile] = jnp.sum(terms, axis=0, keepdims=True)


def kept_shapes(tokens, rows):
    return [
        ((tokens, D), LOW),
        ((tokens, 3 * SIDE), LOW),
        ((tokens * (SIDE // HEAD_DIM), rows), F32),
        ((tokens, SIDE), LOW),
        ((tokens, UNITS), LOW),
        ((tokens, UNITS), F32),
    ]


def weight_scratch():
    return [
        pltpu.VMEM((D, MIXED), LOW),
        pltpu.VMEM((SIDE, D), LOW),
        pltpu.VMEM((UNITS, D), LOW),
        pltpu.SemaphoreType.DMA((2,)),
    ]


def waiter(copies):
    def wait():
        for copy in copies:
            copy.wait()

    return wait


def started(pairs, sem):
    copies = [pltpu.make_async_copy(source, target, sem) for source, target in pairs]
    for copy in copies:
        copy.start()
    return waiter(copies)


def table_scratch(tokens, rows):
    return [pltpu.VMEM((tokens, 128), F32), pltpu.VMEM((tokens, 128), F32), pltpu.VMEM((tokens, rows), F32)]


def cost(flops, moved):
    return pl.CostEstimate(flops=2 * flops, bytes_accessed=2 * moved, transcendentals=0)


def leaving(pairs, sems):
    copies = [pltpu.make_async_copy(near, far, sems.at[i]) for i, (near, far) in enumerate(pairs)]

    def go(i):
        copies[i].start()

    return go, waiter(copies)


def forward_kernel(ring, count, info, *refs):
    parts, refs = refs[:count], refs[count:]
    x_refs, refs = refs[:4], refs[4:]
    tables, refs = refs[:3], refs[3:]
    vecs, refs = refs[:4], refs[4:]
    z_refs, refs = refs[:4], refs[4:]
    far_kept, far_weights, far_tables, refs = refs[:7], refs[7:10], refs[10:13], refs[13:]
    kept, refs = refs[:7], refs[7:]
    out_sems, scratch = refs[0], refs[1:]
    weights = scratch[:3]
    qu_copies, od_copies = weight_copies(ring, info, parts, *scratch)
    for copy in qu_copies + od_copies:
        copy.start()
    pairs = [*zip(kept, far_kept), *zip(weights, far_weights), *zip(tables, far_tables)]
    go, out = leaving(pairs, out_sems)
    for i in range(10, 13):
        go(i)

    def qu_in():
        waiter(qu_copies)()
        go(7)

    def od_in():
        waiter(od_copies)()
        go(8)
        go(9)

    def done(i):
        go(i)
        if i == 0:
            go(6)

    forward_part(x_refs, tables, vecs, *weights, kept[:6], z_refs, (qu_in, od_in, no_wait), done, kept[6])
    out()


def forward(ring, info, parts, xs, tables, vecs, rows):
    tokens = GROUP * rows
    shapes = kept_shapes(tokens, rows) + [((tokens, D), F32)]
    away = [*shapes, ((D, MIXED), LOW), ((SIDE, D), LOW), ((UNITS, D), LOW)] + [(a.shape, F32) for a in tables]
    blocks = (*xs, *tables, *vecs)
    return pl.pallas_call(
        functools.partial(forward_kernel, ring, len(parts)),
        out_shape=(*[shaped((rows, D), LOW)] * GROUP, *[pltpu.HBM(*a) for a in away]),
        in_specs=[smem_spec()] + [any_spec()] * len(parts) + [full_spec(a.shape) for a in blocks],
        out_specs=tuple([full_spec((rows, D))] * GROUP + [far_spec()] * len(away)),
        scratch_shapes=[pltpu.VMEM(*a) for a in shapes]
        + [pltpu.SemaphoreType.DMA((len(away),))]
        + weight_scratch(),
        compiler_params=kernel_params(28),
        cost_estimate=cost(2 * tokens * D * (D + 2 * FF // GROUP), 16 * 1024 * 1024),
        name="forward_shard",
    )(info, *parts, *blocks)


def grad_rows(refs, grad):
    rows = refs[0].shape[0]
    return [(ref, grad.at[pl.ds(r * rows, rows)]) for r, ref in enumerate(refs)]


def middle_kernel(ring, count, info, *refs):
    parts, refs = refs[:count], refs[count:]
    x_refs, refs = refs[:4], refs[4:]
    g_refs, refs = refs[:4], refs[4:]
    far_tables, refs = refs[:3], refs[3:]
    vecs, refs = refs[:4], refs[4:]
    dy_refs, refs = refs[:4], refs[4:]
    sums, away, refs = refs[0], refs[1:10], refs[10:]
    kept, refs = refs[:6], refs[6:]
    z_refs, tables, refs = refs[:4], refs[4:7], refs[7:]
    (grad, normed, dqu, in_sems, out_sems), scratch = refs[:5], refs[5:]
    rows = z_refs[0].shape[0]
    qu_copies, od_copies = weight_copies(ring, info, parts, *scratch)
    for copy in qu_copies:
        copy.start()
    tables_in = started(zip(far_tables, tables), in_sems.at[0])
    for copy in od_copies:
        copy.start()
    grad_in = started(grad_rows(g_refs, grad), in_sems.at[1])
    go, out = leaving(list(zip([kept[0], kept[3], kept[4], dqu, grad, *z_refs], away)), out_sems)

    def done(i):
        if i in (0, 3, 4):
            go((0, 3, 4).index(i))

    waits = (waiter(qu_copies), waiter(od_copies), tables_in)
    forward_part(x_refs, tables, vecs, *scratch[:3], kept, z_refs, waits, done, normed)
    grad_in()
    for i in range(4, 9):
        go(i)
    waits = (no_wait, no_wait, no_wait)
    done = functools.partial(go, 3)
    backward_part(grad, normed, tables, *scratch[:3], kept, dqu, dy_refs, sums, waits, done)
    out()


def middle(ring, info, parts, xs, gs, tables, vecs, rows):
    tokens = GROUP * rows
    shapes = kept_shapes(tokens, rows)
    away = [shapes[0], shapes[3], shapes[4], ((tokens, MIXED), LOW), ((tokens, D), LOW)]
    away += [((rows, D), LOW)] * GROUP
    sums = shaped((1, MIXED + 3 * D), F32)
    return pl.pallas_call(
        functools.partial(middle_kernel, ring, len(parts)),
        out_shape=(*[shaped((rows, D), LOW)] * GROUP, sums, *[pltpu.HBM(*a) for a in away]),
        in_specs=[smem_spec()]
        + [any_spec()] * len(parts)
        + [full_spec(a.shape) for a in xs]
        + [any_spec()] * GROUP
        + [far_spec()] * 3
        + [full_spec(a.shape) for a in vecs],
        out_specs=tuple([full_spec((rows, D))] * GROUP + [full_spec(sums.shape)] + [far_spec()] * len(away)),
        scratch_shapes=[pltpu.VMEM(*a) for a in shapes]
        + [pltpu.VMEM((rows, D), LOW)] * GROUP
        + table_scratch(tokens, rows)
        + [pltpu.VMEM((tokens, D), LOW), pltpu.VMEM((tokens, D), F32), pltpu.VMEM((tokens, MIXED), LOW)]
        + [pltpu.SemaphoreType.DMA((2,)), pltpu.SemaphoreType.DMA((9,))]
        + weight_scratch(),
        compiler_params=kernel_params(32),
        cost_estimate=cost(4 * tokens * D * (D + 2 * FF // GROUP), 16 * 1024 * 1024),
        name="forward_backward_shard",
    )(info, *parts, *xs, *gs, *[far(a) for a in tables], *vecs)


def backward_kernel(ring, info, *refs):
    g_refs, refs = refs[:4], refs[4:]
    far_kept, far_weights, far_tables, refs = refs[:7], refs[7:10], refs[10:13], refs[13:]
    dy_refs, refs = refs[:4], refs[4:]
    (keep, send), refs = refs[:2], refs[2:]
    kept, refs = refs[:7], refs[7:]
    weights, tables, refs = refs[:3], refs[3:6], refs[6:]
    grad, dqu, sums, in_sems = refs
    y, qkv, probs, mixed, active, slope, normed = kept
    wqu, wout, wdown = weights
    far_y, far_qkv, far_probs, far_mixed, far_active, far_slope, far_normed = far_kept
    mixed_in = started([(far_mixed, mixed)], in_sems.at[0])
    active_in = started([(far_active, active)], in_sems.at[1])
    units_in = started([*zip(far_weights[1:], weights[1:]), (far_slope, slope)], in_sems.at[2])
    heads_in = started([(far_qkv, qkv), (far_probs, probs), *zip(far_tables, tables)], in_sems.at[3])
    dy_in = started([(far_weights[0], wqu), (far_normed, normed)], in_sems.at[4])
    y_in = started([(far_y, y)], in_sems.at[5])
    rows = g_refs[0].shape[0]
    for r in range(GROUP):
        grad[r * rows : (r + 1) * rows, :] = g_refs[r][...]
    mixed_in()
    od_part(ring, info, mixed, active, grad, keep, send, active_in)
    waits = (units_in, heads_in, dy_in)
    backward_part(grad, normed, tables, *weights, kept[:6], dqu, dy_refs, sums, waits, no_wait)
    y_in()
    qu_part(ring, info, y, dqu, sums, keep, send)


def backward(ring, info, gs, held, rows):
    tokens = GROUP * rows
    outs = [shaped((rows, D), LOW)] * GROUP + [grads_shape(ring)] * 2
    return pl.pallas_call(
        functools.partial(backward_kernel, ring),
        out_shape=tuple(outs),
        in_specs=[smem_spec()] + [full_spec(a.shape) for a in gs] + [far_spec()] * len(held),
        out_specs=tuple(full_spec(a.shape) for a in outs),
        scratch_shapes=[pltpu.VMEM(a.shape, a.dtype) for a in held]
        + [pltpu.VMEM((tokens, D), LOW), pltpu.VMEM((tokens, MIXED), LOW)]
        + [pltpu.VMEM((1, MIXED + 3 * D), F32), pltpu.SemaphoreType.DMA((6,))],
        compiler_params=kernel_params(36),
        cost_estimate=cost(4 * tokens * D * (D + 2 * FF // GROUP), 16 * 1024 * 1024),
        name="backward_shard",
    )(info, *gs, *[far(a) for a in held])


def slot_in(ring, difference, half):
    straight, turned = ring.slot(difference, 0), ring.slot(difference, 1)
    return straight + half * (turned - straight)


QU_TILES = PART // 128
OD_TILES = D // 2 // 128
SIDES = 112


def slot_rows(ring):
    return GROUP * QU_TILES * (D // ring.count) + OD_TILES * (SIDE + UNITS) // ring.size


def grads_shape(ring):
    return shaped((ring.size * slot_rows(ring) + SIDES, 128), LOW)


def od_part(ring, info, mixed, active, grad, keep, send, active_in):
    core, spot = info[0], info[2]
    out_rows = SIDE // ring.size
    ff_rows = UNITS // ring.size
    ahead = GROUP * QU_TILES * (D // ring.count)
    for i, (out, half) in enumerate(((send, 1 - core), (keep, core))):
        columns = pl.ds(pl.multiple_of(half * (D // 2), D // 2), D // 2)
        part = grad[:, columns]
        block = dot_rows(mixed[...], part).astype(LOW)
        if i == 0:
            active_in()
        for there in range(ring.size):
            slot = slot_in(ring, spot ^ there, half)
            piece = dot_rows(active[:, there * ff_rows : (there + 1) * ff_rows], part).astype(LOW)
            for tile in range(OD_TILES):
                lanes = slice(tile * 128, (tile + 1) * 128)
                row = slot * slot_rows(ring) + ahead + tile * (ff_rows + out_rows)
                out[pl.ds(pl.multiple_of(row, 16), ff_rows), :] = piece[:, lanes]
                row = pl.multiple_of(row + ff_rows, 16)
                out[pl.ds(row, out_rows), :] = block[there * out_rows : (there + 1) * out_rows, lanes]


def vector_rows(group, sums):
    width = SIDE // SPREAD
    run = UNITS // SPREAD
    row = lax.broadcasted_iota(jnp.int32, (SIDES, 128), 0)
    pieces = []
    for at in range(0, 3 * SIDE, 128):
        pieces.append(((at // width * GROUP + group) * (width // 128) + at % width // 128, at))
    for at in range(0, UNITS, 128):
        pieces.append((3 * D // 128 + D // 128 + (at // run * GROUP + group) * (run // 128) + at % run // 128, 3 * SIDE + at))
    tail = (4 * D + FF) // 128
    for i, begin in enumerate((3 * D // 128, tail, tail + D // 128, tail + 2 * D // 128)):
        for at in range(0, D, 128):
            pieces.append((begin + at // 128, MIXED + max(i - 1, 0) * D + at))
    return sum(jnp.where(row == where, sums[:, at : at + 128], 0.0) for where, at in pieces)


def qu_part(ring, info, y, dqu, sums, keep, send):
    core, group, spot = info[0], info[1], info[2]
    rows = D // ring.count
    tile = 256
    last = ring.size * slot_rows(ring)
    extra = vector_rows(group, sums).astype(LOW)
    for out, half in ((send, 1 - core), (keep, core)):
        columns = pl.ds(pl.multiple_of(half * PART, 128), PART)
        out[last : last + SIDES, :] = extra
        for at in range(0, D, tile):
            block = dot_rows(y[:, at : at + tile], dqu[:, columns]).astype(LOW)
            for offset in range(0, tile, rows):
                dp = (at + offset) // rows
                slot = slot_in(ring, spot ^ ring.spot_of(dp), half)
                begin = slot * slot_rows(ring) + (group ^ ring.group_of(dp)) * (QU_TILES * rows)
                for i in range(QU_TILES):
                    row = pl.multiple_of(begin + i * rows, 16)
                    out[pl.ds(row, rows), :] = block[offset : offset + rows, i * 128 : (i + 1) * 128]


def grads_kernel(ring, info, far_mixed, far_active, far_grad, far_y, far_dqu, sums, keep, send, *scratch):
    mixed, active, grad, y, dqu, sems = scratch
    grad_in = started([(far_grad, grad), (far_mixed, mixed)], sems.at[0])
    active_in = started([(far_active, active)], sems.at[1])
    rest_in = started([(far_y, y), (far_dqu, dqu)], sems.at[2])
    grad_in()
    od_part(ring, info, mixed, active, grad, keep, send, active_in)
    rest_in()
    qu_part(ring, info, y, dqu, sums, keep, send)


def weight_grads(ring, info, mixed, active, grad, y, dqu, sums):
    blocks = (mixed, active, grad, y, dqu)
    out = grads_shape(ring)
    return pl.pallas_call(
        functools.partial(grads_kernel, ring),
        out_shape=(out, out),
        in_specs=[smem_spec()] + [far_spec()] * len(blocks) + [full_spec(sums.shape)],
        out_specs=(full_spec(out.shape),) * 2,
        scratch_shapes=[pltpu.VMEM(a.shape, LOW) for a in blocks] + [pltpu.SemaphoreType.DMA((3,))],
        compiler_params=kernel_params(24),
        cost_estimate=cost(50 * 10**9, 12 * 1024 * 1024),
        name="weight_grads",
    )(info, *[far(a) for a in blocks], sums)


def fold_kernel(held, came, kept, sent):
    half = (held.shape[0] - SIDES) // 2
    full = 2 * half
    kept[0:half, :] = held[0:half, :].astype(F32) + came[0:half, :].astype(F32)
    sent[0:half, :] = (held[half:full, :].astype(F32) + came[half:full, :].astype(F32)).astype(LOW)
    sides = held[full : full + SIDES, :].astype(LOW).astype(F32) + came[full : full + SIDES, :].astype(F32)
    kept[half : half + SIDES, :] = sides
    sent[half : half + SIDES, :] = sides.astype(LOW)


def fold(held, came):
    half = (held.shape[0] - SIDES) // 2 + SIDES
    outs = (shaped((half, 128), F32), shaped((half, 128), LOW))
    return pl.pallas_call(
        fold_kernel,
        out_shape=outs,
        in_specs=[full_spec(held.shape), full_spec(came.shape)],
        out_specs=tuple(full_spec(a.shape) for a in outs),
        compiler_params=kernel_params(20),
        cost_estimate=cost(0, 1024 * 1024),
        name="fold_gradients",
    )(held, came)


def close_kernel(held, came, *outs):
    qus, od, squares = outs[:GROUP], outs[GROUP], outs[GROUP + 1]
    rows = qus[0].shape[0] - SIDES
    full = held.shape[0] - SIDES
    sides = held[full : full + SIDES, :].astype(LOW).astype(F32) + came[full : full + SIDES, :].astype(F32)
    lanes = jnp.zeros((8, 128), F32)
    begin = 0
    for piece in (*qus, od):
        length = rows if piece is not od else od.shape[0]
        here = slice(begin, begin + length)
        begin += length
        total = held[here, :].astype(F32) + came[here, :].astype(F32)
        piece[0:length, :] = total.astype(LOW)
        if piece is not od:
            piece[rows : rows + SIDES, :] = sides.astype(LOW)
        lanes = lanes + jnp.sum((total * total).reshape(length // 8, 8, 128), axis=0)
    squares[...] = lanes


def close(ring, held, came):
    rows = QU_TILES * (D // ring.count)
    outs = [shaped((rows + SIDES, 128), LOW)] * GROUP
    outs += [shaped((OD_TILES * (SIDE + UNITS) // ring.size, 128), LOW), shaped((8, 128), F32)]
    return pl.pallas_call(
        close_kernel,
        out_shape=tuple(outs),
        in_specs=[full_spec(held.shape), full_spec(came.shape)],
        out_specs=tuple(full_spec(a.shape) for a in outs),
        compiler_params=kernel_params(16),
        cost_estimate=cost(0, 1024 * 1024),
        name="close_gradients",
    )(held, came)


def join_kernel(info, *refs):
    core = info[0]
    firsts, seconds, (od_first, od_second), outs = refs[:4], refs[4:8], refs[8:10], refs[10:]
    sent, vec, squares = outs
    rows = firsts[0].shape[0] - SIDES
    lanes = jnp.zeros((8, 128), F32)
    sides = []
    for pieces in (firsts, seconds):
        parts = [a[rows : rows + SIDES, :].astype(F32) for a in pieces]
        total = (parts[0] + parts[1]) + (parts[2] + parts[3])
        lanes = lanes + jnp.sum((total * total).reshape(SIDES // 8, 8, 128), axis=0)
        sides.append(total)
    squares[...] = lanes
    vec[...] = jnp.where(core == 0, sides[0], sides[1])

    def write(pieces, od):
        for r in range(GROUP):
            sent[r * rows : (r + 1) * rows, :] = pieces[r][0:rows, :]
        sent[GROUP * rows :, :] = od[...]

    pl.when(core == 0)(functools.partial(write, seconds, od_second))
    pl.when(core == 1)(functools.partial(write, firsts, od_first))


def join(info, firsts, seconds, od_first, od_second):
    rows = firsts[0].shape[0] - SIDES
    outs = (shaped((GROUP * rows + od_first.shape[0], 128), LOW), shaped((SIDES, 128), F32), shaped((8, 128), F32))
    blocks = (*firsts, *seconds, od_first, od_second)
    return pl.pallas_call(
        join_kernel,
        out_shape=outs,
        in_specs=[smem_spec()] + [full_spec(a.shape) for a in blocks],
        out_specs=tuple(full_spec(a.shape) for a in outs),
        compiler_params=kernel_params(16),
        cost_estimate=cost(0, 1024 * 1024),
        name="join_members",
    )(info, *blocks)


def adam_update(weight, grad, first, second, factor, rate):
    clipped = grad * factor
    first_new = BETA_ONE * first + (1.0 - BETA_ONE) * clipped
    second_new = BETA_TWO * second + (1.0 - BETA_TWO) * clipped * clipped
    first_hat = first_new / (1.0 - BETA_ONE**STEP)
    second_hat = second_new / (1.0 - BETA_TWO**STEP)
    weight_new = weight - rate * (
        first_hat / (jnp.sqrt(second_hat) + ADAM_EPS) + WEIGHT_DECAY * weight
    )
    return (weight_new, first_new, second_new)


def mixed_tile(tile, member):
    at = tile * 128
    if at >= 3 * SIDE:
        return 2, up_column(member, at - 3 * SIDE)
    width = SIDE // SPREAD
    kind, within = at // SIDE, at % SIDE
    return 0, qkv_column(kind, within // width, member) + within % width


def adam_kernel(info, factor_ref, *refs):
    core, group = info[0], info[1]
    step = pl.program_id(0)
    factor = factor_ref[0]
    qus, refs = (refs[:4], refs[4:8]), refs[8:]
    ods, came, refs = refs[:2], refs[2], refs[3:]
    olds, news = refs[:12], refs[12:]
    few, many = olds[0].shape[1], olds[9].shape[1]
    rows = (qus[0][0].shape[0] - SIDES) // QU_TILES
    od_rows = ods[0].shape[0] // OD_TILES

    def update(which, column, grad):
        columns = slice(column, column + 128)
        weight, first, second = [olds[3 * which + i][0, :, columns] for i in range(3)]
        fresh = adam_update(weight, grad.astype(F32), first, second, factor, LEARN_RATE)
        for i in range(3):
            news[3 * which + i][0, :, columns] = fresh[i]

    def rows_of(ref, begin, length):
        return ref[pl.ds(pl.multiple_of(begin + step * length, 16), length), :]

    def both_halves(here):
        for half in range(2):
            for tile in range(OD_TILES):
                column = half * (D // 2) + tile * 128
                ref, begin = (ods[here], 0) if half == here else (came, GROUP * QU_TILES * rows)
                begin = begin + tile * od_rows
                update(3, column, rows_of(ref, begin, many))
                update(1, column, rows_of(ref, begin + od_rows - rows, few))
            for member in range(GROUP):
                if half == here:
                    for g in range(GROUP):

                        @pl.when(group == g)
                        def _(ref=qus[here][member ^ g]):
                            for tile in range(QU_TILES):
                                which, column = mixed_tile(half * QU_TILES + tile, member)
                                update(which, column, rows_of(ref, tile * rows, few))
                else:
                    for tile in range(QU_TILES):
                        which, column = mixed_tile(half * QU_TILES + tile, member)
                        begin = ((group ^ member) * QU_TILES + tile) * rows
                        update(which, column, rows_of(came, begin, few))

    for here in range(2):
        pl.when(core == here)(functools.partial(both_halves, here))


def adam(info, factor, qus, ods, came, olds):
    steps = max(1, olds[0].shape[1] // 16)

    def master(a):
        return pl.BlockSpec((1, a.shape[1] // steps, a.shape[2]), lambda i: (0, i, 0))

    grads = (*qus[0], *qus[1], *ods, came)
    return pl.pallas_call(
        adam_kernel,
        grid=(steps,),
        out_shape=tuple(shaped(a.shape, F32) for a in olds),
        in_specs=[smem_spec(), smem_spec()]
        + [full_spec(a.shape) for a in grads]
        + [master(a) for a in olds],
        out_specs=tuple(master(a) for a in olds),
        compiler_params=kernel_params(32),
        name="adamw",
    )(info, factor, *grads, *[far(a) for a in olds])


def doc_tables(lengths, rows):
    seqs = lengths.shape[0]
    ends = jnp.cumsum(lengths, axis=1)
    places = jnp.arange(rows, dtype=jnp.int32)
    past = places[None, :, None] >= ends[:, None, :]
    begins = jnp.sum(jnp.where(past, lengths[:, None, :], 0), axis=2)
    position = (places[None, :] - begins).reshape(seqs * rows, 1)
    half = ROT // 2
    inverse = 10000.0 ** (-(jnp.arange(half, dtype=F32) * 2.0) / ROT)
    lanes = jnp.concatenate([inverse, inverse, jnp.zeros(HEAD_DIM - ROT, F32)])
    angles = position.astype(F32) * jnp.concatenate([lanes, lanes])[None, :]
    allowed = (places[None, None, :] <= places[None, :, None]) & (places[None, None, :] >= begins[:, :, None])
    mask = jnp.where(allowed, 0.0, -1e30).reshape(seqs * rows, rows).astype(F32)
    return jnp.cos(angles), jnp.sin(angles), mask


def shards(
    x_in,
    cotangent,
    doc_lengths,
    w_qkv,
    w_out,
    w_up,
    w_down,
    vectors,
    m_qkv,
    m_out,
    m_up,
    m_down,
    m_vectors,
    v_qkv,
    v_out,
    v_up,
    v_down,
    v_vectors,
):
    place = Place()
    ring, core, group, spot = place.ring, place.core, place.group, place.spot
    info = place.info()
    local_rows, width = x_in.shape
    seqs, docs = doc_lengths.shape
    rows = local_rows // seqs
    in_rows = w_qkv.shape[1]
    shard = vectors.shape[1]
    members = range(1, GROUP)

    vec_block = jnp.pad(vectors[0].astype(LOW), (0, in_rows * 128 - shard)).reshape(in_rows, 128)
    keep_qu, send_qu, keep_od, send_od = pack(info, w_qkv, w_out, w_up, w_down, vec_block)
    came_qu = place.sibling(send_qu)
    came_od = place.sibling(send_od)

    def member_columns(block, *waited):
        qu = jnp.where(core == block, keep_qu, came_qu)
        sent = [after(take(qu, group ^ r), *waited) for r in members]
        return [take(qu, group)] + [place.member(a, r) for a, r in zip(sent, members)]

    def gather(block, *waited):
        late = after(block, *waited)
        return [block] + [place.member(late, r) for r in members]

    def to_owners(slots):
        return [slots[0]] + [place.member(slots[r], r) for r in members]

    def total_of(slots):
        return sum(a.astype(F32) for a in slots)

    def block_vectors(parts):
        pieces = jnp.concatenate([a[:, :, 0 : -(-shard // 128), PART:] for a in parts])
        pieces = pieces.reshape(ring.size * GROUP, -1)[:, :shard]
        dp = jnp.arange(ring.count, dtype=jnp.int32)
        difference = ring.spot_of(dp) ^ spot
        slot = jnp.where(core == 0, ring.slot(difference, 0), ring.slot(difference, 1))
        vec = jnp.take(pieces, slot * GROUP + (ring.group_of(dp) ^ group), axis=0, mode="clip")
        vec = vec.reshape(-1).astype(F32)
        b_qkv, b_out, b_up, b_down, gain, ln_bias = jnp.split(
            vec, [3 * D, 4 * D, 4 * D + FF, 5 * D + FF, 6 * D + FF]
        )
        b_qkv = take(b_qkv.reshape(3 * SPREAD, GROUP, -1), group, 1).reshape(1, -1)
        b_up = take(b_up.reshape(SPREAD, GROUP, -1), group, 1).reshape(1, -1)
        return (b_qkv, b_up, gain[None], ln_bias[None]), (b_out + b_down)[None], gain[None]

    x_own = take(x_in.reshape(2, rows, width), core)
    cot_own = take(cotangent.reshape(2, rows, width), core)
    len_own = take(doc_lengths, core)
    len_rows = jnp.zeros((16, width), LOW).at[0, :docs].set(len_own.astype(LOW))
    x_sent = jnp.concatenate([x_own, len_rows])

    qu_came = member_columns(0)
    qu_own = jnp.stack(qu_came)[None]
    x_group = gather(x_sent, qu_came[1])
    qu_next = member_columns(1, *x_group[2:])
    cot_late = after(cot_own, *x_group[2:])
    cot_group = [cot_own] + [place.member(cot_late, r) for r in members[:-1]]
    od_own = jnp.where(core == 0, keep_od, came_od)[None]
    od = [jnp.concatenate([od_own, place.across(od_own, 0)])]
    qu = [jnp.concatenate([qu_own, place.across(qu_own, 0)])]
    for step in range(1, ring.bits):
        od.append(place.across(jnp.concatenate(od), step))
        qu.append(place.across(jnp.concatenate(qu), step))
    qu_sibling = [place.sibling(a) for a in qu[:-1]] + [place.sibling(after(qu[-1], *x_group[1:]))]
    parts_first = (*qu, *od, *qu_sibling, *(place.sibling(a) for a in od))
    lengths = jnp.stack([a[rows, :docs] for a in x_group]).astype(jnp.int32)
    tables = doc_tables(lengths, rows)
    vecs_first, bias_first, gain_first = block_vectors(qu)

    od_own = after(jnp.where(core == 1, keep_od, came_od)[None], qu[-1])
    od_late = [jnp.concatenate([od_own, place.across(od_own, 0)])]
    x_group[0] = after(x_group[0], od_late[0])
    first = forward(ring, info, parts_first, x_group, tables, vecs_first, rows)
    kept_first, tables = first[GROUP:], first[-3:]
    came = to_owners([first[0]] + [after(a, *cot_group[1:]) for a in first[1:GROUP]])
    cot_group.append(place.member(after(cot_own, first[0]), GROUP - 1))
    came[1] = after(came[1], cot_group[-1])
    hidden_first = (x_own.astype(F32) + total_of(came) + bias_first).astype(LOW)
    hidden_group = gather(hidden_first)
    qu_own = jnp.stack([qu_next[0]] + [after(a, first[0]) for a in qu_next[1:]])[None]
    qu_late = [jnp.concatenate([qu_own, after(place.across(qu_own, 0), hidden_first)])]
    for step in range(1, ring.bits):
        od_late.append(after(place.across(jnp.concatenate(od_late), step), *hidden_group[1:]))
        qu_late.append(after(place.across(jnp.concatenate(qu_late), step), *hidden_group[1:]))
    qu_sibling, od_sibling = [
        [place.sibling(after(a, *hidden_group[1:])) for a in late] for late in (qu_late, od_late)
    ]
    parts_second = (*qu_late, *od_late, *qu_sibling, *od_sibling)
    vecs_second, bias_second, gain_second = block_vectors(qu_late)
    second = middle(ring, info, parts_second, hidden_group, cot_group, tables, vecs_second, rows)
    sums_second, y_second, mixed_second, active_second, dqu_second, grad_second = second[GROUP : GROUP + 6]
    z_second = second[GROUP + 6 :]

    def rows_backward(rows_low, grad_low, dy, gain):
        rows_now = rows_low.astype(F32)
        centered = rows_now - jnp.mean(rows_now, axis=-1, keepdims=True)
        variance = jnp.mean(centered * centered, axis=-1, keepdims=True)
        inverse_std = lax.rsqrt(variance + NORM_EPS)
        normed = centered * inverse_std
        scaled = dy * gain
        inner_mean = jnp.mean(scaled, axis=-1, keepdims=True)
        inner_cross = jnp.mean(scaled * normed, axis=-1, keepdims=True)
        return (grad_low.astype(F32) + inverse_std * (scaled - inner_mean - normed * inner_cross)).astype(LOW)

    def to_members(pieces):
        return [pieces[0]] + [place.member(pieces[r], r) for r in members]

    steps = list(reversed(range(ring.bits)))

    def ring_fold(held, *waited):
        kept, sent = held
        for step in steps[:-1]:
            kept, sent = fold(kept, after(place.across(sent, step), *waited))
        return kept, sent

    dy_second = to_owners(second[:GROUP])
    grads = weight_grads(ring, info, mixed_second, active_second, grad_second, y_second, dqu_second, sums_second)
    mid_grad = rows_backward(hidden_first, cot_own, total_of(dy_second), gain_second)
    mid_group = gather(mid_grad)
    sent = place.sibling(after(grads[1], *dy_second[1:]))
    second_held = fold(grads[0], after(sent, *mid_group[1:]))

    mid_late = [after(mid_group[0], *second_held)] + mid_group[1:]
    back = backward(ring, info, mid_late, kept_first, rows)
    keep, send = back[GROUP:]
    second_held = ring_fold(second_held, send)
    z_came = to_owners([z_second[0]] + [after(a, *mid_group[1:]) for a in z_second[1:]])
    send = after(send, *second_held, *z_came[1:])
    kept, sent = second_held
    *qu_second, od_second, squares_second = close(ring, kept, place.across(sent, 0))
    qu_slots_second = to_members(qu_second)
    kept, sent = ring_fold(fold(keep, place.sibling(send)))
    start_came = to_owners(back[:GROUP])
    *qu_first, od_first, squares_first = close(ring, kept, place.across(after(sent, *start_came[1:]), 0))
    qu_slots_first = to_members(qu_first)
    grads_sent, vec, vec_squares = join(info, qu_slots_first, qu_slots_second, od_first, od_second)
    start_came[1:] = [after(a, grads_sent) for a in start_came[1:]]
    start_grad = rows_backward(x_own, mid_grad, total_of(start_came), gain_first)
    hidden_second = (hidden_first.astype(F32) + total_of(z_came) + bias_second).astype(LOW)

    def all_sum(block, first, last):
        hops = [place.sibling]
        hops += [functools.partial(place.across, step=step) for step in range(ring.bits)]
        hops += [functools.partial(place.member, distance=1), functools.partial(place.member, distance=2)]
        for hop in hops[first:last]:
            block = block + hop(block)
        return block

    squares = all_sum(squares_first + squares_second, 0, 2)
    squares = all_sum(after(squares, *qu_slots_first[1:]), 2, None)
    squares = jnp.sum(squares + vec_squares)
    grad_norm = jnp.sqrt(squares)
    factor = jnp.minimum(1.0, CLIP_LEVEL / (grad_norm + 1e-06))

    def own_block(one, two):
        came = place.sibling(jnp.where(core == 0, two, one))
        mine = jnp.where(core == 0, one, two)
        return [jnp.where(core == h, mine, came) for h in range(2)]

    grads_came = place.sibling(grads_sent)
    vec_share = after(vec, grads_sent).reshape(-1)[: ring.count * shard].reshape(ring.count, shard)
    vec_share = take(vec_share, lax.axis_index("dp"))[None]
    olds = (w_qkv, m_qkv, v_qkv, w_out, m_out, v_out, w_up, m_up, v_up, w_down, m_down, v_down)
    qus = (qu_slots_first, qu_slots_second)
    news = adam(info, factor[None], qus, (od_first, od_second), grads_came, olds)
    new_vec = adam_update(vectors, vec_share, m_vectors, v_vectors, factor, VECTOR_RATE)

    outputs = own_block(jnp.stack([hidden_first, start_grad]), jnp.stack([hidden_second, mid_grad]))
    outputs = jnp.concatenate(outputs, axis=1)
    hidden_out, input_grads = outputs[:1], outputs[1:]
    return (
        hidden_out,
        input_grads,
        *(news[3 * i] for i in range(4)),
        new_vec[0],
        *(news[3 * i + 1] for i in range(4)),
        new_vec[1],
        *(news[3 * i + 2] for i in range(4)),
        new_vec[2],
        grad_norm,
    )


def solution(mesh):
    return jax.shard_map(
        shards,
        mesh=mesh,
        in_specs=(
            P("dp", None),
            P("dp", None),
            P("dp", None),
            P("section", "dp", None),
            P("section", "dp", None),
            P("section", "dp", None),
            P("section", "dp", None),
            P("section", "dp"),
            P("section", "dp", None),
            P("section", "dp", None),
            P("section", "dp", None),
            P("section", "dp", None),
            P("section", "dp"),
            P("section", "dp", None),
            P("section", "dp", None),
            P("section", "dp", None),
            P("section", "dp", None),
            P("section", "dp"),
        ),
        out_specs=(
            P("section", "dp", None),
            P("section", "dp", None),
            P("section", "dp", None),
            P("section", "dp", None),
            P("section", "dp", None),
            P("section", "dp", None),
            P("section", "dp"),
            P("section", "dp", None),
            P("section", "dp", None),
            P("section", "dp", None),
            P("section", "dp", None),
            P("section", "dp"),
            P("section", "dp", None),
            P("section", "dp", None),
            P("section", "dp", None),
            P("section", "dp", None),
            P("section", "dp"),
            P(),
        ),
        check_vma=False,
    )
```

```python
import functools

import jax
import jax.numpy as jnp
from jax import lax
from jax.experimental import pallas as pl
from jax.experimental.pallas import tpu as pltpu
from jax.sharding import PartitionSpec as P

D = 1024
FF = 4096
HEADS = 16
HEAD_DIM = 64
ROT = 16
STEP = 10


NORM_EPS = 1e-05
BETA_ONE = 0.9
BETA_TWO = 0.95
LEARN_RATE = 0.05
VECTOR_RATE = 0.3
WEIGHT_DECAY = 0.01
CLIP_LEVEL = 1.0
ADAM_EPS = 1e-08

AXES = ("section", "dp")
GROUP = 4
SPREAD = 1
LOW = jnp.bfloat16
F32 = jnp.float32
SIDE = D // GROUP
UNITS = FF // GROUP
MIXED = 3 * SIDE + UNITS
PART = MIXED // 2
WIRE = PART + 128


class Ring:
    def __init__(self, count):
        self.count = count
        self.low = count // (GROUP * SPREAD)
        self.size = SPREAD * self.low
        self.bits = self.size.bit_length() - 1

    def index(self, g, t):
        return ((t // self.low) * GROUP + g) * self.low + t % self.low

    def group_of(self, dp):
        return (dp // self.low) % GROUP

    def spot_of(self, dp):
        return (dp // (GROUP * self.low)) * self.low + dp % self.low

    def order(self, core):
        steps = list(range(self.bits))
        if SPREAD > 1 or core == 1:
            steps.reverse()
        return steps

    def turn(self, slot, core):
        return sum(((slot >> s) & 1) << b for s, b in enumerate(self.order(core)))

    def slot(self, difference, core):
        return sum(((difference >> b) & 1) << s for s, b in enumerate(self.order(core)))


class Place:
    def __init__(self):
        self.ring = Ring(lax.axis_size("dp"))
        self.core = lax.axis_index("section")
        dp = lax.axis_index("dp")
        self.group = self.ring.group_of(dp)
        self.spot = self.ring.spot_of(dp)

    def info(self):
        return jnp.stack([self.core, self.group, self.spot]).astype(jnp.int32)

    def move(self, block, where):
        ring = self.ring
        route = []
        for core in range(2):
            for g in range(GROUP):
                for t in range(ring.size):
                    c, h, u = where(core, g, t)
                    route.append((core * ring.count + ring.index(g, t), c * ring.count + ring.index(h, u)))
        return lax.ppermute(block, AXES, route)

    def sibling(self, block):
        return self.move(block, lambda c, g, t: (1 - c, g, t))

    def member(self, block, distance):
        return self.move(block, lambda c, g, t: (c, g ^ distance, t))

    def across(self, block, step):
        return self.move(block, lambda c, g, t: (c, g, t ^ (1 << self.ring.order(c)[step])))


def take(block, index, axis=0):
    return lax.dynamic_index_in_dim(block, index, axis, keepdims=False)


def after(block, *waited):
    return lax.optimization_barrier((block, waited))[0]


def dot(left, right):
    return jnp.dot(left, right, preferred_element_type=F32)


def dot_cols(left, right):
    return lax.dot_general(left, right, (((1,), (1,)), ((), ())), preferred_element_type=F32)


def dot_rows(left, right):
    return lax.dot_general(left, right, (((0,), (0,)), ((), ())), preferred_element_type=F32)


def full_spec(shape):
    return pl.BlockSpec(shape, lambda *_: (0,) * len(shape))


def far_spec():
    return pl.BlockSpec(memory_space=pltpu.HBM)


def far(block):
    return pltpu.with_memory_space_constraint(block, pltpu.HBM)


def any_spec():
    return pl.BlockSpec(memory_space=pl.ANY)


def smem_spec():
    return pl.BlockSpec(memory_space=pltpu.SMEM)


def shaped(shape, dtype):
    return jax.ShapeDtypeStruct(shape, dtype)


def kernel_params(mebibytes):
    return pltpu.CompilerParams(vmem_limit_bytes=mebibytes * 1024 * 1024)


def up_pieces():
    run = UNITS // SPREAD
    cuts = sorted({0, PART - 3 * SIDE, UNITS} | {run * i for i in range(SPREAD)})
    pieces = []
    for begin, end in zip(cuts[:-1], cuts[1:]):
        column = 3 * SIDE + begin
        pieces.append((begin, column // PART, column % PART, end - begin))
    return pieces


def up_column(g, local):
    run = UNITS // SPREAD
    return (local // run * GROUP + g) * run + local % run


def qkv_column(kind, run, g):
    width = SIDE // SPREAD
    return ((kind * SPREAD + run) * GROUP + g) * width


def pack_kernel(info, qkv_hbm, out_hbm, up_hbm, down_hbm, vec, keep_qu, send_qu, keep_od, send_od, *scratch):
    w_qkv, w_out, w_up, w_down, sems = scratch
    pairs = ((qkv_hbm, w_qkv), (up_hbm, w_up), (down_hbm, w_down), (out_hbm, w_out))
    copies = [pltpu.make_async_copy(far.at[0], near, sems.at[i]) for i, (far, near) in enumerate(pairs)]
    for copy in copies:
        copy.start()
    rows = w_qkv.shape[0]
    ff_rows = w_down.shape[0]
    width = SIDE // SPREAD
    core = info[0]

    def write_qu(halves):
        for g in range(GROUP):
            for kind in range(3):
                for run in range(SPREAD):
                    at = (kind * SPREAD + run) * width
                    column = qkv_column(kind, run, g)
                    halves[0][g, :, at : at + width] = w_qkv[:, column : column + width].astype(LOW)
            for local, half, at, length in up_pieces():
                column = up_column(g, local)
                halves[half][g, :, at : at + length] = w_up[:, column : column + length].astype(LOW)
            for half in range(2):
                halves[half][g, :, PART:WIRE] = vec[...]

    def write_od(halves):
        for half in range(2):
            columns = slice(half * (D // 2), (half + 1) * (D // 2))
            halves[half][0:ff_rows] = w_down[:, columns].astype(LOW)
            halves[half][ff_rows : ff_rows + rows] = w_out[:, columns].astype(LOW)

    for first, last, write, kept, sent in ((0, 2, write_qu, keep_qu, send_qu), (2, 4, write_od, keep_od, send_od)):
        for copy in copies[first:last]:
            copy.wait()
        pl.when(core == 0)(functools.partial(write, (kept, sent)))
        pl.when(core == 1)(functools.partial(write, (sent, kept)))


def pack(info, w_qkv, w_out, w_up, w_down, vec):
    rows, ff_rows = w_qkv.shape[1], w_down.shape[1]
    qu = shaped((GROUP, rows, WIRE), LOW)
    od = shaped((ff_rows + rows, D // 2), LOW)
    return pl.pallas_call(
        pack_kernel,
        out_shape=(qu, qu, od, od),
        in_specs=[smem_spec()] + [far_spec()] * 4 + [full_spec(vec.shape)],
        out_specs=tuple(full_spec(a.shape) for a in (qu, qu, od, od)),
        scratch_shapes=[pltpu.VMEM(a.shape[1:], F32) for a in (w_qkv, w_out, w_up, w_down)]
        + [pltpu.SemaphoreType.DMA((4,))],
        compiler_params=kernel_params(20),
        name="pack_weights",
    )(info, far(w_qkv), far(w_out), far(w_up), far(w_down), vec)


def stack_kernel(*refs):
    for i, ref in enumerate(refs[:-1]):
        refs[-1][0, i] = ref[...]


def stack_members(pieces):
    out = shaped((1, len(pieces), *pieces[0].shape), LOW)
    return pl.pallas_call(
        stack_kernel,
        out_shape=out,
        in_specs=[full_spec(a.shape) for a in pieces],
        out_specs=full_spec(out.shape),
        compiler_params=kernel_params(16),
        cost_estimate=cost(50 * 10**9, 1024 * 1024),
        name="stack_members",
    )(*pieces)


def weight_copies(ring, info, parts, wqu, wout, wdown, sems):
    core, group, spot = info[0], info[1], info[2]
    qu_copies, od_copies = [], []
    count = len(parts) // 4
    for which in range(2):
        half = core if which == 0 else 1 - core
        qu_at = pl.multiple_of(half * PART, 128)
        od_at = pl.multiple_of(half * (D // 2), 128)
        slot = 0
        for piece in range(count):
            qu, od = parts[2 * count * which + piece], parts[2 * count * which + count + piece]
            rows = qu.shape[2]
            ff_rows = od.shape[1] - rows
            for i in range(qu.shape[0]):
                straight, turned = ring.turn(slot, 0), ring.turn(slot, 1)
                there = spot ^ (straight + half * (turned - straight))
                slot += 1
                ff_row = pl.multiple_of(there * ff_rows, ff_rows)
                out_row = pl.multiple_of(there * rows, rows)
                far = wdown.at[pl.ds(ff_row, ff_rows), pl.ds(od_at, D // 2)]
                od_copies.append(pltpu.make_async_copy(od.at[i, pl.ds(0, ff_rows)], far, sems.at[0]))
                far = wout.at[pl.ds(out_row, rows), pl.ds(od_at, D // 2)]
                od_copies.append(pltpu.make_async_copy(od.at[i, pl.ds(ff_rows, rows)], far, sems.at[0]))
                for r in range(GROUP):
                    row = pl.multiple_of(ring.index(group ^ r, there) * rows, rows)
                    far = wqu.at[pl.ds(row, rows), pl.ds(qu_at, PART)]
                    qu_copies.append(pltpu.make_async_copy(qu.at[i, r, :, pl.ds(0, PART)], far, sems.at[1]))
    return qu_copies, od_copies


def head_masks(dtype):
    lane = lax.broadcasted_iota(jnp.int32, (1, SIDE), 1) // HEAD_DIM
    return [(lane == h).astype(dtype) for h in range(SIDE // HEAD_DIM)]


def by_head(parts):
    lane = lax.broadcasted_iota(jnp.int32, (1, SIDE), 1) // HEAD_DIM
    total = parts[-1]
    for h in range(len(parts) - 2, -1, -1):
        total = jnp.where(lane == h, parts[h], total)
    return total


def turning(cosine, sine, back):
    lane = lax.broadcasted_iota(jnp.int32, sine.shape, 1) % HEAD_DIM
    first = jnp.where(lane < ROT // 2, sine, 0.0)
    second = jnp.where(lane < ROT // 2, 0.0, sine)
    if back:
        second = -second
    else:
        first = -first
    wide = SIDE // cosine.shape[1]
    return [jnp.concatenate([a] * wide, axis=1) for a in (cosine, first, second)]


def turn(part, tables):
    cosine, first, second = tables
    ahead = pltpu.roll(part, SIDE - ROT // 2, 1)
    behind = pltpu.roll(part, ROT // 2, 1)
    return part * cosine + ahead * first + behind * second


def normalise(rows):
    centered = rows - jnp.mean(rows, axis=-1, keepdims=True)
    variance = jnp.mean(centered * centered, axis=-1, keepdims=True)
    return centered * lax.rsqrt(variance + NORM_EPS)


def no_wait():
    pass


def forward_part(x_refs, tables, vecs, wqu, wout, wdown, kept, z_refs, waits, done, normed_ref=None):
    cosine, sine, mask = tables
    b_qkv, b_up, gain, ln_bias = vecs
    y, qkv, probs, mixed, active, slope = kept
    rows = z_refs[0].shape[0]
    for r in range(GROUP):
        normed = normalise(x_refs[r][0:rows, :].astype(F32))
        if normed_ref is not None:
            normed_ref[r * rows : (r + 1) * rows, :] = normed
        y[r * rows : (r + 1) * rows, :] = (normed * gain[...] + ln_bias[...]).astype(LOW)
    done(0)
    waits[0]()
    waits[2]()
    forth = turning(cosine[...], sine[...], False)
    for kind in range(3):
        columns = slice(kind * SIDE, (kind + 1) * SIDE)
        part = dot(y[...], wqu[:, columns]) + b_qkv[:, columns]
        if kind < 2:
            part = turn(part, forth)
        qkv[:, columns] = part.astype(LOW)
    done(1)
    masks = head_masks(LOW)
    heads = len(masks)
    for r in range(GROUP):
        here = slice(r * rows, (r + 1) * rows)
        query, keys, values = [qkv[here, k * SIDE : (k + 1) * SIDE] for k in range(3)]
        stacked = jnp.concatenate([query * m for m in masks], axis=0)
        scores = dot_cols(stacked, keys) * HEAD_DIM ** (-0.5)
        scores = scores.reshape(heads, rows, rows) + mask[here, :][None]
        expo = jnp.exp(scores - jnp.max(scores, axis=-1, keepdims=True))
        prob = expo / jnp.sum(expo, axis=-1, keepdims=True)
        prob = prob.reshape(heads * rows, rows)
        probs[r * heads * rows : (r + 1) * heads * rows, :] = prob
        full = dot(prob.astype(LOW), values)
        mixed[here, :] = by_head([full[h * rows : (h + 1) * rows] for h in range(heads)]).astype(LOW)
    done(2)
    done(3)
    tile = 256
    for at in range(0, UNITS, tile):
        hidden = dot(y[...], wqu[:, 3 * SIDE + at : 3 * SIDE + at + tile]) + b_up[:, at : at + tile]
        share = 0.5 * (1.0 + lax.erf(hidden * (0.5**0.5)))
        density = jnp.exp(-0.5 * hidden * hidden) * (0.5 / jnp.pi) ** 0.5
        active[:, at : at + tile] = (hidden * share).astype(LOW)
        slope[:, at : at + tile] = share + hidden * density
    done(4)
    done(5)
    waits[1]()
    for at in range(0, D, tile):
        branch = dot(mixed[...], wout[:, at : at + tile]) + dot(active[...], wdown[:, at : at + tile])
        for r in range(GROUP):
            z_refs[r][:, at : at + tile] = branch[r * rows : (r + 1) * rows].astype(LOW)


def backward_part(grad, normed, tables, wqu, wout, wdown, kept, dqu, dy_refs, sums, waits, done):
    cosine, sine, _ = tables
    y, qkv, probs, mixed, active, slope = kept
    rows = grad.shape[0] // GROUP
    tile = 256
    waits[0]()
    dmixed = dot_cols(grad[...], wout[...]).astype(LOW)
    for at in range(0, UNITS, tile):
        dactive = dot_cols(grad[...], wdown[at : at + tile, :])
        dhidden = (dactive * slope[:, at : at + tile]).astype(LOW)
        dqu[:, 3 * SIDE + at : 3 * SIDE + at + tile] = dhidden
    waits[1]()
    masks = head_masks(LOW)
    heads = len(masks)
    back = turning(cosine[...], sine[...], True)
    for r in range(GROUP):
        here = slice(r * rows, (r + 1) * rows)
        query, keys, values = [qkv[here, k * SIDE : (k + 1) * SIDE] for k in range(3)]
        dstack = jnp.concatenate([dmixed[here] * m for m in masks], axis=0)
        dprob = dot_cols(dstack, values)
        prob = probs[r * heads * rows : (r + 1) * heads * rows, :]
        dvalues = dot_rows(prob.astype(LOW), dstack)
        dscore = (prob * (dprob - jnp.sum(prob * dprob, axis=-1, keepdims=True))).astype(LOW)
        full = dot(dscore, keys)
        dquery = by_head([full[h * rows : (h + 1) * rows] for h in range(heads)])
        dkeys = dot_rows(dscore, jnp.concatenate([query * m for m in masks], axis=0))
        scale = HEAD_DIM ** (-0.5)
        slot_tables = [a[here] for a in back]
        dqu[here, 0:SIDE] = turn(dquery * scale, slot_tables).astype(LOW)
        dqu[here, SIDE : 2 * SIDE] = turn(dkeys * scale, slot_tables).astype(LOW)
        dqu[here, 2 * SIDE : 3 * SIDE] = dvalues.astype(LOW)
    done()
    for at in range(0, MIXED, tile):
        sums[:, at : at + tile] = jnp.sum(dqu[:, at : at + tile].astype(F32), axis=0, keepdims=True)
    waits[2]()
    for at in range(0, D, tile):
        dy = dot_cols(dqu[...], wqu[at : at + tile, :])
        for r in range(GROUP):
            dy_refs[r][:, at : at + tile] = dy[r * rows : (r + 1) * rows].astype(LOW)
        own = grad[0:rows, at : at + tile].astype(F32)
        for i, terms in enumerate((own, dy * normed[:, at : at + tile], dy)):
            begin = MIXED + i * D + at
            sums[:, begin : begin + tile] = jnp.sum(terms, axis=0, keepdims=True)


def kept_shapes(tokens, rows):
    return [
        ((tokens, D), LOW),
        ((tokens, 3 * SIDE), LOW),
        ((tokens * (SIDE // HEAD_DIM), rows), F32),
        ((tokens, SIDE), LOW),
        ((tokens, UNITS), LOW),
        ((tokens, UNITS), F32),
    ]


def weight_scratch():
    return [
        pltpu.VMEM((D, MIXED), LOW),
        pltpu.VMEM((SIDE, D), LOW),
        pltpu.VMEM((UNITS, D), LOW),
        pltpu.SemaphoreType.DMA((2,)),
    ]


def waiter(copies):
    def wait():
        for copy in copies:
            copy.wait()

    return wait


def started(pairs, sem):
    copies = [pltpu.make_async_copy(source, target, sem) for source, target in pairs]
    for copy in copies:
        copy.start()
    return waiter(copies)


def table_scratch(tokens, rows):
    return [pltpu.VMEM((tokens, 128), F32), pltpu.VMEM((tokens, 128), F32), pltpu.VMEM((tokens, rows), F32)]


def cost(flops, moved):
    return pl.CostEstimate(flops=2 * flops, bytes_accessed=2 * moved, transcendentals=0)


def leaving(pairs, sems):
    copies = [pltpu.make_async_copy(near, far, sems.at[i]) for i, (near, far) in enumerate(pairs)]

    def go(i):
        copies[i].start()

    return go, waiter(copies)


def forward_kernel(ring, count, info, *refs):
    parts, refs = refs[:count], refs[count:]
    x_refs, refs = refs[:4], refs[4:]
    tables, refs = refs[:3], refs[3:]
    vecs, refs = refs[:4], refs[4:]
    z_refs, refs = refs[:4], refs[4:]
    far_kept, far_weights, far_tables, refs = refs[:7], refs[7:10], refs[10:13], refs[13:]
    kept, refs = refs[:7], refs[7:]
    out_sems, scratch = refs[0], refs[1:]
    weights = scratch[:3]
    qu_copies, od_copies = weight_copies(ring, info, parts, *scratch)
    for copy in qu_copies + od_copies:
        copy.start()
    pairs = [*zip(kept, far_kept), *zip(weights, far_weights), *zip(tables, far_tables)]
    go, out = leaving(pairs, out_sems)
    for i in range(10, 13):
        go(i)

    def qu_in():
        waiter(qu_copies)()
        go(7)

    def od_in():
        waiter(od_copies)()
        go(8)
        go(9)

    def done(i):
        go(i)
        if i == 0:
            go(6)

    forward_part(x_refs, tables, vecs, *weights, kept[:6], z_refs, (qu_in, od_in, no_wait), done, kept[6])
    out()


def forward(ring, info, parts, xs, tables, vecs, rows):
    tokens = GROUP * rows
    shapes = kept_shapes(tokens, rows) + [((tokens, D), F32)]
    away = [*shapes, ((D, MIXED), LOW), ((SIDE, D), LOW), ((UNITS, D), LOW)] + [(a.shape, F32) for a in tables]
    blocks = (*xs, *tables, *vecs)
    return pl.pallas_call(
        functools.partial(forward_kernel, ring, len(parts)),
        out_shape=(*[shaped((rows, D), LOW)] * GROUP, *[pltpu.HBM(*a) for a in away]),
        in_specs=[smem_spec()] + [any_spec()] * len(parts) + [full_spec(a.shape) for a in blocks],
        out_specs=tuple([full_spec((rows, D))] * GROUP + [far_spec()] * len(away)),
        scratch_shapes=[pltpu.VMEM(*a) for a in shapes]
        + [pltpu.SemaphoreType.DMA((len(away),))]
        + weight_scratch(),
        compiler_params=kernel_params(22),
        cost_estimate=cost(2 * tokens * D * (D + 2 * FF // GROUP), 16 * 1024 * 1024),
        name="forward_shard",
    )(info, *parts, *blocks)


def middle_kernel(ring, count, info, *refs):
    parts, refs = refs[:count], refs[count:]
    x_refs, refs = refs[:4], refs[4:]
    g_refs, refs = refs[:4], refs[4:]
    far_tables, refs = refs[:3], refs[3:]
    vecs, refs = refs[:4], refs[4:]
    dy_refs, refs = refs[:4], refs[4:]
    sums, away, refs = refs[0], refs[1:10], refs[10:]
    kept, refs = refs[:6], refs[6:]
    z_refs, tables, refs = refs[:4], refs[4:7], refs[7:]
    (grad, normed, dqu, in_sems, out_sems), scratch = refs[:5], refs[5:]
    rows = z_refs[0].shape[0]
    qu_copies, od_copies = weight_copies(ring, info, parts, *scratch)
    for copy in qu_copies:
        copy.start()
    tables_in = started(zip(far_tables, tables), in_sems.at[0])
    for copy in od_copies:
        copy.start()
    pairs = []
    for r, ref in enumerate(g_refs):
        at = ref.shape[0] - rows
        pairs.append((ref.at[pl.ds(at, rows)], grad.at[pl.ds(r * rows, rows)]))
    grad_in = started(pairs, in_sems.at[1])
    go, out = leaving(list(zip([kept[0], kept[3], kept[4], dqu, grad, *z_refs], away)), out_sems)

    def done(i):
        if i in (0, 3, 4):
            go((0, 3, 4).index(i))

    waits = (waiter(qu_copies), waiter(od_copies), tables_in)
    forward_part(x_refs, tables, vecs, *scratch[:3], kept, z_refs, waits, done, normed)
    grad_in()
    for i in range(4, 9):
        go(i)
    waits = (no_wait, no_wait, no_wait)
    done = functools.partial(go, 3)
    backward_part(grad, normed, tables, *scratch[:3], kept, dqu, dy_refs, sums, waits, done)
    out()


def middle(ring, info, parts, xs, gs, tables, vecs, rows):
    tokens = GROUP * rows
    shapes = kept_shapes(tokens, rows)
    away = [shapes[0], shapes[3], shapes[4], ((tokens, MIXED), LOW), ((tokens, D), LOW)]
    away += [((rows, D), LOW)] * GROUP
    sums = shaped((1, MIXED + 3 * D), F32)
    return pl.pallas_call(
        functools.partial(middle_kernel, ring, len(parts)),
        out_shape=(*[shaped((rows, D), LOW)] * GROUP, sums, *[pltpu.HBM(*a) for a in away]),
        in_specs=[smem_spec()]
        + [any_spec()] * len(parts)
        + [full_spec(a.shape) for a in xs]
        + [far_spec()] * (GROUP + 3)
        + [full_spec(a.shape) for a in vecs],
        out_specs=tuple([full_spec((rows, D))] * GROUP + [full_spec(sums.shape)] + [far_spec()] * len(away)),
        scratch_shapes=[pltpu.VMEM(*a) for a in shapes]
        + [pltpu.VMEM((rows, D), LOW)] * GROUP
        + table_scratch(tokens, rows)
        + [pltpu.VMEM((tokens, D), LOW), pltpu.VMEM((tokens, D), F32), pltpu.VMEM((tokens, MIXED), LOW)]
        + [pltpu.SemaphoreType.DMA((2,)), pltpu.SemaphoreType.DMA((9,))]
        + weight_scratch(),
        compiler_params=kernel_params(27),
        cost_estimate=cost(4 * tokens * D * (D + 2 * FF // GROUP), 16 * 1024 * 1024),
        name="forward_backward_shard",
    )(info, *parts, *xs, *[far(a) for a in (*gs, *tables)], *vecs)


def backward_kernel(ring, info, *refs):
    g_refs, refs = refs[:4], refs[4:]
    far_kept, far_weights, far_tables, refs = refs[:7], refs[7:10], refs[10:13], refs[13:]
    dy_refs, refs = refs[:4], refs[4:]
    (keep, send), refs = refs[:2], refs[2:]
    kept, refs = refs[:7], refs[7:]
    weights, tables, refs = refs[:3], refs[3:6], refs[6:]
    grad, dqu, sums, in_sems = refs
    y, qkv, probs, mixed, active, slope, normed = kept
    wqu, wout, wdown = weights
    far_y, far_qkv, far_probs, far_mixed, far_active, far_slope, far_normed = far_kept
    mixed_in = started([(far_mixed, mixed)], in_sems.at[0])
    active_in = started([(far_active, active)], in_sems.at[1])
    units_in = started([*zip(far_weights[1:], weights[1:]), (far_slope, slope)], in_sems.at[2])
    heads_in = started([(far_qkv, qkv), (far_probs, probs), *zip(far_tables, tables)], in_sems.at[3])
    dy_in = started([(far_weights[0], wqu), (far_normed, normed)], in_sems.at[4])
    y_in = started([(far_y, y)], in_sems.at[5])
    rows = g_refs[0].shape[0]
    for r in range(GROUP):
        grad[r * rows : (r + 1) * rows, :] = g_refs[r][...]
    mixed_in()
    od_part(ring, info, mixed, active, grad, keep, send, active_in)
    waits = (units_in, heads_in, dy_in)
    backward_part(grad, normed, tables, *weights, kept[:6], dqu, dy_refs, sums, waits, no_wait)
    y_in()
    qu_part(ring, info, y, dqu, sums, keep, send)


def backward(ring, info, gs, held, rows):
    tokens = GROUP * rows
    outs = [shaped((rows, D), LOW)] * GROUP + [grads_shape(ring)] * 2
    return pl.pallas_call(
        functools.partial(backward_kernel, ring),
        out_shape=tuple(outs),
        in_specs=[smem_spec()] + [full_spec(a.shape) for a in gs] + [far_spec()] * len(held),
        out_specs=tuple(full_spec(a.shape) for a in outs),
        scratch_shapes=[pltpu.VMEM(a.shape, a.dtype) for a in held]
        + [pltpu.VMEM((tokens, D), LOW), pltpu.VMEM((tokens, MIXED), LOW)]
        + [pltpu.VMEM((1, MIXED + 3 * D), F32), pltpu.SemaphoreType.DMA((6,))],
        compiler_params=kernel_params(28),
        cost_estimate=cost(4 * tokens * D * (D + 2 * FF // GROUP), 16 * 1024 * 1024),
        name="backward_shard",
    )(info, *gs, *[far(a) for a in held])


def slot_in(ring, difference, half):
    straight, turned = ring.slot(difference, 0), ring.slot(difference, 1)
    return straight + half * (turned - straight)


QU_TILES = PART // 128
OD_TILES = D // 2 // 128
SIDES = 112


def slot_rows(ring):
    return GROUP * QU_TILES * (D // ring.count) + OD_TILES * (SIDE + UNITS) // ring.size


def grads_shape(ring):
    return shaped((ring.size * slot_rows(ring) + SIDES, 128), LOW)


def od_part(ring, info, mixed, active, grad, keep, send, active_in):
    core, spot = info[0], info[2]
    out_rows = SIDE // ring.size
    ff_rows = UNITS // ring.size
    ahead = GROUP * QU_TILES * (D // ring.count)
    for i, (out, half) in enumerate(((send, 1 - core), (keep, core))):
        columns = pl.ds(pl.multiple_of(half * (D // 2), D // 2), D // 2)
        part = grad[:, columns]
        block = dot_rows(mixed[...], part).astype(LOW)
        if i == 0:
            active_in()
        for there in range(ring.size):
            slot = slot_in(ring, spot ^ there, half)
            piece = dot_rows(active[:, there * ff_rows : (there + 1) * ff_rows], part).astype(LOW)
            for tile in range(OD_TILES):
                lanes = slice(tile * 128, (tile + 1) * 128)
                row = slot * slot_rows(ring) + ahead + tile * (ff_rows + out_rows)
                out[pl.ds(pl.multiple_of(row, 16), ff_rows), :] = piece[:, lanes]
                row = pl.multiple_of(row + ff_rows, 16)
                out[pl.ds(row, out_rows), :] = block[there * out_rows : (there + 1) * out_rows, lanes]


def vector_rows(group, sums):
    width = SIDE // SPREAD
    run = UNITS // SPREAD
    row = lax.broadcasted_iota(jnp.int32, (SIDES, 128), 0)
    pieces = []
    for at in range(0, 3 * SIDE, 128):
        pieces.append(((at // width * GROUP + group) * (width // 128) + at % width // 128, at))
    for at in range(0, UNITS, 128):
        pieces.append((3 * D // 128 + D // 128 + (at // run * GROUP + group) * (run // 128) + at % run // 128, 3 * SIDE + at))
    tail = (4 * D + FF) // 128
    for i, begin in enumerate((3 * D // 128, tail, tail + D // 128, tail + 2 * D // 128)):
        for at in range(0, D, 128):
            pieces.append((begin + at // 128, MIXED + max(i - 1, 0) * D + at))
    return sum(jnp.where(row == where, sums[:, at : at + 128], 0.0) for where, at in pieces)


def qu_part(ring, info, y, dqu, sums, keep, send):
    core, group, spot = info[0], info[1], info[2]
    rows = D // ring.count
    tile = 256
    last = ring.size * slot_rows(ring)
    extra = vector_rows(group, sums).astype(LOW)
    for out, half in ((send, 1 - core), (keep, core)):
        columns = pl.ds(pl.multiple_of(half * PART, 128), PART)
        out[last : last + SIDES, :] = extra
        for at in range(0, D, tile):
            block = dot_rows(y[:, at : at + tile], dqu[:, columns]).astype(LOW)
            for offset in range(0, tile, rows):
                dp = (at + offset) // rows
                slot = slot_in(ring, spot ^ ring.spot_of(dp), half)
                begin = slot * slot_rows(ring) + (group ^ ring.group_of(dp)) * (QU_TILES * rows)
                for i in range(QU_TILES):
                    row = pl.multiple_of(begin + i * rows, 16)
                    out[pl.ds(row, rows), :] = block[offset : offset + rows, i * 128 : (i + 1) * 128]


def grads_kernel(ring, info, far_mixed, far_active, far_grad, far_y, far_dqu, sums, keep, send, *scratch):
    mixed, active, grad, y, dqu, sems = scratch
    grad_in = started([(far_grad, grad), (far_mixed, mixed)], sems.at[0])
    active_in = started([(far_active, active)], sems.at[1])
    rest_in = started([(far_y, y), (far_dqu, dqu)], sems.at[2])
    grad_in()
    od_part(ring, info, mixed, active, grad, keep, send, active_in)
    rest_in()
    qu_part(ring, info, y, dqu, sums, keep, send)


def weight_grads(ring, info, mixed, active, grad, y, dqu, sums):
    blocks = (mixed, active, grad, y, dqu)
    out = grads_shape(ring)
    return pl.pallas_call(
        functools.partial(grads_kernel, ring),
        out_shape=(out, out),
        in_specs=[smem_spec()] + [far_spec()] * len(blocks) + [full_spec(sums.shape)],
        out_specs=(full_spec(out.shape),) * 2,
        scratch_shapes=[pltpu.VMEM(a.shape, LOW) for a in blocks] + [pltpu.SemaphoreType.DMA((3,))],
        compiler_params=kernel_params(20),
        cost_estimate=cost(50 * 10**9, 12 * 1024 * 1024),
        name="weight_grads",
    )(info, *[far(a) for a in blocks], sums)


def fold_kernel(held, came, kept, sent):
    half = (held.shape[0] - SIDES) // 2
    full = 2 * half
    kept[0:half, :] = held[0:half, :].astype(F32) + came[0:half, :].astype(F32)
    sent[0:half, :] = (held[half:full, :].astype(F32) + came[half:full, :].astype(F32)).astype(LOW)
    sides = held[full : full + SIDES, :].astype(LOW).astype(F32) + came[full : full + SIDES, :].astype(F32)
    kept[half : half + SIDES, :] = sides
    sent[half : half + SIDES, :] = sides.astype(LOW)


def fold(held, came):
    half = (held.shape[0] - SIDES) // 2 + SIDES
    outs = (shaped((half, 128), F32), shaped((half, 128), LOW))
    return pl.pallas_call(
        fold_kernel,
        out_shape=outs,
        in_specs=[full_spec(held.shape), full_spec(came.shape)],
        out_specs=tuple(full_spec(a.shape) for a in outs),
        compiler_params=kernel_params(20),
        cost_estimate=cost(0, 1024 * 1024),
        name="fold_gradients",
    )(held, came)


def close_kernel(held, came, *outs):
    qus, od, squares = outs[:GROUP], outs[GROUP], outs[GROUP + 1]
    rows = qus[0].shape[0] - SIDES
    full = held.shape[0] - SIDES
    sides = held[full : full + SIDES, :].astype(LOW).astype(F32) + came[full : full + SIDES, :].astype(F32)
    lanes = jnp.zeros((8, 128), F32)
    begin = 0
    for piece in (*qus, od):
        length = rows if piece is not od else od.shape[0]
        here = slice(begin, begin + length)
        begin += length
        total = held[here, :].astype(F32) + came[here, :].astype(F32)
        piece[0:length, :] = total.astype(LOW)
        if piece is not od:
            piece[rows : rows + SIDES, :] = sides.astype(LOW)
        lanes = lanes + jnp.sum((total * total).reshape(length // 8, 8, 128), axis=0)
    squares[...] = lanes


def close(ring, held, came):
    rows = QU_TILES * (D // ring.count)
    outs = [shaped((rows + SIDES, 128), LOW)] * GROUP
    outs += [shaped((OD_TILES * (SIDE + UNITS) // ring.size, 128), LOW), shaped((8, 128), F32)]
    return pl.pallas_call(
        close_kernel,
        out_shape=tuple(outs),
        in_specs=[full_spec(held.shape), full_spec(came.shape)],
        out_specs=tuple(full_spec(a.shape) for a in outs),
        compiler_params=kernel_params(16),
        cost_estimate=cost(0, 1024 * 1024),
        name="close_gradients",
    )(held, came)


def join_kernel(info, *refs):
    core = info[0]
    firsts, seconds, (od_first, od_second), outs = refs[:4], refs[4:8], refs[8:10], refs[10:]
    sent, vec, squares = outs
    rows = firsts[0].shape[0] - SIDES
    lanes = jnp.zeros((8, 128), F32)
    sides = []
    for pieces in (firsts, seconds):
        parts = [a[rows : rows + SIDES, :].astype(F32) for a in pieces]
        total = (parts[0] + parts[1]) + (parts[2] + parts[3])
        lanes = lanes + jnp.sum((total * total).reshape(SIDES // 8, 8, 128), axis=0)
        sides.append(total)
    squares[...] = lanes
    vec[...] = jnp.where(core == 0, sides[0], sides[1])

    def write(pieces, od):
        for r in range(GROUP):
            sent[r * rows : (r + 1) * rows, :] = pieces[r][0:rows, :]
        sent[GROUP * rows :, :] = od[...]

    pl.when(core == 0)(functools.partial(write, seconds, od_second))
    pl.when(core == 1)(functools.partial(write, firsts, od_first))


def join(info, firsts, seconds, od_first, od_second):
    rows = firsts[0].shape[0] - SIDES
    outs = (shaped((GROUP * rows + od_first.shape[0], 128), LOW), shaped((SIDES, 128), F32), shaped((8, 128), F32))
    blocks = (*firsts, *seconds, od_first, od_second)
    return pl.pallas_call(
        join_kernel,
        out_shape=outs,
        in_specs=[smem_spec()] + [full_spec(a.shape) for a in blocks],
        out_specs=tuple(full_spec(a.shape) for a in outs),
        compiler_params=kernel_params(16),
        cost_estimate=cost(0, 1024 * 1024),
        name="join_members",
    )(info, *blocks)


def adam_update(weight, grad, first, second, factor, rate):
    clipped = grad * factor
    first_new = BETA_ONE * first + (1.0 - BETA_ONE) * clipped
    second_new = BETA_TWO * second + (1.0 - BETA_TWO) * clipped * clipped
    first_hat = first_new / (1.0 - BETA_ONE**STEP)
    second_hat = second_new / (1.0 - BETA_TWO**STEP)
    weight_new = weight - rate * (
        first_hat / (jnp.sqrt(second_hat) + ADAM_EPS) + WEIGHT_DECAY * weight
    )
    return (weight_new, first_new, second_new)


def mixed_tile(tile, member):
    at = tile * 128
    if at >= 3 * SIDE:
        return 2, up_column(member, at - 3 * SIDE)
    width = SIDE // SPREAD
    kind, within = at // SIDE, at % SIDE
    return 0, qkv_column(kind, within // width, member) + within % width


def adam_kernel(info, factor_ref, *refs):
    core, group = info[0], info[1]
    step = pl.program_id(0)
    factor = factor_ref[0]
    qus, refs = (refs[:4], refs[4:8]), refs[8:]
    ods, came, refs = refs[:2], refs[2], refs[3:]
    olds, news = refs[:12], refs[12:]
    few, many = olds[0].shape[1], olds[9].shape[1]
    rows = (qus[0][0].shape[0] - SIDES) // QU_TILES
    od_rows = ods[0].shape[0] // OD_TILES

    def update(which, column, grad):
        columns = slice(column, column + 128)
        weight, first, second = [olds[3 * which + i][0, :, columns] for i in range(3)]
        fresh = adam_update(weight, grad.astype(F32), first, second, factor, LEARN_RATE)
        for i in range(3):
            news[3 * which + i][0, :, columns] = fresh[i]

    def rows_of(ref, begin, length):
        return ref[pl.ds(pl.multiple_of(begin + step * length, 16), length), :]

    def both_halves(here):
        for half in range(2):
            for tile in range(OD_TILES):
                column = half * (D // 2) + tile * 128
                ref, begin = (ods[here], 0) if half == here else (came, GROUP * QU_TILES * rows)
                begin = begin + tile * od_rows
                update(3, column, rows_of(ref, begin, many))
                update(1, column, rows_of(ref, begin + od_rows - rows, few))
            for member in range(GROUP):
                if half == here:
                    for g in range(GROUP):

                        @pl.when(group == g)
                        def _(ref=qus[here][member ^ g]):
                            for tile in range(QU_TILES):
                                which, column = mixed_tile(half * QU_TILES + tile, member)
                                update(which, column, rows_of(ref, tile * rows, few))
                else:
                    for tile in range(QU_TILES):
                        which, column = mixed_tile(half * QU_TILES + tile, member)
                        begin = ((group ^ member) * QU_TILES + tile) * rows
                        update(which, column, rows_of(came, begin, few))

    for here in range(2):
        pl.when(core == here)(functools.partial(both_halves, here))


def adam(info, factor, qus, ods, came, olds):
    steps = max(1, olds[0].shape[1] // 16)

    def master(a):
        return pl.BlockSpec((1, a.shape[1] // steps, a.shape[2]), lambda i: (0, i, 0))

    grads = (*qus[0], *qus[1], *ods, came)
    return pl.pallas_call(
        adam_kernel,
        grid=(steps,),
        out_shape=tuple(shaped(a.shape, F32) for a in olds),
        in_specs=[smem_spec(), smem_spec()]
        + [full_spec(a.shape) for a in grads]
        + [master(a) for a in olds],
        out_specs=tuple(master(a) for a in olds),
        compiler_params=kernel_params(28),
        name="adamw",
    )(info, factor, *grads, *[far(a) for a in olds])


def doc_tables(lengths, rows):
    seqs = lengths.shape[0]
    ends = jnp.cumsum(lengths, axis=1)
    places = jnp.arange(rows, dtype=jnp.int32)
    past = places[None, :, None] >= ends[:, None, :]
    begins = jnp.sum(jnp.where(past, lengths[:, None, :], 0), axis=2)
    position = (places[None, :] - begins).reshape(seqs * rows, 1)
    half = ROT // 2
    inverse = 10000.0 ** (-(jnp.arange(half, dtype=F32) * 2.0) / ROT)
    lanes = jnp.concatenate([inverse, inverse, jnp.zeros(HEAD_DIM - ROT, F32)])
    angles = position.astype(F32) * jnp.concatenate([lanes, lanes])[None, :]
    allowed = (places[None, None, :] <= places[None, :, None]) & (places[None, None, :] >= begins[:, :, None])
    mask = jnp.where(allowed, 0.0, -1e30).reshape(seqs * rows, rows).astype(F32)
    return jnp.cos(angles), jnp.sin(angles), mask


def shards(
    x_in,
    cotangent,
    doc_lengths,
    w_qkv,
    w_out,
    w_up,
    w_down,
    vectors,
    m_qkv,
    m_out,
    m_up,
    m_down,
    m_vectors,
    v_qkv,
    v_out,
    v_up,
    v_down,
    v_vectors,
):
    place = Place()
    ring, core, group, spot = place.ring, place.core, place.group, place.spot
    info = place.info()
    local_rows, width = x_in.shape
    seqs, docs = doc_lengths.shape
    rows = local_rows // seqs
    in_rows = w_qkv.shape[1]
    shard = vectors.shape[1]
    members = range(1, GROUP)

    vec_block = jnp.pad(vectors[0].astype(LOW), (0, in_rows * 128 - shard)).reshape(in_rows, 128)
    keep_qu, send_qu, keep_od, send_od = pack(info, w_qkv, w_out, w_up, w_down, vec_block)
    came_qu = place.sibling(send_qu)
    came_od = place.sibling(send_od)

    def member_columns(block, *waited):
        qu = jnp.where(core == block, keep_qu, came_qu)
        sent = [after(take(qu, group ^ r), *waited) for r in members]
        return [take(qu, group)] + [place.member(a, r) for a, r in zip(sent, members)]

    def gather(block, *waited):
        late = after(block, *waited)
        return [block] + [place.member(late, r) for r in members]

    def to_owners(slots):
        return [slots[0]] + [place.member(slots[r], r) for r in members]

    def total_of(slots):
        return sum(a.astype(F32) for a in slots)

    def block_vectors(parts):
        pieces = jnp.concatenate([a[:, :, 0 : -(-shard // 128), PART:] for a in parts])
        pieces = pieces.reshape(ring.size * GROUP, -1)[:, :shard]
        dp = jnp.arange(ring.count, dtype=jnp.int32)
        difference = ring.spot_of(dp) ^ spot
        slot = jnp.where(core == 0, ring.slot(difference, 0), ring.slot(difference, 1))
        vec = jnp.take(pieces, slot * GROUP + (ring.group_of(dp) ^ group), axis=0, mode="clip")
        vec = vec.reshape(-1).astype(F32)
        b_qkv, b_out, b_up, b_down, gain, ln_bias = jnp.split(
            vec, [3 * D, 4 * D, 4 * D + FF, 5 * D + FF, 6 * D + FF]
        )
        b_qkv = take(b_qkv.reshape(3 * SPREAD, GROUP, -1), group, 1).reshape(1, -1)
        b_up = take(b_up.reshape(SPREAD, GROUP, -1), group, 1).reshape(1, -1)
        return (b_qkv, b_up, gain[None], ln_bias[None]), (b_out + b_down)[None], gain[None]

    x_own = take(x_in.reshape(2, rows, width), core)
    cot_own = take(cotangent.reshape(2, rows, width), core)
    len_own = take(doc_lengths, core)
    len_rows = jnp.zeros((16, width), LOW).at[0, :docs].set(len_own.astype(LOW))
    x_sent = jnp.concatenate([x_own, len_rows])

    qu_came = member_columns(0)
    qu_own = jnp.stack(qu_came)[None]
    x_group = gather(x_sent, qu_came[1])
    qu_mine = jnp.where(core == 1, keep_qu, came_qu)
    sent = [after(jnp.concatenate([take(qu_mine, group ^ r), cot_own]), *x_group[2:]) for r in members]
    qu_cot = [place.member(a, r) for a, r in zip(sent, members)]
    od_own = jnp.where(core == 0, keep_od, came_od)[None]
    od = [jnp.concatenate([od_own, place.across(od_own, 0)])]
    qu = [jnp.concatenate([qu_own, place.across(qu_own, 0)])]
    for step in range(1, ring.bits):
        od.append(place.across(jnp.concatenate(od), step))
        qu.append(place.across(jnp.concatenate(qu), step))
    qu_sibling = [place.sibling(a) for a in qu[:-1]] + [place.sibling(after(qu[-1], *x_group[1:]))]
    parts_first = (*qu, *od, *qu_sibling, *(place.sibling(a) for a in od))
    lengths = jnp.stack([a[rows, :docs] for a in x_group]).astype(jnp.int32)
    tables = doc_tables(lengths, rows)
    vecs_first, bias_first, gain_first = block_vectors(qu)

    first = forward(ring, info, parts_first, x_group, tables, vecs_first, rows)
    kept_first, tables = first[GROUP:], first[-3:]
    qu_cot = [after(a, first[0]) for a in qu_cot]
    came = to_owners(first[:GROUP])
    od_own = after(jnp.where(core == 1, keep_od, came_od)[None], first[0])
    od_late = [jnp.concatenate([od_own, place.across(od_own, 0)])]
    came[1] = after(came[1], od_late[0])
    hidden_first = (x_own.astype(F32) + total_of(came) + bias_first).astype(LOW)
    hidden_group = gather(hidden_first)
    qu_own = jnp.stack([take(qu_mine, group)] + [a[:in_rows] for a in qu_cot])[None]
    qu_late = [jnp.concatenate([qu_own, after(place.across(qu_own, 0), hidden_first)])]
    for step in range(1, ring.bits):
        od_late.append(after(place.across(jnp.concatenate(od_late), step), *hidden_group[1:]))
        qu_late.append(after(place.across(jnp.concatenate(qu_late), step), *hidden_group[1:]))
    qu_sibling, od_sibling = [
        [place.sibling(after(a, *hidden_group[1:])) for a in late] for late in (qu_late, od_late)
    ]
    parts_second = (*qu_late, *od_late, *qu_sibling, *od_sibling)
    vecs_second, bias_second, gain_second = block_vectors(qu_late)
    second = middle(ring, info, parts_second, hidden_group, [cot_own, *qu_cot], tables, vecs_second, rows)
    sums_second, y_second, mixed_second, active_second, dqu_second, grad_second = second[GROUP : GROUP + 6]
    z_second = second[GROUP + 6 :]

    def rows_backward(rows_low, grad_low, dy, gain):
        rows_now = rows_low.astype(F32)
        centered = rows_now - jnp.mean(rows_now, axis=-1, keepdims=True)
        variance = jnp.mean(centered * centered, axis=-1, keepdims=True)
        inverse_std = lax.rsqrt(variance + NORM_EPS)
        normed = centered * inverse_std
        scaled = dy * gain
        inner_mean = jnp.mean(scaled, axis=-1, keepdims=True)
        inner_cross = jnp.mean(scaled * normed, axis=-1, keepdims=True)
        return (grad_low.astype(F32) + inverse_std * (scaled - inner_mean - normed * inner_cross)).astype(LOW)

    def to_members(pieces):
        return [pieces[0]] + [place.member(pieces[r], r) for r in members]

    steps = list(reversed(range(ring.bits)))

    def ring_fold(held, *waited):
        kept, sent = held
        for step in steps[:-1]:
            kept, sent = fold(kept, after(place.across(sent, step), *waited))
        return kept, sent

    def all_sum(block):
        block = block + place.sibling(block)
        for step in range(ring.bits):
            block = block + place.across(block, step)
        for step in range(2):
            block = block + place.member(block, 1 << step)
        return block

    dy_second = to_owners(second[:GROUP])
    grads = weight_grads(ring, info, mixed_second, active_second, grad_second, y_second, dqu_second, sums_second)
    mid_grad = rows_backward(hidden_first, cot_own, total_of(dy_second), gain_second)
    mid_group = gather(mid_grad)
    sent = place.sibling(after(grads[1], *dy_second[1:]))
    second_held = ring_fold(fold(grads[0], after(sent, mid_grad)))

    mid_late = [after(mid_group[0], *second_held)] + mid_group[1:]
    back = backward(ring, info, mid_late, kept_first, rows)
    keep, send = back[GROUP:]
    z_came = to_owners([z_second[0]] + [after(a, *mid_group[1:]) for a in z_second[1:]])
    kept, sent = second_held
    *qu_second, od_second, squares_second = close(ring, kept, after(place.across(sent, 0), send))
    send = after(send, *qu_second, *z_came[1:])
    qu_slots_second = to_members(qu_second)
    kept, sent = ring_fold(fold(keep, place.sibling(send)))
    start_came = to_owners(back[:GROUP])
    *qu_first, od_first, squares_first = close(ring, kept, place.across(after(sent, *start_came[1:]), 0))
    qu_slots_first = to_members(qu_first)
    squares = all_sum(squares_first + squares_second)
    od_first = after(od_first, squares)
    grads_sent, vec, vec_squares = join(info, qu_slots_first, qu_slots_second, od_first, od_second)
    squares = jnp.sum(squares + vec_squares)
    start_came[1:] = [after(a, grads_sent) for a in start_came[1:]]
    start_grad = rows_backward(x_own, mid_grad, total_of(start_came), gain_first)
    hidden_second = (hidden_first.astype(F32) + total_of(z_came) + bias_second).astype(LOW)

    grad_norm = jnp.sqrt(squares)
    factor = jnp.minimum(1.0, CLIP_LEVEL / (grad_norm + 1e-06))

    def own_block(one, two):
        came = place.sibling(jnp.where(core == 0, two, one))
        mine = jnp.where(core == 0, one, two)
        return [jnp.where(core == h, mine, came) for h in range(2)]

    grads_came = place.sibling(grads_sent)
    vec_share = after(vec, grads_sent).reshape(-1)[: ring.count * shard].reshape(ring.count, shard)
    vec_share = take(vec_share, lax.axis_index("dp"))[None]
    olds = (w_qkv, m_qkv, v_qkv, w_out, m_out, v_out, w_up, m_up, v_up, w_down, m_down, v_down)
    qus = (qu_slots_first, qu_slots_second)
    news = adam(info, factor[None], qus, (od_first, od_second), grads_came, olds)
    new_vec = adam_update(vectors, vec_share, m_vectors, v_vectors, factor, VECTOR_RATE)

    outputs = own_block(jnp.stack([hidden_first, start_grad]), jnp.stack([hidden_second, mid_grad]))
    outputs = jnp.concatenate(outputs, axis=1)
    hidden_out, input_grads = outputs[:1], outputs[1:]
    return (
        hidden_out,
        input_grads,
        *(news[3 * i] for i in range(4)),
        new_vec[0],
        *(news[3 * i + 1] for i in range(4)),
        new_vec[1],
        *(news[3 * i + 2] for i in range(4)),
        new_vec[2],
        grad_norm,
    )


def solution(mesh):
    return jax.shard_map(
        shards,
        mesh=mesh,
        in_specs=(
            P("dp", None),
            P("dp", None),
            P("dp", None),
            P("section", "dp", None),
            P("section", "dp", None),
            P("section", "dp", None),
            P("section", "dp", None),
            P("section", "dp"),
            P("section", "dp", None),
            P("section", "dp", None),
            P("section", "dp", None),
            P("section", "dp", None),
            P("section", "dp"),
            P("section", "dp", None),
            P("section", "dp", None),
            P("section", "dp", None),
            P("section", "dp", None),
            P("section", "dp"),
        ),
        out_specs=(
            P("section", "dp", None),
            P("section", "dp", None),
            P("section", "dp", None),
            P("section", "dp", None),
            P("section", "dp", None),
            P("section", "dp", None),
            P("section", "dp"),
            P("section", "dp", None),
            P("section", "dp", None),
            P("section", "dp", None),
            P("section", "dp", None),
            P("section", "dp"),
            P("section", "dp", None),
            P("section", "dp", None),
            P("section", "dp", None),
            P("section", "dp", None),
            P("section", "dp"),
            P(),
        ),
        check_vma=False,
    )
```

```python
import functools

import jax
import jax.numpy as jnp
from jax import lax
from jax.experimental import pallas as pl
from jax.experimental.pallas import tpu as pltpu
from jax.sharding import PartitionSpec as P

D = 1024
FF = 4096
HEADS = 16
HEAD_DIM = 64
ROT = 16
STEP = 10


NORM_EPS = 1e-05
BETA_ONE = 0.9
BETA_TWO = 0.95
LEARN_RATE = 0.05
VECTOR_RATE = 0.3
WEIGHT_DECAY = 0.01
CLIP_LEVEL = 1.0
ADAM_EPS = 1e-08

AXES = ("section", "dp")
GROUP = 4
SPREAD = 1
LOW = jnp.bfloat16
F32 = jnp.float32
SIDE = D // GROUP
UNITS = FF // GROUP
MIXED = 3 * SIDE + UNITS
PART = MIXED // 2
WIRE = PART + 128


class Ring:
    def __init__(self, count):
        self.count = count
        self.low = count // (GROUP * SPREAD)
        self.size = SPREAD * self.low
        self.bits = self.size.bit_length() - 1

    def index(self, g, t):
        return ((t // self.low) * GROUP + g) * self.low + t % self.low

    def group_of(self, dp):
        return (dp // self.low) % GROUP

    def spot_of(self, dp):
        return (dp // (GROUP * self.low)) * self.low + dp % self.low

    def order(self, core):
        steps = list(range(self.bits))
        if SPREAD > 1 or core == 1:
            steps.reverse()
        return steps

    def turn(self, slot, core):
        return sum(((slot >> s) & 1) << b for s, b in enumerate(self.order(core)))

    def slot(self, difference, core):
        return sum(((difference >> b) & 1) << s for s, b in enumerate(self.order(core)))


class Place:
    def __init__(self):
        self.ring = Ring(lax.axis_size("dp"))
        self.core = lax.axis_index("section")
        dp = lax.axis_index("dp")
        self.group = self.ring.group_of(dp)
        self.spot = self.ring.spot_of(dp)

    def info(self):
        return jnp.stack([self.core, self.group, self.spot]).astype(jnp.int32)

    def move(self, block, where):
        ring = self.ring
        route = []
        for core in range(2):
            for g in range(GROUP):
                for t in range(ring.size):
                    c, h, u = where(core, g, t)
                    route.append((core * ring.count + ring.index(g, t), c * ring.count + ring.index(h, u)))
        return lax.ppermute(block, AXES, route)

    def sibling(self, block):
        return self.move(block, lambda c, g, t: (1 - c, g, t))

    def member(self, block, distance):
        return self.move(block, lambda c, g, t: (c, g ^ distance, t))

    def across(self, block, step):
        return self.move(block, lambda c, g, t: (c, g, t ^ (1 << self.ring.order(c)[step])))


def take(block, index, axis=0):
    return lax.dynamic_index_in_dim(block, index, axis, keepdims=False)


def after(block, *waited):
    return lax.optimization_barrier((block, waited))[0]


def dot(left, right):
    return jnp.dot(left, right, preferred_element_type=F32)


def dot_cols(left, right):
    return lax.dot_general(left, right, (((1,), (1,)), ((), ())), preferred_element_type=F32)


def dot_rows(left, right):
    return lax.dot_general(left, right, (((0,), (0,)), ((), ())), preferred_element_type=F32)


def full_spec(shape):
    return pl.BlockSpec(shape, lambda *_: (0,) * len(shape))


def far_spec():
    return pl.BlockSpec(memory_space=pltpu.HBM)


def far(block):
    return pltpu.with_memory_space_constraint(block, pltpu.HBM)


def any_spec():
    return pl.BlockSpec(memory_space=pl.ANY)


def smem_spec():
    return pl.BlockSpec(memory_space=pltpu.SMEM)


def shaped(shape, dtype):
    return jax.ShapeDtypeStruct(shape, dtype)


def kernel_params(mebibytes):
    return pltpu.CompilerParams(vmem_limit_bytes=mebibytes * 1024 * 1024)


def up_pieces():
    run = UNITS // SPREAD
    cuts = sorted({0, PART - 3 * SIDE, UNITS} | {run * i for i in range(SPREAD)})
    pieces = []
    for begin, end in zip(cuts[:-1], cuts[1:]):
        column = 3 * SIDE + begin
        pieces.append((begin, column // PART, column % PART, end - begin))
    return pieces


def up_column(g, local):
    run = UNITS // SPREAD
    return (local // run * GROUP + g) * run + local % run


def qkv_column(kind, run, g):
    width = SIDE // SPREAD
    return ((kind * SPREAD + run) * GROUP + g) * width


def pack_kernel(info, qkv_hbm, out_hbm, up_hbm, down_hbm, vec, keep_qu, send_qu, keep_od, send_od, *scratch):
    w_qkv, w_out, w_up, w_down, sems = scratch
    pairs = ((qkv_hbm, w_qkv), (up_hbm, w_up), (down_hbm, w_down), (out_hbm, w_out))
    copies = [pltpu.make_async_copy(far.at[0], near, sems.at[i]) for i, (far, near) in enumerate(pairs)]
    for copy in copies:
        copy.start()
    rows = w_qkv.shape[0]
    ff_rows = w_down.shape[0]
    width = SIDE // SPREAD
    core = info[0]

    def write_qu(halves):
        for g in range(GROUP):
            for kind in range(3):
                for run in range(SPREAD):
                    at = (kind * SPREAD + run) * width
                    column = qkv_column(kind, run, g)
                    halves[0][g, :, at : at + width] = w_qkv[:, column : column + width].astype(LOW)
            for local, half, at, length in up_pieces():
                column = up_column(g, local)
                halves[half][g, :, at : at + length] = w_up[:, column : column + length].astype(LOW)
            for half in range(2):
                halves[half][g, :, PART:WIRE] = vec[...]

    def write_od(halves):
        for half in range(2):
            columns = slice(half * (D // 2), (half + 1) * (D // 2))
            halves[half][0:ff_rows] = w_down[:, columns].astype(LOW)
            halves[half][ff_rows : ff_rows + rows] = w_out[:, columns].astype(LOW)

    for first, last, write, kept, sent in ((0, 2, write_qu, keep_qu, send_qu), (2, 4, write_od, keep_od, send_od)):
        for copy in copies[first:last]:
            copy.wait()
        pl.when(core == 0)(functools.partial(write, (kept, sent)))
        pl.when(core == 1)(functools.partial(write, (sent, kept)))


def pack(info, w_qkv, w_out, w_up, w_down, vec):
    rows, ff_rows = w_qkv.shape[1], w_down.shape[1]
    qu = shaped((GROUP, rows, WIRE), LOW)
    od = shaped((ff_rows + rows, D // 2), LOW)
    return pl.pallas_call(
        pack_kernel,
        out_shape=(qu, qu, od, od),
        in_specs=[smem_spec()] + [far_spec()] * 4 + [full_spec(vec.shape)],
        out_specs=tuple(full_spec(a.shape) for a in (qu, qu, od, od)),
        scratch_shapes=[pltpu.VMEM(a.shape[1:], F32) for a in (w_qkv, w_out, w_up, w_down)]
        + [pltpu.SemaphoreType.DMA((4,))],
        compiler_params=kernel_params(20),
        name="pack_weights",
    )(info, far(w_qkv), far(w_out), far(w_up), far(w_down), vec)


def stack_kernel(*refs):
    for i, ref in enumerate(refs[:-1]):
        refs[-1][0, i] = ref[...]


def stack_members(pieces):
    out = shaped((1, len(pieces), *pieces[0].shape), LOW)
    return pl.pallas_call(
        stack_kernel,
        out_shape=out,
        in_specs=[full_spec(a.shape) for a in pieces],
        out_specs=full_spec(out.shape),
        compiler_params=kernel_params(16),
        cost_estimate=cost(50 * 10**9, 1024 * 1024),
        name="stack_members",
    )(*pieces)


def weight_copies(ring, info, parts, wqu, wout, wdown, sems):
    core, group, spot = info[0], info[1], info[2]
    qu_copies, od_copies = [], []
    count = len(parts) // 4
    for which in range(2):
        half = core if which == 0 else 1 - core
        qu_at = pl.multiple_of(half * PART, 128)
        od_at = pl.multiple_of(half * (D // 2), 128)
        slot = 0
        for piece in range(count):
            qu, od = parts[2 * count * which + piece], parts[2 * count * which + count + piece]
            rows = qu.shape[2]
            ff_rows = od.shape[1] - rows
            for i in range(qu.shape[0]):
                straight, turned = ring.turn(slot, 0), ring.turn(slot, 1)
                there = spot ^ (straight + half * (turned - straight))
                slot += 1
                ff_row = pl.multiple_of(there * ff_rows, ff_rows)
                out_row = pl.multiple_of(there * rows, rows)
                far = wdown.at[pl.ds(ff_row, ff_rows), pl.ds(od_at, D // 2)]
                od_copies.append(pltpu.make_async_copy(od.at[i, pl.ds(0, ff_rows)], far, sems.at[0]))
                far = wout.at[pl.ds(out_row, rows), pl.ds(od_at, D // 2)]
                od_copies.append(pltpu.make_async_copy(od.at[i, pl.ds(ff_rows, rows)], far, sems.at[0]))
                for r in range(GROUP):
                    row = pl.multiple_of(ring.index(group ^ r, there) * rows, rows)
                    far = wqu.at[pl.ds(row, rows), pl.ds(qu_at, PART)]
                    qu_copies.append(pltpu.make_async_copy(qu.at[i, r, :, pl.ds(0, PART)], far, sems.at[1]))
    return qu_copies, od_copies


def head_masks(dtype):
    lane = lax.broadcasted_iota(jnp.int32, (1, SIDE), 1) // HEAD_DIM
    return [(lane == h).astype(dtype) for h in range(SIDE // HEAD_DIM)]


def by_head(parts):
    lane = lax.broadcasted_iota(jnp.int32, (1, SIDE), 1) // HEAD_DIM
    total = parts[-1]
    for h in range(len(parts) - 2, -1, -1):
        total = jnp.where(lane == h, parts[h], total)
    return total


def turning(cosine, sine, back):
    lane = lax.broadcasted_iota(jnp.int32, sine.shape, 1) % HEAD_DIM
    first = jnp.where(lane < ROT // 2, sine, 0.0)
    second = jnp.where(lane < ROT // 2, 0.0, sine)
    if back:
        second = -second
    else:
        first = -first
    wide = SIDE // cosine.shape[1]
    return [jnp.concatenate([a] * wide, axis=1) for a in (cosine, first, second)]


def turn(part, tables):
    cosine, first, second = tables
    ahead = pltpu.roll(part, SIDE - ROT // 2, 1)
    behind = pltpu.roll(part, ROT // 2, 1)
    return part * cosine + ahead * first + behind * second


def normalise(rows):
    centered = rows - jnp.mean(rows, axis=-1, keepdims=True)
    variance = jnp.mean(centered * centered, axis=-1, keepdims=True)
    return centered * lax.rsqrt(variance + NORM_EPS)


def no_wait():
    pass


def forward_part(x_refs, tables, vecs, wqu, wout, wdown, kept, z_refs, waits, done, normed_ref=None):
    cosine, sine, mask = tables
    b_qkv, b_up, gain, ln_bias = vecs
    y, qkv, probs, mixed, active, slope = kept
    rows = z_refs[0].shape[0]
    for r in range(GROUP):
        normed = normalise(x_refs[r][0:rows, :].astype(F32))
        if normed_ref is not None:
            normed_ref[r * rows : (r + 1) * rows, :] = normed
        y[r * rows : (r + 1) * rows, :] = (normed * gain[...] + ln_bias[...]).astype(LOW)
    done(0)
    waits[0]()
    waits[2]()
    forth = turning(cosine[...], sine[...], False)
    for kind in range(3):
        columns = slice(kind * SIDE, (kind + 1) * SIDE)
        part = dot(y[...], wqu[:, columns]) + b_qkv[:, columns]
        if kind < 2:
            part = turn(part, forth)
        qkv[:, columns] = part.astype(LOW)
    done(1)
    masks = head_masks(LOW)
    heads = len(masks)
    for r in range(GROUP):
        here = slice(r * rows, (r + 1) * rows)
        query, keys, values = [qkv[here, k * SIDE : (k + 1) * SIDE] for k in range(3)]
        stacked = jnp.concatenate([query * m for m in masks], axis=0)
        scores = dot_cols(stacked, keys) * HEAD_DIM ** (-0.5)
        scores = scores.reshape(heads, rows, rows) + mask[here, :][None]
        expo = jnp.exp(scores - jnp.max(scores, axis=-1, keepdims=True))
        prob = expo / jnp.sum(expo, axis=-1, keepdims=True)
        prob = prob.reshape(heads * rows, rows)
        probs[r * heads * rows : (r + 1) * heads * rows, :] = prob
        full = dot(prob.astype(LOW), values)
        mixed[here, :] = by_head([full[h * rows : (h + 1) * rows] for h in range(heads)]).astype(LOW)
    done(2)
    done(3)
    tile = 256
    for at in range(0, UNITS, tile):
        hidden = dot(y[...], wqu[:, 3 * SIDE + at : 3 * SIDE + at + tile]) + b_up[:, at : at + tile]
        share = 0.5 * (1.0 + lax.erf(hidden * (0.5**0.5)))
        density = jnp.exp(-0.5 * hidden * hidden) * (0.5 / jnp.pi) ** 0.5
        active[:, at : at + tile] = (hidden * share).astype(LOW)
        slope[:, at : at + tile] = share + hidden * density
    done(4)
    done(5)
    waits[1]()
    for at in range(0, D, tile):
        branch = dot(mixed[...], wout[:, at : at + tile]) + dot(active[...], wdown[:, at : at + tile])
        for r in range(GROUP):
            z_refs[r][:, at : at + tile] = branch[r * rows : (r + 1) * rows].astype(LOW)


def backward_part(grad, normed, tables, wqu, wout, wdown, kept, dqu, dy_refs, sums, waits, done):
    cosine, sine, _ = tables
    y, qkv, probs, mixed, active, slope = kept
    rows = grad.shape[0] // GROUP
    tile = 256
    waits[0]()
    dmixed = dot_cols(grad[...], wout[...]).astype(LOW)
    for at in range(0, UNITS, tile):
        dactive = dot_cols(grad[...], wdown[at : at + tile, :])
        dhidden = (dactive * slope[:, at : at + tile]).astype(LOW)
        dqu[:, 3 * SIDE + at : 3 * SIDE + at + tile] = dhidden
    waits[1]()
    masks = head_masks(LOW)
    heads = len(masks)
    back = turning(cosine[...], sine[...], True)
    for r in range(GROUP):
        here = slice(r * rows, (r + 1) * rows)
        query, keys, values = [qkv[here, k * SIDE : (k + 1) * SIDE] for k in range(3)]
        dstack = jnp.concatenate([dmixed[here] * m for m in masks], axis=0)
        dprob = dot_cols(dstack, values)
        prob = probs[r * heads * rows : (r + 1) * heads * rows, :]
        dvalues = dot_rows(prob.astype(LOW), dstack)
        dscore = (prob * (dprob - jnp.sum(prob * dprob, axis=-1, keepdims=True))).astype(LOW)
        full = dot(dscore, keys)
        dquery = by_head([full[h * rows : (h + 1) * rows] for h in range(heads)])
        dkeys = dot_rows(dscore, jnp.concatenate([query * m for m in masks], axis=0))
        scale = HEAD_DIM ** (-0.5)
        slot_tables = [a[here] for a in back]
        dqu[here, 0:SIDE] = turn(dquery * scale, slot_tables).astype(LOW)
        dqu[here, SIDE : 2 * SIDE] = turn(dkeys * scale, slot_tables).astype(LOW)
        dqu[here, 2 * SIDE : 3 * SIDE] = dvalues.astype(LOW)
    done()
    for at in range(0, MIXED, tile):
        sums[:, at : at + tile] = jnp.sum(dqu[:, at : at + tile].astype(F32), axis=0, keepdims=True)
    waits[2]()
    for at in range(0, D, tile):
        dy = dot_cols(dqu[...], wqu[at : at + tile, :])
        for r in range(GROUP):
            dy_refs[r][:, at : at + tile] = dy[r * rows : (r + 1) * rows].astype(LOW)
        own = grad[0:rows, at : at + tile].astype(F32)
        for i, terms in enumerate((own, dy * normed[:, at : at + tile], dy)):
            begin = MIXED + i * D + at
            sums[:, begin : begin + tile] = jnp.sum(terms, axis=0, keepdims=True)


def kept_shapes(tokens, rows):
    return [
        ((tokens, D), LOW),
        ((tokens, 3 * SIDE), LOW),
        ((tokens * (SIDE // HEAD_DIM), rows), F32),
        ((tokens, SIDE), LOW),
        ((tokens, UNITS), LOW),
        ((tokens, UNITS), F32),
    ]


def weight_scratch():
    return [
        pltpu.VMEM((D, MIXED), LOW),
        pltpu.VMEM((SIDE, D), LOW),
        pltpu.VMEM((UNITS, D), LOW),
        pltpu.SemaphoreType.DMA((2,)),
    ]


def waiter(copies):
    def wait():
        for copy in copies:
            copy.wait()

    return wait


def started(pairs, sem):
    copies = [pltpu.make_async_copy(source, target, sem) for source, target in pairs]
    for copy in copies:
        copy.start()
    return waiter(copies)


def table_scratch(tokens, rows):
    return [pltpu.VMEM((tokens, 128), F32), pltpu.VMEM((tokens, 128), F32), pltpu.VMEM((tokens, rows), F32)]


def cost(flops, moved):
    return pl.CostEstimate(flops=2 * flops, bytes_accessed=2 * moved, transcendentals=0)


def leaving(pairs, sems):
    copies = [pltpu.make_async_copy(near, far, sems.at[i]) for i, (near, far) in enumerate(pairs)]

    def go(i):
        copies[i].start()

    return go, waiter(copies)


def forward_kernel(ring, count, info, *refs):
    parts, refs = refs[:count], refs[count:]
    x_refs, refs = refs[:4], refs[4:]
    tables, refs = refs[:3], refs[3:]
    vecs, refs = refs[:4], refs[4:]
    z_refs, refs = refs[:4], refs[4:]
    far_kept, far_weights, far_tables, refs = refs[:7], refs[7:10], refs[10:13], refs[13:]
    kept, refs = refs[:7], refs[7:]
    out_sems, scratch = refs[0], refs[1:]
    weights = scratch[:3]
    qu_copies, od_copies = weight_copies(ring, info, parts, *scratch)
    for copy in qu_copies + od_copies:
        copy.start()
    pairs = [*zip(kept, far_kept), *zip(weights, far_weights), *zip(tables, far_tables)]
    go, out = leaving(pairs, out_sems)
    for i in range(10, 13):
        go(i)

    def qu_in():
        waiter(qu_copies)()
        go(7)

    def od_in():
        waiter(od_copies)()
        go(8)
        go(9)

    def done(i):
        go(i)
        if i == 0:
            go(6)

    forward_part(x_refs, tables, vecs, *weights, kept[:6], z_refs, (qu_in, od_in, no_wait), done, kept[6])
    out()


def forward(ring, info, parts, xs, tables, vecs, rows):
    tokens = GROUP * rows
    shapes = kept_shapes(tokens, rows) + [((tokens, D), F32)]
    away = [*shapes, ((D, MIXED), LOW), ((SIDE, D), LOW), ((UNITS, D), LOW)] + [(a.shape, F32) for a in tables]
    blocks = (*xs, *tables, *vecs)
    return pl.pallas_call(
        functools.partial(forward_kernel, ring, len(parts)),
        out_shape=(*[shaped((rows, D), LOW)] * GROUP, *[pltpu.HBM(*a) for a in away]),
        in_specs=[smem_spec()] + [any_spec()] * len(parts) + [full_spec(a.shape) for a in blocks],
        out_specs=tuple([full_spec((rows, D))] * GROUP + [far_spec()] * len(away)),
        scratch_shapes=[pltpu.VMEM(*a) for a in shapes]
        + [pltpu.SemaphoreType.DMA((len(away),))]
        + weight_scratch(),
        compiler_params=kernel_params(22),
        cost_estimate=cost(2 * tokens * D * (D + 2 * FF // GROUP), 16 * 1024 * 1024),
        name="forward_shard",
    )(info, *parts, *blocks)


def middle_kernel(ring, count, info, *refs):
    parts, refs = refs[:count], refs[count:]
    x_refs, refs = refs[:4], refs[4:]
    g_refs, refs = refs[:4], refs[4:]
    far_tables, refs = refs[:3], refs[3:]
    vecs, refs = refs[:4], refs[4:]
    dy_refs, refs = refs[:4], refs[4:]
    sums, away, refs = refs[0], refs[1:10], refs[10:]
    kept, refs = refs[:6], refs[6:]
    z_refs, tables, refs = refs[:4], refs[4:7], refs[7:]
    (grad, normed, dqu, in_sems, out_sems), scratch = refs[:5], refs[5:]
    rows = z_refs[0].shape[0]
    qu_copies, od_copies = weight_copies(ring, info, parts, *scratch)
    for copy in qu_copies:
        copy.start()
    tables_in = started(zip(far_tables, tables), in_sems.at[0])
    for copy in od_copies:
        copy.start()
    pairs = []
    for r, ref in enumerate(g_refs):
        at = ref.shape[0] - rows
        pairs.append((ref.at[pl.ds(at, rows)], grad.at[pl.ds(r * rows, rows)]))
    grad_in = started(pairs, in_sems.at[1])
    go, out = leaving(list(zip([kept[0], kept[3], kept[4], dqu, grad, *z_refs], away)), out_sems)

    def done(i):
        if i in (0, 3, 4):
            go((0, 3, 4).index(i))

    waits = (waiter(qu_copies), waiter(od_copies), tables_in)
    forward_part(x_refs, tables, vecs, *scratch[:3], kept, z_refs, waits, done, normed)
    grad_in()
    for i in range(4, 9):
        go(i)
    waits = (no_wait, no_wait, no_wait)
    done = functools.partial(go, 3)
    backward_part(grad, normed, tables, *scratch[:3], kept, dqu, dy_refs, sums, waits, done)
    out()


def middle(ring, info, parts, xs, gs, tables, vecs, rows):
    tokens = GROUP * rows
    shapes = kept_shapes(tokens, rows)
    away = [shapes[0], shapes[3], shapes[4], ((tokens, MIXED), LOW), ((tokens, D), LOW)]
    away += [((rows, D), LOW)] * GROUP
    sums = shaped((1, MIXED + 3 * D), F32)
    return pl.pallas_call(
        functools.partial(middle_kernel, ring, len(parts)),
        out_shape=(*[shaped((rows, D), LOW)] * GROUP, sums, *[pltpu.HBM(*a) for a in away]),
        in_specs=[smem_spec()]
        + [any_spec()] * len(parts)
        + [full_spec(a.shape) for a in xs]
        + [far_spec()] * (GROUP + 3)
        + [full_spec(a.shape) for a in vecs],
        out_specs=tuple([full_spec((rows, D))] * GROUP + [full_spec(sums.shape)] + [far_spec()] * len(away)),
        scratch_shapes=[pltpu.VMEM(*a) for a in shapes]
        + [pltpu.VMEM((rows, D), LOW)] * GROUP
        + table_scratch(tokens, rows)
        + [pltpu.VMEM((tokens, D), LOW), pltpu.VMEM((tokens, D), F32), pltpu.VMEM((tokens, MIXED), LOW)]
        + [pltpu.SemaphoreType.DMA((2,)), pltpu.SemaphoreType.DMA((9,))]
        + weight_scratch(),
        compiler_params=kernel_params(27),
        cost_estimate=cost(4 * tokens * D * (D + 2 * FF // GROUP), 16 * 1024 * 1024),
        name="forward_backward_shard",
    )(info, *parts, *xs, *[far(a) for a in (*gs, *tables)], *vecs)


def backward_kernel(ring, info, *refs):
    g_refs, refs = refs[:4], refs[4:]
    far_kept, far_weights, far_tables, refs = refs[:7], refs[7:10], refs[10:13], refs[13:]
    dy_refs, refs = refs[:4], refs[4:]
    (keep, send), refs = refs[:2], refs[2:]
    kept, refs = refs[:7], refs[7:]
    weights, tables, refs = refs[:3], refs[3:6], refs[6:]
    grad, dqu, sums, in_sems = refs
    y, qkv, probs, mixed, active, slope, normed = kept
    wqu, wout, wdown = weights
    far_y, far_qkv, far_probs, far_mixed, far_active, far_slope, far_normed = far_kept
    mixed_in = started([(far_mixed, mixed)], in_sems.at[0])
    active_in = started([(far_active, active)], in_sems.at[1])
    units_in = started([*zip(far_weights[1:], weights[1:]), (far_slope, slope)], in_sems.at[2])
    heads_in = started([(far_qkv, qkv), (far_probs, probs), *zip(far_tables, tables)], in_sems.at[3])
    dy_in = started([(far_weights[0], wqu), (far_normed, normed)], in_sems.at[4])
    y_in = started([(far_y, y)], in_sems.at[5])
    rows = g_refs[0].shape[0]
    for r in range(GROUP):
        grad[r * rows : (r + 1) * rows, :] = g_refs[r][...]
    mixed_in()
    od_part(ring, info, mixed, active, grad, keep, send, active_in)
    waits = (units_in, heads_in, dy_in)
    backward_part(grad, normed, tables, *weights, kept[:6], dqu, dy_refs, sums, waits, no_wait)
    y_in()
    qu_part(ring, info, y, dqu, sums, keep, send)


def backward(ring, info, gs, held, rows):
    tokens = GROUP * rows
    outs = [shaped((rows, D), LOW)] * GROUP + [grads_shape(ring)] * 2
    return pl.pallas_call(
        functools.partial(backward_kernel, ring),
        out_shape=tuple(outs),
        in_specs=[smem_spec()] + [full_spec(a.shape) for a in gs] + [far_spec()] * len(held),
        out_specs=tuple(full_spec(a.shape) for a in outs),
        scratch_shapes=[pltpu.VMEM(a.shape, a.dtype) for a in held]
        + [pltpu.VMEM((tokens, D), LOW), pltpu.VMEM((tokens, MIXED), LOW)]
        + [pltpu.VMEM((1, MIXED + 3 * D), F32), pltpu.SemaphoreType.DMA((6,))],
        compiler_params=kernel_params(28),
        cost_estimate=cost(4 * tokens * D * (D + 2 * FF // GROUP), 16 * 1024 * 1024),
        name="backward_shard",
    )(info, *gs, *[far(a) for a in held])


def slot_in(ring, difference, half):
    straight, turned = ring.slot(difference, 0), ring.slot(difference, 1)
    return straight + half * (turned - straight)


QU_TILES = PART // 128
OD_TILES = D // 2 // 128
SIDES = 112


def slot_rows(ring):
    return GROUP * QU_TILES * (D // ring.count) + OD_TILES * (SIDE + UNITS) // ring.size


def grads_shape(ring):
    return shaped((ring.size * slot_rows(ring) + SIDES, 128), LOW)


def od_part(ring, info, mixed, active, grad, keep, send, active_in):
    core, spot = info[0], info[2]
    out_rows = SIDE // ring.size
    ff_rows = UNITS // ring.size
    ahead = GROUP * QU_TILES * (D // ring.count)
    for i, (out, half) in enumerate(((send, 1 - core), (keep, core))):
        columns = pl.ds(pl.multiple_of(half * (D // 2), D // 2), D // 2)
        part = grad[:, columns]
        block = dot_rows(mixed[...], part).astype(LOW)
        if i == 0:
            active_in()
        for there in range(ring.size):
            slot = slot_in(ring, spot ^ there, half)
            piece = dot_rows(active[:, there * ff_rows : (there + 1) * ff_rows], part).astype(LOW)
            for tile in range(OD_TILES):
                lanes = slice(tile * 128, (tile + 1) * 128)
                row = slot * slot_rows(ring) + ahead + tile * (ff_rows + out_rows)
                out[pl.ds(pl.multiple_of(row, 16), ff_rows), :] = piece[:, lanes]
                row = pl.multiple_of(row + ff_rows, 16)
                out[pl.ds(row, out_rows), :] = block[there * out_rows : (there + 1) * out_rows, lanes]


def vector_rows(group, sums):
    width = SIDE // SPREAD
    run = UNITS // SPREAD
    row = lax.broadcasted_iota(jnp.int32, (SIDES, 128), 0)
    pieces = []
    for at in range(0, 3 * SIDE, 128):
        pieces.append(((at // width * GROUP + group) * (width // 128) + at % width // 128, at))
    for at in range(0, UNITS, 128):
        pieces.append((3 * D // 128 + D // 128 + (at // run * GROUP + group) * (run // 128) + at % run // 128, 3 * SIDE + at))
    tail = (4 * D + FF) // 128
    for i, begin in enumerate((3 * D // 128, tail, tail + D // 128, tail + 2 * D // 128)):
        for at in range(0, D, 128):
            pieces.append((begin + at // 128, MIXED + max(i - 1, 0) * D + at))
    return sum(jnp.where(row == where, sums[:, at : at + 128], 0.0) for where, at in pieces)


def qu_part(ring, info, y, dqu, sums, keep, send):
    core, group, spot = info[0], info[1], info[2]
    rows = D // ring.count
    tile = 256
    last = ring.size * slot_rows(ring)
    extra = vector_rows(group, sums).astype(LOW)
    for out, half in ((send, 1 - core), (keep, core)):
        columns = pl.ds(pl.multiple_of(half * PART, 128), PART)
        out[last : last + SIDES, :] = extra
        for at in range(0, D, tile):
            block = dot_rows(y[:, at : at + tile], dqu[:, columns]).astype(LOW)
            for offset in range(0, tile, rows):
                dp = (at + offset) // rows
                slot = slot_in(ring, spot ^ ring.spot_of(dp), half)
                begin = slot * slot_rows(ring) + (group ^ ring.group_of(dp)) * (QU_TILES * rows)
                for i in range(QU_TILES):
                    row = pl.multiple_of(begin + i * rows, 16)
                    out[pl.ds(row, rows), :] = block[offset : offset + rows, i * 128 : (i + 1) * 128]


def grads_kernel(ring, info, far_mixed, far_active, far_grad, far_y, far_dqu, sums, keep, send, *scratch):
    mixed, active, grad, y, dqu, sems = scratch
    grad_in = started([(far_grad, grad), (far_mixed, mixed)], sems.at[0])
    active_in = started([(far_active, active)], sems.at[1])
    rest_in = started([(far_y, y), (far_dqu, dqu)], sems.at[2])
    grad_in()
    od_part(ring, info, mixed, active, grad, keep, send, active_in)
    rest_in()
    qu_part(ring, info, y, dqu, sums, keep, send)


def weight_grads(ring, info, mixed, active, grad, y, dqu, sums):
    blocks = (mixed, active, grad, y, dqu)
    out = grads_shape(ring)
    return pl.pallas_call(
        functools.partial(grads_kernel, ring),
        out_shape=(out, out),
        in_specs=[smem_spec()] + [far_spec()] * len(blocks) + [full_spec(sums.shape)],
        out_specs=(full_spec(out.shape),) * 2,
        scratch_shapes=[pltpu.VMEM(a.shape, LOW) for a in blocks] + [pltpu.SemaphoreType.DMA((3,))],
        compiler_params=kernel_params(20),
        cost_estimate=cost(50 * 10**9, 12 * 1024 * 1024),
        name="weight_grads",
    )(info, *[far(a) for a in blocks], sums)


def fold_kernel(held, came, kept, sent):
    half = (held.shape[0] - SIDES) // 2
    full = 2 * half
    kept[0:half, :] = held[0:half, :].astype(F32) + came[0:half, :].astype(F32)
    sent[0:half, :] = (held[half:full, :].astype(F32) + came[half:full, :].astype(F32)).astype(LOW)
    sides = held[full : full + SIDES, :].astype(LOW).astype(F32) + came[full : full + SIDES, :].astype(F32)
    kept[half : half + SIDES, :] = sides
    sent[half : half + SIDES, :] = sides.astype(LOW)


def fold(held, came):
    half = (held.shape[0] - SIDES) // 2 + SIDES
    outs = (shaped((half, 128), F32), shaped((half, 128), LOW))
    return pl.pallas_call(
        fold_kernel,
        out_shape=outs,
        in_specs=[full_spec(held.shape), full_spec(came.shape)],
        out_specs=tuple(full_spec(a.shape) for a in outs),
        compiler_params=kernel_params(20),
        cost_estimate=cost(0, 1024 * 1024),
        name="fold_gradients",
    )(held, came)


VECTOR_ROWS = (7 * D + FF) // 128


def close_kernel(held, came, before, *outs):
    qus, od, squares = outs[:GROUP], outs[GROUP], outs[GROUP + 1]
    rows = qus[0].shape[0] - SIDES
    full = held.shape[0] - SIDES
    sides = held[full : full + SIDES, :].astype(LOW).astype(F32) + came[full : full + SIDES, :].astype(F32)
    lanes = before[...]
    begin = 0
    for piece in (*qus, od):
        length = rows if piece is not od else od.shape[0]
        here = slice(begin, begin + length)
        begin += length
        total = held[here, :].astype(F32) + came[here, :].astype(F32)
        piece[0:length, :] = total.astype(LOW)
        lanes = lanes + jnp.sum((total * total).reshape(length // 8, 8, 128), axis=0)
    squares[...] = lanes
    high = lanes.astype(LOW).astype(F32)
    rest = sides[VECTOR_ROWS + 16 :]
    sides = jnp.concatenate([sides[:VECTOR_ROWS], high, lanes - high, rest], axis=0).astype(LOW)
    for piece in qus:
        piece[rows : rows + SIDES, :] = sides


def close(ring, held, came, before):
    rows = QU_TILES * (D // ring.count)
    outs = [shaped((rows + SIDES, 128), LOW)] * GROUP
    outs += [shaped((OD_TILES * (SIDE + UNITS) // ring.size, 128), LOW), shaped((8, 128), F32)]
    return pl.pallas_call(
        close_kernel,
        out_shape=tuple(outs),
        in_specs=[full_spec(held.shape), full_spec(came.shape), full_spec(before.shape)],
        out_specs=tuple(full_spec(a.shape) for a in outs),
        compiler_params=kernel_params(16),
        cost_estimate=cost(0, 1024 * 1024),
        name="close_gradients",
    )(held, came, before)


def join_kernel(info, *refs):
    core = info[0]
    firsts, seconds, (od_first, od_second), outs = refs[:4], refs[4:8], refs[8:10], refs[10:]
    sent, vec, squares, vec_squares = outs
    rows = firsts[0].shape[0] - SIDES
    sides = []
    for pieces in (firsts, seconds):
        parts = [a[rows : rows + SIDES, :].astype(F32) for a in pieces]
        sides.append((parts[0] + parts[1]) + (parts[2] + parts[3]))
    squares[...] = sides[0][VECTOR_ROWS : VECTOR_ROWS + 8] + sides[0][VECTOR_ROWS + 8 : VECTOR_ROWS + 16]
    own = [(a[:VECTOR_ROWS] * a[:VECTOR_ROWS]).reshape(VECTOR_ROWS // 8, 8, 128) for a in sides]
    vec_squares[...] = jnp.sum(own[0], axis=0) + jnp.sum(own[1], axis=0)
    vec[...] = jnp.where(core == 0, sides[0], sides[1])

    def write(pieces, od):
        for r in range(GROUP):
            sent[r * rows : (r + 1) * rows, :] = pieces[r][0:rows, :]
        sent[GROUP * rows :, :] = od[...]

    pl.when(core == 0)(functools.partial(write, seconds, od_second))
    pl.when(core == 1)(functools.partial(write, firsts, od_first))


def join(info, firsts, seconds, od_first, od_second):
    rows = firsts[0].shape[0] - SIDES
    outs = (shaped((GROUP * rows + od_first.shape[0], 128), LOW), shaped((SIDES, 128), F32))
    outs += (shaped((8, 128), F32),) * 2
    blocks = (*firsts, *seconds, od_first, od_second)
    return pl.pallas_call(
        join_kernel,
        out_shape=outs,
        in_specs=[smem_spec()] + [full_spec(a.shape) for a in blocks],
        out_specs=tuple(full_spec(a.shape) for a in outs),
        compiler_params=kernel_params(16),
        cost_estimate=cost(0, 1024 * 1024),
        name="join_members",
    )(info, *blocks)


def adam_update(weight, grad, first, second, factor, rate):
    clipped = grad * factor
    first_new = BETA_ONE * first + (1.0 - BETA_ONE) * clipped
    second_new = BETA_TWO * second + (1.0 - BETA_TWO) * clipped * clipped
    first_hat = first_new / (1.0 - BETA_ONE**STEP)
    second_hat = second_new / (1.0 - BETA_TWO**STEP)
    weight_new = weight - rate * (
        first_hat / (jnp.sqrt(second_hat) + ADAM_EPS) + WEIGHT_DECAY * weight
    )
    return (weight_new, first_new, second_new)


def mixed_tile(tile, member):
    at = tile * 128
    if at >= 3 * SIDE:
        return 2, up_column(member, at - 3 * SIDE)
    width = SIDE // SPREAD
    kind, within = at // SIDE, at % SIDE
    return 0, qkv_column(kind, within // width, member) + within % width


def adam_kernel(info, factor_ref, *refs):
    core, group = info[0], info[1]
    step = pl.program_id(0)
    factor = factor_ref[0]
    qus, refs = (refs[:4], refs[4:8]), refs[8:]
    ods, came, refs = refs[:2], refs[2], refs[3:]
    olds, news = refs[:12], refs[12:]
    few, many = olds[0].shape[1], olds[9].shape[1]
    rows = (qus[0][0].shape[0] - SIDES) // QU_TILES
    od_rows = ods[0].shape[0] // OD_TILES

    def update(which, column, grad):
        columns = slice(column, column + 128)
        weight, first, second = [olds[3 * which + i][0, :, columns] for i in range(3)]
        fresh = adam_update(weight, grad.astype(F32), first, second, factor, LEARN_RATE)
        for i in range(3):
            news[3 * which + i][0, :, columns] = fresh[i]

    def rows_of(ref, begin, length):
        return ref[pl.ds(pl.multiple_of(begin + step * length, 16), length), :]

    def both_halves(here):
        for half in range(2):
            for tile in range(OD_TILES):
                column = half * (D // 2) + tile * 128
                ref, begin = (ods[here], 0) if half == here else (came, GROUP * QU_TILES * rows)
                begin = begin + tile * od_rows
                update(3, column, rows_of(ref, begin, many))
                update(1, column, rows_of(ref, begin + od_rows - rows, few))
            for member in range(GROUP):
                if half == here:
                    for g in range(GROUP):

                        @pl.when(group == g)
                        def _(ref=qus[here][member ^ g]):
                            for tile in range(QU_TILES):
                                which, column = mixed_tile(half * QU_TILES + tile, member)
                                update(which, column, rows_of(ref, tile * rows, few))
                else:
                    for tile in range(QU_TILES):
                        which, column = mixed_tile(half * QU_TILES + tile, member)
                        begin = ((group ^ member) * QU_TILES + tile) * rows
                        update(which, column, rows_of(came, begin, few))

    for here in range(2):
        pl.when(core == here)(functools.partial(both_halves, here))


def adam(info, factor, qus, ods, came, olds):
    steps = max(1, olds[0].shape[1] // 16)

    def master(a):
        return pl.BlockSpec((1, a.shape[1] // steps, a.shape[2]), lambda i: (0, i, 0))

    grads = (*qus[0], *qus[1], *ods, came)
    return pl.pallas_call(
        adam_kernel,
        grid=(steps,),
        out_shape=tuple(shaped(a.shape, F32) for a in olds),
        in_specs=[smem_spec(), smem_spec()]
        + [full_spec(a.shape) for a in grads]
        + [master(a) for a in olds],
        out_specs=tuple(master(a) for a in olds),
        compiler_params=kernel_params(28),
        name="adamw",
    )(info, factor, *grads, *[far(a) for a in olds])


def doc_tables(lengths, rows):
    seqs = lengths.shape[0]
    ends = jnp.cumsum(lengths, axis=1)
    places = jnp.arange(rows, dtype=jnp.int32)
    past = places[None, :, None] >= ends[:, None, :]
    begins = jnp.sum(jnp.where(past, lengths[:, None, :], 0), axis=2)
    position = (places[None, :] - begins).reshape(seqs * rows, 1)
    half = ROT // 2
    inverse = 10000.0 ** (-(jnp.arange(half, dtype=F32) * 2.0) / ROT)
    lanes = jnp.concatenate([inverse, inverse, jnp.zeros(HEAD_DIM - ROT, F32)])
    angles = position.astype(F32) * jnp.concatenate([lanes, lanes])[None, :]
    allowed = (places[None, None, :] <= places[None, :, None]) & (places[None, None, :] >= begins[:, :, None])
    mask = jnp.where(allowed, 0.0, -1e30).reshape(seqs * rows, rows).astype(F32)
    return jnp.cos(angles), jnp.sin(angles), mask


def shards(
    x_in,
    cotangent,
    doc_lengths,
    w_qkv,
    w_out,
    w_up,
    w_down,
    vectors,
    m_qkv,
    m_out,
    m_up,
    m_down,
    m_vectors,
    v_qkv,
    v_out,
    v_up,
    v_down,
    v_vectors,
):
    place = Place()
    ring, core, group, spot = place.ring, place.core, place.group, place.spot
    info = place.info()
    local_rows, width = x_in.shape
    seqs, docs = doc_lengths.shape
    rows = local_rows // seqs
    in_rows = w_qkv.shape[1]
    shard = vectors.shape[1]
    members = range(1, GROUP)

    vec_block = jnp.pad(vectors[0].astype(LOW), (0, in_rows * 128 - shard)).reshape(in_rows, 128)
    keep_qu, send_qu, keep_od, send_od = pack(info, w_qkv, w_out, w_up, w_down, vec_block)
    came_qu = place.sibling(send_qu)
    came_od = place.sibling(send_od)

    def member_columns(block, *waited):
        qu = jnp.where(core == block, keep_qu, came_qu)
        sent = [after(take(qu, group ^ r), *waited) for r in members]
        return [take(qu, group)] + [place.member(a, r) for a, r in zip(sent, members)]

    def gather(block, *waited):
        late = after(block, *waited)
        return [block] + [place.member(late, r) for r in members]

    def to_owners(slots):
        return [slots[0]] + [place.member(slots[r], r) for r in members]

    def total_of(slots):
        return sum(a.astype(F32) for a in slots)

    def block_vectors(parts):
        pieces = jnp.concatenate([a[:, :, 0 : -(-shard // 128), PART:] for a in parts])
        pieces = pieces.reshape(ring.size * GROUP, -1)[:, :shard]
        dp = jnp.arange(ring.count, dtype=jnp.int32)
        difference = ring.spot_of(dp) ^ spot
        slot = jnp.where(core == 0, ring.slot(difference, 0), ring.slot(difference, 1))
        vec = jnp.take(pieces, slot * GROUP + (ring.group_of(dp) ^ group), axis=0, mode="clip")
        vec = vec.reshape(-1).astype(F32)
        b_qkv, b_out, b_up, b_down, gain, ln_bias = jnp.split(
            vec, [3 * D, 4 * D, 4 * D + FF, 5 * D + FF, 6 * D + FF]
        )
        b_qkv = take(b_qkv.reshape(3 * SPREAD, GROUP, -1), group, 1).reshape(1, -1)
        b_up = take(b_up.reshape(SPREAD, GROUP, -1), group, 1).reshape(1, -1)
        return (b_qkv, b_up, gain[None], ln_bias[None]), (b_out + b_down)[None], gain[None]

    x_own = take(x_in.reshape(2, rows, width), core)
    cot_own = take(cotangent.reshape(2, rows, width), core)
    len_own = take(doc_lengths, core)
    len_rows = jnp.zeros((16, width), LOW).at[0, :docs].set(len_own.astype(LOW))
    x_sent = jnp.concatenate([x_own, len_rows])

    qu_came = member_columns(0)
    qu_own = jnp.stack(qu_came)[None]
    x_group = gather(x_sent, qu_came[1])
    qu_mine = jnp.where(core == 1, keep_qu, came_qu)
    sent = [after(jnp.concatenate([take(qu_mine, group ^ r), cot_own]), *x_group[2:]) for r in members]
    qu_cot = [place.member(a, r) for a, r in zip(sent, members)]
    od_own = after(jnp.where(core == 0, keep_od, came_od)[None], x_group[1])
    od = [jnp.concatenate([od_own, place.across(od_own, 0)])]
    qu = [jnp.concatenate([qu_own, place.across(qu_own, 0)])]
    for step in range(1, ring.bits):
        od.append(place.across(jnp.concatenate(od), step))
        qu.append(place.across(jnp.concatenate(qu), step))
    qu_sibling = [place.sibling(a) for a in qu[:-1]] + [place.sibling(after(qu[-1], *x_group[1:]))]
    parts_first = (*qu, *od, *qu_sibling, *(place.sibling(a) for a in od))
    lengths = jnp.stack([a[rows, :docs] for a in x_group]).astype(jnp.int32)
    tables = doc_tables(lengths, rows)
    vecs_first, bias_first, gain_first = block_vectors(qu)

    first = forward(ring, info, parts_first, x_group, tables, vecs_first, rows)
    kept_first, tables = first[GROUP:], first[-3:]
    qu_cot = [after(a, first[0]) for a in qu_cot]
    came = to_owners(first[:GROUP])
    od_own = after(jnp.where(core == 1, keep_od, came_od)[None], first[0])
    od_late = [jnp.concatenate([od_own, place.across(od_own, 0)])]
    came[1] = after(came[1], od_late[0])
    hidden_first = (x_own.astype(F32) + total_of(came) + bias_first).astype(LOW)
    hidden_group = gather(hidden_first)
    qu_own = jnp.stack([take(qu_mine, group)] + [a[:in_rows] for a in qu_cot])[None]
    qu_late = [jnp.concatenate([qu_own, after(place.across(qu_own, 0), hidden_first)])]
    for step in range(1, ring.bits):
        od_late.append(after(place.across(jnp.concatenate(od_late), step), *hidden_group[1:]))
        qu_late.append(after(place.across(jnp.concatenate(qu_late), step), *hidden_group[1:]))
    qu_sibling, od_sibling = [
        [place.sibling(after(a, *hidden_group[1:])) for a in late] for late in (qu_late, od_late)
    ]
    parts_second = (*qu_late, *od_late, *qu_sibling, *od_sibling)
    vecs_second, bias_second, gain_second = block_vectors(qu_late)
    second = middle(ring, info, parts_second, hidden_group, [cot_own, *qu_cot], tables, vecs_second, rows)
    sums_second, y_second, mixed_second, active_second, dqu_second, grad_second = second[GROUP : GROUP + 6]
    z_second = second[GROUP + 6 :]

    def rows_backward(rows_low, grad_low, dy, gain):
        rows_now = rows_low.astype(F32)
        centered = rows_now - jnp.mean(rows_now, axis=-1, keepdims=True)
        variance = jnp.mean(centered * centered, axis=-1, keepdims=True)
        inverse_std = lax.rsqrt(variance + NORM_EPS)
        normed = centered * inverse_std
        scaled = dy * gain
        inner_mean = jnp.mean(scaled, axis=-1, keepdims=True)
        inner_cross = jnp.mean(scaled * normed, axis=-1, keepdims=True)
        return (grad_low.astype(F32) + inverse_std * (scaled - inner_mean - normed * inner_cross)).astype(LOW)

    def to_members(pieces):
        return [pieces[0]] + [place.member(pieces[r], r) for r in members]

    steps = list(reversed(range(ring.bits)))

    def ring_fold(held, *waited):
        kept, sent = held
        for step in steps[:-1]:
            kept, sent = fold(kept, after(place.across(sent, step), *waited))
        return kept, sent

    dy_second = to_owners(second[:GROUP])
    grads = weight_grads(ring, info, mixed_second, active_second, grad_second, y_second, dqu_second, sums_second)
    mid_grad = rows_backward(hidden_first, cot_own, total_of(dy_second), gain_second)
    mid_group = gather(mid_grad)
    sent = place.sibling(after(grads[1], *dy_second[1:]))
    second_held = ring_fold(fold(grads[0], after(sent, mid_grad)))

    mid_late = [after(mid_group[0], *second_held)] + mid_group[1:]
    back = backward(ring, info, mid_late, kept_first, rows)
    keep, send = back[GROUP:]
    z_came = to_owners([z_second[0]] + [after(a, *mid_group[1:]) for a in z_second[1:]])
    kept, sent = second_held
    none = jnp.zeros((8, 128), F32)
    *qu_second, od_second, squares_second = close(ring, kept, after(place.across(sent, 0), send), none)
    send = after(send, *qu_second, *z_came[1:])
    qu_slots_second = to_members(qu_second)
    kept, sent = ring_fold(fold(keep, place.sibling(send)))
    start_came = to_owners(back[:GROUP])
    came = after(place.across(after(sent, *start_came[1:]), 0), *qu_slots_second[1:])
    *qu_first, od_first, _ = close(ring, kept, came, squares_second)
    qu_slots_first = to_members(qu_first)
    grads_sent, vec, squares, vec_squares = join(info, qu_slots_first, qu_slots_second, od_first, od_second)
    squares = squares + place.sibling(squares)
    for step in range(ring.bits):
        squares = squares + place.across(squares, step)
    squares = jnp.sum(squares + vec_squares)
    start_came[1:] = [after(a, grads_sent) for a in start_came[1:]]
    start_grad = rows_backward(x_own, mid_grad, total_of(start_came), gain_first)
    hidden_second = (hidden_first.astype(F32) + total_of(z_came) + bias_second).astype(LOW)

    grad_norm = jnp.sqrt(squares)
    factor = jnp.minimum(1.0, CLIP_LEVEL / (grad_norm + 1e-06))

    def own_block(one, two):
        came = place.sibling(jnp.where(core == 0, two, one))
        mine = jnp.where(core == 0, one, two)
        return [jnp.where(core == h, mine, came) for h in range(2)]

    grads_came = place.sibling(grads_sent)
    vec_share = after(vec, grads_sent).reshape(-1)[: ring.count * shard].reshape(ring.count, shard)
    vec_share = take(vec_share, lax.axis_index("dp"))[None]
    olds = (w_qkv, m_qkv, v_qkv, w_out, m_out, v_out, w_up, m_up, v_up, w_down, m_down, v_down)
    qus = (qu_slots_first, qu_slots_second)
    news = adam(info, factor[None], qus, (od_first, od_second), grads_came, olds)
    new_vec = adam_update(vectors, vec_share, m_vectors, v_vectors, factor, VECTOR_RATE)

    outputs = own_block(jnp.stack([hidden_first, start_grad]), jnp.stack([hidden_second, mid_grad]))
    outputs = jnp.concatenate(outputs, axis=1)
    hidden_out, input_grads = outputs[:1], outputs[1:]
    return (
        hidden_out,
        input_grads,
        *(news[3 * i] for i in range(4)),
        new_vec[0],
        *(news[3 * i + 1] for i in range(4)),
        new_vec[1],
        *(news[3 * i + 2] for i in range(4)),
        new_vec[2],
        grad_norm,
    )


def solution(mesh):
    return jax.shard_map(
        shards,
        mesh=mesh,
        in_specs=(
            P("dp", None),
            P("dp", None),
            P("dp", None),
            P("section", "dp", None),
            P("section", "dp", None),
            P("section", "dp", None),
            P("section", "dp", None),
            P("section", "dp"),
            P("section", "dp", None),
            P("section", "dp", None),
            P("section", "dp", None),
            P("section", "dp", None),
            P("section", "dp"),
            P("section", "dp", None),
            P("section", "dp", None),
            P("section", "dp", None),
            P("section", "dp", None),
            P("section", "dp"),
        ),
        out_specs=(
            P("section", "dp", None),
            P("section", "dp", None),
            P("section", "dp", None),
            P("section", "dp", None),
            P("section", "dp", None),
            P("section", "dp", None),
            P("section", "dp"),
            P("section", "dp", None),
            P("section", "dp", None),
            P("section", "dp", None),
            P("section", "dp", None),
            P("section", "dp"),
            P("section", "dp", None),
            P("section", "dp", None),
            P("section", "dp", None),
            P("section", "dp", None),
            P("section", "dp"),
            P(),
        ),
        check_vma=False,
    )
```

```python
import functools

import jax
import jax.numpy as jnp
from jax import lax
from jax.experimental import pallas as pl
from jax.experimental.pallas import tpu as pltpu
from jax.sharding import PartitionSpec as P

D = 1024
FF = 4096
HEADS = 16
HEAD_DIM = 64
ROT = 16
STEP = 10


NORM_EPS = 1e-05
BETA_ONE = 0.9
BETA_TWO = 0.95
LEARN_RATE = 0.05
VECTOR_RATE = 0.3
WEIGHT_DECAY = 0.01
CLIP_LEVEL = 1.0
ADAM_EPS = 1e-08

AXES = ("section", "dp")
GROUP = 4
SPREAD = 1
LOW = jnp.bfloat16
F32 = jnp.float32
SIDE = D // GROUP
UNITS = FF // GROUP
MIXED = 3 * SIDE + UNITS
PART = MIXED // 2
WIRE = PART + 128


class Ring:
    def __init__(self, count):
        self.count = count
        self.low = count // (GROUP * SPREAD)
        self.size = SPREAD * self.low
        self.bits = self.size.bit_length() - 1

    def index(self, g, t):
        return ((t // self.low) * GROUP + g) * self.low + t % self.low

    def group_of(self, dp):
        return (dp // self.low) % GROUP

    def spot_of(self, dp):
        return (dp // (GROUP * self.low)) * self.low + dp % self.low

    def order(self, core):
        steps = list(range(self.bits))
        if SPREAD > 1 or core == 1:
            steps.reverse()
        return steps

    def turn(self, slot, core):
        return sum(((slot >> s) & 1) << b for s, b in enumerate(self.order(core)))

    def slot(self, difference, core):
        return sum(((difference >> b) & 1) << s for s, b in enumerate(self.order(core)))


class Place:
    def __init__(self):
        self.ring = Ring(lax.axis_size("dp"))
        self.core = lax.axis_index("section")
        dp = lax.axis_index("dp")
        self.group = self.ring.group_of(dp)
        self.spot = self.ring.spot_of(dp)

    def info(self):
        return jnp.stack([self.core, self.group, self.spot]).astype(jnp.int32)

    def move(self, block, where):
        ring = self.ring
        route = []
        for core in range(2):
            for g in range(GROUP):
                for t in range(ring.size):
                    c, h, u = where(core, g, t)
                    route.append((core * ring.count + ring.index(g, t), c * ring.count + ring.index(h, u)))
        return lax.ppermute(block, AXES, route)

    def sibling(self, block):
        return self.move(block, lambda c, g, t: (1 - c, g, t))

    def member(self, block, distance):
        return self.move(block, lambda c, g, t: (c, g ^ distance, t))

    def toward(self, block, step):
        return self.move(block, lambda c, g, t: (c, g ^ (2, 1)[(step + c) % 2], t))

    def across(self, block, step):
        return self.move(block, lambda c, g, t: (c, g, t ^ (1 << self.ring.order(c)[step])))


def take(block, index, axis=0):
    return lax.dynamic_index_in_dim(block, index, axis, keepdims=False)


def after(block, *waited):
    return lax.optimization_barrier((block, waited))[0]


def dot(left, right):
    return jnp.dot(left, right, preferred_element_type=F32)


def dot_cols(left, right):
    return lax.dot_general(left, right, (((1,), (1,)), ((), ())), preferred_element_type=F32)


def dot_rows(left, right):
    return lax.dot_general(left, right, (((0,), (0,)), ((), ())), preferred_element_type=F32)


def full_spec(shape):
    return pl.BlockSpec(shape, lambda *_: (0,) * len(shape))


def far_spec():
    return pl.BlockSpec(memory_space=pltpu.HBM)


def far(block):
    return pltpu.with_memory_space_constraint(block, pltpu.HBM)


def any_spec():
    return pl.BlockSpec(memory_space=pl.ANY)


def smem_spec():
    return pl.BlockSpec(memory_space=pltpu.SMEM)


def shaped(shape, dtype):
    return jax.ShapeDtypeStruct(shape, dtype)


def kernel_params(mebibytes):
    return pltpu.CompilerParams(vmem_limit_bytes=mebibytes * 1024 * 1024)


def up_pieces():
    run = UNITS // SPREAD
    cuts = sorted({0, PART - 3 * SIDE, UNITS} | {run * i for i in range(SPREAD)})
    pieces = []
    for begin, end in zip(cuts[:-1], cuts[1:]):
        column = 3 * SIDE + begin
        pieces.append((begin, column // PART, column % PART, end - begin))
    return pieces


def up_column(g, local):
    run = UNITS // SPREAD
    return (local // run * GROUP + g) * run + local % run


def qkv_column(kind, run, g):
    width = SIDE // SPREAD
    return ((kind * SPREAD + run) * GROUP + g) * width


def pack_kernel(info, qkv_hbm, out_hbm, up_hbm, down_hbm, vec, keep_qu, send_qu, keep_od, send_od, *scratch):
    w_qkv, w_out, w_up, w_down, sems = scratch
    pairs = ((qkv_hbm, w_qkv), (up_hbm, w_up), (down_hbm, w_down), (out_hbm, w_out))
    copies = [pltpu.make_async_copy(far.at[0], near, sems.at[i]) for i, (far, near) in enumerate(pairs)]
    for copy in copies:
        copy.start()
    rows = w_qkv.shape[0]
    ff_rows = w_down.shape[0]
    width = SIDE // SPREAD
    core = info[0]

    def write_qu(halves):
        for g in range(GROUP):
            for kind in range(3):
                for run in range(SPREAD):
                    at = (kind * SPREAD + run) * width
                    column = qkv_column(kind, run, g)
                    halves[0][g, :, at : at + width] = w_qkv[:, column : column + width].astype(LOW)
            for local, half, at, length in up_pieces():
                column = up_column(g, local)
                halves[half][g, :, at : at + length] = w_up[:, column : column + length].astype(LOW)
            for half in range(2):
                halves[half][g, :, PART:WIRE] = vec[...]

    def write_od(halves):
        for half in range(2):
            columns = slice(half * (D // 2), (half + 1) * (D // 2))
            halves[half][0:ff_rows] = w_down[:, columns].astype(LOW)
            halves[half][ff_rows : ff_rows + rows] = w_out[:, columns].astype(LOW)

    for first, last, write, kept, sent in ((0, 2, write_qu, keep_qu, send_qu), (2, 4, write_od, keep_od, send_od)):
        for copy in copies[first:last]:
            copy.wait()
        pl.when(core == 0)(functools.partial(write, (kept, sent)))
        pl.when(core == 1)(functools.partial(write, (sent, kept)))


def pack(info, w_qkv, w_out, w_up, w_down, vec):
    rows, ff_rows = w_qkv.shape[1], w_down.shape[1]
    qu = shaped((GROUP, rows, WIRE), LOW)
    od = shaped((ff_rows + rows, D // 2), LOW)
    return pl.pallas_call(
        pack_kernel,
        out_shape=(qu, qu, od, od),
        in_specs=[smem_spec()] + [far_spec()] * 4 + [full_spec(vec.shape)],
        out_specs=tuple(full_spec(a.shape) for a in (qu, qu, od, od)),
        scratch_shapes=[pltpu.VMEM(a.shape[1:], F32) for a in (w_qkv, w_out, w_up, w_down)]
        + [pltpu.SemaphoreType.DMA((4,))],
        compiler_params=kernel_params(20),
        name="pack_weights",
    )(info, far(w_qkv), far(w_out), far(w_up), far(w_down), vec)


def stack_kernel(*refs):
    for i, ref in enumerate(refs[:-1]):
        refs[-1][0, i] = ref[...]


def stack_members(pieces):
    out = shaped((1, len(pieces), *pieces[0].shape), LOW)
    return pl.pallas_call(
        stack_kernel,
        out_shape=out,
        in_specs=[full_spec(a.shape) for a in pieces],
        out_specs=full_spec(out.shape),
        compiler_params=kernel_params(16),
        cost_estimate=cost(50 * 10**9, 1024 * 1024),
        name="stack_members",
    )(*pieces)


def weight_copies(ring, info, parts, wqu, wout, wdown, sems):
    core, group, spot = info[0], info[1], info[2]
    qu_copies, od_copies = [], []
    count = len(parts) // 4
    for which in range(2):
        half = core if which == 0 else 1 - core
        qu_at = pl.multiple_of(half * PART, 128)
        od_at = pl.multiple_of(half * (D // 2), 128)
        slot = 0
        for piece in range(count):
            qu, od = parts[2 * count * which + piece], parts[2 * count * which + count + piece]
            rows = qu.shape[2]
            ff_rows = od.shape[1] - rows
            for i in range(qu.shape[0]):
                straight, turned = ring.turn(slot, 0), ring.turn(slot, 1)
                there = spot ^ (straight + half * (turned - straight))
                slot += 1
                ff_row = pl.multiple_of(there * ff_rows, ff_rows)
                out_row = pl.multiple_of(there * rows, rows)
                far = wdown.at[pl.ds(ff_row, ff_rows), pl.ds(od_at, D // 2)]
                od_copies.append(pltpu.make_async_copy(od.at[i, pl.ds(0, ff_rows)], far, sems.at[0]))
                far = wout.at[pl.ds(out_row, rows), pl.ds(od_at, D // 2)]
                od_copies.append(pltpu.make_async_copy(od.at[i, pl.ds(ff_rows, rows)], far, sems.at[0]))
                for r in range(GROUP):
                    row = pl.multiple_of(ring.index(group ^ r, there) * rows, rows)
                    far = wqu.at[pl.ds(row, rows), pl.ds(qu_at, PART)]
                    qu_copies.append(pltpu.make_async_copy(qu.at[i, r, :, pl.ds(0, PART)], far, sems.at[1]))
    return qu_copies, od_copies


def head_masks(dtype):
    lane = lax.broadcasted_iota(jnp.int32, (1, SIDE), 1) // HEAD_DIM
    return [(lane == h).astype(dtype) for h in range(SIDE // HEAD_DIM)]


def by_head(parts):
    lane = lax.broadcasted_iota(jnp.int32, (1, SIDE), 1) // HEAD_DIM
    total = parts[-1]
    for h in range(len(parts) - 2, -1, -1):
        total = jnp.where(lane == h, parts[h], total)
    return total


def turning(cosine, sine, back):
    lane = lax.broadcasted_iota(jnp.int32, sine.shape, 1) % HEAD_DIM
    first = jnp.where(lane < ROT // 2, sine, 0.0)
    second = jnp.where(lane < ROT // 2, 0.0, sine)
    if back:
        second = -second
    else:
        first = -first
    wide = SIDE // cosine.shape[1]
    return [jnp.concatenate([a] * wide, axis=1) for a in (cosine, first, second)]


def turn(part, tables):
    cosine, first, second = tables
    ahead = pltpu.roll(part, SIDE - ROT // 2, 1)
    behind = pltpu.roll(part, ROT // 2, 1)
    return part * cosine + ahead * first + behind * second


def normalise(rows):
    centered = rows - jnp.mean(rows, axis=-1, keepdims=True)
    variance = jnp.mean(centered * centered, axis=-1, keepdims=True)
    return centered * lax.rsqrt(variance + NORM_EPS)


def no_wait():
    pass


def forward_part(x_refs, tables, vecs, wqu, wout, wdown, kept, z_refs, waits, done, normed_ref=None):
    cosine, sine, mask = tables
    b_qkv, b_up, gain, ln_bias = vecs
    y, qkv, probs, mixed, active, slope = kept
    rows = z_refs[0].shape[0]
    for r in range(GROUP):
        normed = normalise(x_refs[r][0:rows, :].astype(F32))
        if normed_ref is not None:
            normed_ref[r * rows : (r + 1) * rows, :] = normed
        y[r * rows : (r + 1) * rows, :] = (normed * gain[...] + ln_bias[...]).astype(LOW)
    done(0)
    waits[0]()
    waits[2]()
    forth = turning(cosine[...], sine[...], False)
    for kind in range(3):
        columns = slice(kind * SIDE, (kind + 1) * SIDE)
        part = dot(y[...], wqu[:, columns]) + b_qkv[:, columns]
        if kind < 2:
            part = turn(part, forth)
        qkv[:, columns] = part.astype(LOW)
    done(1)
    masks = head_masks(LOW)
    heads = len(masks)
    for r in range(GROUP):
        here = slice(r * rows, (r + 1) * rows)
        query, keys, values = [qkv[here, k * SIDE : (k + 1) * SIDE] for k in range(3)]
        stacked = jnp.concatenate([query * m for m in masks], axis=0)
        scores = dot_cols(stacked, keys) * HEAD_DIM ** (-0.5)
        scores = scores.reshape(heads, rows, rows) + mask[here, :][None]
        expo = jnp.exp(scores - jnp.max(scores, axis=-1, keepdims=True))
        prob = expo / jnp.sum(expo, axis=-1, keepdims=True)
        prob = prob.reshape(heads * rows, rows)
        probs[r * heads * rows : (r + 1) * heads * rows, :] = prob
        full = dot(prob.astype(LOW), values)
        mixed[here, :] = by_head([full[h * rows : (h + 1) * rows] for h in range(heads)]).astype(LOW)
    done(2)
    done(3)
    tile = 256
    for at in range(0, UNITS, tile):
        hidden = dot(y[...], wqu[:, 3 * SIDE + at : 3 * SIDE + at + tile]) + b_up[:, at : at + tile]
        share = 0.5 * (1.0 + lax.erf(hidden * (0.5**0.5)))
        density = jnp.exp(-0.5 * hidden * hidden) * (0.5 / jnp.pi) ** 0.5
        active[:, at : at + tile] = (hidden * share).astype(LOW)
        slope[:, at : at + tile] = share + hidden * density
    done(4)
    done(5)
    waits[1]()
    for at in range(0, D, tile):
        branch = dot(mixed[...], wout[:, at : at + tile]) + dot(active[...], wdown[:, at : at + tile])
        for r in range(GROUP):
            z_refs[r][:, at : at + tile] = branch[r * rows : (r + 1) * rows].astype(LOW)


def backward_part(grad, normed, tables, wqu, wout, wdown, kept, dqu, dy_refs, sums, waits, done):
    cosine, sine, _ = tables
    y, qkv, probs, mixed, active, slope = kept
    rows = grad.shape[0] // GROUP
    tile = 256
    waits[0]()
    dmixed = dot_cols(grad[...], wout[...]).astype(LOW)
    for at in range(0, UNITS, tile):
        dactive = dot_cols(grad[...], wdown[at : at + tile, :])
        dhidden = (dactive * slope[:, at : at + tile]).astype(LOW)
        dqu[:, 3 * SIDE + at : 3 * SIDE + at + tile] = dhidden
    waits[1]()
    masks = head_masks(LOW)
    heads = len(masks)
    back = turning(cosine[...], sine[...], True)
    for r in range(GROUP):
        here = slice(r * rows, (r + 1) * rows)
        query, keys, values = [qkv[here, k * SIDE : (k + 1) * SIDE] for k in range(3)]
        dstack = jnp.concatenate([dmixed[here] * m for m in masks], axis=0)
        dprob = dot_cols(dstack, values)
        prob = probs[r * heads * rows : (r + 1) * heads * rows, :]
        dvalues = dot_rows(prob.astype(LOW), dstack)
        dscore = (prob * (dprob - jnp.sum(prob * dprob, axis=-1, keepdims=True))).astype(LOW)
        full = dot(dscore, keys)
        dquery = by_head([full[h * rows : (h + 1) * rows] for h in range(heads)])
        dkeys = dot_rows(dscore, jnp.concatenate([query * m for m in masks], axis=0))
        scale = HEAD_DIM ** (-0.5)
        slot_tables = [a[here] for a in back]
        dqu[here, 0:SIDE] = turn(dquery * scale, slot_tables).astype(LOW)
        dqu[here, SIDE : 2 * SIDE] = turn(dkeys * scale, slot_tables).astype(LOW)
        dqu[here, 2 * SIDE : 3 * SIDE] = dvalues.astype(LOW)
    done()
    for at in range(0, MIXED, tile):
        sums[:, at : at + tile] = jnp.sum(dqu[:, at : at + tile].astype(F32), axis=0, keepdims=True)
    waits[2]()
    for at in range(0, D, tile):
        dy = dot_cols(dqu[...], wqu[at : at + tile, :])
        for r in range(GROUP):
            dy_refs[r][:, at : at + tile] = dy[r * rows : (r + 1) * rows].astype(LOW)
        own = grad[0:rows, at : at + tile].astype(F32)
        for i, terms in enumerate((own, dy * normed[:, at : at + tile], dy)):
            begin = MIXED + i * D + at
            sums[:, begin : begin + tile] = jnp.sum(terms, axis=0, keepdims=True)


def kept_shapes(tokens, rows):
    return [
        ((tokens, D), LOW),
        ((tokens, 3 * SIDE), LOW),
        ((tokens * (SIDE // HEAD_DIM), rows), F32),
        ((tokens, SIDE), LOW),
        ((tokens, UNITS), LOW),
        ((tokens, UNITS), F32),
    ]


def weight_scratch():
    return [
        pltpu.VMEM((D, MIXED), LOW),
        pltpu.VMEM((SIDE, D), LOW),
        pltpu.VMEM((UNITS, D), LOW),
        pltpu.SemaphoreType.DMA((2,)),
    ]


def waiter(copies):
    def wait():
        for copy in copies:
            copy.wait()

    return wait


def started(pairs, sem):
    copies = [pltpu.make_async_copy(source, target, sem) for source, target in pairs]
    for copy in copies:
        copy.start()
    return waiter(copies)


def table_scratch(tokens, rows):
    return [pltpu.VMEM((tokens, 128), F32), pltpu.VMEM((tokens, 128), F32), pltpu.VMEM((tokens, rows), F32)]


def cost(flops, moved):
    return pl.CostEstimate(flops=2 * flops, bytes_accessed=2 * moved, transcendentals=0)


def leaving(pairs, sems):
    copies = [pltpu.make_async_copy(near, far, sems.at[i]) for i, (near, far) in enumerate(pairs)]

    def go(i):
        copies[i].start()

    return go, waiter(copies)


def forward_kernel(ring, count, info, *refs):
    parts, refs = refs[:count], refs[count:]
    x_refs, refs = refs[:4], refs[4:]
    tables, refs = refs[:3], refs[3:]
    vecs, refs = refs[:4], refs[4:]
    z_refs, refs = refs[:4], refs[4:]
    far_kept, far_weights, far_tables, refs = refs[:7], refs[7:10], refs[10:13], refs[13:]
    kept, refs = refs[:7], refs[7:]
    out_sems, scratch = refs[0], refs[1:]
    weights = scratch[:3]
    qu_copies, od_copies = weight_copies(ring, info, parts, *scratch)
    for copy in qu_copies + od_copies:
        copy.start()
    pairs = [*zip(kept, far_kept), *zip(weights, far_weights), *zip(tables, far_tables)]
    go, out = leaving(pairs, out_sems)
    for i in range(10, 13):
        go(i)

    def qu_in():
        waiter(qu_copies)()
        go(7)

    def od_in():
        waiter(od_copies)()
        go(8)
        go(9)

    def done(i):
        go(i)
        if i == 0:
            go(6)

    forward_part(x_refs, tables, vecs, *weights, kept[:6], z_refs, (qu_in, od_in, no_wait), done, kept[6])
    out()


def forward(ring, info, parts, xs, tables, vecs, rows):
    tokens = GROUP * rows
    shapes = kept_shapes(tokens, rows) + [((tokens, D), F32)]
    away = [*shapes, ((D, MIXED), LOW), ((SIDE, D), LOW), ((UNITS, D), LOW)] + [(a.shape, F32) for a in tables]
    blocks = (*xs, *tables, *vecs)
    return pl.pallas_call(
        functools.partial(forward_kernel, ring, len(parts)),
        out_shape=(*[shaped((rows, D), LOW)] * GROUP, *[pltpu.HBM(*a) for a in away]),
        in_specs=[smem_spec()] + [any_spec()] * len(parts) + [full_spec(a.shape) for a in blocks],
        out_specs=tuple([full_spec((rows, D))] * GROUP + [far_spec()] * len(away)),
        scratch_shapes=[pltpu.VMEM(*a) for a in shapes]
        + [pltpu.SemaphoreType.DMA((len(away),))]
        + weight_scratch(),
        compiler_params=kernel_params(22),
        cost_estimate=cost(2 * tokens * D * (D + 2 * FF // GROUP), 16 * 1024 * 1024),
        name="forward_shard",
    )(info, *parts, *blocks)


def middle_kernel(ring, count, info, *refs):
    parts, refs = refs[:count], refs[count:]
    x_refs, refs = refs[:4], refs[4:]
    g_refs, refs = refs[:4], refs[4:]
    far_tables, refs = refs[:3], refs[3:]
    vecs, refs = refs[:4], refs[4:]
    dy_refs, refs = refs[:4], refs[4:]
    sums, away, refs = refs[0], refs[1:10], refs[10:]
    kept, refs = refs[:6], refs[6:]
    z_refs, tables, refs = refs[:4], refs[4:7], refs[7:]
    (grad, normed, dqu, in_sems, out_sems), scratch = refs[:5], refs[5:]
    rows = z_refs[0].shape[0]
    qu_copies, od_copies = weight_copies(ring, info, parts, *scratch)
    for copy in qu_copies:
        copy.start()
    tables_in = started(zip(far_tables, tables), in_sems.at[0])
    for copy in od_copies:
        copy.start()
    pairs = []
    for r, ref in enumerate(g_refs):
        at = ref.shape[0] - rows
        pairs.append((ref.at[pl.ds(at, rows)], grad.at[pl.ds(r * rows, rows)]))
    grad_in = started(pairs, in_sems.at[1])
    go, out = leaving(list(zip([kept[0], kept[3], kept[4], dqu, grad, *z_refs], away)), out_sems)

    def done(i):
        if i in (0, 3, 4):
            go((0, 3, 4).index(i))

    waits = (waiter(qu_copies), waiter(od_copies), tables_in)
    forward_part(x_refs, tables, vecs, *scratch[:3], kept, z_refs, waits, done, normed)
    grad_in()
    for i in range(4, 9):
        go(i)
    waits = (no_wait, no_wait, no_wait)
    done = functools.partial(go, 3)
    backward_part(grad, normed, tables, *scratch[:3], kept, dqu, dy_refs, sums, waits, done)
    out()


def middle(ring, info, parts, xs, gs, tables, vecs, rows):
    tokens = GROUP * rows
    shapes = kept_shapes(tokens, rows)
    away = [shapes[0], shapes[3], shapes[4], ((tokens, MIXED), LOW), ((tokens, D), LOW)]
    away += [((rows, D), LOW)] * GROUP
    sums = shaped((1, MIXED + 3 * D), F32)
    return pl.pallas_call(
        functools.partial(middle_kernel, ring, len(parts)),
        out_shape=(*[shaped((rows, D), LOW)] * GROUP, sums, *[pltpu.HBM(*a) for a in away]),
        in_specs=[smem_spec()]
        + [any_spec()] * len(parts)
        + [full_spec(a.shape) for a in xs]
        + [far_spec()] * (GROUP + 3)
        + [full_spec(a.shape) for a in vecs],
        out_specs=tuple([full_spec((rows, D))] * GROUP + [full_spec(sums.shape)] + [far_spec()] * len(away)),
        scratch_shapes=[pltpu.VMEM(*a) for a in shapes]
        + [pltpu.VMEM((rows, D), LOW)] * GROUP
        + table_scratch(tokens, rows)
        + [pltpu.VMEM((tokens, D), LOW), pltpu.VMEM((tokens, D), F32), pltpu.VMEM((tokens, MIXED), LOW)]
        + [pltpu.SemaphoreType.DMA((2,)), pltpu.SemaphoreType.DMA((9,))]
        + weight_scratch(),
        compiler_params=kernel_params(27),
        cost_estimate=cost(4 * tokens * D * (D + 2 * FF // GROUP), 16 * 1024 * 1024),
        name="forward_backward_shard",
    )(info, *parts, *xs, *[far(a) for a in (*gs, *tables)], *vecs)


def backward_kernel(ring, info, *refs):
    core = info[0]
    g_refs, refs = refs[:4], refs[4:]
    z_refs, refs = refs[:4], refs[4:]
    far_kept, far_weights, far_tables, refs = refs[:7], refs[7:10], refs[10:13], refs[13:]
    (dy_keep, dy_send, keep, send), refs = refs[:4], refs[4:]
    kept, refs = refs[:7], refs[7:]
    weights, tables, refs = refs[:3], refs[3:6], refs[6:]
    (grad, dqu, sums, in_sems, out_sems), dyz = refs[:5], refs[5:]
    y, qkv, probs, mixed, active, slope, normed = kept
    wqu, wout, wdown = weights
    far_y, far_qkv, far_probs, far_mixed, far_active, far_slope, far_normed = far_kept
    mixed_in = started([(far_mixed, mixed)], in_sems.at[0])
    active_in = started([(far_active, active)], in_sems.at[1])
    units_in = started([*zip(far_weights[1:], weights[1:]), (far_slope, slope)], in_sems.at[2])
    heads_in = started([(far_qkv, qkv), (far_probs, probs), *zip(far_tables, tables)], in_sems.at[3])
    dy_in = started([(far_weights[0], wqu), (far_normed, normed)], in_sems.at[4])
    y_in = started([(far_y, y)], in_sems.at[5])
    rows = g_refs[0].shape[0]
    z_in = started([(z_refs[r], dyz[r].at[pl.ds(rows, rows)]) for r in range(GROUP)], in_sems.at[6])
    for r in range(GROUP):
        grad[r * rows : (r + 1) * rows, :] = g_refs[r][...]
    mixed_in()
    od_part(ring, info, mixed, active, grad, keep, send, active_in)
    waits = (units_in, heads_in, dy_in)
    dy_refs = [a.at[pl.ds(0, rows)] for a in dyz]
    backward_part(grad, normed, tables, *weights, kept[:6], dqu, dy_refs, sums, waits, no_wait)
    z_in()
    targets = (dy_keep.at[0], dy_keep.at[1], dy_send.at[0], dy_send.at[1])
    outs = [
        [pltpu.make_async_copy(dyz[r], target, out_sems.at[i]) for i, (r, target) in enumerate(zip(order, targets))]
        for order in ((0, 2, 1, 3), (0, 1, 2, 3))
    ]
    for here in range(2):

        @pl.when(core == here)
        def _(copies=outs[here]):
            for copy in copies:
                copy.start()

    y_in()
    qu_part(ring, info, y, dqu, sums, keep, send)
    for here in range(2):
        pl.when(core == here)(waiter(outs[here]))


def backward(ring, info, gs, zs, held, rows):
    tokens = GROUP * rows
    outs = [shaped((2, 2 * rows, D), LOW)] * 2 + [grads_shape(ring)] * 2
    return pl.pallas_call(
        functools.partial(backward_kernel, ring),
        out_shape=tuple(outs),
        in_specs=[smem_spec()] + [full_spec(a.shape) for a in gs] + [far_spec()] * (GROUP + len(held)),
        out_specs=tuple(full_spec(a.shape) for a in outs),
        scratch_shapes=[pltpu.VMEM(a.shape, a.dtype) for a in held]
        + [pltpu.VMEM((tokens, D), LOW), pltpu.VMEM((tokens, MIXED), LOW)]
        + [pltpu.VMEM((1, MIXED + 3 * D), F32), pltpu.SemaphoreType.DMA((7,)), pltpu.SemaphoreType.DMA((4,))]
        + [pltpu.VMEM((2 * rows, D), LOW)] * GROUP,
        compiler_params=kernel_params(28),
        cost_estimate=cost(4 * tokens * D * (D + 2 * FF // GROUP), 16 * 1024 * 1024),
        name="backward_shard",
    )(info, *gs, *[far(a) for a in (*zs, *held)])


def slot_in(ring, difference, half):
    straight, turned = ring.slot(difference, 0), ring.slot(difference, 1)
    return straight + half * (turned - straight)


QU_TILES = PART // 128
OD_TILES = D // 2 // 128
SIDES = 112


def slot_rows(ring):
    return GROUP * QU_TILES * (D // ring.count) + OD_TILES * (SIDE + UNITS) // ring.size


def grads_shape(ring):
    return shaped((ring.size * slot_rows(ring) + SIDES, 128), LOW)


def od_part(ring, info, mixed, active, grad, keep, send, active_in):
    core, spot = info[0], info[2]
    out_rows = SIDE // ring.size
    ff_rows = UNITS // ring.size
    ahead = GROUP * QU_TILES * (D // ring.count)
    for i, (out, half) in enumerate(((send, 1 - core), (keep, core))):
        columns = pl.ds(pl.multiple_of(half * (D // 2), D // 2), D // 2)
        part = grad[:, columns]
        block = dot_rows(mixed[...], part).astype(LOW)
        if i == 0:
            active_in()
        for there in range(ring.size):
            slot = slot_in(ring, spot ^ there, half)
            piece = dot_rows(active[:, there * ff_rows : (there + 1) * ff_rows], part).astype(LOW)
            for tile in range(OD_TILES):
                lanes = slice(tile * 128, (tile + 1) * 128)
                row = slot * slot_rows(ring) + ahead + tile * (ff_rows + out_rows)
                out[pl.ds(pl.multiple_of(row, 16), ff_rows), :] = piece[:, lanes]
                row = pl.multiple_of(row + ff_rows, 16)
                out[pl.ds(row, out_rows), :] = block[there * out_rows : (there + 1) * out_rows, lanes]


def vector_rows(group, sums):
    width = SIDE // SPREAD
    run = UNITS // SPREAD
    row = lax.broadcasted_iota(jnp.int32, (SIDES, 128), 0)
    pieces = []
    for at in range(0, 3 * SIDE, 128):
        pieces.append(((at // width * GROUP + group) * (width // 128) + at % width // 128, at))
    for at in range(0, UNITS, 128):
        pieces.append((3 * D // 128 + D // 128 + (at // run * GROUP + group) * (run // 128) + at % run // 128, 3 * SIDE + at))
    tail = (4 * D + FF) // 128
    for i, begin in enumerate((3 * D // 128, tail, tail + D // 128, tail + 2 * D // 128)):
        for at in range(0, D, 128):
            pieces.append((begin + at // 128, MIXED + max(i - 1, 0) * D + at))
    return sum(jnp.where(row == where, sums[:, at : at + 128], 0.0) for where, at in pieces)


def qu_part(ring, info, y, dqu, sums, keep, send):
    core, group, spot = info[0], info[1], info[2]
    rows = D // ring.count
    tile = 256
    last = ring.size * slot_rows(ring)
    extra = vector_rows(group, sums).astype(LOW)
    for out, half in ((send, 1 - core), (keep, core)):
        columns = pl.ds(pl.multiple_of(half * PART, 128), PART)
        out[last : last + SIDES, :] = extra
        for at in range(0, D, tile):
            block = dot_rows(y[:, at : at + tile], dqu[:, columns]).astype(LOW)
            for offset in range(0, tile, rows):
                dp = (at + offset) // rows
                slot = slot_in(ring, spot ^ ring.spot_of(dp), half)
                begin = slot * slot_rows(ring) + (group ^ ring.group_of(dp)) * (QU_TILES * rows)
                for i in range(QU_TILES):
                    row = pl.multiple_of(begin + i * rows, 16)
                    out[pl.ds(row, rows), :] = block[offset : offset + rows, i * 128 : (i + 1) * 128]


def grads_kernel(ring, info, far_mixed, far_active, far_grad, far_y, far_dqu, sums, keep, send, *scratch):
    mixed, active, grad, y, dqu, sems = scratch
    grad_in = started([(far_grad, grad), (far_mixed, mixed)], sems.at[0])
    active_in = started([(far_active, active)], sems.at[1])
    rest_in = started([(far_y, y), (far_dqu, dqu)], sems.at[2])
    grad_in()
    od_part(ring, info, mixed, active, grad, keep, send, active_in)
    rest_in()
    qu_part(ring, info, y, dqu, sums, keep, send)


def weight_grads(ring, info, mixed, active, grad, y, dqu, sums):
    blocks = (mixed, active, grad, y, dqu)
    out = grads_shape(ring)
    return pl.pallas_call(
        functools.partial(grads_kernel, ring),
        out_shape=(out, out),
        in_specs=[smem_spec()] + [far_spec()] * len(blocks) + [full_spec(sums.shape)],
        out_specs=(full_spec(out.shape),) * 2,
        scratch_shapes=[pltpu.VMEM(a.shape, LOW) for a in blocks] + [pltpu.SemaphoreType.DMA((3,))],
        compiler_params=kernel_params(20),
        cost_estimate=cost(50 * 10**9, 12 * 1024 * 1024),
        name="weight_grads",
    )(info, *[far(a) for a in blocks], sums)


def fold_kernel(held, came, kept, sent):
    half = (held.shape[0] - SIDES) // 2
    full = 2 * half
    kept[0:half, :] = held[0:half, :].astype(F32) + came[0:half, :].astype(F32)
    sent[0:half, :] = (held[half:full, :].astype(F32) + came[half:full, :].astype(F32)).astype(LOW)
    sides = held[full : full + SIDES, :].astype(LOW).astype(F32) + came[full : full + SIDES, :].astype(F32)
    kept[half : half + SIDES, :] = sides
    sent[half : half + SIDES, :] = sides.astype(LOW)


def fold(held, came):
    half = (held.shape[0] - SIDES) // 2 + SIDES
    outs = (shaped((half, 128), F32), shaped((half, 128), LOW))
    return pl.pallas_call(
        fold_kernel,
        out_shape=outs,
        in_specs=[full_spec(held.shape), full_spec(came.shape)],
        out_specs=tuple(full_spec(a.shape) for a in outs),
        compiler_params=kernel_params(20),
        cost_estimate=cost(0, 1024 * 1024),
        name="fold_gradients",
    )(held, came)


VECTOR_ROWS = (7 * D + FF) // 128


def close_kernel(held, came, before, *outs):
    qus, od, squares = outs[:GROUP], outs[GROUP], outs[GROUP + 1]
    rows = qus[0].shape[0] - SIDES
    full = held.shape[0] - SIDES
    sides = held[full : full + SIDES, :].astype(LOW).astype(F32) + came[full : full + SIDES, :].astype(F32)
    lanes = before[...]
    begin = 0
    for piece in (*qus, od):
        length = rows if piece is not od else od.shape[0]
        here = slice(begin, begin + length)
        begin += length
        total = held[here, :].astype(F32) + came[here, :].astype(F32)
        piece[0:length, :] = total.astype(LOW)
        lanes = lanes + jnp.sum((total * total).reshape(length // 8, 8, 128), axis=0)
    squares[...] = lanes
    high = lanes.astype(LOW).astype(F32)
    rest = sides[VECTOR_ROWS + 16 :]
    sides = jnp.concatenate([sides[:VECTOR_ROWS], high, lanes - high, rest], axis=0).astype(LOW)
    for piece in qus:
        piece[rows : rows + SIDES, :] = sides


def close(ring, held, came, before):
    rows = QU_TILES * (D // ring.count)
    outs = [shaped((rows + SIDES, 128), LOW)] * GROUP
    outs += [shaped((OD_TILES * (SIDE + UNITS) // ring.size, 128), LOW), shaped((8, 128), F32)]
    return pl.pallas_call(
        close_kernel,
        out_shape=tuple(outs),
        in_specs=[full_spec(held.shape), full_spec(came.shape), full_spec(before.shape)],
        out_specs=tuple(full_spec(a.shape) for a in outs),
        compiler_params=kernel_params(16),
        cost_estimate=cost(0, 1024 * 1024),
        name="close_gradients",
    )(held, came, before)


def join_kernel(info, *refs):
    core = info[0]
    firsts, seconds, (od_first, od_second), outs = refs[:4], refs[4:8], refs[8:10], refs[10:]
    sent, vec, squares, vec_squares = outs
    rows = firsts[0].shape[0] - SIDES
    sides = []
    for pieces in (firsts, seconds):
        parts = [a[rows : rows + SIDES, :].astype(F32) for a in pieces]
        sides.append((parts[0] + parts[1]) + (parts[2] + parts[3]))
    squares[...] = sides[0][VECTOR_ROWS : VECTOR_ROWS + 8] + sides[0][VECTOR_ROWS + 8 : VECTOR_ROWS + 16]
    own = [(a[:VECTOR_ROWS] * a[:VECTOR_ROWS]).reshape(VECTOR_ROWS // 8, 8, 128) for a in sides]
    vec_squares[...] = jnp.sum(own[0], axis=0) + jnp.sum(own[1], axis=0)
    vec[...] = jnp.where(core == 0, sides[0], sides[1])

    def write(pieces, od):
        for r in range(GROUP):
            sent[r * rows : (r + 1) * rows, :] = pieces[r][0:rows, :]
        sent[GROUP * rows :, :] = od[...]

    pl.when(core == 0)(functools.partial(write, seconds, od_second))
    pl.when(core == 1)(functools.partial(write, firsts, od_first))


def join(info, firsts, seconds, od_first, od_second):
    rows = firsts[0].shape[0] - SIDES
    outs = (shaped((GROUP * rows + od_first.shape[0], 128), LOW), shaped((SIDES, 128), F32))
    outs += (shaped((8, 128), F32),) * 2
    blocks = (*firsts, *seconds, od_first, od_second)
    return pl.pallas_call(
        join_kernel,
        out_shape=outs,
        in_specs=[smem_spec()] + [full_spec(a.shape) for a in blocks],
        out_specs=tuple(full_spec(a.shape) for a in outs),
        compiler_params=kernel_params(16),
        cost_estimate=cost(0, 1024 * 1024),
        name="join_members",
    )(info, *blocks)


def adam_update(weight, grad, first, second, factor, rate):
    clipped = grad * factor
    first_new = BETA_ONE * first + (1.0 - BETA_ONE) * clipped
    second_new = BETA_TWO * second + (1.0 - BETA_TWO) * clipped * clipped
    first_hat = first_new / (1.0 - BETA_ONE**STEP)
    second_hat = second_new / (1.0 - BETA_TWO**STEP)
    weight_new = weight - rate * (
        first_hat / (jnp.sqrt(second_hat) + ADAM_EPS) + WEIGHT_DECAY * weight
    )
    return (weight_new, first_new, second_new)


def mixed_tile(tile, member):
    at = tile * 128
    if at >= 3 * SIDE:
        return 2, up_column(member, at - 3 * SIDE)
    width = SIDE // SPREAD
    kind, within = at // SIDE, at % SIDE
    return 0, qkv_column(kind, within // width, member) + within % width


def adam_kernel(info, factor_ref, *refs):
    core, group = info[0], info[1]
    step = pl.program_id(0)
    factor = factor_ref[0]
    qus, refs = (refs[:4], refs[4:8]), refs[8:]
    ods, came, refs = refs[:2], refs[2], refs[3:]
    olds, news = refs[:12], refs[12:]
    few, many = olds[0].shape[1], olds[9].shape[1]
    rows = (qus[0][0].shape[0] - SIDES) // QU_TILES
    od_rows = ods[0].shape[0] // OD_TILES

    def update(which, column, grad):
        columns = slice(column, column + 128)
        weight, first, second = [olds[3 * which + i][0, :, columns] for i in range(3)]
        fresh = adam_update(weight, grad.astype(F32), first, second, factor, LEARN_RATE)
        for i in range(3):
            news[3 * which + i][0, :, columns] = fresh[i]

    def rows_of(ref, begin, length):
        return ref[pl.ds(pl.multiple_of(begin + step * length, 16), length), :]

    def both_halves(here):
        for half in range(2):
            for tile in range(OD_TILES):
                column = half * (D // 2) + tile * 128
                ref, begin = (ods[here], 0) if half == here else (came, GROUP * QU_TILES * rows)
                begin = begin + tile * od_rows
                update(3, column, rows_of(ref, begin, many))
                update(1, column, rows_of(ref, begin + od_rows - rows, few))
            for member in range(GROUP):
                if half == here:
                    for g in range(GROUP):

                        @pl.when(group == g)
                        def _(ref=qus[here][member ^ g]):
                            for tile in range(QU_TILES):
                                which, column = mixed_tile(half * QU_TILES + tile, member)
                                update(which, column, rows_of(ref, tile * rows, few))
                else:
                    for tile in range(QU_TILES):
                        which, column = mixed_tile(half * QU_TILES + tile, member)
                        begin = ((group ^ member) * QU_TILES + tile) * rows
                        update(which, column, rows_of(came, begin, few))

    for here in range(2):
        pl.when(core == here)(functools.partial(both_halves, here))


def adam(info, factor, qus, ods, came, olds):
    steps = max(1, olds[0].shape[1] // 16)

    def master(a):
        return pl.BlockSpec((1, a.shape[1] // steps, a.shape[2]), lambda i: (0, i, 0))

    grads = (*qus[0], *qus[1], *ods, came)
    return pl.pallas_call(
        adam_kernel,
        grid=(steps,),
        out_shape=tuple(shaped(a.shape, F32) for a in olds),
        in_specs=[smem_spec(), smem_spec()]
        + [full_spec(a.shape) for a in grads]
        + [master(a) for a in olds],
        out_specs=tuple(master(a) for a in olds),
        compiler_params=kernel_params(28),
        name="adamw",
    )(info, factor, *grads, *[far(a) for a in olds])


def doc_tables(lengths, rows):
    seqs = lengths.shape[0]
    ends = jnp.cumsum(lengths, axis=1)
    places = jnp.arange(rows, dtype=jnp.int32)
    past = places[None, :, None] >= ends[:, None, :]
    begins = jnp.sum(jnp.where(past, lengths[:, None, :], 0), axis=2)
    position = (places[None, :] - begins).reshape(seqs * rows, 1)
    half = ROT // 2
    inverse = 10000.0 ** (-(jnp.arange(half, dtype=F32) * 2.0) / ROT)
    lanes = jnp.concatenate([inverse, inverse, jnp.zeros(HEAD_DIM - ROT, F32)])
    angles = position.astype(F32) * jnp.concatenate([lanes, lanes])[None, :]
    allowed = (places[None, None, :] <= places[None, :, None]) & (places[None, None, :] >= begins[:, :, None])
    mask = jnp.where(allowed, 0.0, -1e30).reshape(seqs * rows, rows).astype(F32)
    return jnp.cos(angles), jnp.sin(angles), mask


def shards(
    x_in,
    cotangent,
    doc_lengths,
    w_qkv,
    w_out,
    w_up,
    w_down,
    vectors,
    m_qkv,
    m_out,
    m_up,
    m_down,
    m_vectors,
    v_qkv,
    v_out,
    v_up,
    v_down,
    v_vectors,
):
    place = Place()
    ring, core, group, spot = place.ring, place.core, place.group, place.spot
    info = place.info()
    local_rows, width = x_in.shape
    seqs, docs = doc_lengths.shape
    rows = local_rows // seqs
    in_rows = w_qkv.shape[1]
    shard = vectors.shape[1]
    members = range(1, GROUP)

    vec_block = jnp.pad(vectors[0].astype(LOW), (0, in_rows * 128 - shard)).reshape(in_rows, 128)
    keep_qu, send_qu, keep_od, send_od = pack(info, w_qkv, w_out, w_up, w_down, vec_block)
    came_qu = place.sibling(send_qu)
    came_od = place.sibling(send_od)

    def member_columns(block, *waited):
        qu = jnp.where(core == block, keep_qu, came_qu)
        sent = [after(take(qu, group ^ r), *waited) for r in members]
        return [take(qu, group)] + [place.member(a, r) for a, r in zip(sent, members)]

    def gather(block, *waited):
        late = after(block, *waited)
        return [block] + [place.member(late, r) for r in members]

    def to_owners(slots):
        return [slots[0]] + [place.member(slots[r], r) for r in members]

    def total_of(slots):
        return sum(a.astype(F32) for a in slots)

    def block_vectors(parts):
        pieces = jnp.concatenate([a[:, :, 0 : -(-shard // 128), PART:] for a in parts])
        pieces = pieces.reshape(ring.size * GROUP, -1)[:, :shard]
        dp = jnp.arange(ring.count, dtype=jnp.int32)
        difference = ring.spot_of(dp) ^ spot
        slot = jnp.where(core == 0, ring.slot(difference, 0), ring.slot(difference, 1))
        vec = jnp.take(pieces, slot * GROUP + (ring.group_of(dp) ^ group), axis=0, mode="clip")
        vec = vec.reshape(-1).astype(F32)
        b_qkv, b_out, b_up, b_down, gain, ln_bias = jnp.split(
            vec, [3 * D, 4 * D, 4 * D + FF, 5 * D + FF, 6 * D + FF]
        )
        b_qkv = take(b_qkv.reshape(3 * SPREAD, GROUP, -1), group, 1).reshape(1, -1)
        b_up = take(b_up.reshape(SPREAD, GROUP, -1), group, 1).reshape(1, -1)
        return (b_qkv, b_up, gain[None], ln_bias[None]), (b_out + b_down)[None], gain[None]

    x_own = take(x_in.reshape(2, rows, width), core)
    cot_own = take(cotangent.reshape(2, rows, width), core)
    len_own = take(doc_lengths, core)
    len_rows = jnp.zeros((16, width), LOW).at[0, :docs].set(len_own.astype(LOW))
    x_sent = jnp.concatenate([x_own, len_rows])

    qu_came = member_columns(0)
    qu_own = jnp.stack(qu_came)[None]
    x_group = gather(x_sent, qu_came[1])
    od_own = jnp.where(core == 0, keep_od, came_od)[None]
    od = [jnp.concatenate([od_own, place.across(od_own, 0)])]
    qu = [jnp.concatenate([qu_own, place.across(qu_own, 0)])]
    for step in range(1, ring.bits):
        od.append(place.across(jnp.concatenate(od), step))
        qu.append(place.across(jnp.concatenate(qu), step))
    qu_sibling = [place.sibling(a) for a in qu[:-1]] + [place.sibling(after(qu[-1], *x_group[1:]))]
    qu_mine = jnp.where(core == 1, keep_qu, came_qu)
    waited = (*x_group[2:], od[0], qu_sibling[0])
    sent = [after(jnp.concatenate([take(qu_mine, group ^ r), cot_own]), *waited) for r in members]
    qu_cot = [place.member(a, r) for a, r in zip(sent, members)]
    parts_first = (*qu, *od, *qu_sibling, *(place.sibling(a) for a in od))
    lengths = jnp.stack([a[rows, :docs] for a in x_group]).astype(jnp.int32)
    tables = doc_tables(lengths, rows)
    vecs_first, bias_first, gain_first = block_vectors(qu)

    first = forward(ring, info, parts_first, x_group, tables, vecs_first, rows)
    kept_first, tables = first[GROUP:], first[-3:]
    qu_cot = [after(a, first[0]) for a in qu_cot]
    came = to_owners(first[:GROUP])
    od_own = after(jnp.where(core == 1, keep_od, came_od)[None], first[0])
    od_late = [jnp.concatenate([od_own, place.across(od_own, 0)])]
    came[1] = after(came[1], od_late[0])
    hidden_first = (x_own.astype(F32) + total_of(came) + bias_first).astype(LOW)
    hidden_group = gather(hidden_first)
    qu_own = jnp.stack([take(qu_mine, group)] + [a[:in_rows] for a in qu_cot])[None]
    qu_late = [jnp.concatenate([qu_own, after(place.across(qu_own, 0), hidden_first)])]
    for step in range(1, ring.bits):
        od_late.append(after(place.across(jnp.concatenate(od_late), step), *hidden_group[1:]))
        qu_late.append(after(place.across(jnp.concatenate(qu_late), step), *hidden_group[1:]))
    qu_sibling, od_sibling = [
        [place.sibling(after(a, *hidden_group[1:])) for a in late] for late in (qu_late, od_late)
    ]
    parts_second = (*qu_late, *od_late, *qu_sibling, *od_sibling)
    vecs_second, bias_second, gain_second = block_vectors(qu_late)
    second = middle(ring, info, parts_second, hidden_group, [cot_own, *qu_cot], tables, vecs_second, rows)
    sums_second, y_second, mixed_second, active_second, dqu_second, grad_second = second[GROUP : GROUP + 6]
    z_second = second[GROUP + 6 :]

    def rows_backward(rows_low, grad_low, dy, gain):
        rows_now = rows_low.astype(F32)
        centered = rows_now - jnp.mean(rows_now, axis=-1, keepdims=True)
        variance = jnp.mean(centered * centered, axis=-1, keepdims=True)
        inverse_std = lax.rsqrt(variance + NORM_EPS)
        normed = centered * inverse_std
        scaled = dy * gain
        inner_mean = jnp.mean(scaled, axis=-1, keepdims=True)
        inner_cross = jnp.mean(scaled * normed, axis=-1, keepdims=True)
        return (grad_low.astype(F32) + inverse_std * (scaled - inner_mean - normed * inner_cross)).astype(LOW)

    def to_members(pieces):
        return [pieces[0]] + [place.member(pieces[r], r) for r in members]

    steps = list(reversed(range(ring.bits)))

    def ring_fold(held, *waited):
        kept, sent = held
        for step in steps[:-1]:
            kept, sent = fold(kept, after(place.across(sent, step), *waited))
        return kept, sent

    dy_second = to_owners(second[:GROUP])
    grads = weight_grads(ring, info, mixed_second, active_second, grad_second, y_second, dqu_second, sums_second)
    mid_grad = rows_backward(hidden_first, cot_own, total_of(dy_second), gain_second)
    mid_group = gather(mid_grad)
    sent = place.sibling(after(grads[1], *dy_second[1:]))
    second_held = ring_fold(fold(grads[0], after(sent, mid_grad)))

    mid_late = [after(mid_group[0], *second_held)] + mid_group[1:]
    dyz_keep, dyz_send, keep, send = backward(ring, info, mid_late, z_second, kept_first, rows)
    kept, sent = second_held
    none = jnp.zeros((8, 128), F32)
    *qu_second, od_second, squares_second = close(ring, kept, after(place.across(sent, 0), send), none)
    send = after(send, *qu_second)
    qu_slots_second = to_members(qu_second)
    kept, sent = ring_fold(fold(keep, place.sibling(send)))
    dyz_came = place.toward(dyz_send, 1)
    came = after(place.across(after(sent, *qu_slots_second[1:]), 0), dyz_came)
    *qu_first, od_first, _ = close(ring, kept, came, squares_second)
    qu_slots_first = to_members(qu_first)
    grads_sent, vec, squares, vec_squares = join(info, qu_slots_first, qu_slots_second, od_first, od_second)
    squares = squares + place.sibling(squares)
    second_step = place.toward((dyz_keep[1].astype(F32) + dyz_came[1].astype(F32)).astype(LOW), 0)
    second_step = after(second_step, squares)
    for step in range(ring.bits):
        squares = squares + place.across(squares, step)
    squares = jnp.sum(squares + vec_squares)
    dyz = dyz_keep[0].astype(F32) + dyz_came[0].astype(F32) + second_step.astype(F32)
    start_grad = rows_backward(x_own, mid_grad, dyz[:rows], gain_first)
    hidden_second = (hidden_first.astype(F32) + dyz[rows:] + bias_second).astype(LOW)

    grad_norm = jnp.sqrt(squares)
    factor = jnp.minimum(1.0, CLIP_LEVEL / (grad_norm + 1e-06))

    def own_block(one, two):
        came = place.sibling(jnp.where(core == 0, two, one))
        mine = jnp.where(core == 0, one, two)
        return [jnp.where(core == h, mine, came) for h in range(2)]

    grads_came = place.sibling(grads_sent)
    vec_share = after(vec, grads_sent).reshape(-1)[: ring.count * shard].reshape(ring.count, shard)
    vec_share = take(vec_share, lax.axis_index("dp"))[None]
    olds = (w_qkv, m_qkv, v_qkv, w_out, m_out, v_out, w_up, m_up, v_up, w_down, m_down, v_down)
    qus = (qu_slots_first, qu_slots_second)
    news = adam(info, factor[None], qus, (od_first, od_second), grads_came, olds)
    new_vec = adam_update(vectors, vec_share, m_vectors, v_vectors, factor, VECTOR_RATE)

    outputs = own_block(jnp.stack([hidden_first, start_grad]), jnp.stack([hidden_second, mid_grad]))
    outputs = jnp.concatenate(outputs, axis=1)
    hidden_out, input_grads = outputs[:1], outputs[1:]
    return (
        hidden_out,
        input_grads,
        *(news[3 * i] for i in range(4)),
        new_vec[0],
        *(news[3 * i + 1] for i in range(4)),
        new_vec[1],
        *(news[3 * i + 2] for i in range(4)),
        new_vec[2],
        grad_norm,
    )


def solution(mesh):
    return jax.shard_map(
        shards,
        mesh=mesh,
        in_specs=(
            P("dp", None),
            P("dp", None),
            P("dp", None),
            P("section", "dp", None),
            P("section", "dp", None),
            P("section", "dp", None),
            P("section", "dp", None),
            P("section", "dp"),
            P("section", "dp", None),
            P("section", "dp", None),
            P("section", "dp", None),
            P("section", "dp", None),
            P("section", "dp"),
            P("section", "dp", None),
            P("section", "dp", None),
            P("section", "dp", None),
            P("section", "dp", None),
            P("section", "dp"),
        ),
        out_specs=(
            P("section", "dp", None),
            P("section", "dp", None),
            P("section", "dp", None),
            P("section", "dp", None),
            P("section", "dp", None),
            P("section", "dp", None),
            P("section", "dp"),
            P("section", "dp", None),
            P("section", "dp", None),
            P("section", "dp", None),
            P("section", "dp", None),
            P("section", "dp"),
            P("section", "dp", None),
            P("section", "dp", None),
            P("section", "dp", None),
            P("section", "dp", None),
            P("section", "dp"),
            P(),
        ),
        check_vma=False,
    )
```

```python
import functools

import jax
import jax.numpy as jnp
from jax import lax
from jax.experimental import pallas as pl
from jax.experimental.pallas import tpu as pltpu
from jax.sharding import PartitionSpec as P

D = 1024
FF = 4096
HEADS = 16
HEAD_DIM = 64
ROT = 16
STEP = 10


NORM_EPS = 1e-05
BETA_ONE = 0.9
BETA_TWO = 0.95
LEARN_RATE = 0.05
VECTOR_RATE = 0.3
WEIGHT_DECAY = 0.01
CLIP_LEVEL = 1.0
ADAM_EPS = 1e-08

AXES = ("section", "dp")
GROUP = 4
SPREAD = 1
LOW = jnp.bfloat16
F32 = jnp.float32
SIDE = D // GROUP
UNITS = FF // GROUP
MIXED = 3 * SIDE + UNITS
PART = MIXED // 2
WIRE = PART + 128


class Ring:
    def __init__(self, count):
        self.count = count
        self.low = count // (GROUP * SPREAD)
        self.size = SPREAD * self.low
        self.bits = self.size.bit_length() - 1

    def index(self, g, t):
        return ((t // self.low) * GROUP + g) * self.low + t % self.low

    def group_of(self, dp):
        return (dp // self.low) % GROUP

    def spot_of(self, dp):
        return (dp // (GROUP * self.low)) * self.low + dp % self.low

    def order(self, core):
        steps = list(range(self.bits))
        if SPREAD > 1 or core == 1:
            steps.reverse()
        return steps

    def turn(self, slot, core):
        return sum(((slot >> s) & 1) << b for s, b in enumerate(self.order(core)))

    def slot(self, difference, core):
        return sum(((difference >> b) & 1) << s for s, b in enumerate(self.order(core)))


class Place:
    def __init__(self):
        self.ring = Ring(lax.axis_size("dp"))
        self.core = lax.axis_index("section")
        dp = lax.axis_index("dp")
        self.group = self.ring.group_of(dp)
        self.spot = self.ring.spot_of(dp)

    def info(self):
        return jnp.stack([self.core, self.group, self.spot]).astype(jnp.int32)

    def move(self, block, where):
        ring = self.ring
        route = []
        for core in range(2):
            for g in range(GROUP):
                for t in range(ring.size):
                    c, h, u = where(core, g, t)
                    route.append((core * ring.count + ring.index(g, t), c * ring.count + ring.index(h, u)))
        return lax.ppermute(block, AXES, route)

    def sibling(self, block):
        return self.move(block, lambda c, g, t: (1 - c, g, t))

    def member(self, block, distance):
        return self.move(block, lambda c, g, t: (c, g ^ distance, t))

    def toward(self, block, step):
        return self.move(block, lambda c, g, t: (c, g ^ (2, 1)[(step + c) % 2], t))

    def across(self, block, step):
        return self.move(block, lambda c, g, t: (c, g, t ^ (1 << self.ring.order(c)[step])))


def take(block, index, axis=0):
    return lax.dynamic_index_in_dim(block, index, axis, keepdims=False)


def after(block, *waited):
    return lax.optimization_barrier((block, waited))[0]


def dot(left, right):
    return jnp.dot(left, right, preferred_element_type=F32)


def dot_cols(left, right):
    return lax.dot_general(left, right, (((1,), (1,)), ((), ())), preferred_element_type=F32)


def dot_rows(left, right):
    return lax.dot_general(left, right, (((0,), (0,)), ((), ())), preferred_element_type=F32)


def full_spec(shape):
    return pl.BlockSpec(shape, lambda *_: (0,) * len(shape))


def far_spec():
    return pl.BlockSpec(memory_space=pltpu.HBM)


def far(block):
    return pltpu.with_memory_space_constraint(block, pltpu.HBM)


def any_spec():
    return pl.BlockSpec(memory_space=pl.ANY)


def smem_spec():
    return pl.BlockSpec(memory_space=pltpu.SMEM)


def shaped(shape, dtype):
    return jax.ShapeDtypeStruct(shape, dtype)


def kernel_params(mebibytes):
    return pltpu.CompilerParams(vmem_limit_bytes=mebibytes * 1024 * 1024)


def up_pieces():
    run = UNITS // SPREAD
    cuts = sorted({0, PART - 3 * SIDE, UNITS} | {run * i for i in range(SPREAD)})
    pieces = []
    for begin, end in zip(cuts[:-1], cuts[1:]):
        column = 3 * SIDE + begin
        pieces.append((begin, column // PART, column % PART, end - begin))
    return pieces


def up_column(g, local):
    run = UNITS // SPREAD
    return (local // run * GROUP + g) * run + local % run


def qkv_column(kind, run, g):
    width = SIDE // SPREAD
    return ((kind * SPREAD + run) * GROUP + g) * width


def pack_kernel(info, qkv_hbm, out_hbm, up_hbm, down_hbm, vec, keep_qu, send_qu, keep_od, send_od, *scratch):
    w_qkv, w_out, w_up, w_down, sems = scratch
    pairs = ((qkv_hbm, w_qkv), (up_hbm, w_up), (down_hbm, w_down), (out_hbm, w_out))
    copies = [pltpu.make_async_copy(far.at[0], near, sems.at[i]) for i, (far, near) in enumerate(pairs)]
    for copy in copies:
        copy.start()
    rows = w_qkv.shape[0]
    ff_rows = w_down.shape[0]
    width = SIDE // SPREAD
    core = info[0]

    def write_qu(halves):
        for g in range(GROUP):
            for kind in range(3):
                for run in range(SPREAD):
                    at = (kind * SPREAD + run) * width
                    column = qkv_column(kind, run, g)
                    halves[0][g, :, at : at + width] = w_qkv[:, column : column + width].astype(LOW)
            for local, half, at, length in up_pieces():
                column = up_column(g, local)
                halves[half][g, :, at : at + length] = w_up[:, column : column + length].astype(LOW)
            for half in range(2):
                halves[half][g, :, PART:WIRE] = vec[...]

    def write_od(halves):
        for half in range(2):
            columns = slice(half * (D // 2), (half + 1) * (D // 2))
            halves[half][0:ff_rows] = w_down[:, columns].astype(LOW)
            halves[half][ff_rows : ff_rows + rows] = w_out[:, columns].astype(LOW)

    for first, last, write, kept, sent in ((0, 2, write_qu, keep_qu, send_qu), (2, 4, write_od, keep_od, send_od)):
        for copy in copies[first:last]:
            copy.wait()
        pl.when(core == 0)(functools.partial(write, (kept, sent)))
        pl.when(core == 1)(functools.partial(write, (sent, kept)))


def pack(info, w_qkv, w_out, w_up, w_down, vec):
    rows, ff_rows = w_qkv.shape[1], w_down.shape[1]
    qu = shaped((GROUP, rows, WIRE), LOW)
    od = shaped((ff_rows + rows, D // 2), LOW)
    return pl.pallas_call(
        pack_kernel,
        out_shape=(qu, qu, od, od),
        in_specs=[smem_spec()] + [far_spec()] * 4 + [full_spec(vec.shape)],
        out_specs=tuple(full_spec(a.shape) for a in (qu, qu, od, od)),
        scratch_shapes=[pltpu.VMEM(a.shape[1:], F32) for a in (w_qkv, w_out, w_up, w_down)]
        + [pltpu.SemaphoreType.DMA((4,))],
        compiler_params=kernel_params(20),
        name="pack_weights",
    )(info, far(w_qkv), far(w_out), far(w_up), far(w_down), vec)


def stack_kernel(*refs):
    for i, ref in enumerate(refs[:-1]):
        refs[-1][0, i] = ref[...]


def stack_members(pieces):
    out = shaped((1, len(pieces), *pieces[0].shape), LOW)
    return pl.pallas_call(
        stack_kernel,
        out_shape=out,
        in_specs=[full_spec(a.shape) for a in pieces],
        out_specs=full_spec(out.shape),
        compiler_params=kernel_params(16),
        cost_estimate=cost(50 * 10**9, 1024 * 1024),
        name="stack_members",
    )(*pieces)


def weight_copies(ring, info, parts, wqu, wout, wdown, sems):
    core, group, spot = info[0], info[1], info[2]
    qu_copies, od_copies = [], []
    count = len(parts) // 4
    for which in range(2):
        half = core if which == 0 else 1 - core
        qu_at = pl.multiple_of(half * PART, 128)
        od_at = pl.multiple_of(half * (D // 2), 128)
        slot = 0
        for piece in range(count):
            qu, od = parts[2 * count * which + piece], parts[2 * count * which + count + piece]
            rows = qu.shape[2]
            ff_rows = od.shape[1] - rows
            for i in range(qu.shape[0]):
                straight, turned = ring.turn(slot, 0), ring.turn(slot, 1)
                there = spot ^ (straight + half * (turned - straight))
                slot += 1
                ff_row = pl.multiple_of(there * ff_rows, ff_rows)
                out_row = pl.multiple_of(there * rows, rows)
                far = wdown.at[pl.ds(ff_row, ff_rows), pl.ds(od_at, D // 2)]
                od_copies.append(pltpu.make_async_copy(od.at[i, pl.ds(0, ff_rows)], far, sems.at[0]))
                far = wout.at[pl.ds(out_row, rows), pl.ds(od_at, D // 2)]
                od_copies.append(pltpu.make_async_copy(od.at[i, pl.ds(ff_rows, rows)], far, sems.at[0]))
                for r in range(GROUP):
                    row = pl.multiple_of(ring.index(group ^ r, there) * rows, rows)
                    far = wqu.at[pl.ds(row, rows), pl.ds(qu_at, PART)]
                    qu_copies.append(pltpu.make_async_copy(qu.at[i, r, :, pl.ds(0, PART)], far, sems.at[1]))
    return qu_copies, od_copies


def head_masks(dtype):
    lane = lax.broadcasted_iota(jnp.int32, (1, SIDE), 1) // HEAD_DIM
    return [(lane == h).astype(dtype) for h in range(SIDE // HEAD_DIM)]


def by_head(parts):
    lane = lax.broadcasted_iota(jnp.int32, (1, SIDE), 1) // HEAD_DIM
    total = parts[-1]
    for h in range(len(parts) - 2, -1, -1):
        total = jnp.where(lane == h, parts[h], total)
    return total


def turning(cosine, sine, back):
    lane = lax.broadcasted_iota(jnp.int32, sine.shape, 1) % HEAD_DIM
    first = jnp.where(lane < ROT // 2, sine, 0.0)
    second = jnp.where(lane < ROT // 2, 0.0, sine)
    if back:
        second = -second
    else:
        first = -first
    wide = SIDE // cosine.shape[1]
    return [jnp.concatenate([a] * wide, axis=1) for a in (cosine, first, second)]


def turn(part, tables):
    cosine, first, second = tables
    ahead = pltpu.roll(part, SIDE - ROT // 2, 1)
    behind = pltpu.roll(part, ROT // 2, 1)
    return part * cosine + ahead * first + behind * second


def normalise(rows):
    centered = rows - jnp.mean(rows, axis=-1, keepdims=True)
    variance = jnp.mean(centered * centered, axis=-1, keepdims=True)
    return centered * lax.rsqrt(variance + NORM_EPS)


def no_wait():
    pass


def forward_part(x_refs, tables, vecs, wqu, wout, wdown, kept, z_refs, waits, done, normed_ref=None):
    cosine, sine, mask = tables
    b_qkv, b_up, gain, ln_bias = vecs
    y, qkv, probs, mixed, active, slope = kept
    rows = z_refs[0].shape[0]
    for r in range(GROUP):
        normed = normalise(x_refs[r][0:rows, :].astype(F32))
        if normed_ref is not None:
            normed_ref[r * rows : (r + 1) * rows, :] = normed
        y[r * rows : (r + 1) * rows, :] = (normed * gain[...] + ln_bias[...]).astype(LOW)
    done(0)
    waits[0]()
    waits[2]()
    forth = turning(cosine[...], sine[...], False)
    for kind in range(3):
        columns = slice(kind * SIDE, (kind + 1) * SIDE)
        part = dot(y[...], wqu[:, columns]) + b_qkv[:, columns]
        if kind < 2:
            part = turn(part, forth)
        qkv[:, columns] = part.astype(LOW)
    done(1)
    masks = head_masks(LOW)
    heads = len(masks)
    for r in range(GROUP):
        here = slice(r * rows, (r + 1) * rows)
        query, keys, values = [qkv[here, k * SIDE : (k + 1) * SIDE] for k in range(3)]
        stacked = jnp.concatenate([query * m for m in masks], axis=0)
        scores = dot_cols(stacked, keys) * HEAD_DIM ** (-0.5)
        scores = scores.reshape(heads, rows, rows) + mask[here, :][None]
        expo = jnp.exp(scores - jnp.max(scores, axis=-1, keepdims=True))
        prob = expo / jnp.sum(expo, axis=-1, keepdims=True)
        prob = prob.reshape(heads * rows, rows)
        probs[r * heads * rows : (r + 1) * heads * rows, :] = prob
        full = dot(prob.astype(LOW), values)
        mixed[here, :] = by_head([full[h * rows : (h + 1) * rows] for h in range(heads)]).astype(LOW)
    done(2)
    done(3)
    tile = 256
    for at in range(0, UNITS, tile):
        hidden = dot(y[...], wqu[:, 3 * SIDE + at : 3 * SIDE + at + tile]) + b_up[:, at : at + tile]
        share = 0.5 * (1.0 + lax.erf(hidden * (0.5**0.5)))
        density = jnp.exp(-0.5 * hidden * hidden) * (0.5 / jnp.pi) ** 0.5
        active[:, at : at + tile] = (hidden * share).astype(LOW)
        slope[:, at : at + tile] = share + hidden * density
    done(4)
    done(5)
    waits[1]()
    for at in range(0, D, tile):
        branch = dot(mixed[...], wout[:, at : at + tile]) + dot(active[...], wdown[:, at : at + tile])
        for r in range(GROUP):
            z_refs[r][:, at : at + tile] = branch[r * rows : (r + 1) * rows].astype(LOW)


def backward_part(grad, normed, tables, wqu, wout, wdown, kept, dqu, dy_refs, sums, waits, done):
    cosine, sine, _ = tables
    y, qkv, probs, mixed, active, slope = kept
    rows = grad.shape[0] // GROUP
    tile = 256
    waits[0]()
    dmixed = dot_cols(grad[...], wout[...]).astype(LOW)
    for at in range(0, UNITS, tile):
        dactive = dot_cols(grad[...], wdown[at : at + tile, :])
        dhidden = (dactive * slope[:, at : at + tile]).astype(LOW)
        dqu[:, 3 * SIDE + at : 3 * SIDE + at + tile] = dhidden
    waits[1]()
    masks = head_masks(LOW)
    heads = len(masks)
    back = turning(cosine[...], sine[...], True)
    for r in range(GROUP):
        here = slice(r * rows, (r + 1) * rows)
        query, keys, values = [qkv[here, k * SIDE : (k + 1) * SIDE] for k in range(3)]
        dstack = jnp.concatenate([dmixed[here] * m for m in masks], axis=0)
        dprob = dot_cols(dstack, values)
        prob = probs[r * heads * rows : (r + 1) * heads * rows, :]
        dvalues = dot_rows(prob.astype(LOW), dstack)
        dscore = (prob * (dprob - jnp.sum(prob * dprob, axis=-1, keepdims=True))).astype(LOW)
        full = dot(dscore, keys)
        dquery = by_head([full[h * rows : (h + 1) * rows] for h in range(heads)])
        dkeys = dot_rows(dscore, jnp.concatenate([query * m for m in masks], axis=0))
        scale = HEAD_DIM ** (-0.5)
        slot_tables = [a[here] for a in back]
        dqu[here, 0:SIDE] = turn(dquery * scale, slot_tables).astype(LOW)
        dqu[here, SIDE : 2 * SIDE] = turn(dkeys * scale, slot_tables).astype(LOW)
        dqu[here, 2 * SIDE : 3 * SIDE] = dvalues.astype(LOW)
    done()
    for at in range(0, MIXED, tile):
        sums[:, at : at + tile] = jnp.sum(dqu[:, at : at + tile].astype(F32), axis=0, keepdims=True)
    waits[2]()
    for at in range(0, D, tile):
        dy = dot_cols(dqu[...], wqu[at : at + tile, :])
        for r in range(GROUP):
            dy_refs[r][:, at : at + tile] = dy[r * rows : (r + 1) * rows].astype(LOW)
        own = grad[0:rows, at : at + tile].astype(F32)
        for i, terms in enumerate((own, dy * normed[:, at : at + tile], dy)):
            begin = MIXED + i * D + at
            sums[:, begin : begin + tile] = jnp.sum(terms, axis=0, keepdims=True)


def kept_shapes(tokens, rows):
    return [
        ((tokens, D), LOW),
        ((tokens, 3 * SIDE), LOW),
        ((tokens * (SIDE // HEAD_DIM), rows), F32),
        ((tokens, SIDE), LOW),
        ((tokens, UNITS), LOW),
        ((tokens, UNITS), F32),
    ]


def weight_scratch():
    return [
        pltpu.VMEM((D, MIXED), LOW),
        pltpu.VMEM((SIDE, D), LOW),
        pltpu.VMEM((UNITS, D), LOW),
        pltpu.SemaphoreType.DMA((2,)),
    ]


def waiter(copies):
    def wait():
        for copy in copies:
            copy.wait()

    return wait


def started(pairs, sem):
    copies = [pltpu.make_async_copy(source, target, sem) for source, target in pairs]
    for copy in copies:
        copy.start()
    return waiter(copies)


def table_scratch(tokens, rows):
    return [pltpu.VMEM((tokens, 128), F32), pltpu.VMEM((tokens, 128), F32), pltpu.VMEM((tokens, rows), F32)]


def cost(flops, moved):
    return pl.CostEstimate(flops=2 * flops, bytes_accessed=2 * moved, transcendentals=0)


def leaving(pairs, sems):
    copies = [pltpu.make_async_copy(near, far, sems.at[i]) for i, (near, far) in enumerate(pairs)]

    def go(i):
        copies[i].start()

    return go, waiter(copies)


def forward_kernel(ring, count, info, *refs):
    parts, refs = refs[:count], refs[count:]
    x_refs, refs = refs[:4], refs[4:]
    tables, refs = refs[:3], refs[3:]
    vecs, refs = refs[:4], refs[4:]
    z_refs, refs = refs[:4], refs[4:]
    far_kept, far_weights, far_tables, refs = refs[:7], refs[7:10], refs[10:13], refs[13:]
    kept, refs = refs[:7], refs[7:]
    out_sems, scratch = refs[0], refs[1:]
    weights = scratch[:3]
    qu_copies, od_copies = weight_copies(ring, info, parts, *scratch)
    for copy in qu_copies + od_copies:
        copy.start()
    pairs = [*zip(kept, far_kept), *zip(weights, far_weights), *zip(tables, far_tables)]
    go, out = leaving(pairs, out_sems)
    for i in range(10, 13):
        go(i)

    def qu_in():
        waiter(qu_copies)()
        go(7)

    def od_in():
        waiter(od_copies)()
        go(8)
        go(9)

    def done(i):
        go(i)
        if i == 0:
            go(6)

    forward_part(x_refs, tables, vecs, *weights, kept[:6], z_refs, (qu_in, od_in, no_wait), done, kept[6])
    out()


def forward(ring, info, parts, xs, tables, vecs, rows):
    tokens = GROUP * rows
    shapes = kept_shapes(tokens, rows) + [((tokens, D), F32)]
    away = [*shapes, ((D, MIXED), LOW), ((SIDE, D), LOW), ((UNITS, D), LOW)] + [(a.shape, F32) for a in tables]
    blocks = (*xs, *tables, *vecs)
    return pl.pallas_call(
        functools.partial(forward_kernel, ring, len(parts)),
        out_shape=(*[shaped((rows, D), LOW)] * GROUP, *[pltpu.HBM(*a) for a in away]),
        in_specs=[smem_spec()] + [any_spec()] * len(parts) + [full_spec(a.shape) for a in blocks],
        out_specs=tuple([full_spec((rows, D))] * GROUP + [far_spec()] * len(away)),
        scratch_shapes=[pltpu.VMEM(*a) for a in shapes]
        + [pltpu.SemaphoreType.DMA((len(away),))]
        + weight_scratch(),
        compiler_params=kernel_params(22),
        cost_estimate=cost(2 * tokens * D * (D + 2 * FF // GROUP), 16 * 1024 * 1024),
        name="forward_shard",
    )(info, *parts, *blocks)


def middle_kernel(ring, count, info, *refs):
    parts, refs = refs[:count], refs[count:]
    x_refs, refs = refs[:4], refs[4:]
    g_refs, refs = refs[:4], refs[4:]
    far_tables, refs = refs[:3], refs[3:]
    vecs, refs = refs[:4], refs[4:]
    dy_refs, refs = refs[:4], refs[4:]
    sums, away, refs = refs[0], refs[1:10], refs[10:]
    kept, refs = refs[:6], refs[6:]
    z_refs, tables, refs = refs[:4], refs[4:7], refs[7:]
    (grad, normed, dqu, in_sems, out_sems), scratch = refs[:5], refs[5:]
    rows = z_refs[0].shape[0]
    qu_copies, od_copies = weight_copies(ring, info, parts, *scratch)
    for copy in qu_copies:
        copy.start()
    tables_in = started(zip(far_tables, tables), in_sems.at[0])
    for copy in od_copies:
        copy.start()
    pairs = []
    for r, ref in enumerate(g_refs):
        at = ref.shape[0] - rows
        pairs.append((ref.at[pl.ds(at, rows)], grad.at[pl.ds(r * rows, rows)]))
    grad_in = started(pairs, in_sems.at[1])
    go, out = leaving(list(zip([kept[0], kept[3], kept[4], dqu, grad, *z_refs], away)), out_sems)

    def done(i):
        if i in (0, 3, 4):
            go((0, 3, 4).index(i))

    waits = (waiter(qu_copies), waiter(od_copies), tables_in)
    forward_part(x_refs, tables, vecs, *scratch[:3], kept, z_refs, waits, done, normed)
    grad_in()
    for i in range(4, 9):
        go(i)
    waits = (no_wait, no_wait, no_wait)
    done = functools.partial(go, 3)
    backward_part(grad, normed, tables, *scratch[:3], kept, dqu, dy_refs, sums, waits, done)
    out()


def middle(ring, info, parts, xs, gs, tables, vecs, rows):
    tokens = GROUP * rows
    shapes = kept_shapes(tokens, rows)
    away = [shapes[0], shapes[3], shapes[4], ((tokens, MIXED), LOW), ((tokens, D), LOW)]
    away += [((rows, D), LOW)] * GROUP
    sums = shaped((1, MIXED + 3 * D), F32)
    return pl.pallas_call(
        functools.partial(middle_kernel, ring, len(parts)),
        out_shape=(*[shaped((rows, D), LOW)] * GROUP, sums, *[pltpu.HBM(*a) for a in away]),
        in_specs=[smem_spec()]
        + [any_spec()] * len(parts)
        + [full_spec(a.shape) for a in xs]
        + [far_spec()] * (GROUP + 3)
        + [full_spec(a.shape) for a in vecs],
        out_specs=tuple([full_spec((rows, D))] * GROUP + [full_spec(sums.shape)] + [far_spec()] * len(away)),
        scratch_shapes=[pltpu.VMEM(*a) for a in shapes]
        + [pltpu.VMEM((rows, D), LOW)] * GROUP
        + table_scratch(tokens, rows)
        + [pltpu.VMEM((tokens, D), LOW), pltpu.VMEM((tokens, D), F32), pltpu.VMEM((tokens, MIXED), LOW)]
        + [pltpu.SemaphoreType.DMA((2,)), pltpu.SemaphoreType.DMA((9,))]
        + weight_scratch(),
        compiler_params=kernel_params(27),
        cost_estimate=cost(4 * tokens * D * (D + 2 * FF // GROUP), 16 * 1024 * 1024),
        name="forward_backward_shard",
    )(info, *parts, *xs, *[far(a) for a in (*gs, *tables)], *vecs)


def backward_kernel(ring, info, *refs):
    core = info[0]
    g_refs, refs = refs[:4], refs[4:]
    z_refs, refs = refs[:4], refs[4:]
    far_kept, far_weights, far_tables, refs = refs[:7], refs[7:10], refs[10:13], refs[13:]
    (dy_keep, dy_send, keep, send), refs = refs[:4], refs[4:]
    kept, refs = refs[:7], refs[7:]
    weights, tables, refs = refs[:3], refs[3:6], refs[6:]
    (grad, dqu, sums, in_sems, out_sems), dyz = refs[:5], refs[5:]
    y, qkv, probs, mixed, active, slope, normed = kept
    wqu, wout, wdown = weights
    far_y, far_qkv, far_probs, far_mixed, far_active, far_slope, far_normed = far_kept
    mixed_in = started([(far_mixed, mixed)], in_sems.at[0])
    active_in = started([(far_active, active)], in_sems.at[1])
    units_in = started([*zip(far_weights[1:], weights[1:]), (far_slope, slope)], in_sems.at[2])
    heads_in = started([(far_qkv, qkv), (far_probs, probs), *zip(far_tables, tables)], in_sems.at[3])
    dy_in = started([(far_weights[0], wqu), (far_normed, normed)], in_sems.at[4])
    y_in = started([(far_y, y)], in_sems.at[5])
    rows = g_refs[0].shape[0]
    z_in = started([(z_refs[r], dyz[r].at[pl.ds(rows, rows)]) for r in range(GROUP)], in_sems.at[6])
    for r in range(GROUP):
        grad[r * rows : (r + 1) * rows, :] = g_refs[r][...]
    mixed_in()
    od_part(ring, info, mixed, active, grad, keep, send, active_in)
    waits = (units_in, heads_in, dy_in)
    dy_refs = [a.at[pl.ds(0, rows)] for a in dyz]
    backward_part(grad, normed, tables, *weights, kept[:6], dqu, dy_refs, sums, waits, no_wait)
    z_in()
    targets = (dy_keep.at[0], dy_keep.at[1], dy_send.at[0], dy_send.at[1])
    outs = [
        [pltpu.make_async_copy(dyz[r], target, out_sems.at[i]) for i, (r, target) in enumerate(zip(order, targets))]
        for order in ((0, 2, 1, 3), (0, 1, 2, 3))
    ]
    for here in range(2):

        @pl.when(core == here)
        def _(copies=outs[here]):
            for copy in copies:
                copy.start()

    y_in()
    qu_part(ring, info, y, dqu, sums, keep, send)
    for here in range(2):
        pl.when(core == here)(waiter(outs[here]))


def backward(ring, info, gs, zs, held, rows):
    tokens = GROUP * rows
    outs = [shaped((2, 2 * rows, D), LOW)] * 2 + [grads_shape(ring)] * 2
    return pl.pallas_call(
        functools.partial(backward_kernel, ring),
        out_shape=tuple(outs),
        in_specs=[smem_spec()] + [full_spec(a.shape) for a in gs] + [far_spec()] * (GROUP + len(held)),
        out_specs=tuple(full_spec(a.shape) for a in outs),
        scratch_shapes=[pltpu.VMEM(a.shape, a.dtype) for a in held]
        + [pltpu.VMEM((tokens, D), LOW), pltpu.VMEM((tokens, MIXED), LOW)]
        + [pltpu.VMEM((1, MIXED + 3 * D), F32), pltpu.SemaphoreType.DMA((7,)), pltpu.SemaphoreType.DMA((4,))]
        + [pltpu.VMEM((2 * rows, D), LOW)] * GROUP,
        compiler_params=kernel_params(28),
        cost_estimate=cost(4 * tokens * D * (D + 2 * FF // GROUP), 16 * 1024 * 1024),
        name="backward_shard",
    )(info, *gs, *[far(a) for a in (*zs, *held)])


def slot_in(ring, difference, half):
    straight, turned = ring.slot(difference, 0), ring.slot(difference, 1)
    return straight + half * (turned - straight)


QU_TILES = PART // 128
OD_TILES = D // 2 // 128
SIDES = 112


def slot_rows(ring):
    return GROUP * QU_TILES * (D // ring.count) + OD_TILES * (SIDE + UNITS) // ring.size


def grads_shape(ring):
    return shaped((ring.size * slot_rows(ring) + SIDES, 128), LOW)


def od_part(ring, info, mixed, active, grad, keep, send, active_in):
    core, spot = info[0], info[2]
    out_rows = SIDE // ring.size
    ff_rows = UNITS // ring.size
    ahead = GROUP * QU_TILES * (D // ring.count)
    for i, (out, half) in enumerate(((send, 1 - core), (keep, core))):
        columns = pl.ds(pl.multiple_of(half * (D // 2), D // 2), D // 2)
        part = grad[:, columns]
        block = dot_rows(mixed[...], part).astype(LOW)
        if i == 0:
            active_in()
        for there in range(ring.size):
            slot = slot_in(ring, spot ^ there, half)
            piece = dot_rows(active[:, there * ff_rows : (there + 1) * ff_rows], part).astype(LOW)
            for tile in range(OD_TILES):
                lanes = slice(tile * 128, (tile + 1) * 128)
                row = slot * slot_rows(ring) + ahead + tile * (ff_rows + out_rows)
                out[pl.ds(pl.multiple_of(row, 16), ff_rows), :] = piece[:, lanes]
                row = pl.multiple_of(row + ff_rows, 16)
                out[pl.ds(row, out_rows), :] = block[there * out_rows : (there + 1) * out_rows, lanes]


def vector_rows(group, sums):
    width = SIDE // SPREAD
    run = UNITS // SPREAD
    row = lax.broadcasted_iota(jnp.int32, (SIDES, 128), 0)
    pieces = []
    for at in range(0, 3 * SIDE, 128):
        pieces.append(((at // width * GROUP + group) * (width // 128) + at % width // 128, at))
    for at in range(0, UNITS, 128):
        pieces.append((3 * D // 128 + D // 128 + (at // run * GROUP + group) * (run // 128) + at % run // 128, 3 * SIDE + at))
    tail = (4 * D + FF) // 128
    for i, begin in enumerate((3 * D // 128, tail, tail + D // 128, tail + 2 * D // 128)):
        for at in range(0, D, 128):
            pieces.append((begin + at // 128, MIXED + max(i - 1, 0) * D + at))
    return sum(jnp.where(row == where, sums[:, at : at + 128], 0.0) for where, at in pieces)


def qu_part(ring, info, y, dqu, sums, keep, send):
    core, group, spot = info[0], info[1], info[2]
    rows = D // ring.count
    tile = 256
    last = ring.size * slot_rows(ring)
    extra = vector_rows(group, sums).astype(LOW)
    for out, half in ((send, 1 - core), (keep, core)):
        columns = pl.ds(pl.multiple_of(half * PART, 128), PART)
        out[last : last + SIDES, :] = extra
        for at in range(0, D, tile):
            block = dot_rows(y[:, at : at + tile], dqu[:, columns]).astype(LOW)
            for offset in range(0, tile, rows):
                dp = (at + offset) // rows
                slot = slot_in(ring, spot ^ ring.spot_of(dp), half)
                begin = slot * slot_rows(ring) + (group ^ ring.group_of(dp)) * (QU_TILES * rows)
                for i in range(QU_TILES):
                    row = pl.multiple_of(begin + i * rows, 16)
                    out[pl.ds(row, rows), :] = block[offset : offset + rows, i * 128 : (i + 1) * 128]


def grads_kernel(ring, info, far_mixed, far_active, far_grad, far_y, far_dqu, sums, keep, send, *scratch):
    mixed, active, grad, y, dqu, sems = scratch
    grad_in = started([(far_grad, grad), (far_mixed, mixed)], sems.at[0])
    active_in = started([(far_active, active)], sems.at[1])
    rest_in = started([(far_y, y), (far_dqu, dqu)], sems.at[2])
    grad_in()
    od_part(ring, info, mixed, active, grad, keep, send, active_in)
    rest_in()
    qu_part(ring, info, y, dqu, sums, keep, send)


def weight_grads(ring, info, mixed, active, grad, y, dqu, sums):
    blocks = (mixed, active, grad, y, dqu)
    out = grads_shape(ring)
    return pl.pallas_call(
        functools.partial(grads_kernel, ring),
        out_shape=(out, out),
        in_specs=[smem_spec()] + [far_spec()] * len(blocks) + [full_spec(sums.shape)],
        out_specs=(full_spec(out.shape),) * 2,
        scratch_shapes=[pltpu.VMEM(a.shape, LOW) for a in blocks] + [pltpu.SemaphoreType.DMA((3,))],
        compiler_params=kernel_params(20),
        cost_estimate=cost(50 * 10**9, 12 * 1024 * 1024),
        name="weight_grads",
    )(info, *[far(a) for a in blocks], sums)


def fold_kernel(held, came, kept, sent):
    half = (held.shape[0] - SIDES) // 2
    full = 2 * half
    kept[0:half, :] = held[0:half, :].astype(F32) + came[0:half, :].astype(F32)
    sent[0:half, :] = (held[half:full, :].astype(F32) + came[half:full, :].astype(F32)).astype(LOW)
    sides = held[full : full + SIDES, :].astype(LOW).astype(F32) + came[full : full + SIDES, :].astype(F32)
    kept[half : half + SIDES, :] = sides
    sent[half : half + SIDES, :] = sides.astype(LOW)


def fold(held, came):
    half = (held.shape[0] - SIDES) // 2 + SIDES
    outs = (shaped((half, 128), F32), shaped((half, 128), LOW))
    return pl.pallas_call(
        fold_kernel,
        out_shape=outs,
        in_specs=[full_spec(held.shape), full_spec(came.shape)],
        out_specs=tuple(full_spec(a.shape) for a in outs),
        compiler_params=kernel_params(20),
        cost_estimate=cost(0, 1024 * 1024),
        name="fold_gradients",
    )(held, came)


VECTOR_ROWS = (7 * D + FF) // 128


def close_kernel(held, came, before, *outs):
    qus, od, squares = outs[:GROUP], outs[GROUP], outs[GROUP + 1]
    rows = qus[0].shape[0] - SIDES
    full = held.shape[0] - SIDES
    sides = held[full : full + SIDES, :].astype(LOW).astype(F32) + came[full : full + SIDES, :].astype(F32)
    lanes = before[...]
    begin = 0
    for piece in (*qus, od):
        length = rows if piece is not od else od.shape[0]
        here = slice(begin, begin + length)
        begin += length
        total = held[here, :].astype(F32) + came[here, :].astype(F32)
        piece[0:length, :] = total.astype(LOW)
        lanes = lanes + jnp.sum((total * total).reshape(length // 8, 8, 128), axis=0)
    squares[...] = lanes
    high = lanes.astype(LOW).astype(F32)
    rest = sides[VECTOR_ROWS + 16 :]
    sides = jnp.concatenate([sides[:VECTOR_ROWS], high, lanes - high, rest], axis=0).astype(LOW)
    for piece in qus:
        piece[rows : rows + SIDES, :] = sides


def close(ring, held, came, before):
    rows = QU_TILES * (D // ring.count)
    outs = [shaped((rows + SIDES, 128), LOW)] * GROUP
    outs += [shaped((OD_TILES * (SIDE + UNITS) // ring.size, 128), LOW), shaped((8, 128), F32)]
    return pl.pallas_call(
        close_kernel,
        out_shape=tuple(outs),
        in_specs=[full_spec(held.shape), full_spec(came.shape), full_spec(before.shape)],
        out_specs=tuple(full_spec(a.shape) for a in outs),
        compiler_params=kernel_params(16),
        cost_estimate=cost(0, 1024 * 1024),
        name="close_gradients",
    )(held, came, before)


def join_kernel(info, *refs):
    core = info[0]
    firsts, seconds, (od_first, od_second), outs = refs[:4], refs[4:8], refs[8:10], refs[10:]
    sent, vec, squares, vec_squares = outs
    rows = firsts[0].shape[0] - SIDES
    sides = []
    for pieces in (firsts, seconds):
        parts = [a[rows : rows + SIDES, :].astype(F32) for a in pieces]
        sides.append((parts[0] + parts[1]) + (parts[2] + parts[3]))
    squares[...] = sides[0][VECTOR_ROWS : VECTOR_ROWS + 8] + sides[0][VECTOR_ROWS + 8 : VECTOR_ROWS + 16]
    own = [(a[:VECTOR_ROWS] * a[:VECTOR_ROWS]).reshape(VECTOR_ROWS // 8, 8, 128) for a in sides]
    vec_squares[...] = jnp.sum(own[0], axis=0) + jnp.sum(own[1], axis=0)
    vec[...] = jnp.where(core == 0, sides[0], sides[1])

    def write(pieces, od):
        for r in range(GROUP):
            sent[r * rows : (r + 1) * rows, :] = pieces[r][0:rows, :]
        sent[GROUP * rows :, :] = od[...]

    pl.when(core == 0)(functools.partial(write, seconds, od_second))
    pl.when(core == 1)(functools.partial(write, firsts, od_first))


def join(info, firsts, seconds, od_first, od_second):
    rows = firsts[0].shape[0] - SIDES
    outs = (shaped((GROUP * rows + od_first.shape[0], 128), LOW), shaped((SIDES, 128), F32))
    outs += (shaped((8, 128), F32),) * 2
    blocks = (*firsts, *seconds, od_first, od_second)
    return pl.pallas_call(
        join_kernel,
        out_shape=outs,
        in_specs=[smem_spec()] + [full_spec(a.shape) for a in blocks],
        out_specs=tuple(full_spec(a.shape) for a in outs),
        compiler_params=kernel_params(16),
        cost_estimate=cost(0, 1024 * 1024),
        name="join_members",
    )(info, *blocks)


def adam_update(weight, grad, first, second, factor, rate):
    clipped = grad * factor
    first_new = BETA_ONE * first + (1.0 - BETA_ONE) * clipped
    second_new = BETA_TWO * second + (1.0 - BETA_TWO) * clipped * clipped
    first_hat = first_new / (1.0 - BETA_ONE**STEP)
    second_hat = second_new / (1.0 - BETA_TWO**STEP)
    weight_new = weight - rate * (
        first_hat / (jnp.sqrt(second_hat) + ADAM_EPS) + WEIGHT_DECAY * weight
    )
    return (weight_new, first_new, second_new)


def mixed_tile(tile, member):
    at = tile * 128
    if at >= 3 * SIDE:
        return 2, up_column(member, at - 3 * SIDE)
    width = SIDE // SPREAD
    kind, within = at // SIDE, at % SIDE
    return 0, qkv_column(kind, within // width, member) + within % width


def adam_kernel(info, factor_ref, *refs):
    core, group = info[0], info[1]
    step = pl.program_id(0)
    factor = factor_ref[0]
    qus, refs = (refs[:4], refs[4:8]), refs[8:]
    ods, came, refs = refs[:2], refs[2], refs[3:]
    olds, news = refs[:12], refs[12:]
    few, many = olds[0].shape[1], olds[9].shape[1]
    rows = (qus[0][0].shape[0] - SIDES) // QU_TILES
    od_rows = ods[0].shape[0] // OD_TILES

    def update(which, column, grad):
        columns = slice(column, column + 128)
        weight, first, second = [olds[3 * which + i][0, :, columns] for i in range(3)]
        fresh = adam_update(weight, grad.astype(F32), first, second, factor, LEARN_RATE)
        for i in range(3):
            news[3 * which + i][0, :, columns] = fresh[i]

    def rows_of(ref, begin, length):
        return ref[pl.ds(pl.multiple_of(begin + step * length, 16), length), :]

    def both_halves(here):
        for half in range(2):
            for tile in range(OD_TILES):
                column = half * (D // 2) + tile * 128
                ref, begin = (ods[here], 0) if half == here else (came, GROUP * QU_TILES * rows)
                begin = begin + tile * od_rows
                update(3, column, rows_of(ref, begin, many))
                update(1, column, rows_of(ref, begin + od_rows - rows, few))
            for member in range(GROUP):
                if half == here:
                    for g in range(GROUP):

                        @pl.when(group == g)
                        def _(ref=qus[here][member ^ g]):
                            for tile in range(QU_TILES):
                                which, column = mixed_tile(half * QU_TILES + tile, member)
                                update(which, column, rows_of(ref, tile * rows, few))
                else:
                    for tile in range(QU_TILES):
                        which, column = mixed_tile(half * QU_TILES + tile, member)
                        begin = ((group ^ member) * QU_TILES + tile) * rows
                        update(which, column, rows_of(came, begin, few))

    for here in range(2):
        pl.when(core == here)(functools.partial(both_halves, here))


def adam(info, factor, qus, ods, came, olds):
    steps = max(1, olds[0].shape[1] // 16)

    def master(a):
        return pl.BlockSpec((1, a.shape[1] // steps, a.shape[2]), lambda i: (0, i, 0))

    grads = (*qus[0], *qus[1], *ods, came)
    return pl.pallas_call(
        adam_kernel,
        grid=(steps,),
        out_shape=tuple(shaped(a.shape, F32) for a in olds),
        in_specs=[smem_spec(), smem_spec()]
        + [full_spec(a.shape) for a in grads]
        + [master(a) for a in olds],
        out_specs=tuple(master(a) for a in olds),
        compiler_params=kernel_params(28),
        name="adamw",
    )(info, factor, *grads, *[far(a) for a in olds])


def doc_tables(lengths, rows):
    seqs = lengths.shape[0]
    ends = jnp.cumsum(lengths, axis=1)
    places = jnp.arange(rows, dtype=jnp.int32)
    past = places[None, :, None] >= ends[:, None, :]
    begins = jnp.sum(jnp.where(past, lengths[:, None, :], 0), axis=2)
    position = (places[None, :] - begins).reshape(seqs * rows, 1)
    half = ROT // 2
    inverse = 10000.0 ** (-(jnp.arange(half, dtype=F32) * 2.0) / ROT)
    lanes = jnp.concatenate([inverse, inverse, jnp.zeros(HEAD_DIM - ROT, F32)])
    angles = position.astype(F32) * jnp.concatenate([lanes, lanes])[None, :]
    allowed = (places[None, None, :] <= places[None, :, None]) & (places[None, None, :] >= begins[:, :, None])
    mask = jnp.where(allowed, 0.0, -1e30).reshape(seqs * rows, rows).astype(F32)
    return jnp.cos(angles), jnp.sin(angles), mask


def shards(
    x_in,
    cotangent,
    doc_lengths,
    w_qkv,
    w_out,
    w_up,
    w_down,
    vectors,
    m_qkv,
    m_out,
    m_up,
    m_down,
    m_vectors,
    v_qkv,
    v_out,
    v_up,
    v_down,
    v_vectors,
):
    place = Place()
    ring, core, group, spot = place.ring, place.core, place.group, place.spot
    info = place.info()
    local_rows, width = x_in.shape
    seqs, docs = doc_lengths.shape
    rows = local_rows // seqs
    in_rows = w_qkv.shape[1]
    shard = vectors.shape[1]
    members = range(1, GROUP)

    vec_block = jnp.pad(vectors[0].astype(LOW), (0, in_rows * 128 - shard)).reshape(in_rows, 128)
    keep_qu, send_qu, keep_od, send_od = pack(info, w_qkv, w_out, w_up, w_down, vec_block)
    came_qu = place.sibling(send_qu)
    came_od = place.sibling(send_od)

    def member_columns(block, *waited):
        qu = jnp.where(core == block, keep_qu, came_qu)
        sent = [after(take(qu, group ^ r), *waited) for r in members]
        return [take(qu, group)] + [place.member(a, r) for a, r in zip(sent, members)]

    def gather(block, *waited):
        late = after(block, *waited)
        return [block] + [place.member(late, r) for r in members]

    def to_owners(slots):
        return [slots[0]] + [place.member(slots[r], r) for r in members]

    def total_of(slots):
        return sum(a.astype(F32) for a in slots)

    def block_vectors(parts):
        pieces = jnp.concatenate([a[:, :, 0 : -(-shard // 128), PART:] for a in parts])
        pieces = pieces.reshape(ring.size * GROUP, -1)[:, :shard]
        dp = jnp.arange(ring.count, dtype=jnp.int32)
        difference = ring.spot_of(dp) ^ spot
        slot = jnp.where(core == 0, ring.slot(difference, 0), ring.slot(difference, 1))
        vec = jnp.take(pieces, slot * GROUP + (ring.group_of(dp) ^ group), axis=0, mode="clip")
        vec = vec.reshape(-1).astype(F32)
        b_qkv, b_out, b_up, b_down, gain, ln_bias = jnp.split(
            vec, [3 * D, 4 * D, 4 * D + FF, 5 * D + FF, 6 * D + FF]
        )
        b_qkv = take(b_qkv.reshape(3 * SPREAD, GROUP, -1), group, 1).reshape(1, -1)
        b_up = take(b_up.reshape(SPREAD, GROUP, -1), group, 1).reshape(1, -1)
        return (b_qkv, b_up, gain[None], ln_bias[None]), (b_out + b_down)[None], gain[None]

    x_own = take(x_in.reshape(2, rows, width), core)
    cot_own = take(cotangent.reshape(2, rows, width), core)
    len_own = take(doc_lengths, core)
    len_rows = jnp.zeros((16, width), LOW).at[0, :docs].set(len_own.astype(LOW))
    x_sent = jnp.concatenate([x_own, len_rows])

    qu_came = member_columns(0)
    qu_own = jnp.stack(qu_came)[None]
    x_group = gather(x_sent, qu_came[1])
    od_own = after(jnp.where(core == 0, keep_od, came_od)[None], x_group[1])
    od = [jnp.concatenate([od_own, place.across(od_own, 0)])]
    qu = [jnp.concatenate([qu_own, place.across(qu_own, 0)])]
    for step in range(1, ring.bits):
        od.append(place.across(jnp.concatenate(od), step))
        qu.append(place.across(jnp.concatenate(qu), step))
    qu_sibling = [place.sibling(a) for a in qu[:-1]] + [place.sibling(after(qu[-1], *x_group[1:]))]
    qu_mine = jnp.where(core == 1, keep_qu, came_qu)
    waited = (*x_group[2:], od[0], qu_sibling[0])
    sent = [after(jnp.concatenate([take(qu_mine, group ^ r), cot_own]), *waited) for r in members]
    qu_cot = [place.member(a, r) for a, r in zip(sent, members)]
    parts_first = (*qu, *od, *qu_sibling, *(place.sibling(a) for a in od))
    lengths = jnp.stack([a[rows, :docs] for a in x_group]).astype(jnp.int32)
    tables = doc_tables(lengths, rows)
    vecs_first, bias_first, gain_first = block_vectors(qu)

    first = forward(ring, info, parts_first, x_group, tables, vecs_first, rows)
    kept_first, tables = first[GROUP:], first[-3:]
    qu_cot = [after(a, first[0]) for a in qu_cot]
    came = to_owners(first[:GROUP])
    od_own = after(jnp.where(core == 1, keep_od, came_od)[None], first[0])
    od_late = [jnp.concatenate([od_own, place.across(od_own, 0)])]
    came[1] = after(came[1], od_late[0])
    hidden_first = (x_own.astype(F32) + total_of(came) + bias_first).astype(LOW)
    hidden_group = gather(hidden_first)
    qu_own = jnp.stack([take(qu_mine, group)] + [a[:in_rows] for a in qu_cot])[None]
    qu_late = [jnp.concatenate([qu_own, after(place.across(qu_own, 0), hidden_first)])]
    for step in range(1, ring.bits):
        od_late.append(after(place.across(jnp.concatenate(od_late), step), *hidden_group[1:]))
        qu_late.append(after(place.across(jnp.concatenate(qu_late), step), *hidden_group[1:]))
    qu_sibling, od_sibling = [
        [place.sibling(after(a, *hidden_group[1:])) for a in late] for late in (qu_late, od_late)
    ]
    parts_second = (*qu_late, *od_late, *qu_sibling, *od_sibling)
    vecs_second, bias_second, gain_second = block_vectors(qu_late)
    second = middle(ring, info, parts_second, hidden_group, [cot_own, *qu_cot], tables, vecs_second, rows)
    sums_second, y_second, mixed_second, active_second, dqu_second, grad_second = second[GROUP : GROUP + 6]
    z_second = second[GROUP + 6 :]

    def rows_backward(rows_low, grad_low, dy, gain):
        rows_now = rows_low.astype(F32)
        centered = rows_now - jnp.mean(rows_now, axis=-1, keepdims=True)
        variance = jnp.mean(centered * centered, axis=-1, keepdims=True)
        inverse_std = lax.rsqrt(variance + NORM_EPS)
        normed = centered * inverse_std
        scaled = dy * gain
        inner_mean = jnp.mean(scaled, axis=-1, keepdims=True)
        inner_cross = jnp.mean(scaled * normed, axis=-1, keepdims=True)
        return (grad_low.astype(F32) + inverse_std * (scaled - inner_mean - normed * inner_cross)).astype(LOW)

    def to_members(pieces):
        return [pieces[0]] + [place.member(pieces[r], r) for r in members]

    steps = list(reversed(range(ring.bits)))

    def ring_fold(held, *waited):
        kept, sent = held
        for step in steps[:-1]:
            kept, sent = fold(kept, after(place.across(sent, step), *waited))
        return kept, sent

    dy_second = to_owners(second[:GROUP])
    grads = weight_grads(ring, info, mixed_second, active_second, grad_second, y_second, dqu_second, sums_second)
    mid_grad = rows_backward(hidden_first, cot_own, total_of(dy_second), gain_second)
    mid_group = gather(mid_grad)
    sent = place.sibling(after(grads[1], *dy_second[1:]))
    second_held = ring_fold(fold(grads[0], after(sent, mid_grad)))

    mid_late = [after(mid_group[0], *second_held)] + mid_group[1:]
    dyz_keep, dyz_send, keep, send = backward(ring, info, mid_late, z_second, kept_first, rows)
    kept, sent = second_held
    none = jnp.zeros((8, 128), F32)
    *qu_second, od_second, squares_second = close(ring, kept, after(place.across(sent, 0), send), none)
    send = after(send, *qu_second)
    qu_slots_second = to_members(qu_second)
    kept, sent = ring_fold(fold(keep, place.sibling(send)))
    dyz_came = place.toward(after(dyz_send, *qu_slots_second[1:]), 1)
    came = after(place.across(after(sent, *qu_slots_second[1:]), 0), dyz_came)
    *qu_first, od_first, _ = close(ring, kept, came, squares_second)
    qu_slots_first = to_members(qu_first)
    grads_sent, vec, squares, vec_squares = join(info, qu_slots_first, qu_slots_second, od_first, od_second)
    squares = squares + place.sibling(squares)
    second_step = place.toward((dyz_keep[1].astype(F32) + dyz_came[1].astype(F32)).astype(LOW), 0)
    second_step = after(second_step, squares)
    for step in range(ring.bits):
        squares = squares + place.across(squares, step)
    squares = jnp.sum(squares + vec_squares)
    dyz = dyz_keep[0].astype(F32) + dyz_came[0].astype(F32) + second_step.astype(F32)
    start_grad = rows_backward(x_own, mid_grad, dyz[:rows], gain_first)
    hidden_second = (hidden_first.astype(F32) + dyz[rows:] + bias_second).astype(LOW)

    grad_norm = jnp.sqrt(squares)
    factor = jnp.minimum(1.0, CLIP_LEVEL / (grad_norm + 1e-06))

    def own_block(one, two):
        came = place.sibling(jnp.where(core == 0, two, one))
        mine = jnp.where(core == 0, one, two)
        return [jnp.where(core == h, mine, came) for h in range(2)]

    grads_came = place.sibling(grads_sent)
    vec_share = after(vec, grads_sent).reshape(-1)[: ring.count * shard].reshape(ring.count, shard)
    vec_share = take(vec_share, lax.axis_index("dp"))[None]
    olds = (w_qkv, m_qkv, v_qkv, w_out, m_out, v_out, w_up, m_up, v_up, w_down, m_down, v_down)
    qus = (qu_slots_first, qu_slots_second)
    news = adam(info, factor[None], qus, (od_first, od_second), grads_came, olds)
    new_vec = adam_update(vectors, vec_share, m_vectors, v_vectors, factor, VECTOR_RATE)

    outputs = own_block(jnp.stack([hidden_first, start_grad]), jnp.stack([hidden_second, mid_grad]))
    outputs = jnp.concatenate(outputs, axis=1)
    hidden_out, input_grads = outputs[:1], outputs[1:]
    return (
        hidden_out,
        input_grads,
        *(news[3 * i] for i in range(4)),
        new_vec[0],
        *(news[3 * i + 1] for i in range(4)),
        new_vec[1],
        *(news[3 * i + 2] for i in range(4)),
        new_vec[2],
        grad_norm,
    )


def solution(mesh):
    return jax.shard_map(
        shards,
        mesh=mesh,
        in_specs=(
            P("dp", None),
            P("dp", None),
            P("dp", None),
            P("section", "dp", None),
            P("section", "dp", None),
            P("section", "dp", None),
            P("section", "dp", None),
            P("section", "dp"),
            P("section", "dp", None),
            P("section", "dp", None),
            P("section", "dp", None),
            P("section", "dp", None),
            P("section", "dp"),
            P("section", "dp", None),
            P("section", "dp", None),
            P("section", "dp", None),
            P("section", "dp", None),
            P("section", "dp"),
        ),
        out_specs=(
            P("section", "dp", None),
            P("section", "dp", None),
            P("section", "dp", None),
            P("section", "dp", None),
            P("section", "dp", None),
            P("section", "dp", None),
            P("section", "dp"),
            P("section", "dp", None),
            P("section", "dp", None),
            P("section", "dp", None),
            P("section", "dp", None),
            P("section", "dp"),
            P("section", "dp", None),
            P("section", "dp", None),
            P("section", "dp", None),
            P("section", "dp", None),
            P("section", "dp"),
            P(),
        ),
        check_vma=False,
    )
```

```python
import functools

import jax
import jax.numpy as jnp
from jax import lax
from jax.experimental import pallas as pl
from jax.experimental.pallas import tpu as pltpu
from jax.sharding import PartitionSpec as P

D = 1024
FF = 4096
HEADS = 16
HEAD_DIM = 64
ROT = 16
STEP = 10


NORM_EPS = 1e-05
BETA_ONE = 0.9
BETA_TWO = 0.95
LEARN_RATE = 0.05
VECTOR_RATE = 0.3
WEIGHT_DECAY = 0.01
CLIP_LEVEL = 1.0
ADAM_EPS = 1e-08

AXES = ("section", "dp")
GROUP = 4
SPREAD = 1
LOW = jnp.bfloat16
F32 = jnp.float32
SIDE = D // GROUP
UNITS = FF // GROUP
MIXED = 3 * SIDE + UNITS
PART = MIXED // 2
WIRE = PART + 128


class Ring:
    def __init__(self, count):
        self.count = count
        self.low = count // (GROUP * SPREAD)
        self.size = SPREAD * self.low
        self.bits = self.size.bit_length() - 1

    def index(self, g, t):
        return ((t // self.low) * GROUP + g) * self.low + t % self.low

    def group_of(self, dp):
        return (dp // self.low) % GROUP

    def spot_of(self, dp):
        return (dp // (GROUP * self.low)) * self.low + dp % self.low

    def order(self, core):
        steps = list(range(self.bits))
        if SPREAD > 1 or core == 1:
            steps.reverse()
        return steps

    def turn(self, slot, core):
        return sum(((slot >> s) & 1) << b for s, b in enumerate(self.order(core)))

    def slot(self, difference, core):
        return sum(((difference >> b) & 1) << s for s, b in enumerate(self.order(core)))


class Place:
    def __init__(self):
        self.ring = Ring(lax.axis_size("dp"))
        self.core = lax.axis_index("section")
        dp = lax.axis_index("dp")
        self.group = self.ring.group_of(dp)
        self.spot = self.ring.spot_of(dp)

    def info(self):
        return jnp.stack([self.core, self.group, self.spot]).astype(jnp.int32)

    def move(self, block, where):
        ring = self.ring
        route = []
        for core in range(2):
            for g in range(GROUP):
                for t in range(ring.size):
                    c, h, u = where(core, g, t)
                    route.append((core * ring.count + ring.index(g, t), c * ring.count + ring.index(h, u)))
        return lax.ppermute(block, AXES, route)

    def sibling(self, block):
        return self.move(block, lambda c, g, t: (1 - c, g, t))

    def member(self, block, distance):
        return self.move(block, lambda c, g, t: (c, g ^ distance, t))

    def toward(self, block, step):
        return self.move(block, lambda c, g, t: (c, g ^ (2, 1)[(step + c) % 2], t))

    def across(self, block, step):
        return self.move(block, lambda c, g, t: (c, g, t ^ (1 << self.ring.order(c)[step])))


def take(block, index, axis=0):
    return lax.dynamic_index_in_dim(block, index, axis, keepdims=False)


def after(block, *waited):
    return lax.optimization_barrier((block, waited))[0]


def dot(left, right):
    return jnp.dot(left, right, preferred_element_type=F32)


def dot_cols(left, right):
    return lax.dot_general(left, right, (((1,), (1,)), ((), ())), preferred_element_type=F32)


def dot_rows(left, right):
    return lax.dot_general(left, right, (((0,), (0,)), ((), ())), preferred_element_type=F32)


def full_spec(shape):
    return pl.BlockSpec(shape, lambda *_: (0,) * len(shape))


def far_spec():
    return pl.BlockSpec(memory_space=pltpu.HBM)


def far(block):
    return pltpu.with_memory_space_constraint(block, pltpu.HBM)


def any_spec():
    return pl.BlockSpec(memory_space=pl.ANY)


def smem_spec():
    return pl.BlockSpec(memory_space=pltpu.SMEM)


def shaped(shape, dtype):
    return jax.ShapeDtypeStruct(shape, dtype)


def kernel_params(mebibytes):
    return pltpu.CompilerParams(vmem_limit_bytes=mebibytes * 1024 * 1024)


def up_pieces():
    run = UNITS // SPREAD
    cuts = sorted({0, PART - 3 * SIDE, UNITS} | {run * i for i in range(SPREAD)})
    pieces = []
    for begin, end in zip(cuts[:-1], cuts[1:]):
        column = 3 * SIDE + begin
        pieces.append((begin, column // PART, column % PART, end - begin))
    return pieces


def up_column(g, local):
    run = UNITS // SPREAD
    return (local // run * GROUP + g) * run + local % run


def qkv_column(kind, run, g):
    width = SIDE // SPREAD
    return ((kind * SPREAD + run) * GROUP + g) * width


def pack_kernel(info, qkv_hbm, out_hbm, up_hbm, down_hbm, vec, keep_qu, send_qu, keep_od, send_od, *scratch):
    w_qkv, w_out, w_up, w_down, sems = scratch
    pairs = ((qkv_hbm, w_qkv), (up_hbm, w_up), (down_hbm, w_down), (out_hbm, w_out))
    copies = [pltpu.make_async_copy(far.at[0], near, sems.at[i]) for i, (far, near) in enumerate(pairs)]
    for copy in copies:
        copy.start()
    rows = w_qkv.shape[0]
    ff_rows = w_down.shape[0]
    width = SIDE // SPREAD
    core = info[0]

    def write_qu(halves):
        for g in range(GROUP):
            for kind in range(3):
                for run in range(SPREAD):
                    at = (kind * SPREAD + run) * width
                    column = qkv_column(kind, run, g)
                    halves[0][g, :, at : at + width] = w_qkv[:, column : column + width].astype(LOW)
            for local, half, at, length in up_pieces():
                column = up_column(g, local)
                halves[half][g, :, at : at + length] = w_up[:, column : column + length].astype(LOW)
            for half in range(2):
                halves[half][g, :, PART:WIRE] = vec[...]

    def write_od(halves):
        for half in range(2):
            columns = slice(half * (D // 2), (half + 1) * (D // 2))
            halves[half][0:ff_rows] = w_down[:, columns].astype(LOW)
            halves[half][ff_rows : ff_rows + rows] = w_out[:, columns].astype(LOW)

    for first, last, write, kept, sent in ((0, 2, write_qu, keep_qu, send_qu), (2, 4, write_od, keep_od, send_od)):
        for copy in copies[first:last]:
            copy.wait()
        pl.when(core == 0)(functools.partial(write, (kept, sent)))
        pl.when(core == 1)(functools.partial(write, (sent, kept)))


def pack(info, w_qkv, w_out, w_up, w_down, vec):
    rows, ff_rows = w_qkv.shape[1], w_down.shape[1]
    qu = shaped((GROUP, rows, WIRE), LOW)
    od = shaped((ff_rows + rows, D // 2), LOW)
    return pl.pallas_call(
        pack_kernel,
        out_shape=(qu, qu, od, od),
        in_specs=[smem_spec()] + [far_spec()] * 4 + [full_spec(vec.shape)],
        out_specs=tuple(full_spec(a.shape) for a in (qu, qu, od, od)),
        scratch_shapes=[pltpu.VMEM(a.shape[1:], F32) for a in (w_qkv, w_out, w_up, w_down)]
        + [pltpu.SemaphoreType.DMA((4,))],
        compiler_params=kernel_params(20),
        name="pack_weights",
    )(info, far(w_qkv), far(w_out), far(w_up), far(w_down), vec)


def stack_kernel(*refs):
    for i, ref in enumerate(refs[:-1]):
        refs[-1][0, i] = ref[...]


def stack_members(pieces):
    out = shaped((1, len(pieces), *pieces[0].shape), LOW)
    return pl.pallas_call(
        stack_kernel,
        out_shape=out,
        in_specs=[full_spec(a.shape) for a in pieces],
        out_specs=full_spec(out.shape),
        compiler_params=kernel_params(16),
        cost_estimate=cost(50 * 10**9, 1024 * 1024),
        name="stack_members",
    )(*pieces)


def weight_copies(ring, info, parts, wqu, wout, wdown, sems):
    core, group, spot = info[0], info[1], info[2]
    qu_copies, od_copies = [], []
    count = len(parts) // 4
    for which in range(2):
        half = core if which == 0 else 1 - core
        qu_at = pl.multiple_of(half * PART, 128)
        od_at = pl.multiple_of(half * (D // 2), 128)
        slot = 0
        for piece in range(count):
            qu, od = parts[2 * count * which + piece], parts[2 * count * which + count + piece]
            rows = qu.shape[2]
            ff_rows = od.shape[1] - rows
            for i in range(qu.shape[0]):
                straight, turned = ring.turn(slot, 0), ring.turn(slot, 1)
                there = spot ^ (straight + half * (turned - straight))
                slot += 1
                ff_row = pl.multiple_of(there * ff_rows, ff_rows)
                out_row = pl.multiple_of(there * rows, rows)
                far = wdown.at[pl.ds(ff_row, ff_rows), pl.ds(od_at, D // 2)]
                od_copies.append(pltpu.make_async_copy(od.at[i, pl.ds(0, ff_rows)], far, sems.at[0]))
                far = wout.at[pl.ds(out_row, rows), pl.ds(od_at, D // 2)]
                od_copies.append(pltpu.make_async_copy(od.at[i, pl.ds(ff_rows, rows)], far, sems.at[0]))
                for r in range(GROUP):
                    row = pl.multiple_of(ring.index(group ^ r, there) * rows, rows)
                    far = wqu.at[pl.ds(row, rows), pl.ds(qu_at, PART)]
                    qu_copies.append(pltpu.make_async_copy(qu.at[i, r, :, pl.ds(0, PART)], far, sems.at[1]))
    return qu_copies, od_copies


def head_masks(dtype):
    lane = lax.broadcasted_iota(jnp.int32, (1, SIDE), 1) // HEAD_DIM
    return [(lane == h).astype(dtype) for h in range(SIDE // HEAD_DIM)]


def by_head(parts):
    lane = lax.broadcasted_iota(jnp.int32, (1, SIDE), 1) // HEAD_DIM
    total = parts[-1]
    for h in range(len(parts) - 2, -1, -1):
        total = jnp.where(lane == h, parts[h], total)
    return total


def turning(cosine, sine, back):
    lane = lax.broadcasted_iota(jnp.int32, sine.shape, 1) % HEAD_DIM
    first = jnp.where(lane < ROT // 2, sine, 0.0)
    second = jnp.where(lane < ROT // 2, 0.0, sine)
    if back:
        second = -second
    else:
        first = -first
    wide = SIDE // cosine.shape[1]
    return [jnp.concatenate([a] * wide, axis=1) for a in (cosine, first, second)]


def turn(part, tables):
    cosine, first, second = tables
    ahead = pltpu.roll(part, SIDE - ROT // 2, 1)
    behind = pltpu.roll(part, ROT // 2, 1)
    return part * cosine + ahead * first + behind * second


def normalise(rows):
    centered = rows - jnp.mean(rows, axis=-1, keepdims=True)
    variance = jnp.mean(centered * centered, axis=-1, keepdims=True)
    return centered * lax.rsqrt(variance + NORM_EPS)


def no_wait():
    pass


def forward_part(x_refs, tables, vecs, wqu, wout, wdown, kept, z_refs, waits, done, normed_ref=None):
    cosine, sine, mask = tables
    b_qkv, b_up, gain, ln_bias = vecs
    y, qkv, probs, mixed, active, slope = kept
    rows = z_refs[0].shape[0]
    for r in range(GROUP):
        normed = normalise(x_refs[r][0:rows, :].astype(F32))
        if normed_ref is not None:
            normed_ref[r * rows : (r + 1) * rows, :] = normed
        y[r * rows : (r + 1) * rows, :] = (normed * gain[...] + ln_bias[...]).astype(LOW)
    done(0)
    waits[0]()
    waits[2]()
    forth = turning(cosine[...], sine[...], False)
    for kind in range(3):
        columns = slice(kind * SIDE, (kind + 1) * SIDE)
        part = dot(y[...], wqu[:, columns]) + b_qkv[:, columns]
        if kind < 2:
            part = turn(part, forth)
        qkv[:, columns] = part.astype(LOW)
    done(1)
    masks = head_masks(LOW)
    heads = len(masks)
    for r in range(GROUP):
        here = slice(r * rows, (r + 1) * rows)
        query, keys, values = [qkv[here, k * SIDE : (k + 1) * SIDE] for k in range(3)]
        stacked = jnp.concatenate([query * m for m in masks], axis=0)
        scores = dot_cols(stacked, keys) * HEAD_DIM ** (-0.5)
        scores = scores.reshape(heads, rows, rows) + mask[here, :][None]
        expo = jnp.exp(scores - jnp.max(scores, axis=-1, keepdims=True))
        prob = expo / jnp.sum(expo, axis=-1, keepdims=True)
        prob = prob.reshape(heads * rows, rows)
        probs[r * heads * rows : (r + 1) * heads * rows, :] = prob
        full = dot(prob.astype(LOW), values)
        mixed[here, :] = by_head([full[h * rows : (h + 1) * rows] for h in range(heads)]).astype(LOW)
    done(2)
    done(3)
    tile = 256
    for at in range(0, UNITS, tile):
        hidden = dot(y[...], wqu[:, 3 * SIDE + at : 3 * SIDE + at + tile]) + b_up[:, at : at + tile]
        share = 0.5 * (1.0 + lax.erf(hidden * (0.5**0.5)))
        density = jnp.exp(-0.5 * hidden * hidden) * (0.5 / jnp.pi) ** 0.5
        active[:, at : at + tile] = (hidden * share).astype(LOW)
        slope[:, at : at + tile] = share + hidden * density
    done(4)
    done(5)
    waits[1]()
    for at in range(0, D, tile):
        branch = dot(mixed[...], wout[:, at : at + tile]) + dot(active[...], wdown[:, at : at + tile])
        for r in range(GROUP):
            z_refs[r][:, at : at + tile] = branch[r * rows : (r + 1) * rows].astype(LOW)


def backward_part(grad, normed, tables, wqu, wout, wdown, kept, dqu, dy_refs, sums, waits, done):
    cosine, sine, _ = tables
    y, qkv, probs, mixed, active, slope = kept
    rows = grad.shape[0] // GROUP
    tile = 256
    waits[0]()
    dmixed = dot_cols(grad[...], wout[...]).astype(LOW)
    for at in range(0, UNITS, tile):
        dactive = dot_cols(grad[...], wdown[at : at + tile, :])
        dhidden = (dactive * slope[:, at : at + tile]).astype(LOW)
        dqu[:, 3 * SIDE + at : 3 * SIDE + at + tile] = dhidden
    waits[1]()
    masks = head_masks(LOW)
    heads = len(masks)
    back = turning(cosine[...], sine[...], True)
    for r in range(GROUP):
        here = slice(r * rows, (r + 1) * rows)
        query, keys, values = [qkv[here, k * SIDE : (k + 1) * SIDE] for k in range(3)]
        dstack = jnp.concatenate([dmixed[here] * m for m in masks], axis=0)
        dprob = dot_cols(dstack, values)
        prob = probs[r * heads * rows : (r + 1) * heads * rows, :]
        dvalues = dot_rows(prob.astype(LOW), dstack)
        dscore = (prob * (dprob - jnp.sum(prob * dprob, axis=-1, keepdims=True))).astype(LOW)
        full = dot(dscore, keys)
        dquery = by_head([full[h * rows : (h + 1) * rows] for h in range(heads)])
        dkeys = dot_rows(dscore, jnp.concatenate([query * m for m in masks], axis=0))
        scale = HEAD_DIM ** (-0.5)
        slot_tables = [a[here] for a in back]
        dqu[here, 0:SIDE] = turn(dquery * scale, slot_tables).astype(LOW)
        dqu[here, SIDE : 2 * SIDE] = turn(dkeys * scale, slot_tables).astype(LOW)
        dqu[here, 2 * SIDE : 3 * SIDE] = dvalues.astype(LOW)
    done()
    for at in range(0, MIXED, tile):
        sums[:, at : at + tile] = jnp.sum(dqu[:, at : at + tile].astype(F32), axis=0, keepdims=True)
    waits[2]()
    for at in range(0, D, tile):
        dy = dot_cols(dqu[...], wqu[at : at + tile, :])
        for r in range(GROUP):
            dy_refs[r][:, at : at + tile] = dy[r * rows : (r + 1) * rows].astype(LOW)
        own = grad[0:rows, at : at + tile].astype(F32)
        for i, terms in enumerate((own, dy * normed[:, at : at + tile], dy)):
            begin = MIXED + i * D + at
            sums[:, begin : begin + tile] = jnp.sum(terms, axis=0, keepdims=True)


def kept_shapes(tokens, rows):
    return [
        ((tokens, D), LOW),
        ((tokens, 3 * SIDE), LOW),
        ((tokens * (SIDE // HEAD_DIM), rows), F32),
        ((tokens, SIDE), LOW),
        ((tokens, UNITS), LOW),
        ((tokens, UNITS), F32),
    ]


def weight_scratch():
    return [
        pltpu.VMEM((D, MIXED), LOW),
        pltpu.VMEM((SIDE, D), LOW),
        pltpu.VMEM((UNITS, D), LOW),
        pltpu.SemaphoreType.DMA((2,)),
    ]


def waiter(copies):
    def wait():
        for copy in copies:
            copy.wait()

    return wait


def started(pairs, sem):
    copies = [pltpu.make_async_copy(source, target, sem) for source, target in pairs]
    for copy in copies:
        copy.start()
    return waiter(copies)


def table_scratch(tokens, rows):
    return [pltpu.VMEM((tokens, 128), F32), pltpu.VMEM((tokens, 128), F32), pltpu.VMEM((tokens, rows), F32)]


def cost(flops, moved):
    return pl.CostEstimate(flops=2 * flops, bytes_accessed=2 * moved, transcendentals=0)


def leaving(pairs, sems):
    copies = [pltpu.make_async_copy(near, far, sems.at[i]) for i, (near, far) in enumerate(pairs)]

    def go(i):
        copies[i].start()

    return go, waiter(copies)


def pair_copies(info, slots, keep, send, sems):
    targets = (keep.at[0], keep.at[1], send.at[0], send.at[1])
    return [
        [pltpu.make_async_copy(slots[r], target, sems.at[i]) for i, (r, target) in enumerate(zip(order, targets))]
        for order in ((0, 2, 1, 3), (0, 1, 2, 3))
    ]


def on_core(info, copies, act):
    for here in range(2):

        @pl.when(info[0] == here)
        def _(mine=copies[here]):
            for copy in mine:
                act(copy)


def forward_kernel(ring, count, info, *refs):
    parts, refs = refs[:count], refs[count:]
    x_refs, refs = refs[:4], refs[4:]
    tables, refs = refs[:3], refs[3:]
    vecs, refs = refs[:4], refs[4:]
    z_refs, refs = refs[:4], refs[4:]
    far_kept, far_weights, far_tables, refs = refs[:7], refs[7:10], refs[10:13], refs[13:]
    kept, refs = refs[:7], refs[7:]
    out_sems, scratch = refs[0], refs[1:]
    weights = scratch[:3]
    qu_copies, od_copies = weight_copies(ring, info, parts, *scratch)
    for copy in qu_copies + od_copies:
        copy.start()
    pairs = [*zip(kept, far_kept), *zip(weights, far_weights), *zip(tables, far_tables)]
    go, out = leaving(pairs, out_sems)
    for i in range(10, 13):
        go(i)

    def qu_in():
        waiter(qu_copies)()
        go(7)

    def od_in():
        waiter(od_copies)()
        go(8)
        go(9)

    def done(i):
        go(i)
        if i == 0:
            go(6)

    forward_part(x_refs, tables, vecs, *weights, kept[:6], z_refs, (qu_in, od_in, no_wait), done, kept[6])
    out()


def forward(ring, info, parts, xs, tables, vecs, rows):
    tokens = GROUP * rows
    shapes = kept_shapes(tokens, rows) + [((tokens, D), F32)]
    away = [*shapes, ((D, MIXED), LOW), ((SIDE, D), LOW), ((UNITS, D), LOW)] + [(a.shape, F32) for a in tables]
    blocks = (*xs, *tables, *vecs)
    return pl.pallas_call(
        functools.partial(forward_kernel, ring, len(parts)),
        out_shape=(*[shaped((rows, D), LOW)] * GROUP, *[pltpu.HBM(*a) for a in away]),
        in_specs=[smem_spec()] + [any_spec()] * len(parts) + [full_spec(a.shape) for a in blocks],
        out_specs=tuple([full_spec((rows, D))] * GROUP + [far_spec()] * len(away)),
        scratch_shapes=[pltpu.VMEM(*a) for a in shapes]
        + [pltpu.SemaphoreType.DMA((len(away),))]
        + weight_scratch(),
        compiler_params=kernel_params(22),
        cost_estimate=cost(2 * tokens * D * (D + 2 * FF // GROUP), 16 * 1024 * 1024),
        name="forward_shard",
    )(info, *parts, *blocks)


def middle_kernel(ring, count, info, *refs):
    parts, refs = refs[:count], refs[count:]
    x_refs, refs = refs[:4], refs[4:]
    g_refs, refs = refs[:4], refs[4:]
    far_tables, refs = refs[:3], refs[3:]
    vecs, refs = refs[:4], refs[4:]
    dy_refs, refs = refs[:4], refs[4:]
    sums, away, (z_keep, z_send), refs = refs[0], refs[1:6], refs[6:8], refs[8:]
    kept, refs = refs[:6], refs[6:]
    z_refs, tables, refs = refs[:4], refs[4:7], refs[7:]
    (grad, normed, dqu, in_sems, out_sems, z_sems), scratch = refs[:6], refs[6:]
    rows = z_refs[0].shape[0]
    qu_copies, od_copies = weight_copies(ring, info, parts, *scratch)
    for copy in qu_copies:
        copy.start()
    tables_in = started(zip(far_tables, tables), in_sems.at[0])
    for copy in od_copies:
        copy.start()
    pairs = []
    for r, ref in enumerate(g_refs):
        at = ref.shape[0] - rows
        pairs.append((ref.at[pl.ds(at, rows)], grad.at[pl.ds(r * rows, rows)]))
    grad_in = started(pairs, in_sems.at[1])
    go, out = leaving(list(zip([kept[0], kept[3], kept[4], dqu, grad], away)), out_sems)

    def done(i):
        if i in (0, 3, 4):
            go((0, 3, 4).index(i))

    waits = (waiter(qu_copies), waiter(od_copies), tables_in)
    forward_part(x_refs, tables, vecs, *scratch[:3], kept, z_refs, waits, done, normed)
    grad_in()
    go(4)
    z_copies = pair_copies(info, z_refs, z_keep, z_send, z_sems)
    on_core(info, z_copies, lambda copy: copy.start())
    waits = (no_wait, no_wait, no_wait)
    done = functools.partial(go, 3)
    backward_part(grad, normed, tables, *scratch[:3], kept, dqu, dy_refs, sums, waits, done)
    out()
    on_core(info, z_copies, lambda copy: copy.wait())


def middle(ring, info, parts, xs, gs, tables, vecs, rows):
    tokens = GROUP * rows
    shapes = kept_shapes(tokens, rows)
    away = [shapes[0], shapes[3], shapes[4], ((tokens, MIXED), LOW), ((tokens, D), LOW)]
    away += [((2, rows, D), LOW)] * 2
    sums = shaped((1, MIXED + 3 * D), F32)
    return pl.pallas_call(
        functools.partial(middle_kernel, ring, len(parts)),
        out_shape=(*[shaped((rows, D), LOW)] * GROUP, sums, *[pltpu.HBM(*a) for a in away]),
        in_specs=[smem_spec()]
        + [any_spec()] * len(parts)
        + [full_spec(a.shape) for a in xs]
        + [far_spec()] * (GROUP + 3)
        + [full_spec(a.shape) for a in vecs],
        out_specs=tuple([full_spec((rows, D))] * GROUP + [full_spec(sums.shape)] + [far_spec()] * len(away)),
        scratch_shapes=[pltpu.VMEM(*a) for a in shapes]
        + [pltpu.VMEM((rows, D), LOW)] * GROUP
        + table_scratch(tokens, rows)
        + [pltpu.VMEM((tokens, D), LOW), pltpu.VMEM((tokens, D), F32), pltpu.VMEM((tokens, MIXED), LOW)]
        + [pltpu.SemaphoreType.DMA((2,)), pltpu.SemaphoreType.DMA((5,)), pltpu.SemaphoreType.DMA((4,))]
        + weight_scratch(),
        compiler_params=kernel_params(27),
        cost_estimate=cost(4 * tokens * D * (D + 2 * FF // GROUP), 16 * 1024 * 1024),
        name="forward_backward_shard",
    )(info, *parts, *xs, *[far(a) for a in (*gs, *tables)], *vecs)


def backward_kernel(ring, info, *refs):
    g_refs, refs = refs[:4], refs[4:]
    far_kept, far_weights, far_tables, refs = refs[:7], refs[7:10], refs[10:13], refs[13:]
    (dy_keep, dy_send, keep, send), refs = refs[:4], refs[4:]
    kept, refs = refs[:7], refs[7:]
    weights, tables, refs = refs[:3], refs[3:6], refs[6:]
    (grad, dqu, sums, in_sems, out_sems), dy_refs = refs[:5], refs[5:]
    y, qkv, probs, mixed, active, slope, normed = kept
    wqu, wout, wdown = weights
    far_y, far_qkv, far_probs, far_mixed, far_active, far_slope, far_normed = far_kept
    mixed_in = started([(far_mixed, mixed)], in_sems.at[0])
    active_in = started([(far_active, active)], in_sems.at[1])
    units_in = started([*zip(far_weights[1:], weights[1:]), (far_slope, slope)], in_sems.at[2])
    heads_in = started([(far_qkv, qkv), (far_probs, probs), *zip(far_tables, tables)], in_sems.at[3])
    dy_in = started([(far_weights[0], wqu), (far_normed, normed)], in_sems.at[4])
    y_in = started([(far_y, y)], in_sems.at[5])
    rows = g_refs[0].shape[0]
    for r in range(GROUP):
        grad[r * rows : (r + 1) * rows, :] = g_refs[r][...]
    mixed_in()
    od_part(ring, info, mixed, active, grad, keep, send, active_in)
    waits = (units_in, heads_in, dy_in)
    backward_part(grad, normed, tables, *weights, kept[:6], dqu, dy_refs, sums, waits, no_wait)
    copies = pair_copies(info, dy_refs, dy_keep, dy_send, out_sems)
    on_core(info, copies, lambda copy: copy.start())
    y_in()
    qu_part(ring, info, y, dqu, sums, keep, send)
    on_core(info, copies, lambda copy: copy.wait())


def backward(ring, info, gs, held, rows):
    tokens = GROUP * rows
    outs = [shaped((2, rows, D), LOW)] * 2 + [grads_shape(ring)] * 2
    return pl.pallas_call(
        functools.partial(backward_kernel, ring),
        out_shape=tuple(outs),
        in_specs=[smem_spec()] + [full_spec(a.shape) for a in gs] + [far_spec()] * len(held),
        out_specs=tuple(full_spec(a.shape) for a in outs),
        scratch_shapes=[pltpu.VMEM(a.shape, a.dtype) for a in held]
        + [pltpu.VMEM((tokens, D), LOW), pltpu.VMEM((tokens, MIXED), LOW)]
        + [pltpu.VMEM((1, MIXED + 3 * D), F32), pltpu.SemaphoreType.DMA((6,)), pltpu.SemaphoreType.DMA((4,))]
        + [pltpu.VMEM((rows, D), LOW)] * GROUP,
        compiler_params=kernel_params(28),
        cost_estimate=cost(4 * tokens * D * (D + 2 * FF // GROUP), 16 * 1024 * 1024),
        name="backward_shard",
    )(info, *gs, *[far(a) for a in held])


def slot_in(ring, difference, half):
    straight, turned = ring.slot(difference, 0), ring.slot(difference, 1)
    return straight + half * (turned - straight)


QU_TILES = PART // 128
OD_TILES = D // 2 // 128
SIDES = 112


def slot_rows(ring):
    return GROUP * QU_TILES * (D // ring.count) + OD_TILES * (SIDE + UNITS) // ring.size


def grads_shape(ring):
    return shaped((ring.size * slot_rows(ring) + SIDES, 128), LOW)


def od_part(ring, info, mixed, active, grad, keep, send, active_in):
    core, spot = info[0], info[2]
    out_rows = SIDE // ring.size
    ff_rows = UNITS // ring.size
    ahead = GROUP * QU_TILES * (D // ring.count)
    for i, (out, half) in enumerate(((send, 1 - core), (keep, core))):
        columns = pl.ds(pl.multiple_of(half * (D // 2), D // 2), D // 2)
        part = grad[:, columns]
        block = dot_rows(mixed[...], part).astype(LOW)
        if i == 0:
            active_in()
        for there in range(ring.size):
            slot = slot_in(ring, spot ^ there, half)
            piece = dot_rows(active[:, there * ff_rows : (there + 1) * ff_rows], part).astype(LOW)
            for tile in range(OD_TILES):
                lanes = slice(tile * 128, (tile + 1) * 128)
                row = slot * slot_rows(ring) + ahead + tile * (ff_rows + out_rows)
                out[pl.ds(pl.multiple_of(row, 16), ff_rows), :] = piece[:, lanes]
                row = pl.multiple_of(row + ff_rows, 16)
                out[pl.ds(row, out_rows), :] = block[there * out_rows : (there + 1) * out_rows, lanes]


def vector_rows(group, sums):
    width = SIDE // SPREAD
    run = UNITS // SPREAD
    row = lax.broadcasted_iota(jnp.int32, (SIDES, 128), 0)
    pieces = []
    for at in range(0, 3 * SIDE, 128):
        pieces.append(((at // width * GROUP + group) * (width // 128) + at % width // 128, at))
    for at in range(0, UNITS, 128):
        pieces.append((3 * D // 128 + D // 128 + (at // run * GROUP + group) * (run // 128) + at % run // 128, 3 * SIDE + at))
    tail = (4 * D + FF) // 128
    for i, begin in enumerate((3 * D // 128, tail, tail + D // 128, tail + 2 * D // 128)):
        for at in range(0, D, 128):
            pieces.append((begin + at // 128, MIXED + max(i - 1, 0) * D + at))
    return sum(jnp.where(row == where, sums[:, at : at + 128], 0.0) for where, at in pieces)


def qu_part(ring, info, y, dqu, sums, keep, send):
    core, group, spot = info[0], info[1], info[2]
    rows = D // ring.count
    tile = 256
    last = ring.size * slot_rows(ring)
    extra = vector_rows(group, sums).astype(LOW)
    for out, half in ((send, 1 - core), (keep, core)):
        columns = pl.ds(pl.multiple_of(half * PART, 128), PART)
        out[last : last + SIDES, :] = extra
        for at in range(0, D, tile):
            block = dot_rows(y[:, at : at + tile], dqu[:, columns]).astype(LOW)
            for offset in range(0, tile, rows):
                dp = (at + offset) // rows
                slot = slot_in(ring, spot ^ ring.spot_of(dp), half)
                begin = slot * slot_rows(ring) + (group ^ ring.group_of(dp)) * (QU_TILES * rows)
                for i in range(QU_TILES):
                    row = pl.multiple_of(begin + i * rows, 16)
                    out[pl.ds(row, rows), :] = block[offset : offset + rows, i * 128 : (i + 1) * 128]


def grads_kernel(ring, info, far_mixed, far_active, far_grad, far_y, far_dqu, sums, keep, send, *scratch):
    mixed, active, grad, y, dqu, sems = scratch
    grad_in = started([(far_grad, grad), (far_mixed, mixed)], sems.at[0])
    active_in = started([(far_active, active)], sems.at[1])
    rest_in = started([(far_y, y), (far_dqu, dqu)], sems.at[2])
    grad_in()
    od_part(ring, info, mixed, active, grad, keep, send, active_in)
    rest_in()
    qu_part(ring, info, y, dqu, sums, keep, send)


def weight_grads(ring, info, mixed, active, grad, y, dqu, sums):
    blocks = (mixed, active, grad, y, dqu)
    out = grads_shape(ring)
    return pl.pallas_call(
        functools.partial(grads_kernel, ring),
        out_shape=(out, out),
        in_specs=[smem_spec()] + [far_spec()] * len(blocks) + [full_spec(sums.shape)],
        out_specs=(full_spec(out.shape),) * 2,
        scratch_shapes=[pltpu.VMEM(a.shape, LOW) for a in blocks] + [pltpu.SemaphoreType.DMA((3,))],
        compiler_params=kernel_params(20),
        cost_estimate=cost(50 * 10**9, 12 * 1024 * 1024),
        name="weight_grads",
    )(info, *[far(a) for a in blocks], sums)


def fold_kernel(held, came, kept, sent):
    half = (held.shape[0] - SIDES) // 2
    full = 2 * half
    kept[0:half, :] = held[0:half, :].astype(F32) + came[0:half, :].astype(F32)
    sent[0:half, :] = (held[half:full, :].astype(F32) + came[half:full, :].astype(F32)).astype(LOW)
    sides = held[full : full + SIDES, :].astype(LOW).astype(F32) + came[full : full + SIDES, :].astype(F32)
    kept[half : half + SIDES, :] = sides
    sent[half : half + SIDES, :] = sides.astype(LOW)


def fold(held, came):
    half = (held.shape[0] - SIDES) // 2 + SIDES
    outs = (shaped((half, 128), F32), shaped((half, 128), LOW))
    return pl.pallas_call(
        fold_kernel,
        out_shape=outs,
        in_specs=[full_spec(held.shape), full_spec(came.shape)],
        out_specs=tuple(full_spec(a.shape) for a in outs),
        compiler_params=kernel_params(20),
        cost_estimate=cost(0, 1024 * 1024),
        name="fold_gradients",
    )(held, came)


VECTOR_ROWS = (7 * D + FF) // 128


def close_kernel(held, came, before, *outs):
    qus, od, squares = outs[:GROUP], outs[GROUP], outs[GROUP + 1]
    rows = qus[0].shape[0] - SIDES
    full = held.shape[0] - SIDES
    sides = held[full : full + SIDES, :].astype(LOW).astype(F32) + came[full : full + SIDES, :].astype(F32)
    lanes = before[...]
    begin = 0
    for piece in (*qus, od):
        length = rows if piece is not od else od.shape[0]
        here = slice(begin, begin + length)
        begin += length
        total = held[here, :].astype(F32) + came[here, :].astype(F32)
        piece[0:length, :] = total.astype(LOW)
        lanes = lanes + jnp.sum((total * total).reshape(length // 8, 8, 128), axis=0)
    squares[...] = lanes
    high = lanes.astype(LOW).astype(F32)
    rest = sides[VECTOR_ROWS + 16 :]
    sides = jnp.concatenate([sides[:VECTOR_ROWS], high, lanes - high, rest], axis=0).astype(LOW)
    for piece in qus:
        piece[rows : rows + SIDES, :] = sides


def close(ring, held, came, before):
    rows = QU_TILES * (D // ring.count)
    outs = [shaped((rows + SIDES, 128), LOW)] * GROUP
    outs += [shaped((OD_TILES * (SIDE + UNITS) // ring.size, 128), LOW), shaped((8, 128), F32)]
    return pl.pallas_call(
        close_kernel,
        out_shape=tuple(outs),
        in_specs=[full_spec(held.shape), full_spec(came.shape), full_spec(before.shape)],
        out_specs=tuple(full_spec(a.shape) for a in outs),
        compiler_params=kernel_params(16),
        cost_estimate=cost(0, 1024 * 1024),
        name="close_gradients",
    )(held, came, before)


def join_kernel(info, *refs):
    core = info[0]
    firsts, seconds, (od_first, od_second), outs = refs[:4], refs[4:8], refs[8:10], refs[10:]
    sent, vec, squares, vec_squares = outs
    rows = firsts[0].shape[0] - SIDES
    sides = []
    for pieces in (firsts, seconds):
        parts = [a[rows : rows + SIDES, :].astype(F32) for a in pieces]
        sides.append((parts[0] + parts[1]) + (parts[2] + parts[3]))
    squares[...] = sides[0][VECTOR_ROWS : VECTOR_ROWS + 8] + sides[0][VECTOR_ROWS + 8 : VECTOR_ROWS + 16]
    own = [(a[:VECTOR_ROWS] * a[:VECTOR_ROWS]).reshape(VECTOR_ROWS // 8, 8, 128) for a in sides]
    vec_squares[...] = jnp.sum(own[0], axis=0) + jnp.sum(own[1], axis=0)
    vec[...] = jnp.where(core == 0, sides[0], sides[1])

    def write(pieces, od):
        for r in range(GROUP):
            sent[r * rows : (r + 1) * rows, :] = pieces[r][0:rows, :]
        sent[GROUP * rows :, :] = od[...]

    pl.when(core == 0)(functools.partial(write, seconds, od_second))
    pl.when(core == 1)(functools.partial(write, firsts, od_first))


def join(info, firsts, seconds, od_first, od_second):
    rows = firsts[0].shape[0] - SIDES
    outs = (shaped((GROUP * rows + od_first.shape[0], 128), LOW), shaped((SIDES, 128), F32))
    outs += (shaped((8, 128), F32),) * 2
    blocks = (*firsts, *seconds, od_first, od_second)
    return pl.pallas_call(
        join_kernel,
        out_shape=outs,
        in_specs=[smem_spec()] + [full_spec(a.shape) for a in blocks],
        out_specs=tuple(full_spec(a.shape) for a in outs),
        compiler_params=kernel_params(16),
        cost_estimate=cost(0, 1024 * 1024),
        name="join_members",
    )(info, *blocks)


def adam_update(weight, grad, first, second, factor, rate):
    clipped = grad * factor
    first_new = BETA_ONE * first + (1.0 - BETA_ONE) * clipped
    second_new = BETA_TWO * second + (1.0 - BETA_TWO) * clipped * clipped
    first_hat = first_new / (1.0 - BETA_ONE**STEP)
    second_hat = second_new / (1.0 - BETA_TWO**STEP)
    weight_new = weight - rate * (
        first_hat / (jnp.sqrt(second_hat) + ADAM_EPS) + WEIGHT_DECAY * weight
    )
    return (weight_new, first_new, second_new)


def mixed_tile(tile, member):
    at = tile * 128
    if at >= 3 * SIDE:
        return 2, up_column(member, at - 3 * SIDE)
    width = SIDE // SPREAD
    kind, within = at // SIDE, at % SIDE
    return 0, qkv_column(kind, within // width, member) + within % width


def adam_kernel(info, factor_ref, *refs):
    core, group = info[0], info[1]
    step = pl.program_id(0)
    factor = factor_ref[0]
    qus, refs = (refs[:4], refs[4:8]), refs[8:]
    ods, came, refs = refs[:2], refs[2], refs[3:]
    olds, news = refs[:12], refs[12:]
    few, many = olds[0].shape[1], olds[9].shape[1]
    rows = (qus[0][0].shape[0] - SIDES) // QU_TILES
    od_rows = ods[0].shape[0] // OD_TILES

    def update(which, column, grad):
        columns = slice(column, column + 128)
        weight, first, second = [olds[3 * which + i][0, :, columns] for i in range(3)]
        fresh = adam_update(weight, grad.astype(F32), first, second, factor, LEARN_RATE)
        for i in range(3):
            news[3 * which + i][0, :, columns] = fresh[i]

    def rows_of(ref, begin, length):
        return ref[pl.ds(pl.multiple_of(begin + step * length, 16), length), :]

    def both_halves(here):
        for half in range(2):
            for tile in range(OD_TILES):
                column = half * (D // 2) + tile * 128
                ref, begin = (ods[here], 0) if half == here else (came, GROUP * QU_TILES * rows)
                begin = begin + tile * od_rows
                update(3, column, rows_of(ref, begin, many))
                update(1, column, rows_of(ref, begin + od_rows - rows, few))
            for member in range(GROUP):
                if half == here:
                    for g in range(GROUP):

                        @pl.when(group == g)
                        def _(ref=qus[here][member ^ g]):
                            for tile in range(QU_TILES):
                                which, column = mixed_tile(half * QU_TILES + tile, member)
                                update(which, column, rows_of(ref, tile * rows, few))
                else:
                    for tile in range(QU_TILES):
                        which, column = mixed_tile(half * QU_TILES + tile, member)
                        begin = ((group ^ member) * QU_TILES + tile) * rows
                        update(which, column, rows_of(came, begin, few))

    for here in range(2):
        pl.when(core == here)(functools.partial(both_halves, here))


def adam(info, factor, qus, ods, came, olds):
    steps = max(1, olds[0].shape[1] // 16)

    def master(a):
        return pl.BlockSpec((1, a.shape[1] // steps, a.shape[2]), lambda i: (0, i, 0))

    grads = (*qus[0], *qus[1], *ods, came)
    return pl.pallas_call(
        adam_kernel,
        grid=(steps,),
        out_shape=tuple(shaped(a.shape, F32) for a in olds),
        in_specs=[smem_spec(), smem_spec()]
        + [full_spec(a.shape) for a in grads]
        + [master(a) for a in olds],
        out_specs=tuple(master(a) for a in olds),
        compiler_params=kernel_params(28),
        name="adamw",
    )(info, factor, *grads, *[far(a) for a in olds])


def doc_tables(lengths, rows):
    seqs = lengths.shape[0]
    ends = jnp.cumsum(lengths, axis=1)
    places = jnp.arange(rows, dtype=jnp.int32)
    past = places[None, :, None] >= ends[:, None, :]
    begins = jnp.sum(jnp.where(past, lengths[:, None, :], 0), axis=2)
    position = (places[None, :] - begins).reshape(seqs * rows, 1)
    half = ROT // 2
    inverse = 10000.0 ** (-(jnp.arange(half, dtype=F32) * 2.0) / ROT)
    lanes = jnp.concatenate([inverse, inverse, jnp.zeros(HEAD_DIM - ROT, F32)])
    angles = position.astype(F32) * jnp.concatenate([lanes, lanes])[None, :]
    allowed = (places[None, None, :] <= places[None, :, None]) & (places[None, None, :] >= begins[:, :, None])
    mask = jnp.where(allowed, 0.0, -1e30).reshape(seqs * rows, rows).astype(F32)
    return jnp.cos(angles), jnp.sin(angles), mask


def shards(
    x_in,
    cotangent,
    doc_lengths,
    w_qkv,
    w_out,
    w_up,
    w_down,
    vectors,
    m_qkv,
    m_out,
    m_up,
    m_down,
    m_vectors,
    v_qkv,
    v_out,
    v_up,
    v_down,
    v_vectors,
):
    place = Place()
    ring, core, group, spot = place.ring, place.core, place.group, place.spot
    info = place.info()
    local_rows, width = x_in.shape
    seqs, docs = doc_lengths.shape
    rows = local_rows // seqs
    in_rows = w_qkv.shape[1]
    shard = vectors.shape[1]
    members = range(1, GROUP)

    vec_block = jnp.pad(vectors[0].astype(LOW), (0, in_rows * 128 - shard)).reshape(in_rows, 128)
    keep_qu, send_qu, keep_od, send_od = pack(info, w_qkv, w_out, w_up, w_down, vec_block)
    came_qu = place.sibling(send_qu)
    came_od = place.sibling(send_od)

    def member_columns(block, *waited):
        qu = jnp.where(core == block, keep_qu, came_qu)
        sent = [after(take(qu, group ^ r), *waited) for r in members]
        return [take(qu, group)] + [place.member(a, r) for a, r in zip(sent, members)]

    def gather(block, *waited):
        late = after(block, *waited)
        return [block] + [place.member(late, r) for r in members]

    def to_owners(slots):
        return [slots[0]] + [place.member(slots[r], r) for r in members]

    def total_of(slots):
        return sum(a.astype(F32) for a in slots)

    def block_vectors(parts):
        pieces = jnp.concatenate([a[:, :, 0 : -(-shard // 128), PART:] for a in parts])
        pieces = pieces.reshape(ring.size * GROUP, -1)[:, :shard]
        dp = jnp.arange(ring.count, dtype=jnp.int32)
        difference = ring.spot_of(dp) ^ spot
        slot = jnp.where(core == 0, ring.slot(difference, 0), ring.slot(difference, 1))
        vec = jnp.take(pieces, slot * GROUP + (ring.group_of(dp) ^ group), axis=0, mode="clip")
        vec = vec.reshape(-1).astype(F32)
        b_qkv, b_out, b_up, b_down, gain, ln_bias = jnp.split(
            vec, [3 * D, 4 * D, 4 * D + FF, 5 * D + FF, 6 * D + FF]
        )
        b_qkv = take(b_qkv.reshape(3 * SPREAD, GROUP, -1), group, 1).reshape(1, -1)
        b_up = take(b_up.reshape(SPREAD, GROUP, -1), group, 1).reshape(1, -1)
        return (b_qkv, b_up, gain[None], ln_bias[None]), (b_out + b_down)[None], gain[None]

    x_own = take(x_in.reshape(2, rows, width), core)
    cot_own = take(cotangent.reshape(2, rows, width), core)
    len_own = take(doc_lengths, core)
    len_rows = jnp.zeros((16, width), LOW).at[0, :docs].set(len_own.astype(LOW))
    x_sent = jnp.concatenate([x_own, len_rows])

    qu_came = member_columns(0)
    qu_own = jnp.stack(qu_came)[None]
    x_group = gather(x_sent, qu_came[1])
    od_own = jnp.where(core == 0, keep_od, came_od)[None]
    od = [jnp.concatenate([od_own, place.across(od_own, 0)])]
    qu_own = after(qu_own, od[0])
    qu = [jnp.concatenate([qu_own, place.across(qu_own, 0)])]
    qu_sibling = [place.sibling(qu[0])]
    od_sibling = [place.sibling(od[0])]
    for step in range(1, ring.bits):
        od.append(place.across(jnp.concatenate(od), step))
        qu.append(place.across(after(jnp.concatenate(qu), x_group[1], od[-1]), step))
    qu_sibling += [place.sibling(a) for a in qu[1:]]
    od_sibling += [place.sibling(a) for a in od[1:]]
    qu_mine = jnp.where(core == 1, keep_qu, came_qu)
    waited = (*x_group[1:], qu_sibling[0], od_sibling[0])
    sent = [after(jnp.concatenate([take(qu_mine, group ^ r), cot_own]), *waited) for r in members]
    qu_cot = [place.member(a, r) for a, r in zip(sent, members)]
    parts_first = (*qu, *od, *qu_sibling, *od_sibling)
    lengths = jnp.stack([a[rows, :docs] for a in x_group]).astype(jnp.int32)
    tables = doc_tables(lengths, rows)
    vecs_first, bias_first, gain_first = block_vectors(qu)

    first = forward(ring, info, parts_first, x_group, tables, vecs_first, rows)
    kept_first, tables = first[GROUP:], first[-3:]
    qu_cot = [after(a, first[0]) for a in qu_cot]
    came = to_owners(first[:GROUP])
    od_own = after(jnp.where(core == 1, keep_od, came_od)[None], first[0])
    od_late = [jnp.concatenate([od_own, place.across(od_own, 0)])]
    came[1] = after(came[1], od_late[0])
    hidden_first = (x_own.astype(F32) + total_of(came) + bias_first).astype(LOW)
    hidden_group = gather(hidden_first)
    qu_own = jnp.stack([take(qu_mine, group)] + [a[:in_rows] for a in qu_cot])[None]
    qu_late = [jnp.concatenate([qu_own, after(place.across(qu_own, 0), hidden_first)])]
    for step in range(1, ring.bits):
        od_late.append(after(place.across(jnp.concatenate(od_late), step), *hidden_group[1:]))
        qu_late.append(after(place.across(jnp.concatenate(qu_late), step), *hidden_group[1:]))
    qu_sibling, od_sibling = [
        [place.sibling(after(a, *hidden_group[1:])) for a in late] for late in (qu_late, od_late)
    ]
    parts_second = (*qu_late, *od_late, *qu_sibling, *od_sibling)
    vecs_second, bias_second, gain_second = block_vectors(qu_late)
    second = middle(ring, info, parts_second, hidden_group, [cot_own, *qu_cot], tables, vecs_second, rows)
    sums_second, y_second, mixed_second, active_second, dqu_second, grad_second = second[GROUP : GROUP + 6]
    z_keep, z_send = second[GROUP + 6 :]

    def rows_backward(rows_low, grad_low, dy, gain):
        rows_now = rows_low.astype(F32)
        centered = rows_now - jnp.mean(rows_now, axis=-1, keepdims=True)
        variance = jnp.mean(centered * centered, axis=-1, keepdims=True)
        inverse_std = lax.rsqrt(variance + NORM_EPS)
        normed = centered * inverse_std
        scaled = dy * gain
        inner_mean = jnp.mean(scaled, axis=-1, keepdims=True)
        inner_cross = jnp.mean(scaled * normed, axis=-1, keepdims=True)
        return (grad_low.astype(F32) + inverse_std * (scaled - inner_mean - normed * inner_cross)).astype(LOW)

    def to_members(pieces):
        return [pieces[0]] + [place.member(pieces[r], r) for r in members]

    steps = list(reversed(range(ring.bits)))

    def ring_fold(held, *waited):
        kept, sent = held
        for step in steps[:-1]:
            kept, sent = fold(kept, after(place.across(sent, step), *waited))
        return kept, sent

    dy_second = to_owners(second[:GROUP])
    grads = weight_grads(ring, info, mixed_second, active_second, grad_second, y_second, dqu_second, sums_second)
    mid_grad = rows_backward(hidden_first, cot_own, total_of(dy_second), gain_second)
    mid_group = gather(mid_grad)
    sent = place.sibling(after(grads[1], *dy_second[1:]))
    second_held = ring_fold(fold(grads[0], after(sent, mid_grad)))

    mid_late = [after(mid_group[0], *second_held)] + mid_group[1:]
    z_came = place.toward(after(z_send, *mid_group[1:]), 1)
    dy_keep, dy_send, keep, send = backward(ring, info, mid_late, kept_first, rows)
    z_came = after(z_came, send)
    kept, sent = second_held
    none = jnp.zeros((8, 128), F32)
    *qu_second, od_second, squares_second = close(ring, kept, after(place.across(sent, 0), send), none)
    send = after(send, *qu_second, z_came)
    qu_slots_second = to_members(qu_second)
    kept, sent = ring_fold(fold(keep, place.sibling(send)))
    dy_came = place.toward(after(dy_send, *qu_slots_second[1:]), 1)
    z_step = place.toward((z_keep[1].astype(F32) + z_came[1].astype(F32)).astype(LOW), 0)
    came = after(place.across(after(sent, *qu_slots_second[1:], z_step), 0), dy_came)
    *qu_first, od_first, _ = close(ring, kept, came, squares_second)
    qu_slots_first = to_members(qu_first)
    dy_step = (dy_keep[1].astype(F32) + dy_came[1].astype(F32)).astype(LOW)
    dy_step = place.toward(after(dy_step, *qu_slots_first[1:]), 0)
    grads_sent, vec, squares, vec_squares = join(info, qu_slots_first, qu_slots_second, od_first, od_second)
    squares = squares + place.sibling(squares)
    for step in range(ring.bits):
        if step == 1:
            dy_step = after(dy_step, squares)
        squares = squares + place.across(squares, step)
    squares = jnp.sum(squares + vec_squares)
    dy_total = dy_keep[0].astype(F32) + dy_came[0].astype(F32) + dy_step.astype(F32)
    z_total = z_keep[0].astype(F32) + z_came[0].astype(F32) + z_step.astype(F32)
    start_grad = rows_backward(x_own, mid_grad, dy_total, gain_first)
    hidden_second = (hidden_first.astype(F32) + z_total + bias_second).astype(LOW)

    grad_norm = jnp.sqrt(squares)
    factor = jnp.minimum(1.0, CLIP_LEVEL / (grad_norm + 1e-06))

    def own_block(one, two):
        came = place.sibling(jnp.where(core == 0, two, one))
        mine = jnp.where(core == 0, one, two)
        return [jnp.where(core == h, mine, came) for h in range(2)]

    grads_came = place.sibling(grads_sent)
    vec_share = after(vec, grads_sent).reshape(-1)[: ring.count * shard].reshape(ring.count, shard)
    vec_share = take(vec_share, lax.axis_index("dp"))[None]
    olds = (w_qkv, m_qkv, v_qkv, w_out, m_out, v_out, w_up, m_up, v_up, w_down, m_down, v_down)
    qus = (qu_slots_first, qu_slots_second)
    news = adam(info, factor[None], qus, (od_first, od_second), grads_came, olds)
    new_vec = adam_update(vectors, vec_share, m_vectors, v_vectors, factor, VECTOR_RATE)

    outputs = own_block(jnp.stack([hidden_first, start_grad]), jnp.stack([hidden_second, mid_grad]))
    outputs = jnp.concatenate(outputs, axis=1)
    hidden_out, input_grads = outputs[:1], outputs[1:]
    return (
        hidden_out,
        input_grads,
        *(news[3 * i] for i in range(4)),
        new_vec[0],
        *(news[3 * i + 1] for i in range(4)),
        new_vec[1],
        *(news[3 * i + 2] for i in range(4)),
        new_vec[2],
        grad_norm,
    )


def solution(mesh):
    return jax.shard_map(
        shards,
        mesh=mesh,
        in_specs=(
            P("dp", None),
            P("dp", None),
            P("dp", None),
            P("section", "dp", None),
            P("section", "dp", None),
            P("section", "dp", None),
            P("section", "dp", None),
            P("section", "dp"),
            P("section", "dp", None),
            P("section", "dp", None),
            P("section", "dp", None),
            P("section", "dp", None),
            P("section", "dp"),
            P("section", "dp", None),
            P("section", "dp", None),
            P("section", "dp", None),
            P("section", "dp", None),
            P("section", "dp"),
        ),
        out_specs=(
            P("section", "dp", None),
            P("section", "dp", None),
            P("section", "dp", None),
            P("section", "dp", None),
            P("section", "dp", None),
            P("section", "dp", None),
            P("section", "dp"),
            P("section", "dp", None),
            P("section", "dp", None),
            P("section", "dp", None),
            P("section", "dp", None),
            P("section", "dp"),
            P("section", "dp", None),
            P("section", "dp", None),
            P("section", "dp", None),
            P("section", "dp", None),
            P("section", "dp"),
            P(),
        ),
        check_vma=False,
    )
```

```python
import functools

import jax
import jax.numpy as jnp
from jax import lax
from jax.experimental import pallas as pl
from jax.experimental.pallas import tpu as pltpu
from jax.sharding import PartitionSpec as P

D = 1024
FF = 4096
HEADS = 16
HEAD_DIM = 64
ROT = 16
STEP = 10


NORM_EPS = 1e-05
BETA_ONE = 0.9
BETA_TWO = 0.95
LEARN_RATE = 0.05
VECTOR_RATE = 0.3
WEIGHT_DECAY = 0.01
CLIP_LEVEL = 1.0
ADAM_EPS = 1e-08

AXES = ("section", "dp")
GROUP = 4
SPREAD = 1
LOW = jnp.bfloat16
F32 = jnp.float32
SIDE = D // GROUP
UNITS = FF // GROUP
MIXED = 3 * SIDE + UNITS
PART = MIXED // 2
WIRE = PART + 128


class Ring:
    def __init__(self, count):
        self.count = count
        self.low = count // (GROUP * SPREAD)
        self.size = SPREAD * self.low
        self.bits = self.size.bit_length() - 1

    def index(self, g, t):
        return ((t // self.low) * GROUP + g) * self.low + t % self.low

    def group_of(self, dp):
        return (dp // self.low) % GROUP

    def spot_of(self, dp):
        return (dp // (GROUP * self.low)) * self.low + dp % self.low

    def order(self, core):
        steps = list(range(self.bits))
        if SPREAD > 1 or core == 1:
            steps.reverse()
        return steps

    def turn(self, slot, core):
        return sum(((slot >> s) & 1) << b for s, b in enumerate(self.order(core)))

    def slot(self, difference, core):
        return sum(((difference >> b) & 1) << s for s, b in enumerate(self.order(core)))


class Place:
    def __init__(self):
        self.ring = Ring(lax.axis_size("dp"))
        self.core = lax.axis_index("section")
        dp = lax.axis_index("dp")
        self.group = self.ring.group_of(dp)
        self.spot = self.ring.spot_of(dp)

    def info(self):
        return jnp.stack([self.core, self.group, self.spot]).astype(jnp.int32)

    def move(self, block, where):
        ring = self.ring
        route = []
        for core in range(2):
            for g in range(GROUP):
                for t in range(ring.size):
                    c, h, u = where(core, g, t)
                    route.append((core * ring.count + ring.index(g, t), c * ring.count + ring.index(h, u)))
        return lax.ppermute(block, AXES, route)

    def sibling(self, block):
        return self.move(block, lambda c, g, t: (1 - c, g, t))

    def member(self, block, distance):
        return self.move(block, lambda c, g, t: (c, g ^ distance, t))

    def toward(self, block, step):
        return self.move(block, lambda c, g, t: (c, g ^ (2, 1)[(step + c) % 2], t))

    def across(self, block, step):
        return self.move(block, lambda c, g, t: (c, g, t ^ (1 << self.ring.order(c)[step])))


def take(block, index, axis=0):
    return lax.dynamic_index_in_dim(block, index, axis, keepdims=False)


def after(block, *waited):
    return lax.optimization_barrier((block, waited))[0]


def dot(left, right):
    return jnp.dot(left, right, preferred_element_type=F32)


def dot_cols(left, right):
    return lax.dot_general(left, right, (((1,), (1,)), ((), ())), preferred_element_type=F32)


def dot_rows(left, right):
    return lax.dot_general(left, right, (((0,), (0,)), ((), ())), preferred_element_type=F32)


def full_spec(shape):
    return pl.BlockSpec(shape, lambda *_: (0,) * len(shape))


def far_spec():
    return pl.BlockSpec(memory_space=pltpu.HBM)


def far(block):
    return pltpu.with_memory_space_constraint(block, pltpu.HBM)


def any_spec():
    return pl.BlockSpec(memory_space=pl.ANY)


def smem_spec():
    return pl.BlockSpec(memory_space=pltpu.SMEM)


def shaped(shape, dtype):
    return jax.ShapeDtypeStruct(shape, dtype)


def kernel_params(mebibytes):
    return pltpu.CompilerParams(vmem_limit_bytes=mebibytes * 1024 * 1024)


def up_pieces():
    run = UNITS // SPREAD
    cuts = sorted({0, PART - 3 * SIDE, UNITS} | {run * i for i in range(SPREAD)})
    pieces = []
    for begin, end in zip(cuts[:-1], cuts[1:]):
        column = 3 * SIDE + begin
        pieces.append((begin, column // PART, column % PART, end - begin))
    return pieces


def up_column(g, local):
    run = UNITS // SPREAD
    return (local // run * GROUP + g) * run + local % run


def qkv_column(kind, run, g):
    width = SIDE // SPREAD
    return ((kind * SPREAD + run) * GROUP + g) * width


def pack_kernel(info, qkv_hbm, out_hbm, up_hbm, down_hbm, vec, keep_qu, send_qu, keep_od, send_od, *scratch):
    w_qkv, w_out, w_up, w_down, sems = scratch
    pairs = ((qkv_hbm, w_qkv), (up_hbm, w_up), (down_hbm, w_down), (out_hbm, w_out))
    copies = [pltpu.make_async_copy(far.at[0], near, sems.at[i]) for i, (far, near) in enumerate(pairs)]
    for copy in copies:
        copy.start()
    rows = w_qkv.shape[0]
    ff_rows = w_down.shape[0]
    width = SIDE // SPREAD
    core = info[0]

    def write_qu(halves):
        for g in range(GROUP):
            for kind in range(3):
                for run in range(SPREAD):
                    at = (kind * SPREAD + run) * width
                    column = qkv_column(kind, run, g)
                    halves[0][g, :, at : at + width] = w_qkv[:, column : column + width].astype(LOW)
            for local, half, at, length in up_pieces():
                column = up_column(g, local)
                halves[half][g, :, at : at + length] = w_up[:, column : column + length].astype(LOW)
            for half in range(2):
                halves[half][g, :, PART:WIRE] = vec[...]

    def write_od(halves):
        for half in range(2):
            columns = slice(half * (D // 2), (half + 1) * (D // 2))
            halves[half][0:ff_rows] = w_down[:, columns].astype(LOW)
            halves[half][ff_rows : ff_rows + rows] = w_out[:, columns].astype(LOW)

    for first, last, write, kept, sent in ((0, 2, write_qu, keep_qu, send_qu), (2, 4, write_od, keep_od, send_od)):
        for copy in copies[first:last]:
            copy.wait()
        pl.when(core == 0)(functools.partial(write, (kept, sent)))
        pl.when(core == 1)(functools.partial(write, (sent, kept)))


def pack(info, w_qkv, w_out, w_up, w_down, vec):
    rows, ff_rows = w_qkv.shape[1], w_down.shape[1]
    qu = shaped((GROUP, rows, WIRE), LOW)
    od = shaped((ff_rows + rows, D // 2), LOW)
    return pl.pallas_call(
        pack_kernel,
        out_shape=(qu, qu, od, od),
        in_specs=[smem_spec()] + [far_spec()] * 4 + [full_spec(vec.shape)],
        out_specs=tuple(full_spec(a.shape) for a in (qu, qu, od, od)),
        scratch_shapes=[pltpu.VMEM(a.shape[1:], F32) for a in (w_qkv, w_out, w_up, w_down)]
        + [pltpu.SemaphoreType.DMA((4,))],
        compiler_params=kernel_params(20),
        name="pack_weights",
    )(info, far(w_qkv), far(w_out), far(w_up), far(w_down), vec)


def stack_kernel(*refs):
    for i, ref in enumerate(refs[:-1]):
        refs[-1][0, i] = ref[...]


def stack_members(pieces):
    out = shaped((1, len(pieces), *pieces[0].shape), LOW)
    return pl.pallas_call(
        stack_kernel,
        out_shape=out,
        in_specs=[full_spec(a.shape) for a in pieces],
        out_specs=full_spec(out.shape),
        compiler_params=kernel_params(16),
        cost_estimate=cost(50 * 10**9, 1024 * 1024),
        name="stack_members",
    )(*pieces)


def weight_copies(ring, info, parts, wqu, wout, wdown, sems):
    core, group, spot = info[0], info[1], info[2]
    qu_copies, od_copies = [], []
    count = len(parts) // 4
    for which in range(2):
        half = core if which == 0 else 1 - core
        qu_at = pl.multiple_of(half * PART, 128)
        od_at = pl.multiple_of(half * (D // 2), 128)
        slot = 0
        for piece in range(count):
            qu, od = parts[2 * count * which + piece], parts[2 * count * which + count + piece]
            rows = qu.shape[2]
            ff_rows = od.shape[1] - rows
            for i in range(qu.shape[0]):
                straight, turned = ring.turn(slot, 0), ring.turn(slot, 1)
                there = spot ^ (straight + half * (turned - straight))
                slot += 1
                ff_row = pl.multiple_of(there * ff_rows, ff_rows)
                out_row = pl.multiple_of(there * rows, rows)
                far = wdown.at[pl.ds(ff_row, ff_rows), pl.ds(od_at, D // 2)]
                od_copies.append(pltpu.make_async_copy(od.at[i, pl.ds(0, ff_rows)], far, sems.at[0]))
                far = wout.at[pl.ds(out_row, rows), pl.ds(od_at, D // 2)]
                od_copies.append(pltpu.make_async_copy(od.at[i, pl.ds(ff_rows, rows)], far, sems.at[0]))
                for r in range(GROUP):
                    row = pl.multiple_of(ring.index(group ^ r, there) * rows, rows)
                    far = wqu.at[pl.ds(row, rows), pl.ds(qu_at, PART)]
                    qu_copies.append(pltpu.make_async_copy(qu.at[i, r, :, pl.ds(0, PART)], far, sems.at[1]))
    return qu_copies, od_copies


def head_masks(dtype):
    lane = lax.broadcasted_iota(jnp.int32, (1, SIDE), 1) // HEAD_DIM
    return [(lane == h).astype(dtype) for h in range(SIDE // HEAD_DIM)]


def by_head(parts):
    lane = lax.broadcasted_iota(jnp.int32, (1, SIDE), 1) // HEAD_DIM
    total = parts[-1]
    for h in range(len(parts) - 2, -1, -1):
        total = jnp.where(lane == h, parts[h], total)
    return total


def turning(cosine, sine, back):
    lane = lax.broadcasted_iota(jnp.int32, sine.shape, 1) % HEAD_DIM
    first = jnp.where(lane < ROT // 2, sine, 0.0)
    second = jnp.where(lane < ROT // 2, 0.0, sine)
    if back:
        second = -second
    else:
        first = -first
    wide = SIDE // cosine.shape[1]
    return [jnp.concatenate([a] * wide, axis=1) for a in (cosine, first, second)]


def turn(part, tables):
    cosine, first, second = tables
    ahead = pltpu.roll(part, SIDE - ROT // 2, 1)
    behind = pltpu.roll(part, ROT // 2, 1)
    return part * cosine + ahead * first + behind * second


def normalise(rows):
    centered = rows - jnp.mean(rows, axis=-1, keepdims=True)
    variance = jnp.mean(centered * centered, axis=-1, keepdims=True)
    return centered * lax.rsqrt(variance + NORM_EPS)


def no_wait():
    pass


def forward_part(x_refs, tables, vecs, wqu, wout, wdown, kept, z_refs, waits, done, normed_ref=None):
    cosine, sine, mask = tables
    b_qkv, b_up, gain, ln_bias = vecs
    y, qkv, probs, mixed, active, slope = kept
    rows = z_refs[0].shape[0]
    for r in range(GROUP):
        normed = normalise(x_refs[r][0:rows, :].astype(F32))
        if normed_ref is not None:
            normed_ref[r * rows : (r + 1) * rows, :] = normed
        y[r * rows : (r + 1) * rows, :] = (normed * gain[...] + ln_bias[...]).astype(LOW)
    done(0)
    waits[0]()
    waits[2]()
    forth = turning(cosine[...], sine[...], False)
    for kind in range(3):
        columns = slice(kind * SIDE, (kind + 1) * SIDE)
        part = dot(y[...], wqu[:, columns]) + b_qkv[:, columns]
        if kind < 2:
            part = turn(part, forth)
        qkv[:, columns] = part.astype(LOW)
    done(1)
    masks = head_masks(LOW)
    heads = len(masks)
    for r in range(GROUP):
        here = slice(r * rows, (r + 1) * rows)
        query, keys, values = [qkv[here, k * SIDE : (k + 1) * SIDE] for k in range(3)]
        stacked = jnp.concatenate([query * m for m in masks], axis=0)
        scores = dot_cols(stacked, keys) * HEAD_DIM ** (-0.5)
        scores = scores.reshape(heads, rows, rows) + mask[here, :][None]
        expo = jnp.exp(scores - jnp.max(scores, axis=-1, keepdims=True))
        prob = expo / jnp.sum(expo, axis=-1, keepdims=True)
        prob = prob.reshape(heads * rows, rows)
        probs[r * heads * rows : (r + 1) * heads * rows, :] = prob
        full = dot(prob.astype(LOW), values)
        mixed[here, :] = by_head([full[h * rows : (h + 1) * rows] for h in range(heads)]).astype(LOW)
    done(2)
    done(3)
    tile = 256
    for at in range(0, UNITS, tile):
        hidden = dot(y[...], wqu[:, 3 * SIDE + at : 3 * SIDE + at + tile]) + b_up[:, at : at + tile]
        share = 0.5 * (1.0 + lax.erf(hidden * (0.5**0.5)))
        density = jnp.exp(-0.5 * hidden * hidden) * (0.5 / jnp.pi) ** 0.5
        active[:, at : at + tile] = (hidden * share).astype(LOW)
        slope[:, at : at + tile] = share + hidden * density
    done(4)
    done(5)
    waits[1]()
    for at in range(0, D, tile):
        branch = dot(mixed[...], wout[:, at : at + tile]) + dot(active[...], wdown[:, at : at + tile])
        for r in range(GROUP):
            z_refs[r][:, at : at + tile] = branch[r * rows : (r + 1) * rows].astype(LOW)


def backward_part(grad, normed, tables, wqu, wout, wdown, kept, dqu, dy_refs, sums, waits, done):
    cosine, sine, _ = tables
    y, qkv, probs, mixed, active, slope = kept
    rows = grad.shape[0] // GROUP
    tile = 256
    waits[0]()
    dmixed = dot_cols(grad[...], wout[...]).astype(LOW)
    for at in range(0, UNITS, tile):
        dactive = dot_cols(grad[...], wdown[at : at + tile, :])
        dhidden = (dactive * slope[:, at : at + tile]).astype(LOW)
        dqu[:, 3 * SIDE + at : 3 * SIDE + at + tile] = dhidden
    waits[1]()
    masks = head_masks(LOW)
    heads = len(masks)
    back = turning(cosine[...], sine[...], True)
    for r in range(GROUP):
        here = slice(r * rows, (r + 1) * rows)
        query, keys, values = [qkv[here, k * SIDE : (k + 1) * SIDE] for k in range(3)]
        dstack = jnp.concatenate([dmixed[here] * m for m in masks], axis=0)
        dprob = dot_cols(dstack, values)
        prob = probs[r * heads * rows : (r + 1) * heads * rows, :]
        dvalues = dot_rows(prob.astype(LOW), dstack)
        dscore = (prob * (dprob - jnp.sum(prob * dprob, axis=-1, keepdims=True))).astype(LOW)
        full = dot(dscore, keys)
        dquery = by_head([full[h * rows : (h + 1) * rows] for h in range(heads)])
        dkeys = dot_rows(dscore, jnp.concatenate([query * m for m in masks], axis=0))
        scale = HEAD_DIM ** (-0.5)
        slot_tables = [a[here] for a in back]
        dqu[here, 0:SIDE] = turn(dquery * scale, slot_tables).astype(LOW)
        dqu[here, SIDE : 2 * SIDE] = turn(dkeys * scale, slot_tables).astype(LOW)
        dqu[here, 2 * SIDE : 3 * SIDE] = dvalues.astype(LOW)
    done()
    for at in range(0, MIXED, tile):
        sums[:, at : at + tile] = jnp.sum(dqu[:, at : at + tile].astype(F32), axis=0, keepdims=True)
    waits[2]()
    for at in range(0, D, tile):
        dy = dot_cols(dqu[...], wqu[at : at + tile, :])
        for r in range(GROUP):
            dy_refs[r][:, at : at + tile] = dy[r * rows : (r + 1) * rows].astype(LOW)
        own = grad[0:rows, at : at + tile].astype(F32)
        for i, terms in enumerate((own, dy * normed[:, at : at + tile], dy)):
            begin = MIXED + i * D + at
            sums[:, begin : begin + tile] = jnp.sum(terms, axis=0, keepdims=True)


def kept_shapes(tokens, rows):
    return [
        ((tokens, D), LOW),
        ((tokens, 3 * SIDE), LOW),
        ((tokens * (SIDE // HEAD_DIM), rows), F32),
        ((tokens, SIDE), LOW),
        ((tokens, UNITS), LOW),
        ((tokens, UNITS), F32),
    ]


def weight_scratch():
    return [
        pltpu.VMEM((D, MIXED), LOW),
        pltpu.VMEM((SIDE, D), LOW),
        pltpu.VMEM((UNITS, D), LOW),
        pltpu.SemaphoreType.DMA((2,)),
    ]


def waiter(copies):
    def wait():
        for copy in copies:
            copy.wait()

    return wait


def started(pairs, sem):
    copies = [pltpu.make_async_copy(source, target, sem) for source, target in pairs]
    for copy in copies:
        copy.start()
    return waiter(copies)


def table_scratch(tokens, rows):
    return [pltpu.VMEM((tokens, 128), F32), pltpu.VMEM((tokens, 128), F32), pltpu.VMEM((tokens, rows), F32)]


def cost(flops, moved):
    return pl.CostEstimate(flops=2 * flops, bytes_accessed=2 * moved, transcendentals=0)


def leaving(pairs, sems):
    copies = [pltpu.make_async_copy(near, far, sems.at[i]) for i, (near, far) in enumerate(pairs)]

    def go(i):
        copies[i].start()

    return go, waiter(copies)


def pair_copies(info, slots, keep, send, sems):
    targets = (keep.at[0], keep.at[1], send.at[0], send.at[1])
    return [
        [pltpu.make_async_copy(slots[r], target, sems.at[i]) for i, (r, target) in enumerate(zip(order, targets))]
        for order in ((0, 2, 1, 3), (0, 1, 2, 3))
    ]


def on_core(info, copies, act):
    for here in range(2):

        @pl.when(info[0] == here)
        def _(mine=copies[here]):
            for copy in mine:
                act(copy)


def forward_kernel(ring, count, info, *refs):
    parts, refs = refs[:count], refs[count:]
    x_refs, refs = refs[:4], refs[4:]
    tables, refs = refs[:3], refs[3:]
    vecs, refs = refs[:4], refs[4:]
    z_refs, refs = refs[:4], refs[4:]
    far_kept, far_weights, far_tables, refs = refs[:7], refs[7:10], refs[10:13], refs[13:]
    kept, refs = refs[:7], refs[7:]
    out_sems, scratch = refs[0], refs[1:]
    weights = scratch[:3]
    qu_copies, od_copies = weight_copies(ring, info, parts, *scratch)
    for copy in qu_copies + od_copies:
        copy.start()
    pairs = [*zip(kept, far_kept), *zip(weights, far_weights), *zip(tables, far_tables)]
    go, out = leaving(pairs, out_sems)
    for i in range(10, 13):
        go(i)

    def qu_in():
        waiter(qu_copies)()
        go(7)

    def od_in():
        waiter(od_copies)()
        go(8)
        go(9)

    def done(i):
        go(i)
        if i == 0:
            go(6)

    forward_part(x_refs, tables, vecs, *weights, kept[:6], z_refs, (qu_in, od_in, no_wait), done, kept[6])
    out()


def forward(ring, info, parts, xs, tables, vecs, rows):
    tokens = GROUP * rows
    shapes = kept_shapes(tokens, rows) + [((tokens, D), F32)]
    away = [*shapes, ((D, MIXED), LOW), ((SIDE, D), LOW), ((UNITS, D), LOW)] + [(a.shape, F32) for a in tables]
    blocks = (*xs, *tables, *vecs)
    return pl.pallas_call(
        functools.partial(forward_kernel, ring, len(parts)),
        out_shape=(*[shaped((rows, D), LOW)] * GROUP, *[pltpu.HBM(*a) for a in away]),
        in_specs=[smem_spec()] + [any_spec()] * len(parts) + [full_spec(a.shape) for a in blocks],
        out_specs=tuple([full_spec((rows, D))] * GROUP + [far_spec()] * len(away)),
        scratch_shapes=[pltpu.VMEM(*a) for a in shapes]
        + [pltpu.SemaphoreType.DMA((len(away),))]
        + weight_scratch(),
        compiler_params=kernel_params(22),
        cost_estimate=cost(2 * tokens * D * (D + 2 * FF // GROUP), 16 * 1024 * 1024),
        name="forward_shard",
    )(info, *parts, *blocks)


def middle_kernel(ring, count, info, *refs):
    parts, refs = refs[:count], refs[count:]
    x_refs, refs = refs[:4], refs[4:]
    g_refs, refs = refs[:4], refs[4:]
    far_tables, refs = refs[:3], refs[3:]
    vecs, refs = refs[:4], refs[4:]
    dy_refs, refs = refs[:4], refs[4:]
    sums, away, (z_keep, z_send), refs = refs[0], refs[1:6], refs[6:8], refs[8:]
    kept, refs = refs[:6], refs[6:]
    z_refs, tables, refs = refs[:4], refs[4:7], refs[7:]
    (grad, normed, dqu, in_sems, out_sems, z_sems), scratch = refs[:6], refs[6:]
    rows = z_refs[0].shape[0]
    qu_copies, od_copies = weight_copies(ring, info, parts, *scratch)
    for copy in qu_copies:
        copy.start()
    tables_in = started(zip(far_tables, tables), in_sems.at[0])
    for copy in od_copies:
        copy.start()
    pairs = []
    for r, ref in enumerate(g_refs):
        at = ref.shape[0] - rows
        pairs.append((ref.at[pl.ds(at, rows)], grad.at[pl.ds(r * rows, rows)]))
    grad_in = started(pairs, in_sems.at[1])
    go, out = leaving(list(zip([kept[0], kept[3], kept[4], dqu, grad], away)), out_sems)

    def done(i):
        if i in (0, 3, 4):
            go((0, 3, 4).index(i))

    waits = (waiter(qu_copies), waiter(od_copies), tables_in)
    forward_part(x_refs, tables, vecs, *scratch[:3], kept, z_refs, waits, done, normed)
    grad_in()
    go(4)
    z_copies = pair_copies(info, z_refs, z_keep, z_send, z_sems)
    on_core(info, z_copies, lambda copy: copy.start())
    waits = (no_wait, no_wait, no_wait)
    done = functools.partial(go, 3)
    backward_part(grad, normed, tables, *scratch[:3], kept, dqu, dy_refs, sums, waits, done)
    out()
    on_core(info, z_copies, lambda copy: copy.wait())


def middle(ring, info, parts, xs, gs, tables, vecs, rows):
    tokens = GROUP * rows
    shapes = kept_shapes(tokens, rows)
    away = [shapes[0], shapes[3], shapes[4], ((tokens, MIXED), LOW), ((tokens, D), LOW)]
    away += [((2, rows, D), LOW)] * 2
    sums = shaped((1, MIXED + 3 * D), F32)
    return pl.pallas_call(
        functools.partial(middle_kernel, ring, len(parts)),
        out_shape=(*[shaped((rows, D), LOW)] * GROUP, sums, *[pltpu.HBM(*a) for a in away]),
        in_specs=[smem_spec()]
        + [any_spec()] * len(parts)
        + [full_spec(a.shape) for a in xs]
        + [far_spec()] * (GROUP + 3)
        + [full_spec(a.shape) for a in vecs],
        out_specs=tuple([full_spec((rows, D))] * GROUP + [full_spec(sums.shape)] + [far_spec()] * len(away)),
        scratch_shapes=[pltpu.VMEM(*a) for a in shapes]
        + [pltpu.VMEM((rows, D), LOW)] * GROUP
        + table_scratch(tokens, rows)
        + [pltpu.VMEM((tokens, D), LOW), pltpu.VMEM((tokens, D), F32), pltpu.VMEM((tokens, MIXED), LOW)]
        + [pltpu.SemaphoreType.DMA((2,)), pltpu.SemaphoreType.DMA((5,)), pltpu.SemaphoreType.DMA((4,))]
        + weight_scratch(),
        compiler_params=kernel_params(27),
        cost_estimate=cost(4 * tokens * D * (D + 2 * FF // GROUP), 16 * 1024 * 1024),
        name="forward_backward_shard",
    )(info, *parts, *xs, *[far(a) for a in (*gs, *tables)], *vecs)


def backward_kernel(ring, info, *refs):
    g_refs, refs = refs[:4], refs[4:]
    far_kept, far_weights, far_tables, refs = refs[:7], refs[7:10], refs[10:13], refs[13:]
    (dy_keep, dy_send, keep, send), refs = refs[:4], refs[4:]
    kept, refs = refs[:7], refs[7:]
    weights, tables, refs = refs[:3], refs[3:6], refs[6:]
    (grad, dqu, sums, in_sems, out_sems), dy_refs = refs[:5], refs[5:]
    y, qkv, probs, mixed, active, slope, normed = kept
    wqu, wout, wdown = weights
    far_y, far_qkv, far_probs, far_mixed, far_active, far_slope, far_normed = far_kept
    mixed_in = started([(far_mixed, mixed)], in_sems.at[0])
    active_in = started([(far_active, active)], in_sems.at[1])
    units_in = started([*zip(far_weights[1:], weights[1:]), (far_slope, slope)], in_sems.at[2])
    heads_in = started([(far_qkv, qkv), (far_probs, probs), *zip(far_tables, tables)], in_sems.at[3])
    dy_in = started([(far_weights[0], wqu), (far_normed, normed)], in_sems.at[4])
    y_in = started([(far_y, y)], in_sems.at[5])
    rows = g_refs[0].shape[0]
    for r in range(GROUP):
        grad[r * rows : (r + 1) * rows, :] = g_refs[r][...]
    mixed_in()
    od_part(ring, info, mixed, active, grad, keep, send, active_in)
    waits = (units_in, heads_in, dy_in)
    backward_part(grad, normed, tables, *weights, kept[:6], dqu, dy_refs, sums, waits, no_wait)
    copies = pair_copies(info, dy_refs, dy_keep, dy_send, out_sems)
    on_core(info, copies, lambda copy: copy.start())
    y_in()
    qu_part(ring, info, y, dqu, sums, keep, send)
    on_core(info, copies, lambda copy: copy.wait())


def backward(ring, info, gs, held, rows):
    tokens = GROUP * rows
    outs = [shaped((2, rows, D), LOW)] * 2 + [grads_shape(ring)] * 2
    return pl.pallas_call(
        functools.partial(backward_kernel, ring),
        out_shape=tuple(outs),
        in_specs=[smem_spec()] + [full_spec(a.shape) for a in gs] + [far_spec()] * len(held),
        out_specs=tuple(full_spec(a.shape) for a in outs),
        scratch_shapes=[pltpu.VMEM(a.shape, a.dtype) for a in held]
        + [pltpu.VMEM((tokens, D), LOW), pltpu.VMEM((tokens, MIXED), LOW)]
        + [pltpu.VMEM((1, MIXED + 3 * D), F32), pltpu.SemaphoreType.DMA((6,)), pltpu.SemaphoreType.DMA((4,))]
        + [pltpu.VMEM((rows, D), LOW)] * GROUP,
        compiler_params=kernel_params(28),
        cost_estimate=cost(4 * tokens * D * (D + 2 * FF // GROUP), 16 * 1024 * 1024),
        name="backward_shard",
    )(info, *gs, *[far(a) for a in held])


def slot_in(ring, difference, half):
    straight, turned = ring.slot(difference, 0), ring.slot(difference, 1)
    return straight + half * (turned - straight)


QU_TILES = PART // 128
OD_TILES = D // 2 // 128
SIDES = 112


def slot_rows(ring):
    return GROUP * QU_TILES * (D // ring.count) + OD_TILES * (SIDE + UNITS) // ring.size


def grads_shape(ring):
    return shaped((ring.size * slot_rows(ring) + SIDES, 128), LOW)


def od_part(ring, info, mixed, active, grad, keep, send, active_in):
    core, spot = info[0], info[2]
    out_rows = SIDE // ring.size
    ff_rows = UNITS // ring.size
    ahead = GROUP * QU_TILES * (D // ring.count)
    for i, (out, half) in enumerate(((send, 1 - core), (keep, core))):
        columns = pl.ds(pl.multiple_of(half * (D // 2), D // 2), D // 2)
        part = grad[:, columns]
        block = dot_rows(mixed[...], part).astype(LOW)
        if i == 0:
            active_in()
        for there in range(ring.size):
            slot = slot_in(ring, spot ^ there, half)
            piece = dot_rows(active[:, there * ff_rows : (there + 1) * ff_rows], part).astype(LOW)
            for tile in range(OD_TILES):
                lanes = slice(tile * 128, (tile + 1) * 128)
                row = slot * slot_rows(ring) + ahead + tile * (ff_rows + out_rows)
                out[pl.ds(pl.multiple_of(row, 16), ff_rows), :] = piece[:, lanes]
                row = pl.multiple_of(row + ff_rows, 16)
                out[pl.ds(row, out_rows), :] = block[there * out_rows : (there + 1) * out_rows, lanes]


def vector_rows(group, sums):
    width = SIDE // SPREAD
    run = UNITS // SPREAD
    row = lax.broadcasted_iota(jnp.int32, (SIDES, 128), 0)
    pieces = []
    for at in range(0, 3 * SIDE, 128):
        pieces.append(((at // width * GROUP + group) * (width // 128) + at % width // 128, at))
    for at in range(0, UNITS, 128):
        pieces.append((3 * D // 128 + D // 128 + (at // run * GROUP + group) * (run // 128) + at % run // 128, 3 * SIDE + at))
    tail = (4 * D + FF) // 128
    for i, begin in enumerate((3 * D // 128, tail, tail + D // 128, tail + 2 * D // 128)):
        for at in range(0, D, 128):
            pieces.append((begin + at // 128, MIXED + max(i - 1, 0) * D + at))
    return sum(jnp.where(row == where, sums[:, at : at + 128], 0.0) for where, at in pieces)


def qu_part(ring, info, y, dqu, sums, keep, send):
    core, group, spot = info[0], info[1], info[2]
    rows = D // ring.count
    tile = 256
    last = ring.size * slot_rows(ring)
    extra = vector_rows(group, sums).astype(LOW)
    for out, half in ((send, 1 - core), (keep, core)):
        columns = pl.ds(pl.multiple_of(half * PART, 128), PART)
        out[last : last + SIDES, :] = extra
        for at in range(0, D, tile):
            block = dot_rows(y[:, at : at + tile], dqu[:, columns]).astype(LOW)
            for offset in range(0, tile, rows):
                dp = (at + offset) // rows
                slot = slot_in(ring, spot ^ ring.spot_of(dp), half)
                begin = slot * slot_rows(ring) + (group ^ ring.group_of(dp)) * (QU_TILES * rows)
                for i in range(QU_TILES):
                    row = pl.multiple_of(begin + i * rows, 16)
                    out[pl.ds(row, rows), :] = block[offset : offset + rows, i * 128 : (i + 1) * 128]


def grads_kernel(ring, info, far_mixed, far_active, far_grad, far_y, far_dqu, sums, keep, send, *scratch):
    mixed, active, grad, y, dqu, sems = scratch
    grad_in = started([(far_grad, grad), (far_mixed, mixed)], sems.at[0])
    active_in = started([(far_active, active)], sems.at[1])
    rest_in = started([(far_y, y), (far_dqu, dqu)], sems.at[2])
    grad_in()
    od_part(ring, info, mixed, active, grad, keep, send, active_in)
    rest_in()
    qu_part(ring, info, y, dqu, sums, keep, send)


def weight_grads(ring, info, mixed, active, grad, y, dqu, sums):
    blocks = (mixed, active, grad, y, dqu)
    out = grads_shape(ring)
    return pl.pallas_call(
        functools.partial(grads_kernel, ring),
        out_shape=(out, out),
        in_specs=[smem_spec()] + [far_spec()] * len(blocks) + [full_spec(sums.shape)],
        out_specs=(full_spec(out.shape),) * 2,
        scratch_shapes=[pltpu.VMEM(a.shape, LOW) for a in blocks] + [pltpu.SemaphoreType.DMA((3,))],
        compiler_params=kernel_params(20),
        cost_estimate=cost(50 * 10**9, 12 * 1024 * 1024),
        name="weight_grads",
    )(info, *[far(a) for a in blocks], sums)


def fold_kernel(held, came, kept, sent):
    half = (held.shape[0] - SIDES) // 2
    full = 2 * half
    kept[0:half, :] = held[0:half, :].astype(F32) + came[0:half, :].astype(F32)
    sent[0:half, :] = (held[half:full, :].astype(F32) + came[half:full, :].astype(F32)).astype(LOW)
    sides = held[full : full + SIDES, :].astype(LOW).astype(F32) + came[full : full + SIDES, :].astype(F32)
    kept[half : half + SIDES, :] = sides
    sent[half : half + SIDES, :] = sides.astype(LOW)


def fold(held, came):
    half = (held.shape[0] - SIDES) // 2 + SIDES
    outs = (shaped((half, 128), F32), shaped((half, 128), LOW))
    return pl.pallas_call(
        fold_kernel,
        out_shape=outs,
        in_specs=[full_spec(held.shape), full_spec(came.shape)],
        out_specs=tuple(full_spec(a.shape) for a in outs),
        compiler_params=kernel_params(20),
        cost_estimate=cost(0, 1024 * 1024),
        name="fold_gradients",
    )(held, came)


VECTOR_ROWS = (7 * D + FF) // 128


def close_kernel(held, came, before, *outs):
    qus, od, squares = outs[:GROUP], outs[GROUP], outs[GROUP + 1]
    rows = qus[0].shape[0] - SIDES
    full = held.shape[0] - SIDES
    sides = held[full : full + SIDES, :].astype(LOW).astype(F32) + came[full : full + SIDES, :].astype(F32)
    lanes = before[...]
    begin = 0
    for piece in (*qus, od):
        length = rows if piece is not od else od.shape[0]
        here = slice(begin, begin + length)
        begin += length
        total = held[here, :].astype(F32) + came[here, :].astype(F32)
        piece[0:length, :] = total.astype(LOW)
        lanes = lanes + jnp.sum((total * total).reshape(length // 8, 8, 128), axis=0)
    squares[...] = lanes
    high = lanes.astype(LOW).astype(F32)
    rest = sides[VECTOR_ROWS + 16 :]
    sides = jnp.concatenate([sides[:VECTOR_ROWS], high, lanes - high, rest], axis=0).astype(LOW)
    for piece in qus:
        piece[rows : rows + SIDES, :] = sides


def close(ring, held, came, before):
    rows = QU_TILES * (D // ring.count)
    outs = [shaped((rows + SIDES, 128), LOW)] * GROUP
    outs += [shaped((OD_TILES * (SIDE + UNITS) // ring.size, 128), LOW), shaped((8, 128), F32)]
    return pl.pallas_call(
        close_kernel,
        out_shape=tuple(outs),
        in_specs=[full_spec(held.shape), full_spec(came.shape), full_spec(before.shape)],
        out_specs=tuple(full_spec(a.shape) for a in outs),
        compiler_params=kernel_params(16),
        cost_estimate=cost(0, 1024 * 1024),
        name="close_gradients",
    )(held, came, before)


def join_kernel(info, *refs):
    core = info[0]
    firsts, seconds, (od_first, od_second), outs = refs[:4], refs[4:8], refs[8:10], refs[10:]
    sent, vec, squares, vec_squares = outs
    rows = firsts[0].shape[0] - SIDES
    sides = []
    for pieces in (firsts, seconds):
        parts = [a[rows : rows + SIDES, :].astype(F32) for a in pieces]
        sides.append((parts[0] + parts[1]) + (parts[2] + parts[3]))
    squares[...] = sides[0][VECTOR_ROWS : VECTOR_ROWS + 8] + sides[0][VECTOR_ROWS + 8 : VECTOR_ROWS + 16]
    own = [(a[:VECTOR_ROWS] * a[:VECTOR_ROWS]).reshape(VECTOR_ROWS // 8, 8, 128) for a in sides]
    vec_squares[...] = jnp.sum(own[0], axis=0) + jnp.sum(own[1], axis=0)
    vec[...] = jnp.where(core == 0, sides[0], sides[1])

    def write(pieces, od):
        for r in range(GROUP):
            sent[r * rows : (r + 1) * rows, :] = pieces[r][0:rows, :]
        sent[GROUP * rows :, :] = od[...]

    pl.when(core == 0)(functools.partial(write, seconds, od_second))
    pl.when(core == 1)(functools.partial(write, firsts, od_first))


def join(info, firsts, seconds, od_first, od_second):
    rows = firsts[0].shape[0] - SIDES
    outs = (shaped((GROUP * rows + od_first.shape[0], 128), LOW), shaped((SIDES, 128), F32))
    outs += (shaped((8, 128), F32),) * 2
    blocks = (*firsts, *seconds, od_first, od_second)
    return pl.pallas_call(
        join_kernel,
        out_shape=outs,
        in_specs=[smem_spec()] + [full_spec(a.shape) for a in blocks],
        out_specs=tuple(full_spec(a.shape) for a in outs),
        compiler_params=kernel_params(16),
        cost_estimate=cost(0, 1024 * 1024),
        name="join_members",
    )(info, *blocks)


def adam_update(weight, grad, first, second, factor, rate):
    clipped = grad * factor
    first_new = BETA_ONE * first + (1.0 - BETA_ONE) * clipped
    second_new = BETA_TWO * second + (1.0 - BETA_TWO) * clipped * clipped
    first_hat = first_new / (1.0 - BETA_ONE**STEP)
    second_hat = second_new / (1.0 - BETA_TWO**STEP)
    weight_new = weight - rate * (
        first_hat / (jnp.sqrt(second_hat) + ADAM_EPS) + WEIGHT_DECAY * weight
    )
    return (weight_new, first_new, second_new)


def mixed_tile(tile, member):
    at = tile * 128
    if at >= 3 * SIDE:
        return 2, up_column(member, at - 3 * SIDE)
    width = SIDE // SPREAD
    kind, within = at // SIDE, at % SIDE
    return 0, qkv_column(kind, within // width, member) + within % width


def adam_kernel(info, factor_ref, *refs):
    core, group = info[0], info[1]
    step = pl.program_id(0)
    factor = factor_ref[0]
    qus, refs = (refs[:4], refs[4:8]), refs[8:]
    ods, came, refs = refs[:2], refs[2], refs[3:]
    olds, news = refs[:12], refs[12:]
    few, many = olds[0].shape[1], olds[9].shape[1]
    rows = (qus[0][0].shape[0] - SIDES) // QU_TILES
    od_rows = ods[0].shape[0] // OD_TILES

    def update(which, column, grad):
        columns = slice(column, column + 128)
        weight, first, second = [olds[3 * which + i][0, :, columns] for i in range(3)]
        fresh = adam_update(weight, grad.astype(F32), first, second, factor, LEARN_RATE)
        for i in range(3):
            news[3 * which + i][0, :, columns] = fresh[i]

    def rows_of(ref, begin, length):
        return ref[pl.ds(pl.multiple_of(begin + step * length, 16), length), :]

    def both_halves(here):
        for half in range(2):
            for tile in range(OD_TILES):
                column = half * (D // 2) + tile * 128
                ref, begin = (ods[here], 0) if half == here else (came, GROUP * QU_TILES * rows)
                begin = begin + tile * od_rows
                update(3, column, rows_of(ref, begin, many))
                update(1, column, rows_of(ref, begin + od_rows - rows, few))
            for member in range(GROUP):
                if half == here:
                    for g in range(GROUP):

                        @pl.when(group == g)
                        def _(ref=qus[here][member ^ g]):
                            for tile in range(QU_TILES):
                                which, column = mixed_tile(half * QU_TILES + tile, member)
                                update(which, column, rows_of(ref, tile * rows, few))
                else:
                    for tile in range(QU_TILES):
                        which, column = mixed_tile(half * QU_TILES + tile, member)
                        begin = ((group ^ member) * QU_TILES + tile) * rows
                        update(which, column, rows_of(came, begin, few))

    for here in range(2):
        pl.when(core == here)(functools.partial(both_halves, here))


def adam(info, factor, qus, ods, came, olds):
    steps = max(1, olds[0].shape[1] // 16)

    def master(a):
        return pl.BlockSpec((1, a.shape[1] // steps, a.shape[2]), lambda i: (0, i, 0))

    grads = (*qus[0], *qus[1], *ods, came)
    return pl.pallas_call(
        adam_kernel,
        grid=(steps,),
        out_shape=tuple(shaped(a.shape, F32) for a in olds),
        in_specs=[smem_spec(), smem_spec()]
        + [full_spec(a.shape) for a in grads]
        + [master(a) for a in olds],
        out_specs=tuple(master(a) for a in olds),
        compiler_params=kernel_params(28),
        name="adamw",
    )(info, factor, *grads, *[far(a) for a in olds])


def doc_tables(lengths, rows):
    seqs = lengths.shape[0]
    ends = jnp.cumsum(lengths, axis=1)
    places = jnp.arange(rows, dtype=jnp.int32)
    past = places[None, :, None] >= ends[:, None, :]
    begins = jnp.sum(jnp.where(past, lengths[:, None, :], 0), axis=2)
    position = (places[None, :] - begins).reshape(seqs * rows, 1)
    half = ROT // 2
    inverse = 10000.0 ** (-(jnp.arange(half, dtype=F32) * 2.0) / ROT)
    lanes = jnp.concatenate([inverse, inverse, jnp.zeros(HEAD_DIM - ROT, F32)])
    angles = position.astype(F32) * jnp.concatenate([lanes, lanes])[None, :]
    allowed = (places[None, None, :] <= places[None, :, None]) & (places[None, None, :] >= begins[:, :, None])
    mask = jnp.where(allowed, 0.0, -1e30).reshape(seqs * rows, rows).astype(F32)
    return jnp.cos(angles), jnp.sin(angles), mask


def shards(
    x_in,
    cotangent,
    doc_lengths,
    w_qkv,
    w_out,
    w_up,
    w_down,
    vectors,
    m_qkv,
    m_out,
    m_up,
    m_down,
    m_vectors,
    v_qkv,
    v_out,
    v_up,
    v_down,
    v_vectors,
):
    place = Place()
    ring, core, group, spot = place.ring, place.core, place.group, place.spot
    info = place.info()
    local_rows, width = x_in.shape
    seqs, docs = doc_lengths.shape
    rows = local_rows // seqs
    in_rows = w_qkv.shape[1]
    shard = vectors.shape[1]
    members = range(1, GROUP)

    vec_block = jnp.pad(vectors[0].astype(LOW), (0, 8 * 128 - shard)).reshape(8, 128)
    vec_block = jnp.pad(jnp.concatenate([vec_block, vec_block]), ((0, in_rows - 16), (0, 0)))
    keep_qu, send_qu, keep_od, send_od = pack(info, w_qkv, w_out, w_up, w_down, vec_block)
    came_qu = place.sibling(send_qu)
    came_od = place.sibling(send_od)

    def member_columns():
        row = jnp.arange(in_rows)[None, :, None]
        later = (row >= 8) & (row < 16) & (jnp.arange(WIRE)[None, None, :] >= PART)
        qu = jnp.where((core == 0) ^ later, keep_qu, came_qu)
        return [take(qu, group)] + [place.member(take(qu, group ^ r), r) for r in members]

    def gather(block, *waited):
        late = after(block, *waited)
        return [block] + [place.member(late, r) for r in members]

    def to_owners(slots):
        return [slots[0]] + [place.member(slots[r], r) for r in members]

    def total_of(slots):
        return sum(a.astype(F32) for a in slots)

    def both_vectors(parts):
        pieces = jnp.concatenate([a[:, :, 0:16, PART:] for a in parts])
        pieces = pieces.reshape(ring.size * GROUP, 2, 8 * 128)[:, :, :shard]
        dp = jnp.arange(ring.count, dtype=jnp.int32)
        difference = ring.spot_of(dp) ^ spot
        slot = jnp.where(core == 0, ring.slot(difference, 0), ring.slot(difference, 1))
        vec = jnp.take(pieces, slot * GROUP + (ring.group_of(dp) ^ group), axis=0, mode="clip")
        return [block_vectors(vec[:, block].reshape(-1).astype(F32)) for block in range(2)]

    def block_vectors(vec):
        b_qkv, b_out, b_up, b_down, gain, ln_bias = jnp.split(
            vec, [3 * D, 4 * D, 4 * D + FF, 5 * D + FF, 6 * D + FF]
        )
        b_qkv = take(b_qkv.reshape(3 * SPREAD, GROUP, -1), group, 1).reshape(1, -1)
        b_up = take(b_up.reshape(SPREAD, GROUP, -1), group, 1).reshape(1, -1)
        return (b_qkv, b_up, gain[None], ln_bias[None]), (b_out + b_down)[None], gain[None]

    x_own = take(x_in.reshape(2, rows, width), core)
    cot_own = take(cotangent.reshape(2, rows, width), core)
    len_own = take(doc_lengths, core)
    len_rows = jnp.zeros((16, width), LOW).at[0, :docs].set(len_own.astype(LOW))
    x_sent = jnp.concatenate([x_own, len_rows])

    qu_came = member_columns()
    qu_own = jnp.stack(qu_came)[None]
    x_group = gather(x_sent, qu_came[1])
    od_own = jnp.where(core == 0, keep_od, came_od)[None]
    od = [jnp.concatenate([od_own, place.across(od_own, 0)])]
    qu_own = after(qu_own, od[0])
    qu = [jnp.concatenate([qu_own, place.across(qu_own, 0)])]
    qu_sibling = [place.sibling(qu[0])]
    od_sibling = [place.sibling(od[0])]
    for step in range(1, ring.bits):
        od.append(place.across(jnp.concatenate(od), step))
        qu.append(place.across(after(jnp.concatenate(qu), x_group[1], od[-1]), step))
    qu_sibling += [place.sibling(a) for a in qu[1:]]
    od_sibling += [place.sibling(a) for a in od[1:]]
    qu_mine = jnp.where(core == 1, keep_qu, came_qu)
    waited = (*x_group[1:], qu_sibling[0], od_sibling[0])
    sent = [after(jnp.concatenate([take(qu_mine, group ^ r), cot_own]), *waited) for r in members]
    qu_cot = [place.member(a, r) for a, r in zip(sent, members)]
    parts_first = (*qu, *od, *qu_sibling, *od_sibling)
    lengths = jnp.stack([a[rows, :docs] for a in x_group]).astype(jnp.int32)
    tables = doc_tables(lengths, rows)
    (vecs_first, bias_first, gain_first), (vecs_second, bias_second, gain_second) = both_vectors(qu)

    first = forward(ring, info, parts_first, x_group, tables, vecs_first, rows)
    kept_first, tables = first[GROUP:], first[-3:]
    qu_cot = [after(a, first[0]) for a in qu_cot]
    came = to_owners(first[:GROUP])
    od_own = after(jnp.where(core == 1, keep_od, came_od)[None], first[0])
    od_late = [jnp.concatenate([od_own, place.across(od_own, 0)])]
    came[1] = after(came[1], od_late[0])
    hidden_first = (x_own.astype(F32) + total_of(came) + bias_first).astype(LOW)
    hidden_group = gather(hidden_first)
    qu_own = jnp.stack([take(qu_mine, group)] + [a[:in_rows] for a in qu_cot])[None]
    qu_late = [jnp.concatenate([qu_own, after(place.across(qu_own, 0), hidden_first)])]
    for step in range(1, ring.bits):
        od_late.append(after(place.across(jnp.concatenate(od_late), step), *hidden_group[1:]))
        qu_late.append(after(place.across(jnp.concatenate(qu_late), step), *hidden_group[1:]))
    qu_sibling, od_sibling = [
        [place.sibling(after(a, *hidden_group[1:])) for a in late] for late in (qu_late, od_late)
    ]
    parts_second = (*qu_late, *od_late, *qu_sibling, *od_sibling)
    second = middle(ring, info, parts_second, hidden_group, [cot_own, *qu_cot], tables, vecs_second, rows)
    sums_second, y_second, mixed_second, active_second, dqu_second, grad_second = second[GROUP : GROUP + 6]
    z_keep, z_send = second[GROUP + 6 :]

    def rows_backward(rows_low, grad_low, dy, gain):
        rows_now = rows_low.astype(F32)
        centered = rows_now - jnp.mean(rows_now, axis=-1, keepdims=True)
        variance = jnp.mean(centered * centered, axis=-1, keepdims=True)
        inverse_std = lax.rsqrt(variance + NORM_EPS)
        normed = centered * inverse_std
        scaled = dy * gain
        inner_mean = jnp.mean(scaled, axis=-1, keepdims=True)
        inner_cross = jnp.mean(scaled * normed, axis=-1, keepdims=True)
        return (grad_low.astype(F32) + inverse_std * (scaled - inner_mean - normed * inner_cross)).astype(LOW)

    def to_members(pieces):
        return [pieces[0]] + [place.member(pieces[r], r) for r in members]

    steps = list(reversed(range(ring.bits)))

    def ring_fold(held, *waited):
        kept, sent = held
        for step in steps[:-1]:
            kept, sent = fold(kept, after(place.across(sent, step), *waited))
        return kept, sent

    dy_second = to_owners(second[:GROUP])
    grads = weight_grads(ring, info, mixed_second, active_second, grad_second, y_second, dqu_second, sums_second)
    mid_grad = rows_backward(hidden_first, cot_own, total_of(dy_second), gain_second)
    mid_group = gather(mid_grad)
    sent = place.sibling(after(grads[1], *dy_second[1:]))
    second_held = ring_fold(fold(grads[0], after(sent, mid_grad)))

    mid_late = [after(mid_group[0], *second_held)] + mid_group[1:]
    z_came = place.toward(after(z_send, *mid_group[1:]), 1)
    dy_keep, dy_send, keep, send = backward(ring, info, mid_late, kept_first, rows)
    z_came = after(z_came, send)
    kept, sent = second_held
    none = jnp.zeros((8, 128), F32)
    *qu_second, od_second, squares_second = close(ring, kept, after(place.across(sent, 0), send), none)
    send = after(send, *qu_second, z_came)
    qu_slots_second = to_members(qu_second)
    kept, sent = ring_fold(fold(keep, place.sibling(send)))
    dy_came = place.toward(after(dy_send, *qu_slots_second[1:]), 1)
    z_step = place.toward((z_keep[1].astype(F32) + z_came[1].astype(F32)).astype(LOW), 0)
    came = after(place.across(after(sent, *qu_slots_second[1:], z_step), 0), dy_came)
    *qu_first, od_first, _ = close(ring, kept, came, squares_second)
    qu_slots_first = to_members(qu_first)
    dy_step = (dy_keep[1].astype(F32) + dy_came[1].astype(F32)).astype(LOW)
    dy_step = place.toward(after(dy_step, *qu_slots_first[1:]), 0)
    grads_sent, vec, squares, vec_squares = join(info, qu_slots_first, qu_slots_second, od_first, od_second)
    squares = squares + place.sibling(squares)
    for step in range(ring.bits):
        squares = squares + place.across(squares, step)
    grads_came = place.sibling(grads_sent)
    dy_step = after(dy_step, squares, grads_came)
    squares = jnp.sum(squares + vec_squares)
    dy_total = dy_keep[0].astype(F32) + dy_came[0].astype(F32) + dy_step.astype(F32)
    z_total = z_keep[0].astype(F32) + z_came[0].astype(F32) + z_step.astype(F32)
    start_grad = rows_backward(x_own, mid_grad, dy_total, gain_first)
    hidden_second = (hidden_first.astype(F32) + z_total + bias_second).astype(LOW)

    grad_norm = jnp.sqrt(squares)
    factor = jnp.minimum(1.0, CLIP_LEVEL / (grad_norm + 1e-06))

    def own_block(one, two):
        came = place.sibling(jnp.where(core == 0, two, one))
        mine = jnp.where(core == 0, one, two)
        return [jnp.where(core == h, mine, came) for h in range(2)]

    vec_share = after(vec, grads_sent).reshape(-1)[: ring.count * shard].reshape(ring.count, shard)
    vec_share = take(vec_share, lax.axis_index("dp"))[None]
    olds = (w_qkv, m_qkv, v_qkv, w_out, m_out, v_out, w_up, m_up, v_up, w_down, m_down, v_down)
    qus = (qu_slots_first, qu_slots_second)
    news = adam(info, factor[None], qus, (od_first, od_second), grads_came, olds)
    new_vec = adam_update(vectors, vec_share, m_vectors, v_vectors, factor, VECTOR_RATE)

    outputs = own_block(jnp.stack([hidden_first, start_grad]), jnp.stack([hidden_second, mid_grad]))
    outputs = jnp.concatenate(outputs, axis=1)
    hidden_out, input_grads = outputs[:1], outputs[1:]
    return (
        hidden_out,
        input_grads,
        *(news[3 * i] for i in range(4)),
        new_vec[0],
        *(news[3 * i + 1] for i in range(4)),
        new_vec[1],
        *(news[3 * i + 2] for i in range(4)),
        new_vec[2],
        grad_norm,
    )


def solution(mesh):
    return jax.shard_map(
        shards,
        mesh=mesh,
        in_specs=(
            P("dp", None),
            P("dp", None),
            P("dp", None),
            P("section", "dp", None),
            P("section", "dp", None),
            P("section", "dp", None),
            P("section", "dp", None),
            P("section", "dp"),
            P("section", "dp", None),
            P("section", "dp", None),
            P("section", "dp", None),
            P("section", "dp", None),
            P("section", "dp"),
            P("section", "dp", None),
            P("section", "dp", None),
            P("section", "dp", None),
            P("section", "dp", None),
            P("section", "dp"),
        ),
        out_specs=(
            P("section", "dp", None),
            P("section", "dp", None),
            P("section", "dp", None),
            P("section", "dp", None),
            P("section", "dp", None),
            P("section", "dp", None),
            P("section", "dp"),
            P("section", "dp", None),
            P("section", "dp", None),
            P("section", "dp", None),
            P("section", "dp", None),
            P("section", "dp"),
            P("section", "dp", None),
            P("section", "dp", None),
            P("section", "dp", None),
            P("section", "dp", None),
            P("section", "dp"),
            P(),
        ),
        check_vma=False,
    )
```

```python
import functools

import jax
import jax.numpy as jnp
from jax import lax
from jax.experimental import pallas as pl
from jax.experimental.pallas import tpu as pltpu
from jax.sharding import PartitionSpec as P

D = 1024
FF = 4096
HEADS = 16
HEAD_DIM = 64
ROT = 16
STEP = 10


NORM_EPS = 1e-05
BETA_ONE = 0.9
BETA_TWO = 0.95
LEARN_RATE = 0.05
VECTOR_RATE = 0.3
WEIGHT_DECAY = 0.01
CLIP_LEVEL = 1.0
ADAM_EPS = 1e-08

AXES = ("section", "dp")
GROUP = 4
SPREAD = 1
LOW = jnp.bfloat16
F32 = jnp.float32
SIDE = D // GROUP
UNITS = FF // GROUP
MIXED = 3 * SIDE + UNITS
PART = MIXED // 2
WIRE = PART + 128


class Ring:
    def __init__(self, count):
        self.count = count
        self.low = count // (GROUP * SPREAD)
        self.size = SPREAD * self.low
        self.bits = self.size.bit_length() - 1

    def index(self, g, t):
        return ((t // self.low) * GROUP + g) * self.low + t % self.low

    def group_of(self, dp):
        return (dp // self.low) % GROUP

    def spot_of(self, dp):
        return (dp // (GROUP * self.low)) * self.low + dp % self.low

    def order(self, core):
        steps = list(range(self.bits))
        if SPREAD > 1 or core == 1:
            steps.reverse()
        return steps

    def turn(self, slot, core):
        return sum(((slot >> s) & 1) << b for s, b in enumerate(self.order(core)))

    def slot(self, difference, core):
        return sum(((difference >> b) & 1) << s for s, b in enumerate(self.order(core)))


class Place:
    def __init__(self):
        self.ring = Ring(lax.axis_size("dp"))
        self.core = lax.axis_index("section")
        dp = lax.axis_index("dp")
        self.group = self.ring.group_of(dp)
        self.spot = self.ring.spot_of(dp)

    def info(self):
        return jnp.stack([self.core, self.group, self.spot]).astype(jnp.int32)

    def move(self, block, where):
        ring = self.ring
        route = []
        for core in range(2):
            for g in range(GROUP):
                for t in range(ring.size):
                    c, h, u = where(core, g, t)
                    route.append((core * ring.count + ring.index(g, t), c * ring.count + ring.index(h, u)))
        return lax.ppermute(block, AXES, route)

    def sibling(self, block):
        return self.move(block, lambda c, g, t: (1 - c, g, t))

    def member(self, block, distance):
        return self.move(block, lambda c, g, t: (c, g ^ distance, t))

    def toward(self, block, step):
        return self.move(block, lambda c, g, t: (c, g ^ (2, 1)[(step + c) % 2], t))

    def across(self, block, step):
        return self.move(block, lambda c, g, t: (c, g, t ^ (1 << self.ring.order(c)[step])))


def take(block, index, axis=0):
    return lax.dynamic_index_in_dim(block, index, axis, keepdims=False)


def after(block, *waited):
    return lax.optimization_barrier((block, waited))[0]


def dot(left, right):
    return jnp.dot(left, right, preferred_element_type=F32)


def dot_cols(left, right):
    return lax.dot_general(left, right, (((1,), (1,)), ((), ())), preferred_element_type=F32)


def dot_rows(left, right):
    return lax.dot_general(left, right, (((0,), (0,)), ((), ())), preferred_element_type=F32)


def full_spec(shape):
    return pl.BlockSpec(shape, lambda *_: (0,) * len(shape))


def far_spec():
    return pl.BlockSpec(memory_space=pltpu.HBM)


def far(block):
    return pltpu.with_memory_space_constraint(block, pltpu.HBM)


def any_spec():
    return pl.BlockSpec(memory_space=pl.ANY)


def smem_spec():
    return pl.BlockSpec(memory_space=pltpu.SMEM)


def shaped(shape, dtype):
    return jax.ShapeDtypeStruct(shape, dtype)


def kernel_params(mebibytes):
    return pltpu.CompilerParams(vmem_limit_bytes=mebibytes * 1024 * 1024)


def up_pieces():
    run = UNITS // SPREAD
    cuts = sorted({0, PART - 3 * SIDE, UNITS} | {run * i for i in range(SPREAD)})
    pieces = []
    for begin, end in zip(cuts[:-1], cuts[1:]):
        column = 3 * SIDE + begin
        pieces.append((begin, column // PART, column % PART, end - begin))
    return pieces


def up_column(g, local):
    run = UNITS // SPREAD
    return (local // run * GROUP + g) * run + local % run


def qkv_column(kind, run, g):
    width = SIDE // SPREAD
    return ((kind * SPREAD + run) * GROUP + g) * width


def pack_kernel(info, qkv_hbm, out_hbm, up_hbm, down_hbm, vec, keep_qu, send_qu, keep_od, send_od, *scratch):
    w_qkv, w_out, w_up, w_down, sems = scratch
    pairs = ((qkv_hbm, w_qkv), (up_hbm, w_up), (down_hbm, w_down), (out_hbm, w_out))
    copies = [pltpu.make_async_copy(far.at[0], near, sems.at[i]) for i, (far, near) in enumerate(pairs)]
    for copy in copies:
        copy.start()
    rows = w_qkv.shape[0]
    ff_rows = w_down.shape[0]
    width = SIDE // SPREAD
    core = info[0]

    def write_qu(halves):
        for g in range(GROUP):
            for kind in range(3):
                for run in range(SPREAD):
                    at = (kind * SPREAD + run) * width
                    column = qkv_column(kind, run, g)
                    halves[0][g, :, at : at + width] = w_qkv[:, column : column + width].astype(LOW)
            for local, half, at, length in up_pieces():
                column = up_column(g, local)
                halves[half][g, :, at : at + length] = w_up[:, column : column + length].astype(LOW)
            for half in range(2):
                halves[half][g, :, PART:WIRE] = vec[...]

    def write_od(halves):
        for half in range(2):
            columns = slice(half * (D // 2), (half + 1) * (D // 2))
            halves[half][0:ff_rows] = w_down[:, columns].astype(LOW)
            halves[half][ff_rows : ff_rows + rows] = w_out[:, columns].astype(LOW)

    for first, last, write, kept, sent in ((0, 2, write_qu, keep_qu, send_qu), (2, 4, write_od, keep_od, send_od)):
        for copy in copies[first:last]:
            copy.wait()
        pl.when(core == 0)(functools.partial(write, (kept, sent)))
        pl.when(core == 1)(functools.partial(write, (sent, kept)))


def pack(info, w_qkv, w_out, w_up, w_down, vec):
    rows, ff_rows = w_qkv.shape[1], w_down.shape[1]
    qu = shaped((GROUP, rows, WIRE), LOW)
    od = shaped((ff_rows + rows, D // 2), LOW)
    return pl.pallas_call(
        pack_kernel,
        out_shape=(qu, qu, od, od),
        in_specs=[smem_spec()] + [far_spec()] * 4 + [full_spec(vec.shape)],
        out_specs=tuple(full_spec(a.shape) for a in (qu, qu, od, od)),
        scratch_shapes=[pltpu.VMEM(a.shape[1:], F32) for a in (w_qkv, w_out, w_up, w_down)]
        + [pltpu.SemaphoreType.DMA((4,))],
        compiler_params=kernel_params(20),
        name="pack_weights",
    )(info, far(w_qkv), far(w_out), far(w_up), far(w_down), vec)


def stack_kernel(*refs):
    for i, ref in enumerate(refs[:-1]):
        refs[-1][0, i] = ref[...]


def stack_members(pieces):
    out = shaped((1, len(pieces), *pieces[0].shape), LOW)
    return pl.pallas_call(
        stack_kernel,
        out_shape=out,
        in_specs=[full_spec(a.shape) for a in pieces],
        out_specs=full_spec(out.shape),
        compiler_params=kernel_params(16),
        cost_estimate=cost(50 * 10**9, 1024 * 1024),
        name="stack_members",
    )(*pieces)


def weight_copies(ring, info, parts, wqu, wout, wdown, sems):
    core, group, spot = info[0], info[1], info[2]
    qu_copies, od_copies = [], []
    count = len(parts) // 4
    for which in range(2):
        half = core if which == 0 else 1 - core
        qu_at = pl.multiple_of(half * PART, 128)
        od_at = pl.multiple_of(half * (D // 2), 128)
        slot = 0
        for piece in range(count):
            qu, od = parts[2 * count * which + piece], parts[2 * count * which + count + piece]
            rows = qu.shape[2]
            ff_rows = od.shape[1] - rows
            for i in range(qu.shape[0]):
                straight, turned = ring.turn(slot, 0), ring.turn(slot, 1)
                there = spot ^ (straight + half * (turned - straight))
                slot += 1
                ff_row = pl.multiple_of(there * ff_rows, ff_rows)
                out_row = pl.multiple_of(there * rows, rows)
                far = wdown.at[pl.ds(ff_row, ff_rows), pl.ds(od_at, D // 2)]
                od_copies.append(pltpu.make_async_copy(od.at[i, pl.ds(0, ff_rows)], far, sems.at[0]))
                far = wout.at[pl.ds(out_row, rows), pl.ds(od_at, D // 2)]
                od_copies.append(pltpu.make_async_copy(od.at[i, pl.ds(ff_rows, rows)], far, sems.at[0]))
                for r in range(GROUP):
                    row = pl.multiple_of(ring.index(group ^ r, there) * rows, rows)
                    far = wqu.at[pl.ds(row, rows), pl.ds(qu_at, PART)]
                    qu_copies.append(pltpu.make_async_copy(qu.at[i, r, :, pl.ds(0, PART)], far, sems.at[1]))
    return qu_copies, od_copies


def head_masks(dtype):
    lane = lax.broadcasted_iota(jnp.int32, (1, SIDE), 1) // HEAD_DIM
    return [(lane == h).astype(dtype) for h in range(SIDE // HEAD_DIM)]


def by_head(parts):
    lane = lax.broadcasted_iota(jnp.int32, (1, SIDE), 1) // HEAD_DIM
    total = parts[-1]
    for h in range(len(parts) - 2, -1, -1):
        total = jnp.where(lane == h, parts[h], total)
    return total


def turning(cosine, sine, back):
    lane = lax.broadcasted_iota(jnp.int32, sine.shape, 1) % HEAD_DIM
    first = jnp.where(lane < ROT // 2, sine, 0.0)
    second = jnp.where(lane < ROT // 2, 0.0, sine)
    if back:
        second = -second
    else:
        first = -first
    wide = SIDE // cosine.shape[1]
    return [jnp.concatenate([a] * wide, axis=1) for a in (cosine, first, second)]


def turn(part, tables):
    cosine, first, second = tables
    ahead = pltpu.roll(part, SIDE - ROT // 2, 1)
    behind = pltpu.roll(part, ROT // 2, 1)
    return part * cosine + ahead * first + behind * second


def normalise(rows):
    centered = rows - jnp.mean(rows, axis=-1, keepdims=True)
    variance = jnp.mean(centered * centered, axis=-1, keepdims=True)
    return centered * lax.rsqrt(variance + NORM_EPS)


def no_wait():
    pass


def forward_part(x_refs, tables, vecs, wqu, wout, wdown, kept, z_refs, waits, done, normed_ref=None):
    cosine, sine, mask = tables
    b_qkv, b_up, gain, ln_bias = vecs
    y, qkv, probs, mixed, active, slope = kept
    rows = z_refs[0].shape[0]
    for r in range(GROUP):
        normed = normalise(x_refs[r][0:rows, :].astype(F32))
        if normed_ref is not None:
            normed_ref[r * rows : (r + 1) * rows, :] = normed
        y[r * rows : (r + 1) * rows, :] = (normed * gain[...] + ln_bias[...]).astype(LOW)
    done(0)
    waits[0]()
    waits[2]()
    forth = turning(cosine[...], sine[...], False)
    for kind in range(3):
        columns = slice(kind * SIDE, (kind + 1) * SIDE)
        part = dot(y[...], wqu[:, columns]) + b_qkv[:, columns]
        if kind < 2:
            part = turn(part, forth)
        qkv[:, columns] = part.astype(LOW)
    done(1)
    masks = head_masks(LOW)
    heads = len(masks)
    for r in range(GROUP):
        here = slice(r * rows, (r + 1) * rows)
        query, keys, values = [qkv[here, k * SIDE : (k + 1) * SIDE] for k in range(3)]
        stacked = jnp.concatenate([query * m for m in masks], axis=0)
        scores = dot_cols(stacked, keys) * HEAD_DIM ** (-0.5)
        scores = scores.reshape(heads, rows, rows) + mask[here, :][None]
        expo = jnp.exp(scores - jnp.max(scores, axis=-1, keepdims=True))
        prob = expo / jnp.sum(expo, axis=-1, keepdims=True)
        prob = prob.reshape(heads * rows, rows)
        probs[r * heads * rows : (r + 1) * heads * rows, :] = prob
        full = dot(prob.astype(LOW), values)
        mixed[here, :] = by_head([full[h * rows : (h + 1) * rows] for h in range(heads)]).astype(LOW)
    done(2)
    done(3)
    tile = 256
    for at in range(0, UNITS, tile):
        hidden = dot(y[...], wqu[:, 3 * SIDE + at : 3 * SIDE + at + tile]) + b_up[:, at : at + tile]
        share = 0.5 * (1.0 + lax.erf(hidden * (0.5**0.5)))
        density = jnp.exp(-0.5 * hidden * hidden) * (0.5 / jnp.pi) ** 0.5
        active[:, at : at + tile] = (hidden * share).astype(LOW)
        slope[:, at : at + tile] = share + hidden * density
    done(4)
    done(5)
    waits[1]()
    for at in range(0, D, tile):
        branch = dot(mixed[...], wout[:, at : at + tile]) + dot(active[...], wdown[:, at : at + tile])
        for r in range(GROUP):
            z_refs[r][:, at : at + tile] = branch[r * rows : (r + 1) * rows].astype(LOW)


def backward_part(grad, normed, tables, wqu, wout, wdown, kept, dqu, dy_refs, sums, waits, done):
    cosine, sine, _ = tables
    y, qkv, probs, mixed, active, slope = kept
    rows = grad.shape[0] // GROUP
    tile = 256
    waits[0]()
    dmixed = dot_cols(grad[...], wout[...]).astype(LOW)
    for at in range(0, UNITS, tile):
        dactive = dot_cols(grad[...], wdown[at : at + tile, :])
        dhidden = (dactive * slope[:, at : at + tile]).astype(LOW)
        dqu[:, 3 * SIDE + at : 3 * SIDE + at + tile] = dhidden
    waits[1]()
    masks = head_masks(LOW)
    heads = len(masks)
    back = turning(cosine[...], sine[...], True)
    for r in range(GROUP):
        here = slice(r * rows, (r + 1) * rows)
        query, keys, values = [qkv[here, k * SIDE : (k + 1) * SIDE] for k in range(3)]
        dstack = jnp.concatenate([dmixed[here] * m for m in masks], axis=0)
        dprob = dot_cols(dstack, values)
        prob = probs[r * heads * rows : (r + 1) * heads * rows, :]
        dvalues = dot_rows(prob.astype(LOW), dstack)
        dscore = (prob * (dprob - jnp.sum(prob * dprob, axis=-1, keepdims=True))).astype(LOW)
        full = dot(dscore, keys)
        dquery = by_head([full[h * rows : (h + 1) * rows] for h in range(heads)])
        dkeys = dot_rows(dscore, jnp.concatenate([query * m for m in masks], axis=0))
        scale = HEAD_DIM ** (-0.5)
        slot_tables = [a[here] for a in back]
        dqu[here, 0:SIDE] = turn(dquery * scale, slot_tables).astype(LOW)
        dqu[here, SIDE : 2 * SIDE] = turn(dkeys * scale, slot_tables).astype(LOW)
        dqu[here, 2 * SIDE : 3 * SIDE] = dvalues.astype(LOW)
    done()
    for at in range(0, MIXED, tile):
        sums[:, at : at + tile] = jnp.sum(dqu[:, at : at + tile].astype(F32), axis=0, keepdims=True)
    waits[2]()
    for at in range(0, D, tile):
        dy = dot_cols(dqu[...], wqu[at : at + tile, :])
        for r in range(GROUP):
            dy_refs[r][:, at : at + tile] = dy[r * rows : (r + 1) * rows].astype(LOW)
        own = grad[0:rows, at : at + tile].astype(F32)
        for i, terms in enumerate((own, dy * normed[:, at : at + tile], dy)):
            begin = MIXED + i * D + at
            sums[:, begin : begin + tile] = jnp.sum(terms, axis=0, keepdims=True)


def kept_shapes(tokens, rows):
    return [
        ((tokens, D), LOW),
        ((tokens, 3 * SIDE), LOW),
        ((tokens * (SIDE // HEAD_DIM), rows), F32),
        ((tokens, SIDE), LOW),
        ((tokens, UNITS), LOW),
        ((tokens, UNITS), F32),
    ]


def weight_scratch():
    return [
        pltpu.VMEM((D, MIXED), LOW),
        pltpu.VMEM((SIDE, D), LOW),
        pltpu.VMEM((UNITS, D), LOW),
        pltpu.SemaphoreType.DMA((2,)),
    ]


def waiter(copies):
    def wait():
        for copy in copies:
            copy.wait()

    return wait


def started(pairs, sem):
    copies = [pltpu.make_async_copy(source, target, sem) for source, target in pairs]
    for copy in copies:
        copy.start()
    return waiter(copies)


def table_scratch(tokens, rows):
    return [pltpu.VMEM((tokens, 128), F32), pltpu.VMEM((tokens, 128), F32), pltpu.VMEM((tokens, rows), F32)]


def cost(flops, moved):
    return pl.CostEstimate(flops=2 * flops, bytes_accessed=2 * moved, transcendentals=0)


def leaving(pairs, sems):
    copies = [pltpu.make_async_copy(near, far, sems.at[i]) for i, (near, far) in enumerate(pairs)]

    def go(i):
        copies[i].start()

    return go, waiter(copies)


def pair_copies(info, slots, keep, send, sems):
    targets = (keep.at[0], keep.at[1], send.at[0], send.at[1])
    return [
        [pltpu.make_async_copy(slots[r], target, sems.at[i]) for i, (r, target) in enumerate(zip(order, targets))]
        for order in ((0, 2, 1, 3), (0, 1, 2, 3))
    ]


def on_core(info, copies, act):
    for here in range(2):

        @pl.when(info[0] == here)
        def _(mine=copies[here]):
            for copy in mine:
                act(copy)


def forward_kernel(ring, count, info, *refs):
    parts, refs = refs[:count], refs[count:]
    x_refs, refs = refs[:4], refs[4:]
    tables, refs = refs[:3], refs[3:]
    vecs, refs = refs[:4], refs[4:]
    z_refs, refs = refs[:4], refs[4:]
    far_kept, far_weights, far_tables, refs = refs[:7], refs[7:10], refs[10:13], refs[13:]
    kept, refs = refs[:7], refs[7:]
    out_sems, scratch = refs[0], refs[1:]
    weights = scratch[:3]
    qu_copies, od_copies = weight_copies(ring, info, parts, *scratch)
    for copy in qu_copies + od_copies:
        copy.start()
    pairs = [*zip(kept, far_kept), *zip(weights, far_weights), *zip(tables, far_tables)]
    go, out = leaving(pairs, out_sems)
    for i in range(10, 13):
        go(i)

    def qu_in():
        waiter(qu_copies)()
        go(7)

    def od_in():
        waiter(od_copies)()
        go(8)
        go(9)

    def done(i):
        go(i)
        if i == 0:
            go(6)

    forward_part(x_refs, tables, vecs, *weights, kept[:6], z_refs, (qu_in, od_in, no_wait), done, kept[6])
    out()


def forward(ring, info, parts, xs, tables, vecs, rows):
    tokens = GROUP * rows
    shapes = kept_shapes(tokens, rows) + [((tokens, D), F32)]
    away = [*shapes, ((D, MIXED), LOW), ((SIDE, D), LOW), ((UNITS, D), LOW)] + [(a.shape, F32) for a in tables]
    blocks = (*xs, *tables, *vecs)
    return pl.pallas_call(
        functools.partial(forward_kernel, ring, len(parts)),
        out_shape=(*[shaped((rows, D), LOW)] * GROUP, *[pltpu.HBM(*a) for a in away]),
        in_specs=[smem_spec()] + [any_spec()] * len(parts) + [full_spec(a.shape) for a in blocks],
        out_specs=tuple([full_spec((rows, D))] * GROUP + [far_spec()] * len(away)),
        scratch_shapes=[pltpu.VMEM(*a) for a in shapes]
        + [pltpu.SemaphoreType.DMA((len(away),))]
        + weight_scratch(),
        compiler_params=kernel_params(22),
        cost_estimate=cost(2 * tokens * D * (D + 2 * FF // GROUP), 16 * 1024 * 1024),
        name="forward_shard",
    )(info, *parts, *blocks)


def middle_kernel(ring, count, info, *refs):
    parts, refs = refs[:count], refs[count:]
    x_refs, refs = refs[:4], refs[4:]
    g_refs, refs = refs[:4], refs[4:]
    far_tables, refs = refs[:3], refs[3:]
    vecs, refs = refs[:4], refs[4:]
    dy_refs, refs = refs[:4], refs[4:]
    sums, away, (z_keep, z_send), refs = refs[0], refs[1:6], refs[6:8], refs[8:]
    kept, refs = refs[:6], refs[6:]
    z_refs, tables, refs = refs[:4], refs[4:7], refs[7:]
    (grad, normed, dqu, in_sems, out_sems, z_sems), scratch = refs[:6], refs[6:]
    rows = z_refs[0].shape[0]
    qu_copies, od_copies = weight_copies(ring, info, parts, *scratch)
    for copy in qu_copies:
        copy.start()
    tables_in = started(zip(far_tables, tables), in_sems.at[0])
    for copy in od_copies:
        copy.start()
    pairs = []
    for r, ref in enumerate(g_refs):
        at = ref.shape[0] - rows
        pairs.append((ref.at[pl.ds(at, rows)], grad.at[pl.ds(r * rows, rows)]))
    grad_in = started(pairs, in_sems.at[1])
    go, out = leaving(list(zip([kept[0], kept[3], kept[4], dqu, grad], away)), out_sems)

    def done(i):
        if i in (0, 3, 4):
            go((0, 3, 4).index(i))

    waits = (waiter(qu_copies), waiter(od_copies), tables_in)
    forward_part(x_refs, tables, vecs, *scratch[:3], kept, z_refs, waits, done, normed)
    grad_in()
    go(4)
    z_copies = pair_copies(info, z_refs, z_keep, z_send, z_sems)
    on_core(info, z_copies, lambda copy: copy.start())
    waits = (no_wait, no_wait, no_wait)
    done = functools.partial(go, 3)
    backward_part(grad, normed, tables, *scratch[:3], kept, dqu, dy_refs, sums, waits, done)
    out()
    on_core(info, z_copies, lambda copy: copy.wait())


def middle(ring, info, parts, xs, gs, tables, vecs, rows):
    tokens = GROUP * rows
    shapes = kept_shapes(tokens, rows)
    away = [shapes[0], shapes[3], shapes[4], ((tokens, MIXED), LOW), ((tokens, D), LOW)]
    away += [((2, rows, D), LOW)] * 2
    sums = shaped((1, MIXED + 3 * D), F32)
    return pl.pallas_call(
        functools.partial(middle_kernel, ring, len(parts)),
        out_shape=(*[shaped((rows, D), LOW)] * GROUP, sums, *[pltpu.HBM(*a) for a in away]),
        in_specs=[smem_spec()]
        + [any_spec()] * len(parts)
        + [full_spec(a.shape) for a in xs]
        + [far_spec()] * (GROUP + 3)
        + [full_spec(a.shape) for a in vecs],
        out_specs=tuple([full_spec((rows, D))] * GROUP + [full_spec(sums.shape)] + [far_spec()] * len(away)),
        scratch_shapes=[pltpu.VMEM(*a) for a in shapes]
        + [pltpu.VMEM((rows, D), LOW)] * GROUP
        + table_scratch(tokens, rows)
        + [pltpu.VMEM((tokens, D), LOW), pltpu.VMEM((tokens, D), F32), pltpu.VMEM((tokens, MIXED), LOW)]
        + [pltpu.SemaphoreType.DMA((2,)), pltpu.SemaphoreType.DMA((5,)), pltpu.SemaphoreType.DMA((4,))]
        + weight_scratch(),
        compiler_params=kernel_params(27),
        cost_estimate=cost(4 * tokens * D * (D + 2 * FF // GROUP), 16 * 1024 * 1024),
        name="forward_backward_shard",
    )(info, *parts, *xs, *[far(a) for a in (*gs, *tables)], *vecs)


def backward_kernel(ring, info, *refs):
    g_refs, refs = refs[:4], refs[4:]
    far_kept, far_weights, far_tables, refs = refs[:7], refs[7:10], refs[10:13], refs[13:]
    (dy_keep, dy_send, keep, send), refs = refs[:4], refs[4:]
    kept, refs = refs[:7], refs[7:]
    weights, tables, refs = refs[:3], refs[3:6], refs[6:]
    (grad, dqu, sums, in_sems, out_sems), dy_refs = refs[:5], refs[5:]
    y, qkv, probs, mixed, active, slope, normed = kept
    wqu, wout, wdown = weights
    far_y, far_qkv, far_probs, far_mixed, far_active, far_slope, far_normed = far_kept
    mixed_in = started([(far_mixed, mixed)], in_sems.at[0])
    active_in = started([(far_active, active)], in_sems.at[1])
    units_in = started([*zip(far_weights[1:], weights[1:]), (far_slope, slope)], in_sems.at[2])
    heads_in = started([(far_qkv, qkv), (far_probs, probs), *zip(far_tables, tables)], in_sems.at[3])
    dy_in = started([(far_weights[0], wqu), (far_normed, normed)], in_sems.at[4])
    y_in = started([(far_y, y)], in_sems.at[5])
    rows = g_refs[0].shape[0]
    for r in range(GROUP):
        grad[r * rows : (r + 1) * rows, :] = g_refs[r][...]
    mixed_in()
    od_part(ring, info, mixed, active, grad, keep, send, active_in)
    waits = (units_in, heads_in, dy_in)
    backward_part(grad, normed, tables, *weights, kept[:6], dqu, dy_refs, sums, waits, no_wait)
    copies = pair_copies(info, dy_refs, dy_keep, dy_send, out_sems)
    on_core(info, copies, lambda copy: copy.start())
    y_in()
    qu_part(ring, info, y, dqu, sums, keep, send)
    on_core(info, copies, lambda copy: copy.wait())


def backward(ring, info, gs, held, rows):
    tokens = GROUP * rows
    outs = [shaped((2, rows, D), LOW)] * 2 + [grads_shape(ring)] * 2
    return pl.pallas_call(
        functools.partial(backward_kernel, ring),
        out_shape=tuple(outs),
        in_specs=[smem_spec()] + [full_spec(a.shape) for a in gs] + [far_spec()] * len(held),
        out_specs=tuple(full_spec(a.shape) for a in outs),
        scratch_shapes=[pltpu.VMEM(a.shape, a.dtype) for a in held]
        + [pltpu.VMEM((tokens, D), LOW), pltpu.VMEM((tokens, MIXED), LOW)]
        + [pltpu.VMEM((1, MIXED + 3 * D), F32), pltpu.SemaphoreType.DMA((6,)), pltpu.SemaphoreType.DMA((4,))]
        + [pltpu.VMEM((rows, D), LOW)] * GROUP,
        compiler_params=kernel_params(28),
        cost_estimate=cost(4 * tokens * D * (D + 2 * FF // GROUP), 16 * 1024 * 1024),
        name="backward_shard",
    )(info, *gs, *[far(a) for a in held])


def slot_in(ring, difference, half):
    straight, turned = ring.slot(difference, 0), ring.slot(difference, 1)
    return straight + half * (turned - straight)


QU_TILES = PART // 128
OD_TILES = D // 2 // 128
SIDES = 112


def slot_rows(ring):
    return GROUP * QU_TILES * (D // ring.count) + OD_TILES * (SIDE + UNITS) // ring.size


def grads_shape(ring):
    return shaped((ring.size * slot_rows(ring) + SIDES, 128), LOW)


def od_part(ring, info, mixed, active, grad, keep, send, active_in):
    core, spot = info[0], info[2]
    out_rows = SIDE // ring.size
    ff_rows = UNITS // ring.size
    ahead = GROUP * QU_TILES * (D // ring.count)
    for i, (out, half) in enumerate(((send, 1 - core), (keep, core))):
        columns = pl.ds(pl.multiple_of(half * (D // 2), D // 2), D // 2)
        part = grad[:, columns]
        block = dot_rows(mixed[...], part).astype(LOW)
        if i == 0:
            active_in()
        for there in range(ring.size):
            slot = slot_in(ring, spot ^ there, half)
            piece = dot_rows(active[:, there * ff_rows : (there + 1) * ff_rows], part).astype(LOW)
            for tile in range(OD_TILES):
                lanes = slice(tile * 128, (tile + 1) * 128)
                row = slot * slot_rows(ring) + ahead + tile * (ff_rows + out_rows)
                out[pl.ds(pl.multiple_of(row, 16), ff_rows), :] = piece[:, lanes]
                row = pl.multiple_of(row + ff_rows, 16)
                out[pl.ds(row, out_rows), :] = block[there * out_rows : (there + 1) * out_rows, lanes]


def vector_rows(group, sums):
    width = SIDE // SPREAD
    run = UNITS // SPREAD
    row = lax.broadcasted_iota(jnp.int32, (SIDES, 128), 0)
    pieces = []
    for at in range(0, 3 * SIDE, 128):
        pieces.append(((at // width * GROUP + group) * (width // 128) + at % width // 128, at))
    for at in range(0, UNITS, 128):
        pieces.append((3 * D // 128 + D // 128 + (at // run * GROUP + group) * (run // 128) + at % run // 128, 3 * SIDE + at))
    tail = (4 * D + FF) // 128
    for i, begin in enumerate((3 * D // 128, tail, tail + D // 128, tail + 2 * D // 128)):
        for at in range(0, D, 128):
            pieces.append((begin + at // 128, MIXED + max(i - 1, 0) * D + at))
    return sum(jnp.where(row == where, sums[:, at : at + 128], 0.0) for where, at in pieces)


def qu_part(ring, info, y, dqu, sums, keep, send):
    core, group, spot = info[0], info[1], info[2]
    rows = D // ring.count
    tile = 256
    last = ring.size * slot_rows(ring)
    extra = vector_rows(group, sums).astype(LOW)
    for out, half in ((send, 1 - core), (keep, core)):
        columns = pl.ds(pl.multiple_of(half * PART, 128), PART)
        out[last : last + SIDES, :] = extra
        for at in range(0, D, tile):
            block = dot_rows(y[:, at : at + tile], dqu[:, columns]).astype(LOW)
            for offset in range(0, tile, rows):
                dp = (at + offset) // rows
                slot = slot_in(ring, spot ^ ring.spot_of(dp), half)
                begin = slot * slot_rows(ring) + (group ^ ring.group_of(dp)) * (QU_TILES * rows)
                for i in range(QU_TILES):
                    row = pl.multiple_of(begin + i * rows, 16)
                    out[pl.ds(row, rows), :] = block[offset : offset + rows, i * 128 : (i + 1) * 128]


def grads_kernel(ring, info, far_mixed, far_active, far_grad, far_y, far_dqu, sums, keep, send, *scratch):
    mixed, active, grad, y, dqu, sems = scratch
    grad_in = started([(far_grad, grad), (far_mixed, mixed)], sems.at[0])
    active_in = started([(far_active, active)], sems.at[1])
    rest_in = started([(far_y, y), (far_dqu, dqu)], sems.at[2])
    grad_in()
    od_part(ring, info, mixed, active, grad, keep, send, active_in)
    rest_in()
    qu_part(ring, info, y, dqu, sums, keep, send)


def weight_grads(ring, info, mixed, active, grad, y, dqu, sums):
    blocks = (mixed, active, grad, y, dqu)
    out = grads_shape(ring)
    return pl.pallas_call(
        functools.partial(grads_kernel, ring),
        out_shape=(out, out),
        in_specs=[smem_spec()] + [far_spec()] * len(blocks) + [full_spec(sums.shape)],
        out_specs=(full_spec(out.shape),) * 2,
        scratch_shapes=[pltpu.VMEM(a.shape, LOW) for a in blocks] + [pltpu.SemaphoreType.DMA((3,))],
        compiler_params=kernel_params(20),
        cost_estimate=cost(50 * 10**9, 12 * 1024 * 1024),
        name="weight_grads",
    )(info, *[far(a) for a in blocks], sums)


def fold_kernel(held, came, kept, sent):
    half = (held.shape[0] - SIDES) // 2
    full = 2 * half
    kept[0:half, :] = held[0:half, :].astype(F32) + came[0:half, :].astype(F32)
    sent[0:half, :] = (held[half:full, :].astype(F32) + came[half:full, :].astype(F32)).astype(LOW)
    sides = held[full : full + SIDES, :].astype(LOW).astype(F32) + came[full : full + SIDES, :].astype(F32)
    kept[half : half + SIDES, :] = sides
    sent[half : half + SIDES, :] = sides.astype(LOW)


def fold(held, came):
    half = (held.shape[0] - SIDES) // 2 + SIDES
    outs = (shaped((half, 128), F32), shaped((half, 128), LOW))
    return pl.pallas_call(
        fold_kernel,
        out_shape=outs,
        in_specs=[full_spec(held.shape), full_spec(came.shape)],
        out_specs=tuple(full_spec(a.shape) for a in outs),
        compiler_params=kernel_params(20),
        cost_estimate=cost(0, 1024 * 1024),
        name="fold_gradients",
    )(held, came)


VECTOR_ROWS = (7 * D + FF) // 128


def close_kernel(held, came, before, *outs):
    qus, od, squares = outs[:GROUP], outs[GROUP], outs[GROUP + 1]
    rows = qus[0].shape[0] - SIDES
    full = held.shape[0] - SIDES
    sides = held[full : full + SIDES, :].astype(LOW).astype(F32) + came[full : full + SIDES, :].astype(F32)
    lanes = before[...]
    begin = 0
    for piece in (*qus, od):
        length = rows if piece is not od else od.shape[0]
        here = slice(begin, begin + length)
        begin += length
        total = held[here, :].astype(F32) + came[here, :].astype(F32)
        piece[0:length, :] = total.astype(LOW)
        lanes = lanes + jnp.sum((total * total).reshape(length // 8, 8, 128), axis=0)
    squares[...] = lanes
    high = lanes.astype(LOW).astype(F32)
    rest = sides[VECTOR_ROWS + 16 :]
    sides = jnp.concatenate([sides[:VECTOR_ROWS], high, lanes - high, rest], axis=0).astype(LOW)
    for piece in qus:
        piece[rows : rows + SIDES, :] = sides


def close(ring, held, came, before):
    rows = QU_TILES * (D // ring.count)
    outs = [shaped((rows + SIDES, 128), LOW)] * GROUP
    outs += [shaped((OD_TILES * (SIDE + UNITS) // ring.size, 128), LOW), shaped((8, 128), F32)]
    return pl.pallas_call(
        close_kernel,
        out_shape=tuple(outs),
        in_specs=[full_spec(held.shape), full_spec(came.shape), full_spec(before.shape)],
        out_specs=tuple(full_spec(a.shape) for a in outs),
        compiler_params=kernel_params(16),
        cost_estimate=cost(0, 1024 * 1024),
        name="close_gradients",
    )(held, came, before)


def join_kernel(info, *refs):
    core = info[0]
    firsts, seconds, (od_first, od_second), outs = refs[:4], refs[4:8], refs[8:10], refs[10:]
    sent, vec, squares, vec_squares = outs
    rows = firsts[0].shape[0] - SIDES
    sides = []
    for pieces in (firsts, seconds):
        parts = [a[rows : rows + SIDES, :].astype(F32) for a in pieces]
        sides.append((parts[0] + parts[1]) + (parts[2] + parts[3]))
    squares[...] = sides[0][VECTOR_ROWS : VECTOR_ROWS + 8] + sides[0][VECTOR_ROWS + 8 : VECTOR_ROWS + 16]
    own = [(a[:VECTOR_ROWS] * a[:VECTOR_ROWS]).reshape(VECTOR_ROWS // 8, 8, 128) for a in sides]
    vec_squares[...] = jnp.sum(own[0], axis=0) + jnp.sum(own[1], axis=0)
    vec[...] = jnp.where(core == 0, sides[0], sides[1])

    def write(pieces, od):
        for r in range(GROUP):
            sent[r * rows : (r + 1) * rows, :] = pieces[r][0:rows, :]
        sent[GROUP * rows :, :] = od[...]

    pl.when(core == 0)(functools.partial(write, seconds, od_second))
    pl.when(core == 1)(functools.partial(write, firsts, od_first))


def join(info, firsts, seconds, od_first, od_second):
    rows = firsts[0].shape[0] - SIDES
    outs = (shaped((GROUP * rows + od_first.shape[0], 128), LOW), shaped((SIDES, 128), F32))
    outs += (shaped((8, 128), F32),) * 2
    blocks = (*firsts, *seconds, od_first, od_second)
    return pl.pallas_call(
        join_kernel,
        out_shape=outs,
        in_specs=[smem_spec()] + [full_spec(a.shape) for a in blocks],
        out_specs=tuple(full_spec(a.shape) for a in outs),
        compiler_params=kernel_params(16),
        cost_estimate=cost(0, 1024 * 1024),
        name="join_members",
    )(info, *blocks)


def adam_update(weight, grad, first, second, factor, rate):
    clipped = grad * factor
    first_new = BETA_ONE * first + (1.0 - BETA_ONE) * clipped
    second_new = BETA_TWO * second + (1.0 - BETA_TWO) * clipped * clipped
    first_hat = first_new / (1.0 - BETA_ONE**STEP)
    second_hat = second_new / (1.0 - BETA_TWO**STEP)
    weight_new = weight - rate * (
        first_hat / (jnp.sqrt(second_hat) + ADAM_EPS) + WEIGHT_DECAY * weight
    )
    return (weight_new, first_new, second_new)


def mixed_tile(tile, member):
    at = tile * 128
    if at >= 3 * SIDE:
        return 2, up_column(member, at - 3 * SIDE)
    width = SIDE // SPREAD
    kind, within = at // SIDE, at % SIDE
    return 0, qkv_column(kind, within // width, member) + within % width


def adam_kernel(info, factor_ref, *refs):
    core, group = info[0], info[1]
    step = pl.program_id(0)
    factor = factor_ref[0]
    qus, refs = (refs[:4], refs[4:8]), refs[8:]
    ods, came, refs = refs[:2], refs[2], refs[3:]
    olds, news = refs[:12], refs[12:]
    few, many = olds[0].shape[1], olds[9].shape[1]
    rows = (qus[0][0].shape[0] - SIDES) // QU_TILES
    od_rows = ods[0].shape[0] // OD_TILES

    def update(which, column, grad):
        columns = slice(column, column + 128)
        weight, first, second = [olds[3 * which + i][0, :, columns] for i in range(3)]
        fresh = adam_update(weight, grad.astype(F32), first, second, factor, LEARN_RATE)
        for i in range(3):
            news[3 * which + i][0, :, columns] = fresh[i]

    def rows_of(ref, begin, length):
        return ref[pl.ds(pl.multiple_of(begin + step * length, 16), length), :]

    def both_halves(here):
        for half in range(2):
            for tile in range(OD_TILES):
                column = half * (D // 2) + tile * 128
                ref, begin = (ods[here], 0) if half == here else (came, GROUP * QU_TILES * rows)
                begin = begin + tile * od_rows
                update(3, column, rows_of(ref, begin, many))
                update(1, column, rows_of(ref, begin + od_rows - rows, few))
            for member in range(GROUP):
                if half == here:
                    for g in range(GROUP):

                        @pl.when(group == g)
                        def _(ref=qus[here][member ^ g]):
                            for tile in range(QU_TILES):
                                which, column = mixed_tile(half * QU_TILES + tile, member)
                                update(which, column, rows_of(ref, tile * rows, few))
                else:
                    for tile in range(QU_TILES):
                        which, column = mixed_tile(half * QU_TILES + tile, member)
                        begin = ((group ^ member) * QU_TILES + tile) * rows
                        update(which, column, rows_of(came, begin, few))

    for here in range(2):
        pl.when(core == here)(functools.partial(both_halves, here))


def adam(info, factor, qus, ods, came, olds):
    steps = max(1, olds[0].shape[1] // 16)

    def master(a):
        return pl.BlockSpec((1, a.shape[1] // steps, a.shape[2]), lambda i: (0, i, 0))

    grads = (*qus[0], *qus[1], *ods, came)
    return pl.pallas_call(
        adam_kernel,
        grid=(steps,),
        out_shape=tuple(shaped(a.shape, F32) for a in olds),
        in_specs=[smem_spec(), smem_spec()]
        + [full_spec(a.shape) for a in grads]
        + [master(a) for a in olds],
        out_specs=tuple(master(a) for a in olds),
        compiler_params=kernel_params(28),
        name="adamw",
    )(info, factor, *grads, *[far(a) for a in olds])


def doc_tables(lengths, rows):
    seqs = lengths.shape[0]
    ends = jnp.cumsum(lengths, axis=1)
    places = jnp.arange(rows, dtype=jnp.int32)
    past = places[None, :, None] >= ends[:, None, :]
    begins = jnp.sum(jnp.where(past, lengths[:, None, :], 0), axis=2)
    position = (places[None, :] - begins).reshape(seqs * rows, 1)
    half = ROT // 2
    inverse = 10000.0 ** (-(jnp.arange(half, dtype=F32) * 2.0) / ROT)
    lanes = jnp.concatenate([inverse, inverse, jnp.zeros(HEAD_DIM - ROT, F32)])
    angles = position.astype(F32) * jnp.concatenate([lanes, lanes])[None, :]
    allowed = (places[None, None, :] <= places[None, :, None]) & (places[None, None, :] >= begins[:, :, None])
    mask = jnp.where(allowed, 0.0, -1e30).reshape(seqs * rows, rows).astype(F32)
    return jnp.cos(angles), jnp.sin(angles), mask


def shards(
    x_in,
    cotangent,
    doc_lengths,
    w_qkv,
    w_out,
    w_up,
    w_down,
    vectors,
    m_qkv,
    m_out,
    m_up,
    m_down,
    m_vectors,
    v_qkv,
    v_out,
    v_up,
    v_down,
    v_vectors,
):
    place = Place()
    ring, core, group, spot = place.ring, place.core, place.group, place.spot
    info = place.info()
    local_rows, width = x_in.shape
    seqs, docs = doc_lengths.shape
    rows = local_rows // seqs
    in_rows = w_qkv.shape[1]
    shard = vectors.shape[1]
    members = range(1, GROUP)

    vec_block = jnp.pad(vectors[0].astype(LOW), (0, 8 * 128 - shard)).reshape(8, 128)
    vec_block = jnp.pad(jnp.concatenate([vec_block, vec_block]), ((0, in_rows - 16), (0, 0)))
    keep_qu, send_qu, keep_od, send_od = pack(info, w_qkv, w_out, w_up, w_down, vec_block)
    came_qu = place.sibling(send_qu)
    came_od = place.sibling(send_od)

    def member_columns():
        row = jnp.arange(in_rows)[None, :, None]
        later = (row >= 8) & (row < 16) & (jnp.arange(WIRE)[None, None, :] >= PART)
        qu = jnp.where((core == 0) ^ later, keep_qu, came_qu)
        return [take(qu, group)] + [place.member(take(qu, group ^ r), r) for r in members]

    def gather(block, *waited):
        late = after(block, *waited)
        return [block] + [place.member(late, r) for r in members]

    def to_owners(slots):
        return [slots[0]] + [place.member(slots[r], r) for r in members]

    def total_of(slots):
        return sum(a.astype(F32) for a in slots)

    def both_vectors(parts):
        pieces = jnp.concatenate([a[:, :, 0:16, PART:] for a in parts])
        pieces = pieces.reshape(ring.size * GROUP, 2, 8 * 128)[:, :, :shard]
        dp = jnp.arange(ring.count, dtype=jnp.int32)
        difference = ring.spot_of(dp) ^ spot
        slot = jnp.where(core == 0, ring.slot(difference, 0), ring.slot(difference, 1))
        vec = jnp.take(pieces, slot * GROUP + (ring.group_of(dp) ^ group), axis=0, mode="clip")
        return [block_vectors(vec[:, block].reshape(-1).astype(F32)) for block in range(2)]

    def block_vectors(vec):
        b_qkv, b_out, b_up, b_down, gain, ln_bias = jnp.split(
            vec, [3 * D, 4 * D, 4 * D + FF, 5 * D + FF, 6 * D + FF]
        )
        b_qkv = take(b_qkv.reshape(3 * SPREAD, GROUP, -1), group, 1).reshape(1, -1)
        b_up = take(b_up.reshape(SPREAD, GROUP, -1), group, 1).reshape(1, -1)
        return (b_qkv, b_up, gain[None], ln_bias[None]), (b_out + b_down)[None], gain[None]

    x_own = take(x_in.reshape(2, rows, width), core)
    cot_own = take(cotangent.reshape(2, rows, width), core)
    len_own = take(doc_lengths, core)
    len_rows = jnp.zeros((16, width), LOW).at[0, :docs].set(len_own.astype(LOW))
    x_sent = jnp.concatenate([x_own, len_rows])

    qu_came = member_columns()
    qu_own = jnp.stack(qu_came)[None]
    x_near = [place.member(after(x_sent, qu_came[1]), r) for r in (1, 2)]
    x_group = [x_sent, *x_near]
    od_own = jnp.where(core == 0, keep_od, came_od)[None]
    od = [jnp.concatenate([od_own, place.across(od_own, 0)])]
    qu_own = after(qu_own, od[0])
    qu = [jnp.concatenate([qu_own, place.across(qu_own, 0)])]
    x_group.append(place.member(after(x_near[1], qu[0], od[0]), 1))
    qu_sibling = [place.sibling(qu[0])]
    od_sibling = [place.sibling(od[0])]
    for step in range(1, ring.bits):
        od.append(place.across(jnp.concatenate(od), step))
        qu.append(place.across(after(jnp.concatenate(qu), od[-1]), step))
    qu_sibling += [place.sibling(a) for a in qu[1:]]
    od_sibling += [place.sibling(a) for a in od[1:]]
    qu_mine = jnp.where(core == 1, keep_qu, came_qu)
    waited = (*x_group[1:], qu_sibling[0], od_sibling[0])
    sent = [after(jnp.concatenate([take(qu_mine, group ^ r), cot_own]), *waited) for r in members]
    qu_cot = [place.member(a, r) for a, r in zip(sent, members)]
    parts_first = (*qu, *od, *qu_sibling, *od_sibling)
    lengths = jnp.stack([a[rows, :docs] for a in x_group]).astype(jnp.int32)
    tables = doc_tables(lengths, rows)
    (vecs_first, bias_first, gain_first), (vecs_second, bias_second, gain_second) = both_vectors(qu)

    first = forward(ring, info, parts_first, x_group, tables, vecs_first, rows)
    kept_first, tables = first[GROUP:], first[-3:]
    qu_cot = [after(a, first[0]) for a in qu_cot]
    came = to_owners(first[:GROUP])
    od_own = after(jnp.where(core == 1, keep_od, came_od)[None], first[0])
    od_late = [jnp.concatenate([od_own, place.across(od_own, 0)])]
    came[1] = after(came[1], od_late[0])
    came[2] = after(came[2], *vecs_second, bias_second, gain_second)
    hidden_first = (x_own.astype(F32) + total_of(came) + bias_first).astype(LOW)
    hidden_group = gather(hidden_first)
    qu_own = jnp.stack([take(qu_mine, group)] + [a[:in_rows] for a in qu_cot])[None]
    qu_late = [jnp.concatenate([qu_own, after(place.across(qu_own, 0), hidden_first)])]
    for step in range(1, ring.bits):
        od_late.append(after(place.across(jnp.concatenate(od_late), step), *hidden_group[1:]))
        qu_late.append(after(place.across(jnp.concatenate(qu_late), step), *hidden_group[1:]))
    qu_sibling, od_sibling = [
        [place.sibling(after(a, *hidden_group[1:])) for a in late] for late in (qu_late, od_late)
    ]
    parts_second = (*qu_late, *od_late, *qu_sibling, *od_sibling)
    second = middle(ring, info, parts_second, hidden_group, [cot_own, *qu_cot], tables, vecs_second, rows)
    sums_second, y_second, mixed_second, active_second, dqu_second, grad_second = second[GROUP : GROUP + 6]
    z_keep, z_send = second[GROUP + 6 :]

    def rows_backward(rows_low, grad_low, dy, gain):
        rows_now = rows_low.astype(F32)
        centered = rows_now - jnp.mean(rows_now, axis=-1, keepdims=True)
        variance = jnp.mean(centered * centered, axis=-1, keepdims=True)
        inverse_std = lax.rsqrt(variance + NORM_EPS)
        normed = centered * inverse_std
        scaled = dy * gain
        inner_mean = jnp.mean(scaled, axis=-1, keepdims=True)
        inner_cross = jnp.mean(scaled * normed, axis=-1, keepdims=True)
        return (grad_low.astype(F32) + inverse_std * (scaled - inner_mean - normed * inner_cross)).astype(LOW)

    def to_members(pieces):
        return [pieces[0]] + [place.member(pieces[r], r) for r in members]

    steps = list(reversed(range(ring.bits)))

    def ring_fold(held, *waited):
        kept, sent = held
        for step in steps[:-1]:
            kept, sent = fold(kept, after(place.across(sent, step), *waited))
        return kept, sent

    dy_second = to_owners(second[:GROUP])
    grads = weight_grads(ring, info, mixed_second, active_second, grad_second, y_second, dqu_second, sums_second)
    mid_grad = rows_backward(hidden_first, cot_own, total_of(dy_second), gain_second)
    mid_group = gather(mid_grad)
    sent = place.sibling(after(grads[1], *dy_second[1:]))
    second_held = ring_fold(fold(grads[0], after(sent, mid_grad)))

    mid_late = [after(mid_group[0], *second_held)] + mid_group[1:]
    z_came = place.toward(after(z_send, *mid_group[1:]), 1)
    dy_keep, dy_send, keep, send = backward(ring, info, mid_late, kept_first, rows)
    z_came = after(z_came, send)
    kept, sent = second_held
    none = jnp.zeros((8, 128), F32)
    *qu_second, od_second, squares_second = close(ring, kept, after(place.across(sent, 0), send), none)
    send = after(send, *qu_second, z_came)
    qu_slots_second = to_members(qu_second)
    kept, sent = ring_fold(fold(keep, place.sibling(send)))
    dy_came = place.toward(after(dy_send, *qu_slots_second[1:]), 1)
    z_step = place.toward((z_keep[1].astype(F32) + z_came[1].astype(F32)).astype(LOW), 0)
    came = after(place.across(after(sent, *qu_slots_second[1:], z_step), 0), dy_came)
    *qu_first, od_first, _ = close(ring, kept, came, squares_second)
    qu_slots_first = to_members(qu_first)
    dy_step = (dy_keep[1].astype(F32) + dy_came[1].astype(F32)).astype(LOW)
    dy_step = place.toward(after(dy_step, *qu_slots_first[1:]), 0)
    grads_sent, vec, squares, vec_squares = join(info, qu_slots_first, qu_slots_second, od_first, od_second)
    squares = squares + place.sibling(squares)
    for step in range(ring.bits):
        squares = squares + place.across(squares, step)
    grads_came = place.sibling(grads_sent)
    dy_step = after(dy_step, squares, grads_came)
    squares = jnp.sum(squares + vec_squares)
    dy_total = dy_keep[0].astype(F32) + dy_came[0].astype(F32) + dy_step.astype(F32)
    z_total = z_keep[0].astype(F32) + z_came[0].astype(F32) + z_step.astype(F32)
    start_grad = rows_backward(x_own, mid_grad, dy_total, gain_first)
    hidden_second = (hidden_first.astype(F32) + z_total + bias_second).astype(LOW)

    grad_norm = jnp.sqrt(squares)
    factor = jnp.minimum(1.0, CLIP_LEVEL / (grad_norm + 1e-06))

    def own_block(one, two):
        came = place.sibling(jnp.where(core == 0, two, one))
        mine = jnp.where(core == 0, one, two)
        return [jnp.where(core == h, mine, came) for h in range(2)]

    vec_share = after(vec, grads_sent).reshape(-1)[: ring.count * shard].reshape(ring.count, shard)
    vec_share = take(vec_share, lax.axis_index("dp"))[None]
    olds = (w_qkv, m_qkv, v_qkv, w_out, m_out, v_out, w_up, m_up, v_up, w_down, m_down, v_down)
    qus = (qu_slots_first, qu_slots_second)
    news = adam(info, factor[None], qus, (od_first, od_second), grads_came, olds)
    new_vec = adam_update(vectors, vec_share, m_vectors, v_vectors, factor, VECTOR_RATE)

    outputs = own_block(jnp.stack([hidden_first, start_grad]), jnp.stack([hidden_second, mid_grad]))
    outputs = jnp.concatenate(outputs, axis=1)
    hidden_out, input_grads = outputs[:1], outputs[1:]
    return (
        hidden_out,
        input_grads,
        *(news[3 * i] for i in range(4)),
        new_vec[0],
        *(news[3 * i + 1] for i in range(4)),
        new_vec[1],
        *(news[3 * i + 2] for i in range(4)),
        new_vec[2],
        grad_norm,
    )


def solution(mesh):
    return jax.shard_map(
        shards,
        mesh=mesh,
        in_specs=(
            P("dp", None),
            P("dp", None),
            P("dp", None),
            P("section", "dp", None),
            P("section", "dp", None),
            P("section", "dp", None),
            P("section", "dp", None),
            P("section", "dp"),
            P("section", "dp", None),
            P("section", "dp", None),
            P("section", "dp", None),
            P("section", "dp", None),
            P("section", "dp"),
            P("section", "dp", None),
            P("section", "dp", None),
            P("section", "dp", None),
            P("section", "dp", None),
            P("section", "dp"),
        ),
        out_specs=(
            P("section", "dp", None),
            P("section", "dp", None),
            P("section", "dp", None),
            P("section", "dp", None),
            P("section", "dp", None),
            P("section", "dp", None),
            P("section", "dp"),
            P("section", "dp", None),
            P("section", "dp", None),
            P("section", "dp", None),
            P("section", "dp", None),
            P("section", "dp"),
            P("section", "dp", None),
            P("section", "dp", None),
            P("section", "dp", None),
            P("section", "dp", None),
            P("section", "dp"),
            P(),
        ),
        check_vma=False,
    )
```

```python
import functools

import jax
import jax.numpy as jnp
from jax import lax
from jax.experimental import pallas as pl
from jax.experimental.pallas import tpu as pltpu
from jax.sharding import PartitionSpec as P

D = 1024
FF = 4096
HEADS = 16
HEAD_DIM = 64
ROT = 16
STEP = 10


NORM_EPS = 1e-05
BETA_ONE = 0.9
BETA_TWO = 0.95
LEARN_RATE = 0.05
VECTOR_RATE = 0.3
WEIGHT_DECAY = 0.01
CLIP_LEVEL = 1.0
ADAM_EPS = 1e-08

AXES = ("section", "dp")
GROUP = 4
SPREAD = 1
LOW = jnp.bfloat16
F32 = jnp.float32
SIDE = D // GROUP
UNITS = FF // GROUP
MIXED = 3 * SIDE + UNITS
PART = MIXED // 2
WIRE = PART + 128


class Ring:
    def __init__(self, count):
        self.count = count
        self.low = count // (GROUP * SPREAD)
        self.size = SPREAD * self.low
        self.bits = self.size.bit_length() - 1

    def index(self, g, t):
        return ((t // self.low) * GROUP + g) * self.low + t % self.low

    def group_of(self, dp):
        return (dp // self.low) % GROUP

    def spot_of(self, dp):
        return (dp // (GROUP * self.low)) * self.low + dp % self.low

    def order(self, core):
        steps = list(range(self.bits))
        if SPREAD > 1 or core == 1:
            steps.reverse()
        return steps

    def turn(self, slot, core):
        return sum(((slot >> s) & 1) << b for s, b in enumerate(self.order(core)))

    def slot(self, difference, core):
        return sum(((difference >> b) & 1) << s for s, b in enumerate(self.order(core)))


class Place:
    def __init__(self):
        self.ring = Ring(lax.axis_size("dp"))
        self.core = lax.axis_index("section")
        dp = lax.axis_index("dp")
        self.group = self.ring.group_of(dp)
        self.spot = self.ring.spot_of(dp)

    def info(self):
        return jnp.stack([self.core, self.group, self.spot]).astype(jnp.int32)

    def move(self, block, where):
        ring = self.ring
        route = []
        for core in range(2):
            for g in range(GROUP):
                for t in range(ring.size):
                    c, h, u = where(core, g, t)
                    route.append((core * ring.count + ring.index(g, t), c * ring.count + ring.index(h, u)))
        return lax.ppermute(block, AXES, route)

    def sibling(self, block):
        return self.move(block, lambda c, g, t: (1 - c, g, t))

    def member(self, block, distance):
        return self.move(block, lambda c, g, t: (c, g ^ distance, t))

    def toward(self, block, step):
        return self.move(block, lambda c, g, t: (c, g ^ (2, 1)[(step + c) % 2], t))

    def across(self, block, step):
        return self.move(block, lambda c, g, t: (c, g, t ^ (1 << self.ring.order(c)[step])))


def take(block, index, axis=0):
    return lax.dynamic_index_in_dim(block, index, axis, keepdims=False)


def after(block, *waited):
    return lax.optimization_barrier((block, waited))[0]


def dot(left, right):
    return jnp.dot(left, right, preferred_element_type=F32)


def dot_cols(left, right):
    return lax.dot_general(left, right, (((1,), (1,)), ((), ())), preferred_element_type=F32)


def dot_rows(left, right):
    return lax.dot_general(left, right, (((0,), (0,)), ((), ())), preferred_element_type=F32)


def full_spec(shape):
    return pl.BlockSpec(shape, lambda *_: (0,) * len(shape))


def far_spec():
    return pl.BlockSpec(memory_space=pltpu.HBM)


def far(block):
    return pltpu.with_memory_space_constraint(block, pltpu.HBM)


def any_spec():
    return pl.BlockSpec(memory_space=pl.ANY)


def smem_spec():
    return pl.BlockSpec(memory_space=pltpu.SMEM)


def shaped(shape, dtype):
    return jax.ShapeDtypeStruct(shape, dtype)


def kernel_params(mebibytes):
    return pltpu.CompilerParams(vmem_limit_bytes=mebibytes * 1024 * 1024)


def up_pieces():
    run = UNITS // SPREAD
    cuts = sorted({0, PART - 3 * SIDE, UNITS} | {run * i for i in range(SPREAD)})
    pieces = []
    for begin, end in zip(cuts[:-1], cuts[1:]):
        column = 3 * SIDE + begin
        pieces.append((begin, column // PART, column % PART, end - begin))
    return pieces


def up_column(g, local):
    run = UNITS // SPREAD
    return (local // run * GROUP + g) * run + local % run


def qkv_column(kind, run, g):
    width = SIDE // SPREAD
    return ((kind * SPREAD + run) * GROUP + g) * width


def pack_kernel(info, qkv_hbm, out_hbm, up_hbm, down_hbm, vec, keep_qu, send_qu, keep_od, send_od, *scratch):
    w_qkv, w_out, w_up, w_down, sems = scratch
    pairs = ((qkv_hbm, w_qkv), (up_hbm, w_up), (down_hbm, w_down), (out_hbm, w_out))
    copies = [pltpu.make_async_copy(far.at[0], near, sems.at[i]) for i, (far, near) in enumerate(pairs)]
    for copy in copies:
        copy.start()
    rows = w_qkv.shape[0]
    ff_rows = w_down.shape[0]
    width = SIDE // SPREAD
    core = info[0]

    def write_qu(halves):
        for g in range(GROUP):
            for kind in range(3):
                for run in range(SPREAD):
                    at = (kind * SPREAD + run) * width
                    column = qkv_column(kind, run, g)
                    halves[0][g, :, at : at + width] = w_qkv[:, column : column + width].astype(LOW)
            for local, half, at, length in up_pieces():
                column = up_column(g, local)
                halves[half][g, :, at : at + length] = w_up[:, column : column + length].astype(LOW)
            for half in range(2):
                halves[half][g, :, PART:WIRE] = vec[...]

    def write_od(halves):
        for half in range(2):
            columns = slice(half * (D // 2), (half + 1) * (D // 2))
            halves[half][0:ff_rows] = w_down[:, columns].astype(LOW)
            halves[half][ff_rows : ff_rows + rows] = w_out[:, columns].astype(LOW)

    for first, last, write, kept, sent in ((0, 2, write_qu, keep_qu, send_qu), (2, 4, write_od, keep_od, send_od)):
        for copy in copies[first:last]:
            copy.wait()
        pl.when(core == 0)(functools.partial(write, (kept, sent)))
        pl.when(core == 1)(functools.partial(write, (sent, kept)))


def pack(info, w_qkv, w_out, w_up, w_down, vec):
    rows, ff_rows = w_qkv.shape[1], w_down.shape[1]
    qu = shaped((GROUP, rows, WIRE), LOW)
    od = shaped((ff_rows + rows, D // 2), LOW)
    return pl.pallas_call(
        pack_kernel,
        out_shape=(qu, qu, od, od),
        in_specs=[smem_spec()] + [far_spec()] * 4 + [full_spec(vec.shape)],
        out_specs=tuple(full_spec(a.shape) for a in (qu, qu, od, od)),
        scratch_shapes=[pltpu.VMEM(a.shape[1:], F32) for a in (w_qkv, w_out, w_up, w_down)]
        + [pltpu.SemaphoreType.DMA((4,))],
        compiler_params=kernel_params(20),
        name="pack_weights",
    )(info, far(w_qkv), far(w_out), far(w_up), far(w_down), vec)


def stack_kernel(*refs):
    for i, ref in enumerate(refs[:-1]):
        refs[-1][0, i] = ref[...]


def stack_members(pieces):
    out = shaped((1, len(pieces), *pieces[0].shape), LOW)
    return pl.pallas_call(
        stack_kernel,
        out_shape=out,
        in_specs=[full_spec(a.shape) for a in pieces],
        out_specs=full_spec(out.shape),
        compiler_params=kernel_params(16),
        cost_estimate=cost(50 * 10**9, 1024 * 1024),
        name="stack_members",
    )(*pieces)


def weight_copies(ring, info, parts, wqu, wout, wdown, sems):
    core, group, spot = info[0], info[1], info[2]
    qu_copies, od_copies = [], []
    count = len(parts) // 4
    for which in range(2):
        half = core if which == 0 else 1 - core
        qu_at = pl.multiple_of(half * PART, 128)
        od_at = pl.multiple_of(half * (D // 2), 128)
        slot = 0
        for piece in range(count):
            qu, od = parts[2 * count * which + piece], parts[2 * count * which + count + piece]
            rows = qu.shape[2]
            ff_rows = od.shape[1] - rows
            for i in range(qu.shape[0]):
                straight, turned = ring.turn(slot, 0), ring.turn(slot, 1)
                there = spot ^ (straight + half * (turned - straight))
                slot += 1
                ff_row = pl.multiple_of(there * ff_rows, ff_rows)
                out_row = pl.multiple_of(there * rows, rows)
                far = wdown.at[pl.ds(ff_row, ff_rows), pl.ds(od_at, D // 2)]
                od_copies.append(pltpu.make_async_copy(od.at[i, pl.ds(0, ff_rows)], far, sems.at[0]))
                far = wout.at[pl.ds(out_row, rows), pl.ds(od_at, D // 2)]
                od_copies.append(pltpu.make_async_copy(od.at[i, pl.ds(ff_rows, rows)], far, sems.at[0]))
                for r in range(GROUP):
                    row = pl.multiple_of(ring.index(group ^ r, there) * rows, rows)
                    far = wqu.at[pl.ds(row, rows), pl.ds(qu_at, PART)]
                    qu_copies.append(pltpu.make_async_copy(qu.at[i, r, :, pl.ds(0, PART)], far, sems.at[1]))
    return qu_copies, od_copies


def head_masks(dtype):
    lane = lax.broadcasted_iota(jnp.int32, (1, SIDE), 1) // HEAD_DIM
    return [(lane == h).astype(dtype) for h in range(SIDE // HEAD_DIM)]


def by_head(parts):
    lane = lax.broadcasted_iota(jnp.int32, (1, SIDE), 1) // HEAD_DIM
    total = parts[-1]
    for h in range(len(parts) - 2, -1, -1):
        total = jnp.where(lane == h, parts[h], total)
    return total


def turning(cosine, sine, back):
    lane = lax.broadcasted_iota(jnp.int32, sine.shape, 1) % HEAD_DIM
    first = jnp.where(lane < ROT // 2, sine, 0.0)
    second = jnp.where(lane < ROT // 2, 0.0, sine)
    if back:
        second = -second
    else:
        first = -first
    wide = SIDE // cosine.shape[1]
    return [jnp.concatenate([a] * wide, axis=1) for a in (cosine, first, second)]


def turn(part, tables):
    cosine, first, second = tables
    ahead = pltpu.roll(part, SIDE - ROT // 2, 1)
    behind = pltpu.roll(part, ROT // 2, 1)
    return part * cosine + ahead * first + behind * second


def normalise(rows):
    centered = rows - jnp.mean(rows, axis=-1, keepdims=True)
    variance = jnp.mean(centered * centered, axis=-1, keepdims=True)
    return centered * lax.rsqrt(variance + NORM_EPS)


def no_wait():
    pass


def forward_part(x_refs, tables, vecs, wqu, wout, wdown, kept, z_refs, waits, done, normed_ref=None):
    cosine, sine, mask = tables
    b_qkv, b_up, gain, ln_bias = vecs
    y, qkv, probs, mixed, active, slope = kept
    rows = z_refs[0].shape[0]
    for r in range(GROUP):
        normed = normalise(x_refs[r][0:rows, :].astype(F32))
        if normed_ref is not None:
            normed_ref[r * rows : (r + 1) * rows, :] = normed
        y[r * rows : (r + 1) * rows, :] = (normed * gain[...] + ln_bias[...]).astype(LOW)
    done(0)
    waits[0]()
    waits[2]()
    forth = turning(cosine[...], sine[...], False)
    for kind in range(3):
        columns = slice(kind * SIDE, (kind + 1) * SIDE)
        part = dot(y[...], wqu[:, columns]) + b_qkv[:, columns]
        if kind < 2:
            part = turn(part, forth)
        qkv[:, columns] = part.astype(LOW)
    done(1)
    masks = head_masks(LOW)
    heads = len(masks)
    for r in range(GROUP):
        here = slice(r * rows, (r + 1) * rows)
        query, keys, values = [qkv[here, k * SIDE : (k + 1) * SIDE] for k in range(3)]
        stacked = jnp.concatenate([query * m for m in masks], axis=0)
        scores = dot_cols(stacked, keys) * HEAD_DIM ** (-0.5)
        scores = scores.reshape(heads, rows, rows) + mask[here, :][None]
        expo = jnp.exp(scores - jnp.max(scores, axis=-1, keepdims=True))
        prob = expo / jnp.sum(expo, axis=-1, keepdims=True)
        prob = prob.reshape(heads * rows, rows)
        probs[r * heads * rows : (r + 1) * heads * rows, :] = prob
        full = dot(prob.astype(LOW), values)
        mixed[here, :] = by_head([full[h * rows : (h + 1) * rows] for h in range(heads)]).astype(LOW)
    done(2)
    done(3)
    tile = 256
    for at in range(0, UNITS, tile):
        hidden = dot(y[...], wqu[:, 3 * SIDE + at : 3 * SIDE + at + tile]) + b_up[:, at : at + tile]
        share = 0.5 * (1.0 + lax.erf(hidden * (0.5**0.5)))
        density = jnp.exp(-0.5 * hidden * hidden) * (0.5 / jnp.pi) ** 0.5
        active[:, at : at + tile] = (hidden * share).astype(LOW)
        slope[:, at : at + tile] = share + hidden * density
    done(4)
    done(5)
    waits[1]()
    for at in range(0, D, tile):
        branch = dot(mixed[...], wout[:, at : at + tile]) + dot(active[...], wdown[:, at : at + tile])
        for r in range(GROUP):
            z_refs[r][:, at : at + tile] = branch[r * rows : (r + 1) * rows].astype(LOW)


def backward_part(grad, normed, tables, wqu, wout, wdown, kept, dqu, dy_refs, sums, waits, done):
    cosine, sine, _ = tables
    y, qkv, probs, mixed, active, slope = kept
    rows = grad.shape[0] // GROUP
    tile = 256
    waits[0]()
    dmixed = dot_cols(grad[...], wout[...]).astype(LOW)
    for at in range(0, UNITS, tile):
        dactive = dot_cols(grad[...], wdown[at : at + tile, :])
        dhidden = (dactive * slope[:, at : at + tile]).astype(LOW)
        dqu[:, 3 * SIDE + at : 3 * SIDE + at + tile] = dhidden
    waits[1]()
    masks = head_masks(LOW)
    heads = len(masks)
    back = turning(cosine[...], sine[...], True)
    for r in range(GROUP):
        here = slice(r * rows, (r + 1) * rows)
        query, keys, values = [qkv[here, k * SIDE : (k + 1) * SIDE] for k in range(3)]
        dstack = jnp.concatenate([dmixed[here] * m for m in masks], axis=0)
        dprob = dot_cols(dstack, values)
        prob = probs[r * heads * rows : (r + 1) * heads * rows, :]
        dvalues = dot_rows(prob.astype(LOW), dstack)
        dscore = (prob * (dprob - jnp.sum(prob * dprob, axis=-1, keepdims=True))).astype(LOW)
        full = dot(dscore, keys)
        dquery = by_head([full[h * rows : (h + 1) * rows] for h in range(heads)])
        dkeys = dot_rows(dscore, jnp.concatenate([query * m for m in masks], axis=0))
        scale = HEAD_DIM ** (-0.5)
        slot_tables = [a[here] for a in back]
        dqu[here, 0:SIDE] = turn(dquery * scale, slot_tables).astype(LOW)
        dqu[here, SIDE : 2 * SIDE] = turn(dkeys * scale, slot_tables).astype(LOW)
        dqu[here, 2 * SIDE : 3 * SIDE] = dvalues.astype(LOW)
    done()
    for at in range(0, MIXED, tile):
        sums[:, at : at + tile] = jnp.sum(dqu[:, at : at + tile].astype(F32), axis=0, keepdims=True)
    waits[2]()
    for at in range(0, D, tile):
        dy = dot_cols(dqu[...], wqu[at : at + tile, :])
        for r in range(GROUP):
            dy_refs[r][:, at : at + tile] = dy[r * rows : (r + 1) * rows].astype(LOW)
        own = grad[0:rows, at : at + tile].astype(F32)
        for i, terms in enumerate((own, dy * normed[:, at : at + tile], dy)):
            begin = MIXED + i * D + at
            sums[:, begin : begin + tile] = jnp.sum(terms, axis=0, keepdims=True)


def kept_shapes(tokens, rows):
    return [
        ((tokens, D), LOW),
        ((tokens, 3 * SIDE), LOW),
        ((tokens * (SIDE // HEAD_DIM), rows), F32),
        ((tokens, SIDE), LOW),
        ((tokens, UNITS), LOW),
        ((tokens, UNITS), F32),
    ]


def weight_scratch():
    return [
        pltpu.VMEM((D, MIXED), LOW),
        pltpu.VMEM((SIDE, D), LOW),
        pltpu.VMEM((UNITS, D), LOW),
        pltpu.SemaphoreType.DMA((2,)),
    ]


def waiter(copies):
    def wait():
        for copy in copies:
            copy.wait()

    return wait


def started(pairs, sem):
    copies = [pltpu.make_async_copy(source, target, sem) for source, target in pairs]
    for copy in copies:
        copy.start()
    return waiter(copies)


def table_scratch(tokens, rows):
    return [pltpu.VMEM((tokens, 128), F32), pltpu.VMEM((tokens, 128), F32), pltpu.VMEM((tokens, rows), F32)]


def cost(flops, moved):
    return pl.CostEstimate(flops=2 * flops, bytes_accessed=2 * moved, transcendentals=0)


def leaving(pairs, sems):
    copies = [pltpu.make_async_copy(near, far, sems.at[i]) for i, (near, far) in enumerate(pairs)]

    def go(i):
        copies[i].start()

    return go, waiter(copies)


def pair_copies(info, slots, keep, send, sems):
    targets = (keep.at[0], keep.at[1], send.at[0], send.at[1])
    return [
        [pltpu.make_async_copy(slots[r], target, sems.at[i]) for i, (r, target) in enumerate(zip(order, targets))]
        for order in ((0, 2, 1, 3), (0, 1, 2, 3))
    ]


def on_core(info, copies, act):
    for here in range(2):

        @pl.when(info[0] == here)
        def _(mine=copies[here]):
            for copy in mine:
                act(copy)


def forward_kernel(ring, count, info, *refs):
    parts, refs = refs[:count], refs[count:]
    x_refs, refs = refs[:4], refs[4:]
    tables, refs = refs[:3], refs[3:]
    vecs, refs = refs[:4], refs[4:]
    z_refs, refs = refs[:4], refs[4:]
    far_kept, far_weights, far_tables, refs = refs[:7], refs[7:10], refs[10:13], refs[13:]
    kept, refs = refs[:7], refs[7:]
    out_sems, scratch = refs[0], refs[1:]
    weights = scratch[:3]
    qu_copies, od_copies = weight_copies(ring, info, parts, *scratch)
    for copy in qu_copies + od_copies:
        copy.start()
    pairs = [*zip(kept, far_kept), *zip(weights, far_weights), *zip(tables, far_tables)]
    go, out = leaving(pairs, out_sems)
    for i in range(10, 13):
        go(i)

    def qu_in():
        waiter(qu_copies)()
        go(7)

    def od_in():
        waiter(od_copies)()
        go(8)
        go(9)

    def done(i):
        go(i)
        if i == 0:
            go(6)

    forward_part(x_refs, tables, vecs, *weights, kept[:6], z_refs, (qu_in, od_in, no_wait), done, kept[6])
    out()


def forward(ring, info, parts, xs, tables, vecs, rows):
    tokens = GROUP * rows
    shapes = kept_shapes(tokens, rows) + [((tokens, D), F32)]
    away = [*shapes, ((D, MIXED), LOW), ((SIDE, D), LOW), ((UNITS, D), LOW)] + [(a.shape, F32) for a in tables]
    blocks = (*xs, *tables, *vecs)
    return pl.pallas_call(
        functools.partial(forward_kernel, ring, len(parts)),
        out_shape=(*[shaped((rows, D), LOW)] * GROUP, *[pltpu.HBM(*a) for a in away]),
        in_specs=[smem_spec()] + [any_spec()] * len(parts) + [full_spec(a.shape) for a in blocks],
        out_specs=tuple([full_spec((rows, D))] * GROUP + [far_spec()] * len(away)),
        scratch_shapes=[pltpu.VMEM(*a) for a in shapes]
        + [pltpu.SemaphoreType.DMA((len(away),))]
        + weight_scratch(),
        compiler_params=kernel_params(22),
        cost_estimate=cost(2 * tokens * D * (D + 2 * FF // GROUP), 16 * 1024 * 1024),
        name="forward_shard",
    )(info, *parts, *blocks)


def middle_kernel(ring, count, info, *refs):
    parts, refs = refs[:count], refs[count:]
    x_refs, refs = refs[:4], refs[4:]
    g_refs, refs = refs[:4], refs[4:]
    far_tables, refs = refs[:3], refs[3:]
    vecs, refs = refs[:4], refs[4:]
    dy_refs, refs = refs[:4], refs[4:]
    sums, away, (z_keep, z_send), refs = refs[0], refs[1:6], refs[6:8], refs[8:]
    kept, refs = refs[:6], refs[6:]
    z_refs, tables, refs = refs[:4], refs[4:7], refs[7:]
    (grad, normed, dqu, in_sems, out_sems, z_sems), scratch = refs[:6], refs[6:]
    rows = z_refs[0].shape[0]
    qu_copies, od_copies = weight_copies(ring, info, parts, *scratch)
    for copy in qu_copies:
        copy.start()
    tables_in = started(zip(far_tables, tables), in_sems.at[0])
    for copy in od_copies:
        copy.start()
    pairs = []
    for r, ref in enumerate(g_refs):
        at = ref.shape[0] - rows
        pairs.append((ref.at[pl.ds(at, rows)], grad.at[pl.ds(r * rows, rows)]))
    grad_in = started(pairs, in_sems.at[1])
    go, out = leaving(list(zip([kept[0], kept[3], kept[4], dqu, grad], away)), out_sems)

    def done(i):
        if i in (0, 3, 4):
            go((0, 3, 4).index(i))

    waits = (waiter(qu_copies), waiter(od_copies), tables_in)
    forward_part(x_refs, tables, vecs, *scratch[:3], kept, z_refs, waits, done, normed)
    grad_in()
    go(4)
    z_copies = pair_copies(info, z_refs, z_keep, z_send, z_sems)
    on_core(info, z_copies, lambda copy: copy.start())
    waits = (no_wait, no_wait, no_wait)
    done = functools.partial(go, 3)
    backward_part(grad, normed, tables, *scratch[:3], kept, dqu, dy_refs, sums, waits, done)
    out()
    on_core(info, z_copies, lambda copy: copy.wait())


def middle(ring, info, parts, xs, gs, tables, vecs, rows):
    tokens = GROUP * rows
    shapes = kept_shapes(tokens, rows)
    away = [shapes[0], shapes[3], shapes[4], ((tokens, MIXED), LOW), ((tokens, D), LOW)]
    away += [((2, rows, D), LOW)] * 2
    sums = shaped((1, MIXED + 3 * D), F32)
    return pl.pallas_call(
        functools.partial(middle_kernel, ring, len(parts)),
        out_shape=(*[shaped((rows, D), LOW)] * GROUP, sums, *[pltpu.HBM(*a) for a in away]),
        in_specs=[smem_spec()]
        + [any_spec()] * len(parts)
        + [full_spec(a.shape) for a in xs]
        + [far_spec()] * (GROUP + 3)
        + [full_spec(a.shape) for a in vecs],
        out_specs=tuple([full_spec((rows, D))] * GROUP + [full_spec(sums.shape)] + [far_spec()] * len(away)),
        scratch_shapes=[pltpu.VMEM(*a) for a in shapes]
        + [pltpu.VMEM((rows, D), LOW)] * GROUP
        + table_scratch(tokens, rows)
        + [pltpu.VMEM((tokens, D), LOW), pltpu.VMEM((tokens, D), F32), pltpu.VMEM((tokens, MIXED), LOW)]
        + [pltpu.SemaphoreType.DMA((2,)), pltpu.SemaphoreType.DMA((5,)), pltpu.SemaphoreType.DMA((4,))]
        + weight_scratch(),
        compiler_params=kernel_params(27),
        cost_estimate=cost(4 * tokens * D * (D + 2 * FF // GROUP), 16 * 1024 * 1024),
        name="forward_backward_shard",
    )(info, *parts, *xs, *[far(a) for a in (*gs, *tables)], *vecs)


def backward_kernel(ring, info, *refs):
    g_refs, refs = refs[:4], refs[4:]
    far_kept, far_weights, far_tables, refs = refs[:7], refs[7:10], refs[10:13], refs[13:]
    (dy_keep, dy_send, keep, send), refs = refs[:4], refs[4:]
    kept, refs = refs[:7], refs[7:]
    weights, tables, refs = refs[:3], refs[3:6], refs[6:]
    (grad, dqu, sums, in_sems, out_sems), dy_refs = refs[:5], refs[5:]
    y, qkv, probs, mixed, active, slope, normed = kept
    wqu, wout, wdown = weights
    far_y, far_qkv, far_probs, far_mixed, far_active, far_slope, far_normed = far_kept
    mixed_in = started([(far_mixed, mixed)], in_sems.at[0])
    active_in = started([(far_active, active)], in_sems.at[1])
    units_in = started([*zip(far_weights[1:], weights[1:]), (far_slope, slope)], in_sems.at[2])
    heads_in = started([(far_qkv, qkv), (far_probs, probs), *zip(far_tables, tables)], in_sems.at[3])
    dy_in = started([(far_weights[0], wqu), (far_normed, normed)], in_sems.at[4])
    y_in = started([(far_y, y)], in_sems.at[5])
    rows = g_refs[0].shape[0]
    for r in range(GROUP):
        grad[r * rows : (r + 1) * rows, :] = g_refs[r][...]
    mixed_in()
    od_part(ring, info, mixed, active, grad, keep, send, active_in)
    waits = (units_in, heads_in, dy_in)
    backward_part(grad, normed, tables, *weights, kept[:6], dqu, dy_refs, sums, waits, no_wait)
    copies = pair_copies(info, dy_refs, dy_keep, dy_send, out_sems)
    on_core(info, copies, lambda copy: copy.start())
    y_in()
    qu_part(ring, info, y, dqu, sums, keep, send)
    on_core(info, copies, lambda copy: copy.wait())


def backward(ring, info, gs, held, rows):
    tokens = GROUP * rows
    outs = [shaped((2, rows, D), LOW)] * 2 + [grads_shape(ring)] * 2
    return pl.pallas_call(
        functools.partial(backward_kernel, ring),
        out_shape=tuple(outs),
        in_specs=[smem_spec()] + [full_spec(a.shape) for a in gs] + [far_spec()] * len(held),
        out_specs=tuple(full_spec(a.shape) for a in outs),
        scratch_shapes=[pltpu.VMEM(a.shape, a.dtype) for a in held]
        + [pltpu.VMEM((tokens, D), LOW), pltpu.VMEM((tokens, MIXED), LOW)]
        + [pltpu.VMEM((1, MIXED + 3 * D), F32), pltpu.SemaphoreType.DMA((6,)), pltpu.SemaphoreType.DMA((4,))]
        + [pltpu.VMEM((rows, D), LOW)] * GROUP,
        compiler_params=kernel_params(28),
        cost_estimate=cost(4 * tokens * D * (D + 2 * FF // GROUP), 16 * 1024 * 1024),
        name="backward_shard",
    )(info, *gs, *[far(a) for a in held])


def slot_in(ring, difference, half):
    straight, turned = ring.slot(difference, 0), ring.slot(difference, 1)
    return straight + half * (turned - straight)


QU_TILES = PART // 128
OD_TILES = D // 2 // 128
SIDES = 112


def slot_rows(ring):
    return GROUP * QU_TILES * (D // ring.count) + OD_TILES * (SIDE + UNITS) // ring.size


def grads_shape(ring):
    return shaped((ring.size * slot_rows(ring) + SIDES, 128), LOW)


def od_part(ring, info, mixed, active, grad, keep, send, active_in):
    core, spot = info[0], info[2]
    out_rows = SIDE // ring.size
    ff_rows = UNITS // ring.size
    ahead = GROUP * QU_TILES * (D // ring.count)
    for i, (out, half) in enumerate(((send, 1 - core), (keep, core))):
        columns = pl.ds(pl.multiple_of(half * (D // 2), D // 2), D // 2)
        part = grad[:, columns]
        block = dot_rows(mixed[...], part).astype(LOW)
        if i == 0:
            active_in()
        for there in range(ring.size):
            slot = slot_in(ring, spot ^ there, half)
            piece = dot_rows(active[:, there * ff_rows : (there + 1) * ff_rows], part).astype(LOW)
            for tile in range(OD_TILES):
                lanes = slice(tile * 128, (tile + 1) * 128)
                row = slot * slot_rows(ring) + ahead + tile * (ff_rows + out_rows)
                out[pl.ds(pl.multiple_of(row, 16), ff_rows), :] = piece[:, lanes]
                row = pl.multiple_of(row + ff_rows, 16)
                out[pl.ds(row, out_rows), :] = block[there * out_rows : (there + 1) * out_rows, lanes]


def vector_rows(group, sums):
    width = SIDE // SPREAD
    run = UNITS // SPREAD
    row = lax.broadcasted_iota(jnp.int32, (SIDES, 128), 0)
    pieces = []
    for at in range(0, 3 * SIDE, 128):
        pieces.append(((at // width * GROUP + group) * (width // 128) + at % width // 128, at))
    for at in range(0, UNITS, 128):
        pieces.append((3 * D // 128 + D // 128 + (at // run * GROUP + group) * (run // 128) + at % run // 128, 3 * SIDE + at))
    tail = (4 * D + FF) // 128
    for i, begin in enumerate((3 * D // 128, tail, tail + D // 128, tail + 2 * D // 128)):
        for at in range(0, D, 128):
            pieces.append((begin + at // 128, MIXED + max(i - 1, 0) * D + at))
    return sum(jnp.where(row == where, sums[:, at : at + 128], 0.0) for where, at in pieces)


def qu_part(ring, info, y, dqu, sums, keep, send):
    core, group, spot = info[0], info[1], info[2]
    rows = D // ring.count
    tile = 256
    last = ring.size * slot_rows(ring)
    extra = vector_rows(group, sums).astype(LOW)
    for out, half in ((send, 1 - core), (keep, core)):
        columns = pl.ds(pl.multiple_of(half * PART, 128), PART)
        out[last : last + SIDES, :] = extra
        for at in range(0, D, tile):
            block = dot_rows(y[:, at : at + tile], dqu[:, columns]).astype(LOW)
            for offset in range(0, tile, rows):
                dp = (at + offset) // rows
                slot = slot_in(ring, spot ^ ring.spot_of(dp), half)
                begin = slot * slot_rows(ring) + (group ^ ring.group_of(dp)) * (QU_TILES * rows)
                for i in range(QU_TILES):
                    row = pl.multiple_of(begin + i * rows, 16)
                    out[pl.ds(row, rows), :] = block[offset : offset + rows, i * 128 : (i + 1) * 128]


def grads_kernel(ring, info, far_mixed, far_active, far_grad, far_y, far_dqu, sums, keep, send, *scratch):
    mixed, active, grad, y, dqu, sems = scratch
    grad_in = started([(far_grad, grad), (far_mixed, mixed)], sems.at[0])
    active_in = started([(far_active, active)], sems.at[1])
    rest_in = started([(far_y, y), (far_dqu, dqu)], sems.at[2])
    grad_in()
    od_part(ring, info, mixed, active, grad, keep, send, active_in)
    rest_in()
    qu_part(ring, info, y, dqu, sums, keep, send)


def weight_grads(ring, info, mixed, active, grad, y, dqu, sums):
    blocks = (mixed, active, grad, y, dqu)
    out = grads_shape(ring)
    return pl.pallas_call(
        functools.partial(grads_kernel, ring),
        out_shape=(out, out),
        in_specs=[smem_spec()] + [far_spec()] * len(blocks) + [full_spec(sums.shape)],
        out_specs=(full_spec(out.shape),) * 2,
        scratch_shapes=[pltpu.VMEM(a.shape, LOW) for a in blocks] + [pltpu.SemaphoreType.DMA((3,))],
        compiler_params=kernel_params(20),
        cost_estimate=cost(50 * 10**9, 12 * 1024 * 1024),
        name="weight_grads",
    )(info, *[far(a) for a in blocks], sums)


def fold_kernel(held, came, kept, sent):
    half = (held.shape[0] - SIDES) // 2
    full = 2 * half
    kept[0:half, :] = held[0:half, :].astype(F32) + came[0:half, :].astype(F32)
    sent[0:half, :] = (held[half:full, :].astype(F32) + came[half:full, :].astype(F32)).astype(LOW)
    sides = held[full : full + SIDES, :].astype(LOW).astype(F32) + came[full : full + SIDES, :].astype(F32)
    kept[half : half + SIDES, :] = sides
    sent[half : half + SIDES, :] = sides.astype(LOW)


def fold(held, came):
    half = (held.shape[0] - SIDES) // 2 + SIDES
    outs = (shaped((half, 128), F32), shaped((half, 128), LOW))
    return pl.pallas_call(
        fold_kernel,
        out_shape=outs,
        in_specs=[full_spec(held.shape), full_spec(came.shape)],
        out_specs=tuple(full_spec(a.shape) for a in outs),
        compiler_params=kernel_params(20),
        cost_estimate=cost(0, 1024 * 1024),
        name="fold_gradients",
    )(held, came)


VECTOR_ROWS = (7 * D + FF) // 128


def close_kernel(held, came, before, *outs):
    qus, od, squares = outs[:GROUP], outs[GROUP], outs[GROUP + 1]
    rows = qus[0].shape[0] - SIDES
    full = held.shape[0] - SIDES
    sides = held[full : full + SIDES, :].astype(LOW).astype(F32) + came[full : full + SIDES, :].astype(F32)
    lanes = before[...]
    begin = 0
    for piece in (*qus, od):
        length = rows if piece is not od else od.shape[0]
        here = slice(begin, begin + length)
        begin += length
        total = held[here, :].astype(F32) + came[here, :].astype(F32)
        piece[0:length, :] = total.astype(LOW)
        lanes = lanes + jnp.sum((total * total).reshape(length // 8, 8, 128), axis=0)
    squares[...] = lanes
    high = lanes.astype(LOW).astype(F32)
    rest = sides[VECTOR_ROWS + 16 :]
    sides = jnp.concatenate([sides[:VECTOR_ROWS], high, lanes - high, rest], axis=0).astype(LOW)
    for piece in qus:
        piece[rows : rows + SIDES, :] = sides


def close(ring, held, came, before):
    rows = QU_TILES * (D // ring.count)
    outs = [shaped((rows + SIDES, 128), LOW)] * GROUP
    outs += [shaped((OD_TILES * (SIDE + UNITS) // ring.size, 128), LOW), shaped((8, 128), F32)]
    return pl.pallas_call(
        close_kernel,
        out_shape=tuple(outs),
        in_specs=[full_spec(held.shape), full_spec(came.shape), full_spec(before.shape)],
        out_specs=tuple(full_spec(a.shape) for a in outs),
        compiler_params=kernel_params(16),
        cost_estimate=cost(0, 1024 * 1024),
        name="close_gradients",
    )(held, came, before)


def join_kernel(info, *refs):
    core = info[0]
    firsts, seconds, (od_first, od_second), outs = refs[:4], refs[4:8], refs[8:10], refs[10:]
    sent, vec, squares, vec_squares = outs
    rows = firsts[0].shape[0] - SIDES
    sides = []
    for pieces in (firsts, seconds):
        parts = [a[rows : rows + SIDES, :].astype(F32) for a in pieces]
        sides.append((parts[0] + parts[1]) + (parts[2] + parts[3]))
    squares[...] = sides[0][VECTOR_ROWS : VECTOR_ROWS + 8] + sides[0][VECTOR_ROWS + 8 : VECTOR_ROWS + 16]
    own = [(a[:VECTOR_ROWS] * a[:VECTOR_ROWS]).reshape(VECTOR_ROWS // 8, 8, 128) for a in sides]
    vec_squares[...] = jnp.sum(own[0], axis=0) + jnp.sum(own[1], axis=0)
    vec[...] = jnp.where(core == 0, sides[0], sides[1])

    def write(pieces, od):
        for r in range(GROUP):
            sent[r * rows : (r + 1) * rows, :] = pieces[r][0:rows, :]
        sent[GROUP * rows :, :] = od[...]

    pl.when(core == 0)(functools.partial(write, seconds, od_second))
    pl.when(core == 1)(functools.partial(write, firsts, od_first))


def join(info, firsts, seconds, od_first, od_second):
    rows = firsts[0].shape[0] - SIDES
    outs = (shaped((GROUP * rows + od_first.shape[0], 128), LOW), shaped((SIDES, 128), F32))
    outs += (shaped((8, 128), F32),) * 2
    blocks = (*firsts, *seconds, od_first, od_second)
    return pl.pallas_call(
        join_kernel,
        out_shape=outs,
        in_specs=[smem_spec()] + [full_spec(a.shape) for a in blocks],
        out_specs=tuple(full_spec(a.shape) for a in outs),
        compiler_params=kernel_params(16),
        cost_estimate=cost(0, 1024 * 1024),
        name="join_members",
    )(info, *blocks)


def adam_update(weight, grad, first, second, factor, rate):
    clipped = grad * factor
    first_new = BETA_ONE * first + (1.0 - BETA_ONE) * clipped
    second_new = BETA_TWO * second + (1.0 - BETA_TWO) * clipped * clipped
    first_hat = first_new / (1.0 - BETA_ONE**STEP)
    second_hat = second_new / (1.0 - BETA_TWO**STEP)
    weight_new = weight - rate * (
        first_hat / (jnp.sqrt(second_hat) + ADAM_EPS) + WEIGHT_DECAY * weight
    )
    return (weight_new, first_new, second_new)


def mixed_tile(tile, member):
    at = tile * 128
    if at >= 3 * SIDE:
        return 2, up_column(member, at - 3 * SIDE)
    width = SIDE // SPREAD
    kind, within = at // SIDE, at % SIDE
    return 0, qkv_column(kind, within // width, member) + within % width


def adam_kernel(info, factor_ref, *refs):
    core, group = info[0], info[1]
    step = pl.program_id(0)
    factor = factor_ref[0]
    qus, refs = (refs[:4], refs[4:8]), refs[8:]
    ods, came, refs = refs[:2], refs[2], refs[3:]
    olds, news = refs[:12], refs[12:]
    few, many = olds[0].shape[1], olds[9].shape[1]
    rows = (qus[0][0].shape[0] - SIDES) // QU_TILES
    od_rows = ods[0].shape[0] // OD_TILES

    def update(which, column, grad):
        columns = slice(column, column + 128)
        weight, first, second = [olds[3 * which + i][0, :, columns] for i in range(3)]
        fresh = adam_update(weight, grad.astype(F32), first, second, factor, LEARN_RATE)
        for i in range(3):
            news[3 * which + i][0, :, columns] = fresh[i]

    def rows_of(ref, begin, length):
        return ref[pl.ds(pl.multiple_of(begin + step * length, 16), length), :]

    def both_halves(here):
        for half in range(2):
            for tile in range(OD_TILES):
                column = half * (D // 2) + tile * 128
                ref, begin = (ods[here], 0) if half == here else (came, GROUP * QU_TILES * rows)
                begin = begin + tile * od_rows
                update(3, column, rows_of(ref, begin, many))
                update(1, column, rows_of(ref, begin + od_rows - rows, few))
            for member in range(GROUP):
                if half == here:
                    for g in range(GROUP):

                        @pl.when(group == g)
                        def _(ref=qus[here][member ^ g]):
                            for tile in range(QU_TILES):
                                which, column = mixed_tile(half * QU_TILES + tile, member)
                                update(which, column, rows_of(ref, tile * rows, few))
                else:
                    for tile in range(QU_TILES):
                        which, column = mixed_tile(half * QU_TILES + tile, member)
                        begin = ((group ^ member) * QU_TILES + tile) * rows
                        update(which, column, rows_of(came, begin, few))

    for here in range(2):
        pl.when(core == here)(functools.partial(both_halves, here))


def adam(info, factor, qus, ods, came, olds):
    steps = max(1, olds[0].shape[1] // 16)

    def master(a):
        return pl.BlockSpec((1, a.shape[1] // steps, a.shape[2]), lambda i: (0, i, 0))

    grads = (*qus[0], *qus[1], *ods, came)
    return pl.pallas_call(
        adam_kernel,
        grid=(steps,),
        out_shape=tuple(shaped(a.shape, F32) for a in olds),
        in_specs=[smem_spec(), smem_spec()]
        + [full_spec(a.shape) for a in grads]
        + [master(a) for a in olds],
        out_specs=tuple(master(a) for a in olds),
        compiler_params=kernel_params(28),
        name="adamw",
    )(info, factor, *grads, *[far(a) for a in olds])


def doc_tables(lengths, rows):
    seqs = lengths.shape[0]
    ends = jnp.cumsum(lengths, axis=1)
    places = jnp.arange(rows, dtype=jnp.int32)
    past = places[None, :, None] >= ends[:, None, :]
    begins = jnp.sum(jnp.where(past, lengths[:, None, :], 0), axis=2)
    position = (places[None, :] - begins).reshape(seqs * rows, 1)
    half = ROT // 2
    inverse = 10000.0 ** (-(jnp.arange(half, dtype=F32) * 2.0) / ROT)
    lanes = jnp.concatenate([inverse, inverse, jnp.zeros(HEAD_DIM - ROT, F32)])
    angles = position.astype(F32) * jnp.concatenate([lanes, lanes])[None, :]
    allowed = (places[None, None, :] <= places[None, :, None]) & (places[None, None, :] >= begins[:, :, None])
    mask = jnp.where(allowed, 0.0, -1e30).reshape(seqs * rows, rows).astype(F32)
    return jnp.cos(angles), jnp.sin(angles), mask


def shards(
    x_in,
    cotangent,
    doc_lengths,
    w_qkv,
    w_out,
    w_up,
    w_down,
    vectors,
    m_qkv,
    m_out,
    m_up,
    m_down,
    m_vectors,
    v_qkv,
    v_out,
    v_up,
    v_down,
    v_vectors,
):
    place = Place()
    ring, core, group, spot = place.ring, place.core, place.group, place.spot
    info = place.info()
    local_rows, width = x_in.shape
    seqs, docs = doc_lengths.shape
    rows = local_rows // seqs
    in_rows = w_qkv.shape[1]
    shard = vectors.shape[1]
    members = range(1, GROUP)

    vec_block = jnp.pad(vectors[0].astype(LOW), (0, 8 * 128 - shard)).reshape(8, 128)
    vec_block = jnp.pad(jnp.concatenate([vec_block, vec_block]), ((0, in_rows - 16), (0, 0)))
    keep_qu, send_qu, keep_od, send_od = pack(info, w_qkv, w_out, w_up, w_down, vec_block)
    came_qu = place.sibling(send_qu)
    came_od = place.sibling(send_od)

    def member_columns():
        row = jnp.arange(in_rows)[None, :, None]
        later = (row >= 8) & (row < 16) & (jnp.arange(WIRE)[None, None, :] >= PART)
        qu = jnp.where((core == 0) ^ later, keep_qu, came_qu)
        return [take(qu, group)] + [place.member(take(qu, group ^ r), r) for r in members]

    def gather(block):
        near = [place.member(block, r) for r in (1, 2)]
        return [block, *near, place.member(near[1], 1)]

    def to_owners(slots):
        return [slots[0]] + [place.member(slots[r], r) for r in members]

    def total_of(slots):
        return sum(a.astype(F32) for a in slots)

    def both_vectors(parts):
        pieces = jnp.concatenate([a[:, :, 0:16, PART:] for a in parts])
        pieces = pieces.reshape(ring.size * GROUP, 2, 8 * 128)[:, :, :shard]
        dp = jnp.arange(ring.count, dtype=jnp.int32)
        difference = ring.spot_of(dp) ^ spot
        slot = jnp.where(core == 0, ring.slot(difference, 0), ring.slot(difference, 1))
        vec = jnp.take(pieces, slot * GROUP + (ring.group_of(dp) ^ group), axis=0, mode="clip")
        return [block_vectors(vec[:, block].reshape(-1).astype(F32)) for block in range(2)]

    def block_vectors(vec):
        b_qkv, b_out, b_up, b_down, gain, ln_bias = jnp.split(
            vec, [3 * D, 4 * D, 4 * D + FF, 5 * D + FF, 6 * D + FF]
        )
        b_qkv = take(b_qkv.reshape(3 * SPREAD, GROUP, -1), group, 1).reshape(1, -1)
        b_up = take(b_up.reshape(SPREAD, GROUP, -1), group, 1).reshape(1, -1)
        return (b_qkv, b_up, gain[None], ln_bias[None]), (b_out + b_down)[None], gain[None]

    x_own = take(x_in.reshape(2, rows, width), core)
    cot_own = take(cotangent.reshape(2, rows, width), core)
    len_own = take(doc_lengths, core)
    len_rows = jnp.zeros((16, width), LOW).at[0, :docs].set(len_own.astype(LOW))
    x_sent = jnp.concatenate([x_own, len_rows])

    qu_came = member_columns()
    qu_own = jnp.stack(qu_came)[None]
    x_near = [place.member(after(x_sent, qu_came[1]), r) for r in (1, 2)]
    x_group = [x_sent, *x_near]
    od_own = jnp.where(core == 0, keep_od, came_od)[None]
    od = [jnp.concatenate([od_own, place.across(od_own, 0)])]
    qu_own = after(qu_own, od[0])
    qu = [jnp.concatenate([qu_own, place.across(qu_own, 0)])]
    x_group.append(place.member(after(x_near[1], qu[0], od[0]), 1))
    qu_sibling = [place.sibling(qu[0])]
    od_sibling = [place.sibling(od[0])]
    for step in range(1, ring.bits):
        od.append(place.across(jnp.concatenate(od), step))
        qu.append(place.across(after(jnp.concatenate(qu), od[-1]), step))
    qu_sibling += [place.sibling(a) for a in qu[1:]]
    od_sibling += [place.sibling(a) for a in od[1:]]
    qu_mine = jnp.where(core == 1, keep_qu, came_qu)
    waited = (*x_group[1:], qu_sibling[0], od_sibling[0])
    sent = [after(jnp.concatenate([take(qu_mine, group ^ r), cot_own]), *waited) for r in members]
    qu_cot = [place.member(a, r) for a, r in zip(sent, members)]
    parts_first = (*qu, *od, *qu_sibling, *od_sibling)
    lengths = jnp.stack([a[rows, :docs] for a in x_group]).astype(jnp.int32)
    tables = doc_tables(lengths, rows)
    (vecs_first, bias_first, gain_first), (vecs_second, bias_second, gain_second) = both_vectors(qu)

    first = forward(ring, info, parts_first, x_group, tables, vecs_first, rows)
    kept_first, tables = first[GROUP:], first[-3:]
    qu_cot = [after(a, first[0]) for a in qu_cot]
    came = to_owners(first[:GROUP])
    od_own = after(jnp.where(core == 1, keep_od, came_od)[None], first[0])
    od_late = [jnp.concatenate([od_own, place.across(od_own, 0)])]
    came[1] = after(came[1], od_late[0])
    came[2] = after(came[2], *vecs_second, bias_second, gain_second)
    hidden_first = (x_own.astype(F32) + total_of(came) + bias_first).astype(LOW)
    hidden_group = gather(hidden_first)
    qu_own = jnp.stack([take(qu_mine, group)] + [a[:in_rows] for a in qu_cot])[None]
    qu_late = [jnp.concatenate([qu_own, after(place.across(qu_own, 0), hidden_first)])]
    for step in range(1, ring.bits):
        od_late.append(after(place.across(jnp.concatenate(od_late), step), *hidden_group[1:]))
        qu_late.append(after(place.across(jnp.concatenate(qu_late), step), *hidden_group[1:]))
    qu_sibling, od_sibling = [
        [place.sibling(after(a, *hidden_group[1:])) for a in late] for late in (qu_late, od_late)
    ]
    parts_second = (*qu_late, *od_late, *qu_sibling, *od_sibling)
    second = middle(ring, info, parts_second, hidden_group, [cot_own, *qu_cot], tables, vecs_second, rows)
    sums_second, y_second, mixed_second, active_second, dqu_second, grad_second = second[GROUP : GROUP + 6]
    z_keep, z_send = second[GROUP + 6 :]

    def rows_backward(rows_low, grad_low, dy, gain):
        rows_now = rows_low.astype(F32)
        centered = rows_now - jnp.mean(rows_now, axis=-1, keepdims=True)
        variance = jnp.mean(centered * centered, axis=-1, keepdims=True)
        inverse_std = lax.rsqrt(variance + NORM_EPS)
        normed = centered * inverse_std
        scaled = dy * gain
        inner_mean = jnp.mean(scaled, axis=-1, keepdims=True)
        inner_cross = jnp.mean(scaled * normed, axis=-1, keepdims=True)
        return (grad_low.astype(F32) + inverse_std * (scaled - inner_mean - normed * inner_cross)).astype(LOW)

    def to_members(pieces):
        return [pieces[0]] + [place.member(pieces[r], r) for r in members]

    steps = list(reversed(range(ring.bits)))

    def ring_fold(held, *waited):
        kept, sent = held
        for step in steps[:-1]:
            kept, sent = fold(kept, after(place.across(sent, step), *waited))
        return kept, sent

    dy_second = to_owners(second[:GROUP])
    grads = weight_grads(ring, info, mixed_second, active_second, grad_second, y_second, dqu_second, sums_second)
    mid_grad = rows_backward(hidden_first, cot_own, total_of(dy_second), gain_second)
    mid_group = gather(mid_grad)
    sent = place.sibling(after(grads[1], *dy_second[1:]))
    second_held = ring_fold(fold(grads[0], after(sent, mid_grad)))

    mid_late = [after(mid_group[0], *second_held)] + mid_group[1:]
    z_came = place.toward(after(z_send, *mid_group[1:]), 1)
    dy_keep, dy_send, keep, send = backward(ring, info, mid_late, kept_first, rows)
    z_came = after(z_came, send)
    kept, sent = second_held
    none = jnp.zeros((8, 128), F32)
    *qu_second, od_second, squares_second = close(ring, kept, after(place.across(sent, 0), send), none)
    send = after(send, *qu_second, z_came)
    qu_slots_second = to_members(qu_second)
    kept, sent = ring_fold(fold(keep, place.sibling(send)))
    dy_came = place.toward(after(dy_send, *qu_slots_second[1:]), 1)
    z_step = place.toward((z_keep[1].astype(F32) + z_came[1].astype(F32)).astype(LOW), 0)
    came = after(place.across(after(sent, *qu_slots_second[1:], z_step), 0), dy_came)
    *qu_first, od_first, _ = close(ring, kept, came, squares_second)
    qu_slots_first = to_members(qu_first)
    dy_step = (dy_keep[1].astype(F32) + dy_came[1].astype(F32)).astype(LOW)
    dy_step = place.toward(after(dy_step, *qu_slots_first[1:]), 0)
    grads_sent, vec, squares, vec_squares = join(info, qu_slots_first, qu_slots_second, od_first, od_second)
    squares = squares + place.sibling(squares)
    for step in range(ring.bits):
        squares = squares + place.across(squares, step)
    grads_came = place.sibling(grads_sent)
    dy_step = after(dy_step, squares, grads_came)
    squares = jnp.sum(squares + vec_squares)
    dy_total = dy_keep[0].astype(F32) + dy_came[0].astype(F32) + dy_step.astype(F32)
    z_total = z_keep[0].astype(F32) + z_came[0].astype(F32) + z_step.astype(F32)
    start_grad = rows_backward(x_own, mid_grad, dy_total, gain_first)
    hidden_second = (hidden_first.astype(F32) + z_total + bias_second).astype(LOW)

    grad_norm = jnp.sqrt(squares)
    factor = jnp.minimum(1.0, CLIP_LEVEL / (grad_norm + 1e-06))

    def own_block(one, two):
        came = place.sibling(jnp.where(core == 0, two, one))
        mine = jnp.where(core == 0, one, two)
        return [jnp.where(core == h, mine, came) for h in range(2)]

    vec_share = after(vec, grads_sent).reshape(-1)[: ring.count * shard].reshape(ring.count, shard)
    vec_share = take(vec_share, lax.axis_index("dp"))[None]
    olds = (w_qkv, m_qkv, v_qkv, w_out, m_out, v_out, w_up, m_up, v_up, w_down, m_down, v_down)
    qus = (qu_slots_first, qu_slots_second)
    news = adam(info, factor[None], qus, (od_first, od_second), grads_came, olds)
    new_vec = adam_update(vectors, vec_share, m_vectors, v_vectors, factor, VECTOR_RATE)

    outputs = own_block(jnp.stack([hidden_first, start_grad]), jnp.stack([hidden_second, mid_grad]))
    outputs = jnp.concatenate(outputs, axis=1)
    hidden_out, input_grads = outputs[:1], outputs[1:]
    return (
        hidden_out,
        input_grads,
        *(news[3 * i] for i in range(4)),
        new_vec[0],
        *(news[3 * i + 1] for i in range(4)),
        new_vec[1],
        *(news[3 * i + 2] for i in range(4)),
        new_vec[2],
        grad_norm,
    )


def solution(mesh):
    return jax.shard_map(
        shards,
        mesh=mesh,
        in_specs=(
            P("dp", None),
            P("dp", None),
            P("dp", None),
            P("section", "dp", None),
            P("section", "dp", None),
            P("section", "dp", None),
            P("section", "dp", None),
            P("section", "dp"),
            P("section", "dp", None),
            P("section", "dp", None),
            P("section", "dp", None),
            P("section", "dp", None),
            P("section", "dp"),
            P("section", "dp", None),
            P("section", "dp", None),
            P("section", "dp", None),
            P("section", "dp", None),
            P("section", "dp"),
        ),
        out_specs=(
            P("section", "dp", None),
            P("section", "dp", None),
            P("section", "dp", None),
            P("section", "dp", None),
            P("section", "dp", None),
            P("section", "dp", None),
            P("section", "dp"),
            P("section", "dp", None),
            P("section", "dp", None),
            P("section", "dp", None),
            P("section", "dp", None),
            P("section", "dp"),
            P("section", "dp", None),
            P("section", "dp", None),
            P("section", "dp", None),
            P("section", "dp", None),
            P("section", "dp"),
            P(),
        ),
        check_vma=False,
    )
```
